32 devices in a mesh: exp: 8 (over y, x, core), tp: 4 (over z).
Axes of the slice: x: 2, y: 2, z: 4, core: 2. Of those that a mesh axis runs over, the one named last changes fastest.
Arguments:
- hidden_in: bfloat16 [4096, 2048], P('exp'), may hold values from -6 to 6
- attn_gain: float32 [2048], replicated, may hold values from 0.5 to 1.5
- query_weight: bfloat16 [2048, 2048], P(None, 'tp'), may hold values from -0.125 to 0.125
- key_weight: bfloat16 [2048, 2048], P(None, 'tp'), may hold values from -0.125 to 0.125
- value_weight: bfloat16 [2048, 2048], P(None, 'tp'), may hold values from -0.125 to 0.125
- qnorm_gain: float32 [128], replicated, may hold values from 1 to 2
- knorm_gain: float32 [128], replicated, may hold values from 1 to 2
- out_weight: bfloat16 [2048, 2048], P('tp'), may hold values from -0.5 to 0.5
- ffn_gain: float32 [2048], replicated, may hold values from 0.5 to 1.5
- router_weight: bfloat16 [2048, 16], replicated, may hold values from -0.0625 to 0.0625
- gate_weight: bfloat16 [16, 2048, 1024], P('exp', None, 'tp'), may hold values from -0.125 to 0.125
- up_weight: bfloat16 [16, 2048, 1024], P('exp', None, 'tp'), may hold values from -0.125 to 0.125
- down_weight: bfloat16 [16, 1024, 2048], P('exp', 'tp'), may hold values from -0.5 to 0.5
- expert_routes: int32 [4096, 8], P(('exp', 'tp')), may hold values from 0 to 15, all different within a row; in each aligned block of 128 rows (0 to 127, 128 to 255, ...) at most 128 rows name the same one
- seq_lengths: int32 [8, 4], P('exp'), may hold values from 1 to 256, 512 in all within a row
- grad_out: bfloat16 [4096, 2048], P(('exp', 'tp')), may hold values from -6 to 6
Outputs:
- block_out: bfloat16 [4096, 2048], P(('exp', 'tp'))
- grad_hidden_in: bfloat16 [4096, 2048], P('exp')
- grad_attn_gain: float32 [2048], replicated
- grad_query_weight: float32 [2048, 2048], P(None, 'tp')
- grad_key_weight: float32 [2048, 2048], P(None, 'tp')
- grad_value_weight: float32 [2048, 2048], P(None, 'tp')
- grad_out_weight: float32 [2048, 2048], P('tp')
- grad_qnorm_gain: float32 [128], replicated
- grad_knorm_gain: float32 [128], replicated
- grad_ffn_gain: float32 [2048], replicated
- grad_router_weight: float32 [2048, 16], replicated
- grad_gate_weight: float32 [16, 2048, 1024], P('exp', None, 'tp')
- grad_up_weight: float32 [16, 2048, 1024], P('exp', None, 'tp')
- grad_down_weight: float32 [16, 1024, 2048], P('exp', 'tp')
The draws below stay inside these ranges and needn't reach their ends.
Inputs may be any that keep to these rules, and one draw needn't show every extreme that they name: `expert_routes`: in each aligned block of 128 rows (the rows of one device) no expert is named by more than 128 routes. `seq_lengths`: each row sums to 512 and its largest entry is 256.
All inputs are finite; a program needn't handle non-finite values.
Results may differ from the reference program's by a relative error of at most 0.017.
Values may be sent and summed in bfloat16 or wider, within the bound.
A program may use at most 448 MiB of HBM per device.

```python
import math
import jax
import jax.numpy as jnp
import numpy as np
from jax import lax

D = 2048
H = 16
HD = 128
FF_E = 1024
TOP = 8
SEQS_DEV = 4
TOK_DEV = 512
SEQ_MAX = 256
QROWS = 128
EXPERTS = 16
CAP = 128
TOKENS = 4096
BATCHES = 8
MAXR = 4096


def block_scale(rng, extent, cuts, least, largest):
    level = 1.0
    for dim, shards_of in cuts:
        heights = jax.random.uniform(jax.random.fold_in(jax.random.fold_in(rng, 6), dim), (shards_of,), jnp.float32, least / len(cuts), largest / len(cuts))
        level = level * jnp.repeat(jnp.exp(heights), extent[dim] // shards_of).reshape((-1,) + (1,) * (len(extent) - 1 - dim))
    return level


def length_profile(amount, total, limit, skew):
    loads = [(1 << 20) // math.isqrt(standing ** skew) + 1 for standing in range(2, amount + 1)]
    rest, given = total - limit - (amount - 1), [1] * (amount - 1)
    while rest > 0:
        movable = [i for i in range(amount - 1) if given[i] < limit]
        pool, remaining = sum([loads[i] for i in movable]), rest
        for i in movable:
            addition = min(limit - given[i], max(1, remaining * loads[i] // pool), rest)
            given[i] = given[i] + addition
            rest = rest - addition
    return np.array([limit] + given)


def ragged_sizes(key, count, total, reach, skew):
    if count == 2:
        one = jax.random.randint(key, (), max(1, total - reach), min(reach, total - 1) + 1)
        return jnp.stack([one, total - one])
    lengths = jnp.asarray(length_profile(count, total, reach, skew), jnp.int32)
    couples = (count - 1) // 2
    giver, receiver = lengths[1:1 + 2 * couples:2], lengths[2:2 + 2 * couples:2]
    slack = jnp.minimum(giver - 1, reach - receiver)
    moved = jax.random.randint(jax.random.fold_in(key, 1), (couples,), 0, 1 << 20) % (slack + 1)
    lengths = lengths.at[1:1 + 2 * couples:2].set(giver - moved).at[2:2 + 2 * couples:2].set(receiver + moved)
    return lengths[jax.random.permutation(jax.random.fold_in(key, 2), count)]


def assign_block(stream_key, own, number, rows, count, top, reach, lean):
    sequence = jax.random.permutation(stream_key, count)
    packed, usual = portions_of(count, rows * top, reach, lean, True), portions_of(count, rows * top, reach, lean, False)
    places = jnp.arange(count)

    def named(sizes, turn):
        used = int((sizes > 0).sum())
        fixed = max(1, used // 4)
        shifted = fixed + (places - fixed + turn * (used - fixed)) % max(1, count - fixed)
        return jnp.zeros((count,), jnp.int32).at[sequence[jnp.where(places < fixed, places, shifted)]].set(jnp.asarray(sizes, jnp.int32))

    sizes = jnp.where(number % 4 == 0, named(packed, number // 4), named(usual, number - number // 4 - 1))
    mixed = jax.random.permutation(jax.random.fold_in(own, 3), count)
    source_of, receiver = mixed[0:count // 2 * 2:2], mixed[1:count // 2 * 2:2]
    margin = jnp.minimum(sizes[source_of] - 1, reach - sizes[receiver]) // 2
    margin = jnp.where((source_of == sequence[0]) | (receiver == sequence[0]) | (sizes[receiver] == 0), 0, jnp.maximum(margin, 0))
    shifted = jax.random.randint(jax.random.fold_in(own, 4), (count // 2,), 0, 1 << 20) % (margin + 1)
    sizes = sizes.at[source_of].add(-shifted).at[receiver].add(shifted)
    labels = jnp.searchsorted(jnp.cumsum(sizes), jnp.arange(rows * top), side="right").astype(jnp.int32)
    grid = labels.reshape(top, rows).T
    grid = grid[jax.random.permutation(jax.random.fold_in(own, 1), rows)]
    turn = jax.random.randint(jax.random.fold_in(own, 2), (rows, 1), 0, top)
    return jnp.take_along_axis(grid, (jnp.arange(top)[None, :] + turn) % top, axis=1)


def portions_of(amount, total, bound, lean, full):
    loads = [(1 << 20) // math.isqrt(rank ** lean) + 1 for rank in range(1, amount + 1)]
    largest = bound if full else min(bound, max(-(-total // amount), total * loads[0] // sum(loads)))
    least = 1 if total - largest >= amount - 1 else 0
    given, surplus = [largest] + [least] * (amount - 1), total - largest - least * (amount - 1)
    while surplus > 0:
        movable = [i for i in range(1, amount) if given[i] < largest] or [i for i in range(1, amount) if given[i] < bound]
        mass, remaining = sum([loads[i] for i in movable]), surplus
        for i in movable:
            addition = min(bound - given[i], max(1, remaining * loads[i] // mass), surplus)
            given[i] = given[i] + addition
            surplus = surplus - addition
    return np.array(given)


def bell_draw(rng, extent, spread, limit, cuts=(), held_as=jnp.bfloat16):
    drawn = jax.random.normal(rng, extent, jnp.float32) * spread
    if len(cuts) > 0:
        drawn = block_scale(rng, extent, cuts, -0.22, 0.18) * drawn
    return jnp.clip(drawn, min=-limit, max=limit).astype(held_as)


def setup_inputs(seed: int = 0) -> dict:
    arg_keys = jax.random.split(jax.random.key(seed), 17)
    hidden_in = bell_draw(arg_keys[0], (TOKENS, D), 1.0, 6.0, ((0, 8),))
    attn_gain = jnp.clip(1.0 + 0.1 * jax.random.normal(arg_keys[1], (D,), jnp.float32), 0.5, 1.5)
    query_weight = bell_draw(arg_keys[2], (D, H * HD), D ** -0.5, 0.125, ((1, 4),))
    key_weight = bell_draw(arg_keys[3], (D, H * HD), D ** -0.5, 0.125, ((1, 4),))
    value_weight = bell_draw(arg_keys[4], (D, H * HD), D ** -0.5, 0.125, ((1, 4),))
    qnorm_gain = jnp.clip(jax.random.uniform(arg_keys[5], (HD,), jnp.float32, 1.0, 2.0), 1.0, 2.0)
    knorm_gain = jnp.clip(jax.random.uniform(arg_keys[6], (HD,), jnp.float32, 1.0, 2.0), 1.0, 2.0)
    out_weight = bell_draw(arg_keys[7], (H * HD, D), (H * HD // 16) ** -0.5, 0.5, ((0, 4),))
    ffn_gain = jnp.clip(1.0 + 0.1 * jax.random.normal(arg_keys[8], (D,), jnp.float32), 0.5, 1.5)
    router_weight = bell_draw(arg_keys[9], (D, EXPERTS), (4 * D) ** -0.5, 0.0625)
    gate_weight = bell_draw(arg_keys[10], (EXPERTS, D, FF_E), D ** -0.5, 0.125, ((0, 8), (2, 4)))
    up_weight = bell_draw(arg_keys[11], (EXPERTS, D, FF_E), D ** -0.5, 0.125, ((0, 8), (2, 4)))
    down_weight = bell_draw(arg_keys[12], (EXPERTS, FF_E, D), (FF_E // 8) ** -0.5, 0.5, ((0, 8), (1, 4)))
    expert_routes_keys = jax.random.split(jax.random.fold_in(arg_keys[13], 1), TOKENS // QROWS)
    expert_routes_turns = jax.random.permutation(jax.random.fold_in(arg_keys[13], 3), TOKENS // QROWS)
    expert_routes = jax.vmap(lambda own, number: assign_block(jax.random.fold_in(arg_keys[13], 2), own, number, QROWS, EXPERTS, TOP, CAP, 1))(expert_routes_keys, expert_routes_turns).reshape((TOKENS, TOP))
    seq_lengths = jax.vmap(lambda own: ragged_sizes(own, SEQS_DEV, TOK_DEV, SEQ_MAX, 2))(jax.random.split(arg_keys[14], BATCHES)).reshape((BATCHES, SEQS_DEV)).astype(jnp.int32)
    grad_out = bell_draw(arg_keys[15], (TOKENS, D), 1.0, 6.0, ((0, 32),))
    return {"hidden_in": hidden_in, "attn_gain": attn_gain, "query_weight": query_weight, "key_weight": key_weight, "value_weight": value_weight, "qnorm_gain": qnorm_gain, "knorm_gain": knorm_gain, "out_weight": out_weight, "ffn_gain": ffn_gain, "router_weight": router_weight, "gate_weight": gate_weight, "up_weight": up_weight, "down_weight": down_weight, "expert_routes": expert_routes, "seq_lengths": seq_lengths, "grad_out": grad_out}


eps = 1e-06
rope_base = 10000.0

@jax.custom_vjp
def low(v):
    return lax.optimization_barrier(v.astype(jnp.bfloat16)).astype(jnp.float32)

@jax.custom_vjp
def low_back(v):
    return v

def low_keep(v):
    return (low(v), None)

def low_pass(kept, grad):
    return (grad,)

def back_keep(v):
    return (v, None)

def back_low(kept, grad):
    return (low(grad),)
low.defvjp(low_keep, low_pass)
low_back.defvjp(back_keep, back_low)

def rms_norm(values, gain):
    return values * lax.rsqrt(lax.optimization_barrier(jnp.mean(values * values, axis=-1, keepdims=True)) + eps) * gain

def rotary_tables(lengths_row, count, head_size):
    token_index = jnp.arange(count, dtype=jnp.int32)
    seq_ends = jnp.cumsum(lengths_row).astype(jnp.int32)
    starts = (seq_ends - lengths_row).astype(jnp.int32)
    member = ((token_index[:, None] >= starts[None, :]) & (token_index[:, None] < seq_ends[None, :])).astype(jnp.int32)
    segment = lax.optimization_barrier(jnp.sum(member * jnp.arange(lengths_row.shape[0], dtype=jnp.int32)[None, :], axis=1)).astype(jnp.int32)
    offset = lax.optimization_barrier(jnp.sum(member * starts[None, :], axis=1)).astype(jnp.int32)
    position = (token_index - offset).astype(jnp.float32)
    frequency = rope_base ** (-jnp.arange(0, head_size, 2, dtype=jnp.float32) / head_size)
    angles = position[:, None] * frequency[None, :]
    return (segment, jnp.cos(angles)[:, None, :], jnp.sin(angles)[:, None, :])

def rotate(values, cosine, sine):
    half = values.shape[-1] // 2
    first = values[..., :half]
    second = values[..., half:]
    return jnp.concatenate([first * cosine - second * sine, second * cosine + first * sine], axis=-1)

def head_prep(projected, gain, cosine, sine):
    head_size = gain.shape[0]
    shaped = projected.reshape(projected.shape[0], projected.shape[1] // head_size, head_size)
    return rotate(rms_norm(shaped, gain), cosine, sine)

def attend(block, lengths_row, query_weight, key_weight, value_weight, qnorm_gain, knorm_gain, out_weight):
    count = block.shape[0]
    head_size = qnorm_gain.shape[0]
    segment, cosine, sine = rotary_tables(lengths_row, count, head_size)
    highest = lax.Precision.HIGHEST
    queries = low(head_prep(low_back(jnp.dot(block, query_weight, precision=highest)), qnorm_gain, cosine, sine))
    keys = low(head_prep(low_back(jnp.dot(block, key_weight, precision=highest)), knorm_gain, cosine, sine))
    values = low(low_back(jnp.dot(block, value_weight, precision=highest)))
    values = values.reshape(count, values.shape[1] // head_size, head_size)
    scores = low_back(jnp.einsum('thd,shd->hts', queries, keys, precision=highest) / math.sqrt(head_size))
    same_seq = segment[:, None] == segment[None, :]
    scores = jnp.where(same_seq[None], scores, -1e+30)
    probs = low(jax.nn.softmax(scores, axis=-1))
    mixed = low(low_back(jnp.einsum('hts,shd->thd', probs, values, precision=highest)))
    return jnp.dot(mixed.reshape(count, -1), out_weight, precision=highest)

def reference(hidden_in, attn_gain, query_weight, key_weight, value_weight, qnorm_gain, knorm_gain, out_weight, ffn_gain, router_weight, gate_weight, up_weight, down_weight, expert_routes, seq_lengths, grad_out):
    highest = lax.Precision.HIGHEST
    flat_route = expert_routes.reshape(-1).astype(jnp.int32)
    total_rows = flat_route.shape[0]
    order = jnp.argsort(flat_route, stable=True).astype(jnp.int32)
    counts = lax.optimization_barrier(jnp.sum((flat_route[:, None] == jnp.arange(EXPERTS, dtype=jnp.int32)[None, :]).astype(jnp.int32), axis=0)).astype(jnp.int32)
    starts = (jnp.cumsum(counts) - counts).astype(jnp.int32)
    picked = expert_routes[:, :, None] == jnp.arange(EXPERTS, dtype=jnp.int32)[None, None, :]

    def expert_term(gate_block, up_block, down_block, expert, routed, gates):
        slot = starts[expert] + jnp.arange(MAXR, dtype=jnp.int32)
        live = (jnp.arange(MAXR, dtype=jnp.int32) < counts[expert]).astype(jnp.float32)
        rows = order[jnp.minimum(slot, total_rows - 1)]
        tokens = (rows // TOP).astype(jnp.int32)
        inputs = low_back(routed[tokens])
        gate_act = low_back(jnp.dot(inputs, gate_block, precision=highest))
        up_act = low_back(jnp.dot(inputs, up_block, precision=highest))
        hidden_low = low(jax.nn.silu(gate_act) * up_act)
        outputs = low(low_back(jnp.dot(hidden_low, down_block, precision=highest)))
        weighted = (gates[rows] * live)[:, None] * outputs
        return jnp.zeros((TOKENS, D), jnp.float32).at[tokens].add(weighted)

    def forward_map(hidden_in, attn_gain, query_weight, key_weight, value_weight, qnorm_gain, knorm_gain, out_weight, ffn_gain, router_weight, gate_weight, up_weight, down_weight):
        attend_block = jax.checkpoint(attend)
        term_block = jax.checkpoint(expert_term)
        normed_one = low(rms_norm(hidden_in, attn_gain))

        def group_step(carry, pieces):
            block, lengths_row = pieces
            return (carry, attend_block(block, lengths_row, query_weight, key_weight, value_weight, qnorm_gain, knorm_gain, out_weight))
        unused, attn = lax.scan(group_step, None, (normed_one.reshape(BATCHES, TOK_DEV, D), seq_lengths))
        attn = low_back(attn.reshape(TOKENS, D))
        resid = hidden_in + attn
        routed = low(rms_norm(resid, ffn_gain))
        logits = jnp.dot(routed, router_weight, precision=highest)
        chosen = lax.optimization_barrier(jnp.sum(jnp.where(picked, logits[:, None, :], 0.0), axis=-1))
        gates = jax.nn.softmax(chosen, axis=-1).reshape(-1)

        def expert_step(total, pieces):
            gate_block, up_block, down_block, expert = pieces
            return (total + term_block(gate_block, up_block, down_block, expert, routed, gates), None)
        moe, unused = lax.scan(expert_step, jnp.zeros((TOKENS, D), jnp.float32), (gate_weight, up_weight, down_weight, jnp.arange(EXPERTS, dtype=jnp.int32)))
        return resid + moe
    inputs = tuple((value.astype(jnp.float32) for value in (hidden_in, attn_gain, query_weight, key_weight, value_weight, qnorm_gain, knorm_gain, out_weight, ffn_gain, router_weight, gate_weight, up_weight, down_weight)))
    block_out, pullback = jax.vjp(forward_map, *inputs)
    grads = pullback(grad_out.astype(jnp.float32))
    return (block_out.astype(jnp.bfloat16), grads[0].astype(jnp.bfloat16), grads[1], grads[2], grads[3], grads[4], grads[7], grads[5], grads[6], grads[8], grads[9], grads[10], grads[11], grads[12])
```

```python
import math

import jax
import jax.numpy as jnp
from jax import lax
from jax.sharding import PartitionSpec as P

eps = 1e-06
rope_base = 10000.0


def rms_norm(values, gain):
    return values * lax.rsqrt(jnp.mean(values * values, axis=-1, keepdims=True) + eps) * gain


def rotary_tables(lengths_row, count, head_size):
    token_index = jnp.arange(count, dtype=jnp.int32)
    seq_ends = jnp.cumsum(lengths_row)
    starts = seq_ends - lengths_row
    member = (
        (token_index[:, None] >= starts[None, :]) & (token_index[:, None] < seq_ends[None, :])
    ).astype(jnp.int32)
    segment = jnp.sum(member * jnp.arange(lengths_row.shape[0], dtype=jnp.int32)[None, :], axis=1)
    offset = jnp.sum(member * starts[None, :], axis=1)
    position = (token_index - offset).astype(jnp.float32)
    frequency = rope_base ** (-jnp.arange(0, head_size, 2, dtype=jnp.float32) / head_size)
    angles = position[:, None] * frequency[None, :]
    return (segment, jnp.cos(angles)[:, None, :], jnp.sin(angles)[:, None, :])


def rotate(values, cosine, sine):
    half = values.shape[-1] // 2
    first = values[..., :half]
    second = values[..., half:]
    return jnp.concatenate(
        [first * cosine - second * sine, second * cosine + first * sine], axis=-1
    )


def head_prep(projected, gain, cosine, sine):
    head_size = gain.shape[0]
    shaped = projected.reshape(projected.shape[0], projected.shape[1] // head_size, head_size)
    return rotate(rms_norm(shaped, gain), cosine, sine)


def masked_scores(query_low, key_low, same_seq, head_size):
    scores = jnp.einsum(
        "thd,shd->hts", query_low, key_low, preferred_element_type=jnp.float32
    ) / math.sqrt(head_size)
    return jnp.where(same_seq[None], scores, -1e30)


def slot_experts(routed_low, gates, picked, grad_out, expert_routes, gate_weight, up_weight, down_weight):
    highest = lax.Precision.HIGHEST
    quarter, width = grad_out.shape
    top_count = expert_routes.shape[1]
    experts = picked.shape[2]
    capacity = max(2, 2 * quarter * top_count // experts)
    picked_wide = picked.astype(jnp.float32)
    grad_rows = grad_out.astype(jnp.float32)
    flat_route = expert_routes.reshape(-1)
    flat_pick = picked.reshape(-1, experts).astype(jnp.int32)
    rank = jnp.sum((jnp.cumsum(flat_pick, axis=0) - 1) * flat_pick, axis=1)
    place = flat_route * capacity + rank
    row_token = jnp.arange(quarter * top_count, dtype=jnp.int32) // top_count
    send_rows = (
        jnp.zeros((experts * capacity, width), jnp.bfloat16).at[place].set(routed_low[row_token])
    )
    arrived = lax.all_to_all(
        send_rows.reshape(experts, capacity, width), "exp", split_axis=0, concat_axis=1, tiled=True
    )
    rows_used = lax.all_gather(arrived, "tp", axis=1, tiled=True)
    gate_act = jnp.einsum(
        "erd,edf->erf", rows_used, gate_weight, preferred_element_type=jnp.float32
    )
    up_act = jnp.einsum("erd,edf->erf", rows_used, up_weight, preferred_element_type=jnp.float32)
    hidden_low = (jax.nn.silu(gate_act) * up_act).astype(jnp.bfloat16)
    partial_out = jnp.einsum(
        "erf,efd->erd", hidden_low, down_weight, preferred_element_type=jnp.float32
    )
    expert_out = lax.psum_scatter(partial_out, "tp", scatter_dimension=1, tiled=True)
    returned = lax.all_to_all(
        expert_out.astype(jnp.bfloat16), "exp", split_axis=1, concat_axis=0, tiled=True
    )
    back_rows = (
        returned.reshape(experts * capacity, width)[place]
        .reshape(quarter, top_count, width)
        .astype(jnp.float32)
    )
    moe = jnp.einsum("tk,tkd->td", gates, back_rows, precision=highest)
    grad_gates = jnp.einsum("tkd,td->tk", back_rows, grad_rows, precision=highest)
    grad_chosen = gates * (grad_gates - jnp.sum(gates * grad_gates, axis=-1, keepdims=True))
    grad_logits = jnp.einsum("tke,tk->te", picked_wide, grad_chosen, precision=highest)
    weighted_grad = (
        (gates[:, :, None] * grad_rows[:, None, :])
        .astype(jnp.bfloat16)
        .reshape(quarter * top_count, width)
    )
    send_grads = jnp.zeros((experts * capacity, width), jnp.bfloat16).at[place].set(weighted_grad)
    grad_arrived = lax.all_to_all(
        send_grads.reshape(experts, capacity, width), "exp", split_axis=0, concat_axis=1, tiled=True
    )
    sigmoid_gate = jax.nn.sigmoid(gate_act)
    silu_gate = gate_act * sigmoid_gate
    slope = sigmoid_gate * (1.0 + gate_act * (1.0 - sigmoid_gate))
    grad_used = lax.all_gather(grad_arrived, "tp", axis=1, tiled=True)
    grad_hid = jnp.einsum(
        "erd,efd->erf", grad_used, down_weight, preferred_element_type=jnp.float32
    )
    grad_down = jnp.einsum(
        "erf,erd->efd", hidden_low, grad_used, preferred_element_type=jnp.float32
    )
    grad_gate = (grad_hid * up_act * slope).astype(jnp.bfloat16)
    grad_up = (grad_hid * silu_gate).astype(jnp.bfloat16)
    grad_gate_w = jnp.einsum(
        "erd,erf->edf", rows_used, grad_gate, preferred_element_type=jnp.float32
    )
    grad_up_w = jnp.einsum("erd,erf->edf", rows_used, grad_up, preferred_element_type=jnp.float32)
    input_part = jnp.einsum(
        "erf,edf->erd", grad_gate, gate_weight, preferred_element_type=jnp.float32
    ) + jnp.einsum("erf,edf->erd", grad_up, up_weight, preferred_element_type=jnp.float32)
    grad_input = lax.psum_scatter(input_part, "tp", scatter_dimension=1, tiled=True).astype(
        jnp.bfloat16
    )
    grad_back = lax.all_to_all(grad_input, "exp", split_axis=1, concat_axis=0, tiled=True)
    expert_grad = jnp.sum(
        grad_back.reshape(experts * capacity, width)[place]
        .reshape(quarter, top_count, width)
        .astype(jnp.float32),
        axis=1,
    )
    return moe, grad_logits, expert_grad, grad_gate_w, grad_up_w, grad_down


def dense_experts(routed_low, gates, picked, grad_out, expert_routes, gate_weight, up_weight, down_weight):
    highest = lax.Precision.HIGHEST
    experts = picked.shape[2]
    picked_wide = picked.astype(jnp.float32)
    dense_gates = jnp.einsum("tke,tk->te", picked_wide, gates, precision=highest)
    tokens_all = lax.all_gather(routed_low, ("exp", "tp"), axis=0, tiled=True)
    gates_all = lax.all_gather(dense_gates, ("exp", "tp"), axis=0, tiled=True)
    grads_all = lax.all_gather(grad_out, ("exp", "tp"), axis=0, tiled=True)
    local_experts = gate_weight.shape[0]
    first_expert = lax.axis_index("exp") * local_experts
    own_gates = lax.dynamic_slice_in_dim(gates_all, first_expert, local_experts, 1).T[:, :, None]
    gate_act = jnp.einsum(
        "td,edf->etf", tokens_all, gate_weight, preferred_element_type=jnp.float32
    )
    up_act = jnp.einsum("td,edf->etf", tokens_all, up_weight, preferred_element_type=jnp.float32)
    grad_hid = jnp.einsum(
        "td,efd->etf", grads_all, down_weight, preferred_element_type=jnp.float32
    )
    sigmoid_gate = jax.nn.sigmoid(gate_act)
    silu_gate = gate_act * sigmoid_gate
    hidden = silu_gate * up_act
    gate_sums = jnp.sum(hidden * grad_hid, axis=-1).T
    hidden_low = (hidden * own_gates).astype(jnp.bfloat16)
    partial_out = jnp.einsum(
        "etf,efd->td", hidden_low, down_weight, preferred_element_type=jnp.float32
    ).astype(jnp.bfloat16)
    slope = sigmoid_gate * (1.0 + gate_act * (1.0 - sigmoid_gate))
    grad_hid = grad_hid * own_gates
    grad_gate = (grad_hid * up_act * slope).astype(jnp.bfloat16)
    grad_up = (grad_hid * silu_gate).astype(jnp.bfloat16)
    input_part = (
        jnp.einsum("etf,edf->td", grad_gate, gate_weight, preferred_element_type=jnp.float32)
        + jnp.einsum("etf,edf->td", grad_up, up_weight, preferred_element_type=jnp.float32)
    ).astype(jnp.bfloat16)
    gate_parts = lax.dynamic_update_slice_in_dim(
        jnp.zeros((gates_all.shape[0], experts), jnp.float32), gate_sums, first_expert, 1
    )
    grad_gates = lax.psum_scatter(
        gate_parts, ("exp", "tp"), scatter_dimension=0, tiled=True
    )
    expert_grad = lax.psum_scatter(
        lax.psum_scatter(input_part, "exp", scatter_dimension=0, tiled=True),
        "tp",
        scatter_dimension=0,
        tiled=True,
    ).astype(jnp.float32)
    moe = lax.psum_scatter(
        lax.psum_scatter(partial_out, "exp", scatter_dimension=0, tiled=True),
        "tp",
        scatter_dimension=0,
        tiled=True,
    ).astype(jnp.float32)
    grad_down = jnp.einsum(
        "etf,td->efd", hidden_low, grads_all, preferred_element_type=jnp.float32
    )
    grad_gate_w = jnp.einsum(
        "td,etf->edf", tokens_all, grad_gate, preferred_element_type=jnp.float32
    )
    grad_up_w = jnp.einsum("td,etf->edf", tokens_all, grad_up, preferred_element_type=jnp.float32)
    grad_logits = dense_gates * (
        grad_gates - jnp.sum(dense_gates * grad_gates, axis=-1, keepdims=True)
    )
    return moe, grad_logits, expert_grad, grad_gate_w, grad_up_w, grad_down


def per_device(
    hidden_in,
    attn_gain,
    query_weight,
    key_weight,
    value_weight,
    qnorm_gain,
    knorm_gain,
    out_weight,
    ffn_gain,
    router_weight,
    gate_weight,
    up_weight,
    down_weight,
    expert_routes,
    seq_lengths,
    grad_out,
):
    highest = lax.Precision.HIGHEST
    group_rows = hidden_in.shape[0]
    width = hidden_in.shape[1]
    head_size = qnorm_gain.shape[0]
    quarter = grad_out.shape[0]
    experts = router_weight.shape[1]
    tp_index = lax.axis_index("tp")
    widened = hidden_in.astype(jnp.float32)
    normed_one, norm_one_back = jax.vjp(rms_norm, widened, attn_gain)
    normed_low = normed_one.astype(jnp.bfloat16)
    segment, cosine, sine = rotary_tables(seq_lengths[0], group_rows, head_size)
    same_seq = segment[:, None] == segment[None, :]

    def prepare(projected, gain):
        return head_prep(projected, gain, cosine, sine)

    query_proj = jnp.dot(normed_low, query_weight, preferred_element_type=jnp.float32)
    key_proj = jnp.dot(normed_low, key_weight, preferred_element_type=jnp.float32)
    value_proj = jnp.dot(normed_low, value_weight, preferred_element_type=jnp.float32)
    queries, query_back = jax.vjp(prepare, query_proj, qnorm_gain)
    keys, key_back = jax.vjp(prepare, key_proj, knorm_gain)
    query_low = queries.astype(jnp.bfloat16)
    key_low = keys.astype(jnp.bfloat16)
    value_low = value_proj.astype(jnp.bfloat16).reshape(group_rows, -1, head_size)
    scores = masked_scores(query_low, key_low, same_seq, head_size)
    top_score = jnp.max(scores, axis=-1, keepdims=True)
    log_total = top_score + jnp.log(jnp.sum(jnp.exp(scores - top_score), axis=-1, keepdims=True))
    probs_low = jnp.exp(scores - log_total).astype(jnp.bfloat16)
    mixed = jnp.einsum("hts,shd->thd", probs_low, value_low, preferred_element_type=jnp.float32)
    mixed_low = mixed.astype(jnp.bfloat16).reshape(group_rows, -1)
    attn_part = jnp.dot(mixed_low, out_weight, preferred_element_type=jnp.float32)
    attn_rows = lax.psum_scatter(attn_part, "tp", scatter_dimension=0, tiled=True)
    own_rows = lax.dynamic_slice_in_dim(widened, tp_index * quarter, quarter, 0)
    resid = own_rows + attn_rows
    normed_two, norm_two_back = jax.vjp(rms_norm, resid, ffn_gain)
    routed_low = normed_two.astype(jnp.bfloat16)
    logits = jnp.dot(routed_low, router_weight, preferred_element_type=jnp.float32)
    picked = expert_routes[:, :, None] == jnp.arange(experts, dtype=jnp.int32)[None, None, :]
    picked_wide = picked.astype(jnp.float32)
    chosen = jnp.einsum("tke,te->tk", picked_wide, logits, precision=highest)
    gates = jax.nn.softmax(chosen, axis=-1)
    grad_rows = grad_out.astype(jnp.float32)
    run_experts = dense_experts if experts <= 2 * expert_routes.shape[1] else slot_experts
    moe, grad_logits, expert_grad, grad_gate_w, grad_up_w, grad_down = run_experts(
        routed_low,
        gates,
        picked,
        grad_out,
        expert_routes,
        gate_weight,
        up_weight,
        down_weight,
    )
    block_out = (resid + moe).astype(jnp.bfloat16)
    grad_normed = (
        jnp.dot(grad_logits, router_weight.astype(jnp.float32).T, precision=highest) + expert_grad
    )
    grad_router = jnp.dot(routed_low.astype(jnp.float32).T, grad_logits, precision=highest)
    grad_resid, grad_ffn_gain = norm_two_back(grad_normed)
    grad_resid = grad_resid + grad_rows
    grad_group = lax.all_gather(grad_resid.astype(jnp.bfloat16), "tp", axis=0, tiled=True).astype(
        grad_resid.dtype
    )
    grad_attn_low = grad_group.astype(jnp.bfloat16)
    grad_out_weight = jnp.dot(mixed_low.T, grad_attn_low, preferred_element_type=jnp.float32)
    grad_mixed = jnp.dot(grad_attn_low, out_weight.T, preferred_element_type=jnp.float32)
    grad_mixed_low = grad_mixed.astype(jnp.bfloat16).reshape(group_rows, -1, head_size)
    probs = jnp.exp(masked_scores(query_low, key_low, same_seq, head_size) - log_total)
    grad_probs = jnp.einsum(
        "thd,shd->hts", grad_mixed_low, value_low, preferred_element_type=jnp.float32
    )
    grad_value = jnp.einsum(
        "hts,thd->shd", probs_low, grad_mixed_low, preferred_element_type=jnp.float32
    )
    row_delta = jnp.sum(probs * grad_probs, axis=-1, keepdims=True)
    grad_scores = (probs * (grad_probs - row_delta)).astype(jnp.bfloat16)
    grad_query = jnp.einsum(
        "hts,shd->thd", grad_scores, key_low, preferred_element_type=jnp.float32
    ) / math.sqrt(head_size)
    grad_key = jnp.einsum(
        "hts,thd->shd", grad_scores, query_low, preferred_element_type=jnp.float32
    ) / math.sqrt(head_size)
    grad_query_proj, grad_qgain = query_back(grad_query)
    grad_key_proj, grad_kgain = key_back(grad_key)
    grad_query_low = grad_query_proj.astype(jnp.bfloat16)
    grad_key_low = grad_key_proj.astype(jnp.bfloat16)
    grad_value_low = grad_value.reshape(group_rows, -1).astype(jnp.bfloat16)
    normed_part = (
        jnp.dot(grad_query_low, query_weight.T, preferred_element_type=jnp.float32)
        + jnp.dot(grad_key_low, key_weight.T, preferred_element_type=jnp.float32)
        + jnp.dot(grad_value_low, value_weight.T, preferred_element_type=jnp.float32)
    )
    grad_query_w = jnp.dot(normed_low.T, grad_query_low, preferred_element_type=jnp.float32)
    grad_key_w = jnp.dot(normed_low.T, grad_key_low, preferred_element_type=jnp.float32)
    grad_value_w = jnp.dot(normed_low.T, grad_value_low, preferred_element_type=jnp.float32)
    grad_normed_one, grad_qgain, grad_kgain, grad_ffn_gain, grad_router = lax.psum(
        (normed_part, grad_qgain, grad_kgain, grad_ffn_gain, grad_router), "tp"
    )
    grad_from_norm, grad_attn_gain = norm_one_back(grad_normed_one)
    grad_input_rows = (grad_group + grad_from_norm).astype(jnp.bfloat16)
    low_totals = lax.psum(
        tuple(
            part.astype(jnp.bfloat16)
            for part in (grad_query_w, grad_key_w, grad_value_w, grad_out_weight)
        ),
        "exp",
    )
    totals = tuple(part.astype(jnp.float32) for part in low_totals) + lax.psum(
        (
            grad_attn_gain,
            grad_qgain,
            grad_kgain,
            grad_ffn_gain,
            grad_router,
        ),
        "exp",
    )
    return (
        block_out,
        grad_input_rows,
        totals[4],
        totals[0],
        totals[1],
        totals[2],
        totals[3],
        totals[5],
        totals[6],
        totals[7],
        totals[8],
        grad_gate_w,
        grad_up_w,
        grad_down,
    )


def solution(mesh):
    in_specs = (
        P("exp", None),
        P(),
        P(None, "tp"),
        P(None, "tp"),
        P(None, "tp"),
        P(),
        P(),
        P("tp", None),
        P(),
        P(),
        P("exp", None, "tp"),
        P("exp", None, "tp"),
        P("exp", "tp", None),
        P(("exp", "tp"), None),
        P("exp", None),
        P(("exp", "tp"), None),
    )
    out_specs = (
        P(("exp", "tp"), None),
        P("exp", None),
        P(),
        P(None, "tp"),
        P(None, "tp"),
        P(None, "tp"),
        P("tp", None),
        P(),
        P(),
        P(),
        P(),
        P("exp", None, "tp"),
        P("exp", None, "tp"),
        P("exp", "tp", None),
    )
    return jax.shard_map(
        per_device, mesh=mesh, in_specs=in_specs, out_specs=out_specs, check_vma=False
    )
```

```python
import functools
import math

import jax
import jax.numpy as jnp
from jax import lax
from jax.experimental import pallas as pl
from jax.experimental.pallas import tpu as pltpu
from jax.sharding import PartitionSpec as P

eps = 1e-06
rope_base = 10000.0
gate_lanes = 128
MESH = pl.DeviceIdType.MESH
bf = jnp.bfloat16
f32 = jnp.float32
NT = (((1,), (1,)), ((), ()))
TN = (((0,), (0,)), ((), ()))


def rms_norm(values, gain):
    return values * lax.rsqrt(jnp.mean(values * values, axis=-1, keepdims=True) + eps) * gain


def rotary_tables(lengths_row, count, head_size):
    token_index = jnp.arange(count, dtype=jnp.int32)
    seq_ends = jnp.cumsum(lengths_row)
    starts = seq_ends - lengths_row
    member = (
        (token_index[:, None] >= starts[None, :]) & (token_index[:, None] < seq_ends[None, :])
    ).astype(jnp.int32)
    segment = jnp.sum(member * jnp.arange(lengths_row.shape[0], dtype=jnp.int32)[None, :], axis=1)
    offset = jnp.sum(member * starts[None, :], axis=1)
    position = (token_index - offset).astype(jnp.float32)
    frequency = rope_base ** (-jnp.arange(0, head_size, 2, dtype=jnp.float32) / head_size)
    angles = position[:, None] * frequency[None, :]
    return (segment, jnp.cos(angles)[:, None, :], jnp.sin(angles)[:, None, :])


def rotate(values, cosine, sine):
    half = values.shape[-1] // 2
    first = values[..., :half]
    second = values[..., half:]
    return jnp.concatenate(
        [first * cosine - second * sine, second * cosine + first * sine], axis=-1
    )


def head_prep(projected, gain, cosine, sine):
    head_size = gain.shape[0]
    shaped = projected.reshape(projected.shape[0], projected.shape[1] // head_size, head_size)
    return rotate(rms_norm(shaped, gain), cosine, sine)


def masked_scores(query_low, key_low, same_seq, head_size):
    scores = jnp.einsum(
        "thd,shd->hts", query_low, key_low, preferred_element_type=jnp.float32
    ) / math.sqrt(head_size)
    return jnp.where(same_seq[None], scores, -1e30)


def slot_experts(routed_low, gates, picked, grad_out, expert_routes, gate_weight, up_weight, down_weight):
    highest = lax.Precision.HIGHEST
    quarter, width = grad_out.shape
    top_count = expert_routes.shape[1]
    experts = picked.shape[2]
    capacity = max(2, 2 * quarter * top_count // experts)
    picked_wide = picked.astype(jnp.float32)
    grad_rows = grad_out.astype(jnp.float32)
    flat_route = expert_routes.reshape(-1)
    flat_pick = picked.reshape(-1, experts).astype(jnp.int32)
    rank = jnp.sum((jnp.cumsum(flat_pick, axis=0) - 1) * flat_pick, axis=1)
    place = flat_route * capacity + rank
    row_token = jnp.arange(quarter * top_count, dtype=jnp.int32) // top_count
    send_rows = (
        jnp.zeros((experts * capacity, width), jnp.bfloat16).at[place].set(routed_low[row_token])
    )
    arrived = lax.all_to_all(
        send_rows.reshape(experts, capacity, width), "exp", split_axis=0, concat_axis=1, tiled=True
    )
    rows_used = lax.all_gather(arrived, "tp", axis=1, tiled=True)
    gate_act = jnp.einsum(
        "erd,edf->erf", rows_used, gate_weight, preferred_element_type=jnp.float32
    )
    up_act = jnp.einsum("erd,edf->erf", rows_used, up_weight, preferred_element_type=jnp.float32)
    hidden_low = (jax.nn.silu(gate_act) * up_act).astype(jnp.bfloat16)
    partial_out = jnp.einsum(
        "erf,efd->erd", hidden_low, down_weight, preferred_element_type=jnp.float32
    )
    expert_out = lax.psum_scatter(partial_out, "tp", scatter_dimension=1, tiled=True)
    returned = lax.all_to_all(
        expert_out.astype(jnp.bfloat16), "exp", split_axis=1, concat_axis=0, tiled=True
    )
    back_rows = (
        returned.reshape(experts * capacity, width)[place]
        .reshape(quarter, top_count, width)
        .astype(jnp.float32)
    )
    moe = jnp.einsum("tk,tkd->td", gates, back_rows, precision=highest)
    grad_gates = jnp.einsum("tkd,td->tk", back_rows, grad_rows, precision=highest)
    grad_chosen = gates * (grad_gates - jnp.sum(gates * grad_gates, axis=-1, keepdims=True))
    grad_logits = jnp.einsum("tke,tk->te", picked_wide, grad_chosen, precision=highest)
    weighted_grad = (
        (gates[:, :, None] * grad_rows[:, None, :])
        .astype(jnp.bfloat16)
        .reshape(quarter * top_count, width)
    )
    send_grads = jnp.zeros((experts * capacity, width), jnp.bfloat16).at[place].set(weighted_grad)
    grad_arrived = lax.all_to_all(
        send_grads.reshape(experts, capacity, width), "exp", split_axis=0, concat_axis=1, tiled=True
    )
    sigmoid_gate = jax.nn.sigmoid(gate_act)
    silu_gate = gate_act * sigmoid_gate
    slope = sigmoid_gate * (1.0 + gate_act * (1.0 - sigmoid_gate))
    grad_used = lax.all_gather(grad_arrived, "tp", axis=1, tiled=True)
    grad_hid = jnp.einsum(
        "erd,efd->erf", grad_used, down_weight, preferred_element_type=jnp.float32
    )
    grad_down = jnp.einsum(
        "erf,erd->efd", hidden_low, grad_used, preferred_element_type=jnp.float32
    )
    grad_gate = (grad_hid * up_act * slope).astype(jnp.bfloat16)
    grad_up = (grad_hid * silu_gate).astype(jnp.bfloat16)
    grad_gate_w = jnp.einsum(
        "erd,erf->edf", rows_used, grad_gate, preferred_element_type=jnp.float32
    )
    grad_up_w = jnp.einsum("erd,erf->edf", rows_used, grad_up, preferred_element_type=jnp.float32)
    input_part = jnp.einsum(
        "erf,edf->erd", grad_gate, gate_weight, preferred_element_type=jnp.float32
    ) + jnp.einsum("erf,edf->erd", grad_up, up_weight, preferred_element_type=jnp.float32)
    grad_input = lax.psum_scatter(input_part, "tp", scatter_dimension=1, tiled=True).astype(
        jnp.bfloat16
    )
    grad_back = lax.all_to_all(grad_input, "exp", split_axis=1, concat_axis=0, tiled=True)
    expert_grad = jnp.sum(
        grad_back.reshape(experts * capacity, width)[place]
        .reshape(quarter, top_count, width)
        .astype(jnp.float32),
        axis=1,
    )
    return moe, grad_logits, expert_grad, grad_gate_w, grad_up_w, grad_down


def plane_at(z, step):
    from_end = step
    from_middle = jnp.where(step == 0, 1, jnp.where(step == 1, 0, step))
    base = jnp.where((z == 0) | (z == 3), from_end, from_middle)
    return jnp.where(z < 2, base, 3 - base)

Z, X, Y, FX, FY, CO, CX, CY, CA, CB = range(10)

def gather_kernel(own_ref, grad_hbm, wg_hbm, wu_hbm, wd_hbm,
                  act_hbm, dg_ref, du_ref, dd_ref,
                  rows, grads, wg, wu, wd, act, send, up_send, recv, load, store, wload):
    e = lax.axis_index("exp")
    z = lax.axis_index("tp")
    ex, ey, ec, ed = (jnp.bitwise_xor(e, m) for m in (2, 4, 1, 6))
    width = wg.shape[1]
    quarter = own_ref.shape[0]
    half = quarter // 2
    hid = wg.shape[2]
    experts_here = wg.shape[0]
    at_x, at_y, at_c = (ex, z), (ey, z), (ec, z)
    at_up, at_down = (e, z + 1), (e, z - 1)

    wcopies = [pltpu.make_async_copy(s, d, wload.at[i]) for i, (s, d) in enumerate(((wg_hbm, wg), (wu_hbm, wu), (wd_hbm, wd)))]
    for c in wcopies: c.start()

    def grad_copy(step):
        k, h = step // 2, lax.rem(step, 2)
        first = jnp.bitwise_xor(jnp.bitwise_and(e, 4), h * 4)
        return pltpu.make_async_copy(grad_hbm.at[pl.ds(first, 4), plane_at(z, k)], grads.at[h], load.at[h])
    grad_copy(0).start()

    bar = pltpu.get_barrier_semaphore()
    for d in (at_x, at_y, at_c):
        pl.semaphore_signal(bar, inc=1, device_id=d, device_id_type=MESH)
    @pl.when(z < 3)
    def _(): pl.semaphore_signal(bar, inc=1, device_id=at_up, device_id_type=MESH)
    @pl.when(z > 0)
    def _(): pl.semaphore_signal(bar, inc=1, device_id=at_down, device_id_type=MESH)
    pl.semaphore_wait(bar, 3 + jnp.where(z < 3, 1, 0) + jnp.where(z > 0, 1, 0))

    TOP, BOT, ALLR = pl.ds(0, half), pl.ds(half, half), pl.ds(0, quarter)

    def copy(kind, plane, group, part, to, src=None, sem=None):
        place = rows.at[plane, group, part]
        return pltpu.make_async_remote_copy(
            src_ref=place if src is None else src, dst_ref=place,
            send_sem=(send.at[kind, plane] if sem is None else sem), recv_sem=recv.at[kind, plane],
            device_id=to, device_id_type=MESH)

    def up(plane, src=None): return copy(Z, plane, e, ALLR, at_up, src, up_send.at[plane])
    def down(plane, src=None): return copy(Z, plane, e, ALLR, at_down, src)
    def to_x(plane, src=None): return copy(X, plane, e, ALLR, at_x, src)
    def to_y(plane, src=None): return copy(Y, plane, e, ALLR, at_y, src)
    def to_c(plane, src=None): return copy(CO, plane, e, ALLR, at_c, src)
    def fwd_y(plane): return copy(FY, plane, ex, TOP, at_y)
    def fwd_x(plane): return copy(FX, plane, ey, BOT, at_x)
    def c_x(plane): return copy(CX, plane, ex, ALLR, at_c)
    def c_y(plane): return copy(CY, plane, ey, ALLR, at_c)
    def c_a(plane): return copy(CA, plane, ed, TOP, at_c)
    def c_b(plane): return copy(CB, plane, ed, BOT, at_c)

    def arrived(kind, plane, group, part):
        place = rows.at[plane, group, part]
        pltpu.make_async_copy(place, place, recv.at[kind, plane]).wait()

    @pl.when(z < 3)
    def _(): up(z, own_ref).start()
    @pl.when(z > 0)
    def _(): down(z, own_ref).start()
    to_x(z, own_ref).start()
    to_y(z, own_ref).start()
    to_c(z, own_ref).start()
    rows[z, e] = own_ref[...]

    def serve_line(k):
        p = plane_at(z, k)
        arrived(Z, p, e, ALLR)
        @pl.when((p < z) & (z < 3))
        def _(): up(p).start()
        @pl.when((p > z) & (z > 0))
        def _(): down(p).start()
        to_x(p).start()
        to_y(p).start()
        to_c(p).start()

    def serve_sides(k):
        p = plane_at(z, k)
        arrived(X, p, ex, ALLR)
        fwd_y(p).start()
        c_x(p).start()
        arrived(Y, p, ey, ALLR)
        fwd_x(p).start()
        c_y(p).start()

    def serve_far(k):
        p = plane_at(z, k)
        arrived(FY, p, ed, TOP)
        c_a(p).start()
        arrived(FX, p, ed, BOT)
        c_b(p).start()

    def store_copy(step):
        k, h = step // 2, lax.rem(step, 2)
        first = jnp.bitwise_xor(jnp.bitwise_and(e, 4), h * 4)
        return pltpu.make_async_copy(act, act_hbm.at[pl.ds(first // 2, 2), :, plane_at(z, k)], store)

    middle = (z == 1) | (z == 2)
    serve_line(1)
    @pl.when(middle)
    def _(): serve_line(2)
    serve_sides(0)
    for c in wcopies: c.wait()

    def step_body(step, _):
        k, h = step // 2, lax.rem(step, 2)
        p = plane_at(z, k)
        first = jnp.bitwise_xor(jnp.bitwise_and(e, 4), h * 4)
        sib_x = jnp.bitwise_xor(ec, 2)
        sib_y = jnp.bitwise_xor(ec, 4)
        sib_d = jnp.bitwise_xor(ec, 6)
        @pl.when(h == 0)
        def _():
            arrived(CO, p, ec, ALLR)
            arrived(CX, p, sib_x, ALLR)
        @pl.when(h == 1)
        def _():
            arrived(CY, p, sib_y, ALLR)
            arrived(CA, p, sib_d, TOP)
            arrived(CB, p, sib_d, BOT)
        grad_copy(step).wait()
        @pl.when(step < 7)
        def _(): grad_copy(step + 1).start()
        lane = lax.broadcasted_iota(jnp.int32, (4 * quarter, gate_lanes), 1)

        def expert_body(j, _):
            x = rows[p, pl.ds(first, 4), :, :width].reshape(4 * quarter, width)
            g = grads[h].reshape(4 * quarter, width)
            extra = rows[p, pl.ds(first, 4), :, width:].reshape(4 * quarter, gate_lanes).astype(f32)
            expert = e * experts_here + j
            mine = (lane == expert) | (lane == expert + gate_lanes // 2)
            gate = jnp.sum(jnp.where(mine, extra, 0.0), axis=1, keepdims=True)
            ga = jnp.dot(x, wg[j], preferred_element_type=f32)
            ua = jnp.dot(x, wu[j], preferred_element_type=f32)
            gh = lax.dot_general(g, wd[j], (((1,), (1,)), ((), ())), preferred_element_type=f32)
            sg = jax.nn.sigmoid(ga)
            silu = ga * sg
            hidden = silu * ua
            score = jnp.sum(hidden * gh, axis=1, keepdims=True)
            gh = gh * gate
            hg = (hidden * gate).astype(bf)
            da = (gh * ua * (sg * (1.0 + ga * (1.0 - sg)))).astype(bf)
            du = (gh * silu).astype(bf)
            @pl.when((step > 0) & (j == 0))
            def _(): store_copy(step - 1).wait()
            base = j * 3 * hid
            shape3 = (2, 2, quarter, hid)
            act[:, :, :, pl.ds(pl.multiple_of(base, hid), hid)] = da.reshape(shape3)
            act[:, :, :, pl.ds(pl.multiple_of(base + hid, hid), hid)] = du.reshape(shape3)
            act[:, :, :, pl.ds(pl.multiple_of(base + 2 * hid, hid), hid)] = hg.reshape(shape3)
            scores = jnp.where(lane == expert, score, 0.0).astype(bf).reshape(2, 2, quarter, gate_lanes)
            act[:, :, :, pl.ds(pl.multiple_of(experts_here * 3 * hid + j * gate_lanes, gate_lanes), gate_lanes)] = scores
            @pl.when(step == 0)
            def _():
                dg_ref[j] = jnp.zeros(dg_ref.shape[1:], f32)
                du_ref[j] = jnp.zeros(du_ref.shape[1:], f32)
                dd_ref[j] = jnp.zeros(dd_ref.shape[1:], f32)
            slot = 2 * step + j
            for at, work, which in (
                (1, serve_far, 0), (2, serve_sides, 1), (4, serve_far, 1), (5, serve_sides, 2),
                (7, serve_far, 2), (7, serve_sides, 3), (9, serve_far, 3)):
                @pl.when(slot == at)
                def _(): work(which)
            @pl.when((slot == 1) & middle)
            def _(): serve_line(3)
            @pl.when((slot == 1) & ~middle)
            def _(): serve_line(2)
            @pl.when((slot == 3) & ~middle)
            def _(): serve_line(3)
            dd_ref[j] += lax.dot_general(hg, g, TN, preferred_element_type=f32)
            dg_ref[j] += lax.dot_general(x, da, TN, preferred_element_type=f32)
            du_ref[j] += lax.dot_general(x, du, TN, preferred_element_type=f32)
            return 0
        lax.fori_loop(0, experts_here, expert_body, 0)
        store_copy(step).start()
        return 0
    lax.fori_loop(0, 8, step_body, 0)
    store_copy(7).wait()

    def drain(k, _):
        p = plane_at(z, k)
        @pl.when((z < 3) & (p <= z))
        def _(): up(p).wait_send()
        @pl.when((z > 0) & (p >= z))
        def _(): down(p).wait_send()
        for c in (to_x, to_y, to_c, fwd_y, fwd_x, c_x, c_y, c_a, c_b):
            c(p).wait_send()
        return 0
    lax.fori_loop(0, 4, drain, 0)

def gather_experts(own, grads_all, wg, wu, wd):
    n_here, width, hid = wg.shape
    quarter, wide = own.shape
    lanes = wide - width
    cols = n_here * 3 * hid + n_here * lanes
    any_ = pl.BlockSpec(memory_space=pl.ANY)
    vm = pl.BlockSpec(memory_space=pltpu.VMEM)
    return pl.pallas_call(
        gather_kernel,
        out_shape=(jax.ShapeDtypeStruct((4, 2, 4, quarter, cols), bf),
                   jax.ShapeDtypeStruct(wg.shape, f32), jax.ShapeDtypeStruct(wu.shape, f32), jax.ShapeDtypeStruct(wd.shape, f32)),
        in_specs=[vm, any_, any_, any_, any_],
        out_specs=(any_, vm, vm, vm),
        scratch_shapes=[
            pltpu.VMEM((4, 8, quarter, wide), bf),
            pltpu.VMEM((2, 4, quarter, width), bf),
            pltpu.VMEM(wg.shape, bf), pltpu.VMEM(wu.shape, bf), pltpu.VMEM(wd.shape, bf),
            pltpu.VMEM((2, 2, quarter, cols), bf),
            pltpu.SemaphoreType.DMA((10, 4)), pltpu.SemaphoreType.DMA((4,)), pltpu.SemaphoreType.DMA((10, 4)),
            pltpu.SemaphoreType.DMA((2,)), pltpu.SemaphoreType.DMA, pltpu.SemaphoreType.DMA((3,)),
        ],
        compiler_params=pltpu.CompilerParams(collective_id=1, has_side_effects=True, vmem_limit_bytes=62 << 20),
        cost_estimate=pl.CostEstimate(flops=12 * 4096 * 2048 * hid * n_here, bytes_accessed=64 << 20, transcendentals=0),
    )(own, grads_all, wg, wu, wd)


def input_product(acts, weights, cols):
    wg, wu = weights
    hid = wg.shape[2]
    total = None
    for j in range(wg.shape[0]):
        for w, i in ((wg, 0), (wu, 1)):
            lhs = acts[:, :, (3 * j + i) * hid:(3 * j + i + 1) * hid].reshape(-1, hid)
            part = lax.dot_general(lhs, w[j, cols, :], NT, preferred_element_type=f32)
            total = part if total is None else total + part
    return total

def output_product(acts, weights, cols):
    (wd,) = weights
    hid = wd.shape[1]
    total = None
    for j in range(wd.shape[0]):
        lhs = acts[:, :, (3 * j + 2) * hid:(3 * j + 3) * hid].reshape(-1, hid)
        part = jnp.dot(lhs, wd[j, :, cols], preferred_element_type=f32)
        total = part if total is None else total + part
    return total

C1, DT, DB, XT, XB, YT, YB, ZU, ZD = range(9)

def scatter_kernel(product, n_weights, width, score_at, *refs):
    act_hbm, *rest = refs
    w_hbm, rest = rest[:n_weights], rest[n_weights:]
    out_ref, acts, *rest = rest
    weights, rest = rest[:n_weights], rest[n_weights:]
    sendbuf, acc, r1, rdt, rdb, rx, ry, rzu, rzd, send, recv, load, wload = rest
    e = lax.axis_index("exp")
    z = lax.axis_index("tp")
    quarter = acc.shape[2]
    half = quarter // 2
    chip = e // 2
    core = lax.rem(e, 2)
    chip_x, chip_y, chip_d = (jnp.bitwise_xor(chip, m) for m in (1, 2, 3))
    at_x, at_y, at_c = (jnp.bitwise_xor(e, 2), z), (jnp.bitwise_xor(e, 4), z), (jnp.bitwise_xor(e, 1), z)
    at_up, at_down = (e, z + 1), (e, z - 1)
    TOP, BOT = pl.ds(0, half), pl.ds(half, half)

    wcopies = [pltpu.make_async_copy(s, d, wload.at[i]) for i, (s, d) in enumerate(zip(w_hbm, weights))]
    for c in wcopies: c.start()

    def act_copy(n):
        k, own = n // 2, lax.rem(n, 2)
        which = jnp.bitwise_xor(core, 1 - own)
        return pltpu.make_async_copy(act_hbm.at[:, which, plane_at(z, 3 - k)], acts.at[own], load.at[own])
    act_copy(0).start()

    bar = pltpu.get_barrier_semaphore()
    for d in (at_x, at_y, at_c):
        pl.semaphore_signal(bar, inc=1, device_id=d, device_id_type=MESH)
    @pl.when(z < 3)
    def _(): pl.semaphore_signal(bar, inc=1, device_id=at_up, device_id_type=MESH)
    @pl.when(z > 0)
    def _(): pl.semaphore_signal(bar, inc=1, device_id=at_down, device_id_type=MESH)
    pl.semaphore_wait(bar, 3 + jnp.where(z < 3, 1, 0) + jnp.where(z > 0, 1, 0))
    for c in wcopies: c.wait()

    def remote(kind, k, src, dst, to):
        return pltpu.make_async_remote_copy(src_ref=src, dst_ref=dst, send_sem=send.at[kind, k], recv_sem=recv.at[kind, k],
                                            device_id=to, device_id_type=MESH)
    def to_core(k): return remote(C1, k, sendbuf.at[lax.rem(k, 2)], r1.at[k], at_c)
    def far_x(k): return remote(DT, k, acc.at[k, chip_d, TOP], rdt.at[k], at_x)
    def far_y(k): return remote(DB, k, acc.at[k, chip_d, BOT], rdb.at[k], at_y)
    def x_top(k): return remote(XT, k, acc.at[k, chip_x, TOP], rx.at[k, TOP], at_x)
    def x_bot(k): return remote(XB, k, acc.at[k, chip_x, BOT], rx.at[k, BOT], at_x)
    def y_top(k): return remote(YT, k, acc.at[k, chip_y, TOP], ry.at[k, TOP], at_y)
    def y_bot(k): return remote(YB, k, acc.at[k, chip_y, BOT], ry.at[k, BOT], at_y)
    def line_up(k, p): return remote(ZU, p, acc.at[k, chip], rzu.at[p], at_up)
    def line_down(k, p): return remote(ZD, p, acc.at[k, chip], rzd.at[p], at_down)
    def arrived(kind, k, place):
        pltpu.make_async_copy(place, place, recv.at[kind, k]).wait()

    cols_step = 512
    def multiply(slot, target):
        def tile(n, _):
            cols = pl.ds(pl.multiple_of(n * cols_step, cols_step), cols_step)
            total = product(acts.at[slot], weights, cols)
            target[:, :, cols] = total.astype(bf).reshape(4, quarter, cols_step)
            return 0
        lax.fori_loop(0, width // cols_step, tile, 0)
        if score_at is not None:
            lanes = target.shape[2] - width
            target[:, :, width:] = acts[slot, :, :, score_at:score_at + lanes] + acts[slot, :, :, score_at + lanes:score_at + 2 * lanes]

    def add(place, other):
        place[...] = (place[...].astype(f32) + other[...].astype(f32)).astype(bf)

    def begin(k):
        act_copy(2 * k).wait()
        act_copy(2 * k + 1).start()
        @pl.when(k >= 2)
        def _(): to_core(k - 2).wait_send()
        multiply(0, sendbuf.at[lax.rem(k, 2)])
        to_core(k).start()
        act_copy(2 * k + 1).wait()
        @pl.when(k < 3)
        def _(): act_copy(2 * k + 2).start()
        multiply(1, acc.at[k])
        arrived(C1, k, r1.at[k])
        add(acc.at[k, chip_d], r1.at[k, chip_d])
        far_x(k).start()
        far_y(k).start()
        add(acc.at[k, chip_x], r1.at[k, chip_x])
        x_top(k).start()
        add(acc.at[k, chip_y], r1.at[k, chip_y])
        y_bot(k).start()
        add(acc.at[k, chip], r1.at[k, chip])

    def middle(k):
        arrived(DB, k, rdb.at[k])
        add(acc.at[k, chip_x, BOT], rdb.at[k])
        x_bot(k).start()
        arrived(DT, k, rdt.at[k])
        add(acc.at[k, chip_y, TOP], rdt.at[k])
        y_top(k).start()

    def finish(k):
        p = plane_at(z, 3 - k)
        arrived(XT, k, rx.at[k, TOP])
        arrived(YB, k, ry.at[k, BOT])
        arrived(XB, k, rx.at[k, BOT])
        arrived(YT, k, ry.at[k, TOP])
        total = acc[k, chip].astype(f32) + rx[k].astype(f32) + ry[k].astype(f32)
        out_ref[...] = total
        @pl.when((z > 0) & (p >= z))
        def _():
            arrived(ZU, p, rzu.at[p])
            out_ref[...] += rzu[p].astype(f32)
        @pl.when((z < 3) & (p <= z))
        def _():
            arrived(ZD, p, rzd.at[p])
            out_ref[...] += rzd[p].astype(f32)
        @pl.when(p != z)
        def _():
            acc[k, chip] = out_ref[...].astype(bf)
        @pl.when(p > z)
        def _(): line_up(k, p).start()
        @pl.when(p < z)
        def _(): line_down(k, p).start()

    def body(k, _):
        @pl.when(k < 4)
        def _(): begin(k)
        @pl.when(k > 0)
        def _(): finish(k - 1)
        @pl.when(k < 4)
        def _(): middle(k)
        return 0
    lax.fori_loop(0, 5, body, 0)

    def drain(k, _):
        p = plane_at(z, 3 - k)
        @pl.when(k >= 2)
        def _(): to_core(k).wait_send()
        for c in (far_x, far_y, x_top, x_bot, y_top, y_bot):
            c(k).wait_send()
        @pl.when(p > z)
        def _(): line_up(k, p).wait_send()
        @pl.when(p < z)
        def _(): line_down(k, p).wait_send()
        return 0
    lax.fori_loop(0, 4, drain, 0)

def scatter_sums(act, weights, product, scores, collective_id):
    hid = min(weights[0].shape[1:])
    width = max(weights[0].shape[1:])
    n_here = weights[0].shape[0]
    quarter, cols = act.shape[3:]
    score_at = 3 * hid * n_here
    lanes = (cols - score_at) // n_here
    wide = width + (lanes if scores else 0)
    any_ = pl.BlockSpec(memory_space=pl.ANY)
    n = len(weights)
    return pl.pallas_call(
        functools.partial(scatter_kernel, product, n, width, score_at if scores else None),
        out_shape=jax.ShapeDtypeStruct((quarter, wide), f32),
        in_specs=[any_] * (1 + n),
        out_specs=pl.BlockSpec(memory_space=pltpu.VMEM),
        scratch_shapes=[pltpu.VMEM((2, 4, quarter, cols), bf)] + [pltpu.VMEM(w.shape, bf) for w in weights] + [
            pltpu.VMEM((2, 4, quarter, wide), bf),
            pltpu.VMEM((4, 4, quarter, wide), bf),
            pltpu.VMEM((4, 4, quarter, wide), bf),
            pltpu.VMEM((4, quarter // 2, wide), bf), pltpu.VMEM((4, quarter // 2, wide), bf),
            pltpu.VMEM((4, quarter, wide), bf), pltpu.VMEM((4, quarter, wide), bf),
            pltpu.VMEM((4, quarter, wide), bf), pltpu.VMEM((4, quarter, wide), bf),
            pltpu.SemaphoreType.DMA((9, 4)), pltpu.SemaphoreType.DMA((9, 4)),
            pltpu.SemaphoreType.DMA((2,)), pltpu.SemaphoreType.DMA((n,)),
        ],
        compiler_params=pltpu.CompilerParams(collective_id=collective_id, has_side_effects=True, vmem_limit_bytes=60 << 20),
    )(act, *weights)


def dense_experts(routed_low, gates, picked, grads_all, gate_weight, up_weight, down_weight):
    highest = lax.Precision.HIGHEST
    quarter, experts = picked.shape[0], picked.shape[2]
    width = routed_low.shape[1]
    picked_wide = picked.astype(f32)
    dense_gates = jnp.einsum("tke,tk->te", picked_wide, gates, precision=highest)
    high = dense_gates.astype(bf)
    low = (dense_gates - high.astype(f32)).astype(bf)
    pad = jnp.zeros((quarter, gate_lanes // 2 - experts), bf)
    own = jnp.concatenate([routed_low, high, pad, low, pad], axis=1)
    act, grad_gate_w, grad_up_w, grad_down = gather_experts(
        own, grads_all, gate_weight, up_weight, down_weight
    )
    sums = scatter_sums(act, (gate_weight, up_weight), input_product, True, 2)
    moe = scatter_sums(act, (down_weight,), output_product, False, 3)
    expert_grad = sums[:, :width]
    grad_gates = sums[:, width : width + experts]
    grad_logits = dense_gates * (
        grad_gates - jnp.sum(dense_gates * grad_gates, axis=-1, keepdims=True)
    )
    return moe, grad_logits, expert_grad, grad_gate_w, grad_up_w, grad_down


def per_device(
    fits,
    hidden_in,
    attn_gain,
    query_weight,
    key_weight,
    value_weight,
    qnorm_gain,
    knorm_gain,
    out_weight,
    ffn_gain,
    router_weight,
    gate_weight,
    up_weight,
    down_weight,
    expert_routes,
    seq_lengths,
    grad_out,
):
    highest = lax.Precision.HIGHEST
    group_rows = hidden_in.shape[0]
    width = hidden_in.shape[1]
    head_size = qnorm_gain.shape[0]
    quarter = grad_out.shape[0]
    experts = router_weight.shape[1]
    tp_index = lax.axis_index("tp")
    widened = hidden_in.astype(jnp.float32)
    normed_one = rms_norm(widened, attn_gain)
    normed_low = normed_one.astype(jnp.bfloat16)
    segment, cosine, sine = rotary_tables(seq_lengths[0], group_rows, head_size)
    same_seq = segment[:, None] == segment[None, :]

    def prepare(projected, gain):
        return head_prep(projected, gain, cosine, sine)

    query_proj = jnp.dot(normed_low, query_weight, preferred_element_type=jnp.float32)
    key_proj = jnp.dot(normed_low, key_weight, preferred_element_type=jnp.float32)
    value_proj = jnp.dot(normed_low, value_weight, preferred_element_type=jnp.float32)
    queries, query_back = jax.vjp(prepare, query_proj, qnorm_gain)
    keys, key_back = jax.vjp(prepare, key_proj, knorm_gain)
    query_low = queries.astype(jnp.bfloat16)
    key_low = keys.astype(jnp.bfloat16)
    value_low = value_proj.astype(jnp.bfloat16).reshape(group_rows, -1, head_size)
    scores = masked_scores(query_low, key_low, same_seq, head_size)
    top_score = jnp.max(scores, axis=-1, keepdims=True)
    log_total = top_score + jnp.log(jnp.sum(jnp.exp(scores - top_score), axis=-1, keepdims=True))
    probs_low = jnp.exp(scores - log_total).astype(jnp.bfloat16)
    mixed = jnp.einsum("hts,shd->thd", probs_low, value_low, preferred_element_type=jnp.float32)
    mixed_low = mixed.astype(jnp.bfloat16).reshape(group_rows, -1)
    attn_part = jnp.dot(mixed_low, out_weight, preferred_element_type=jnp.float32)
    attn_rows = lax.psum_scatter(attn_part, "tp", scatter_dimension=0, tiled=True)
    own_rows = lax.dynamic_slice_in_dim(widened, tp_index * quarter, quarter, 0)
    resid = own_rows + attn_rows
    normed_two, norm_two_back = jax.vjp(rms_norm, resid, ffn_gain)
    routed_low = normed_two.astype(jnp.bfloat16)
    logits = jnp.dot(routed_low, router_weight, preferred_element_type=jnp.float32)
    picked = expert_routes[:, :, None] == jnp.arange(experts, dtype=jnp.int32)[None, None, :]
    picked_wide = picked.astype(jnp.float32)
    chosen = jnp.einsum("tke,te->tk", picked_wide, logits, precision=highest)
    gates = jax.nn.softmax(chosen, axis=-1)
    grad_rows = grad_out.astype(jnp.float32)
    if fits:
        grads_all = lax.all_gather(grad_out, ("exp", "tp"), axis=0, tiled=True)
        moe, grad_logits, expert_grad, grad_gate_w, grad_up_w, grad_down = dense_experts(
            routed_low,
            gates,
            picked,
            grads_all.reshape(8, 4, quarter, width),
            gate_weight,
            up_weight,
            down_weight,
        )
    else:
        moe, grad_logits, expert_grad, grad_gate_w, grad_up_w, grad_down = slot_experts(
            routed_low,
            gates,
            picked,
            grad_out,
            expert_routes,
            gate_weight,
            up_weight,
            down_weight,
        )
    block_out = (resid + moe).astype(jnp.bfloat16)
    grad_normed = (
        jnp.dot(grad_logits, router_weight.astype(jnp.float32).T, precision=highest) + expert_grad
    )
    grad_router = jnp.dot(routed_low.astype(jnp.float32).T, grad_logits, precision=highest)
    grad_resid, grad_ffn_gain = norm_two_back(grad_normed)
    grad_resid = grad_resid + grad_rows
    grad_group = lax.all_gather(grad_resid.astype(jnp.bfloat16), "tp", axis=0, tiled=True).astype(
        grad_resid.dtype
    )
    grad_attn_low = grad_group.astype(jnp.bfloat16)
    grad_out_weight = jnp.dot(mixed_low.T, grad_attn_low, preferred_element_type=jnp.float32)
    grad_mixed = jnp.dot(grad_attn_low, out_weight.T, preferred_element_type=jnp.float32)
    grad_mixed_low = grad_mixed.astype(jnp.bfloat16).reshape(group_rows, -1, head_size)
    probs = jnp.exp(masked_scores(query_low, key_low, same_seq, head_size) - log_total)
    grad_probs = jnp.einsum(
        "thd,shd->hts", grad_mixed_low, value_low, preferred_element_type=jnp.float32
    )
    grad_value = jnp.einsum(
        "hts,thd->shd", probs_low, grad_mixed_low, preferred_element_type=jnp.float32
    )
    row_delta = jnp.sum(probs * grad_probs, axis=-1, keepdims=True)
    grad_scores = (probs * (grad_probs - row_delta)).astype(jnp.bfloat16)
    grad_query = jnp.einsum(
        "hts,shd->thd", grad_scores, key_low, preferred_element_type=jnp.float32
    ) / math.sqrt(head_size)
    grad_key = jnp.einsum(
        "hts,thd->shd", grad_scores, query_low, preferred_element_type=jnp.float32
    ) / math.sqrt(head_size)
    grad_query_proj, grad_qgain = query_back(grad_query)
    grad_key_proj, grad_kgain = key_back(grad_key)
    grad_query_low = grad_query_proj.astype(jnp.bfloat16)
    grad_key_low = grad_key_proj.astype(jnp.bfloat16)
    grad_value_low = grad_value.reshape(group_rows, -1).astype(jnp.bfloat16)
    normed_part = (
        jnp.dot(grad_query_low, query_weight.T, preferred_element_type=jnp.float32)
        + jnp.dot(grad_key_low, key_weight.T, preferred_element_type=jnp.float32)
        + jnp.dot(grad_value_low, value_weight.T, preferred_element_type=jnp.float32)
    )
    grad_query_w = jnp.dot(normed_low.T, grad_query_low, preferred_element_type=jnp.float32)
    grad_key_w = jnp.dot(normed_low.T, grad_key_low, preferred_element_type=jnp.float32)
    grad_value_w = jnp.dot(normed_low.T, grad_value_low, preferred_element_type=jnp.float32)
    scale_one = lax.rsqrt(jnp.mean(widened * widened, axis=-1, keepdims=True) + eps)
    unit_one = widened * scale_one
    grad_attn_gain = jnp.sum(normed_part * unit_one, axis=0)
    grad_normed_one = lax.psum(normed_part.astype(bf), "tp").astype(f32)
    scaled = grad_normed_one * attn_gain
    grad_from_norm = scale_one * (
        scaled - unit_one * jnp.mean(unit_one * scaled, axis=-1, keepdims=True)
    )
    grad_input_rows = (grad_group + grad_from_norm).astype(jnp.bfloat16)
    low_totals = lax.psum(
        tuple(
            part.astype(jnp.bfloat16)
            for part in (grad_query_w, grad_key_w, grad_value_w, grad_out_weight)
        ),
        "exp",
    )
    small = lax.psum(
        (grad_attn_gain, grad_qgain, grad_kgain, grad_ffn_gain, grad_router), ("exp", "tp")
    )
    totals = tuple(part.astype(jnp.float32) for part in low_totals) + small
    return (
        block_out,
        grad_input_rows,
        totals[4],
        totals[0],
        totals[1],
        totals[2],
        totals[3],
        totals[5],
        totals[6],
        totals[7],
        totals[8],
        grad_gate_w,
        grad_up_w,
        grad_down,
    )


def solution(mesh):
    in_specs = (
        P("exp", None),
        P(),
        P(None, "tp"),
        P(None, "tp"),
        P(None, "tp"),
        P(),
        P(),
        P("tp", None),
        P(),
        P(),
        P("exp", None, "tp"),
        P("exp", None, "tp"),
        P("exp", "tp", None),
        P(("exp", "tp"), None),
        P("exp", None),
        P(("exp", "tp"), None),
    )
    out_specs = (
        P(("exp", "tp"), None),
        P("exp", None),
        P(),
        P(None, "tp"),
        P(None, "tp"),
        P(None, "tp"),
        P("tp", None),
        P(),
        P(),
        P(),
        P(),
        P("exp", None, "tp"),
        P("exp", None, "tp"),
        P("exp", "tp", None),
    )
    fits = dict(mesh.shape) == {"exp": 8, "tp": 4}
    return jax.shard_map(
        functools.partial(per_device, fits), mesh=mesh, in_specs=in_specs, out_specs=out_specs, check_vma=False
    )
```

```python
import functools
import math

import jax
import jax.numpy as jnp
from jax import lax
from jax.experimental import pallas as pl
from jax.experimental.pallas import tpu as pltpu
from jax.sharding import PartitionSpec as P

eps = 1e-06
rope_base = 10000.0
gate_lanes = 128
MESH = pl.DeviceIdType.MESH
bf = jnp.bfloat16
f32 = jnp.float32
NT = (((1,), (1,)), ((), ()))
TN = (((0,), (0,)), ((), ()))


def rms_norm(values, gain):
    return values * lax.rsqrt(jnp.mean(values * values, axis=-1, keepdims=True) + eps) * gain


def rotary_tables(lengths_row, count, head_size):
    token_index = jnp.arange(count, dtype=jnp.int32)
    seq_ends = jnp.cumsum(lengths_row)
    starts = seq_ends - lengths_row
    member = (
        (token_index[:, None] >= starts[None, :]) & (token_index[:, None] < seq_ends[None, :])
    ).astype(jnp.int32)
    segment = jnp.sum(member * jnp.arange(lengths_row.shape[0], dtype=jnp.int32)[None, :], axis=1)
    offset = jnp.sum(member * starts[None, :], axis=1)
    position = (token_index - offset).astype(jnp.float32)
    frequency = rope_base ** (-jnp.arange(0, head_size, 2, dtype=jnp.float32) / head_size)
    angles = position[:, None] * frequency[None, :]
    return (segment, jnp.cos(angles)[:, None, :], jnp.sin(angles)[:, None, :])


def rotate(values, cosine, sine):
    half = values.shape[-1] // 2
    first = values[..., :half]
    second = values[..., half:]
    return jnp.concatenate(
        [first * cosine - second * sine, second * cosine + first * sine], axis=-1
    )


def head_prep(projected, gain, cosine, sine):
    head_size = gain.shape[0]
    shaped = projected.reshape(projected.shape[0], projected.shape[1] // head_size, head_size)
    return rotate(rms_norm(shaped, gain), cosine, sine)


def masked_scores(query_low, key_low, same_seq, head_size):
    scores = jnp.einsum(
        "thd,shd->hts", query_low, key_low, preferred_element_type=jnp.float32
    ) / math.sqrt(head_size)
    return jnp.where(same_seq[None], scores, -1e30)


def plane_at(z, step):
    from_end = step
    from_middle = jnp.where(step == 0, 1, jnp.where(step == 1, 0, step))
    base = jnp.where((z == 0) | (z == 3), from_end, from_middle)
    return jnp.where(z < 2, base, 3 - base)

Z, X, Y, FX, FY, CO, CX, CY, CA, CB = range(10)

def gather_kernel(own_ref, grad_hbm, wg_hbm, wu_hbm, wd_hbm,
                  act_hbm, dg_ref, du_ref, dd_ref,
                  rows, grads, wg, wu, wd, act, send, up_send, recv, gsend, gline, grecv, load, store, wload):
    e = lax.axis_index("exp")
    z = lax.axis_index("tp")
    ex, ey, ec, ed = (jnp.bitwise_xor(e, m) for m in (2, 4, 1, 6))
    width = wg.shape[1]
    quarter = own_ref.shape[0]
    half = quarter // 2
    hid = wg.shape[2]
    experts_here = wg.shape[0]
    at_x, at_y, at_c = (ex, z), (ey, z), (ec, z)
    at_up, at_down = (e, z + 1), (e, z - 1)

    wcopies = [pltpu.make_async_copy(s, d, wload.at[i]) for i, (s, d) in enumerate(((wg_hbm, wg), (wu_hbm, wu), (wd_hbm, wd)))]
    for c in wcopies: c.start()

    loads = [pltpu.make_async_copy(grad_hbm.at[plane_at(z, k)], grads.at[k], load.at[k]) for k in range(2)]
    for c in loads: c.start()
    middle = (z == 1) | (z == 2)
    def second_load():
        return pltpu.make_async_copy(grad_hbm.at[plane_at(z, 2), e], grads.at[2, e], load.at[2])
    @pl.when(middle)
    def _(): second_load().start()

    bar = pltpu.get_barrier_semaphore()
    for d in (at_x, at_y, at_c):
        pl.semaphore_signal(bar, inc=1, device_id=d, device_id_type=MESH)
    @pl.when(z < 3)
    def _(): pl.semaphore_signal(bar, inc=1, device_id=at_up, device_id_type=MESH)
    @pl.when(z > 0)
    def _(): pl.semaphore_signal(bar, inc=1, device_id=at_down, device_id_type=MESH)
    pl.semaphore_wait(bar, 3 + jnp.where(z < 3, 1, 0) + jnp.where(z > 0, 1, 0))

    TOP, BOT, ALLR = pl.ds(0, half), pl.ds(half, half), pl.ds(0, quarter)

    def copy(kind, plane, group, part, to, src=None, sem=None):
        place = rows.at[plane, group, part]
        return pltpu.make_async_remote_copy(
            src_ref=place if src is None else src, dst_ref=place,
            send_sem=(send.at[kind, plane] if sem is None else sem), recv_sem=recv.at[kind, plane],
            device_id=to, device_id_type=MESH)

    def up(plane, src=None): return copy(Z, plane, e, ALLR, at_up, src, up_send.at[plane])
    def down(plane, src=None): return copy(Z, plane, e, ALLR, at_down, src)
    def to_x(plane, src=None): return copy(X, plane, e, ALLR, at_x, src)
    def to_y(plane, src=None): return copy(Y, plane, e, ALLR, at_y, src)
    def to_c(plane, src=None): return copy(CO, plane, e, ALLR, at_c, src)
    def fwd_y(plane): return copy(FY, plane, ex, TOP, at_y)
    def fwd_x(plane): return copy(FX, plane, ey, BOT, at_x)
    def c_x(plane): return copy(CX, plane, ex, ALLR, at_c)
    def c_y(plane): return copy(CY, plane, ey, ALLR, at_c)
    def c_a(plane): return copy(CA, plane, ed, TOP, at_c)
    def c_b(plane): return copy(CB, plane, ed, BOT, at_c)

    def arrived(kind, plane, group, part):
        place = rows.at[plane, group, part]
        pltpu.make_async_copy(place, place, recv.at[kind, plane]).wait()

    outward = (e, jnp.where(z == 1, 0, 3))
    inward = (e, 3 - z)
    def grad_line(which, src, step, to):
        return pltpu.make_async_remote_copy(src_ref=src, dst_ref=grads.at[step, e], send_sem=gline.at[which],
                                            recv_sem=grecv.at[Z, step - 2], device_id=to, device_id_type=MESH)
    def line_a(): return grad_line(0, grad_hbm.at[plane_at(z, 2), e], 2, outward)
    def line_b(): return grad_line(1, grad_hbm.at[plane_at(z, 1), e], 3, inward)
    def line_c(): return grad_line(2, grads.at[3, e], 3, outward)
    def gcopy(kind, k, group, part, to):
        place = grads.at[k, group, part]
        return pltpu.make_async_remote_copy(src_ref=place, dst_ref=place, send_sem=gsend.at[kind, k - 2],
                                            recv_sem=grecv.at[kind, k - 2], device_id=to, device_id_type=MESH)
    def g_x(k): return gcopy(X, k, e, ALLR, at_x)
    def g_y(k): return gcopy(Y, k, e, ALLR, at_y)
    def g_c(k): return gcopy(CO, k, e, ALLR, at_c)
    def gfwd_y(k): return gcopy(FY, k, ex, TOP, at_y)
    def gfwd_x(k): return gcopy(FX, k, ey, BOT, at_x)
    def gc_x(k): return gcopy(CX, k, ex, ALLR, at_c)
    def gc_y(k): return gcopy(CY, k, ey, ALLR, at_c)
    def gc_a(k): return gcopy(CA, k, ed, TOP, at_c)
    def gc_b(k): return gcopy(CB, k, ed, BOT, at_c)
    def garrived(kind, k, group, part):
        place = grads.at[k, group, part]
        pltpu.make_async_copy(place, place, grecv.at[kind, k - 2]).wait()

    def grad_row(k):
        if k == 2:
            @pl.when(middle)
            def _(): second_load().wait()
            @pl.when(~middle)
            def _(): garrived(Z, 2, e, ALLR)
        else:
            garrived(Z, 3, e, ALLR)
            @pl.when(middle)
            def _(): line_c().start()
        g_x(k).start()
        g_y(k).start()
        g_c(k).start()

    def grad_sides(k):
        garrived(X, k, ex, ALLR)
        gfwd_y(k).start()
        gc_x(k).start()
        garrived(Y, k, ey, ALLR)
        gfwd_x(k).start()
        gc_y(k).start()

    def grad_far(k):
        garrived(FY, k, ed, TOP)
        gc_a(k).start()
        garrived(FX, k, ed, BOT)
        gc_b(k).start()

    @pl.when(z < 3)
    def _(): up(z, own_ref).start()
    @pl.when(z > 0)
    def _(): down(z, own_ref).start()
    to_x(z, own_ref).start()
    to_y(z, own_ref).start()
    to_c(z, own_ref).start()
    rows[z, e] = own_ref[...]

    def serve_line(k):
        p = plane_at(z, k)
        arrived(Z, p, e, ALLR)
        @pl.when((p < z) & (z < 3))
        def _(): up(p).start()
        @pl.when((p > z) & (z > 0))
        def _(): down(p).start()
        to_x(p).start()
        to_y(p).start()
        to_c(p).start()

    def serve_sides(k):
        p = plane_at(z, k)
        arrived(X, p, ex, ALLR)
        fwd_y(p).start()
        c_x(p).start()
        arrived(Y, p, ey, ALLR)
        fwd_x(p).start()
        c_y(p).start()

    def serve_far(k):
        p = plane_at(z, k)
        arrived(FY, p, ed, TOP)
        c_a(p).start()
        arrived(FX, p, ed, BOT)
        c_b(p).start()

    def store_copy(step):
        k, h = step // 2, lax.rem(step, 2)
        first = jnp.bitwise_xor(jnp.bitwise_and(e, 4), h * 4)
        return pltpu.make_async_copy(act, act_hbm.at[pl.ds(first // 2, 2), :, plane_at(z, k)], store)

    @pl.when(middle)
    def _():
        line_a().start()
        line_b().start()
    serve_line(1)
    @pl.when(middle)
    def _(): serve_line(2)
    serve_sides(0)
    for c in wcopies + loads: c.wait()

    def step_body(step, _):
        k, h = step // 2, lax.rem(step, 2)
        p = plane_at(z, k)
        first = jnp.bitwise_xor(jnp.bitwise_and(e, 4), h * 4)
        sib_x = jnp.bitwise_xor(ec, 2)
        sib_y = jnp.bitwise_xor(ec, 4)
        sib_d = jnp.bitwise_xor(ec, 6)
        @pl.when(h == 0)
        def _():
            arrived(CO, p, ec, ALLR)
            arrived(CX, p, sib_x, ALLR)
            @pl.when(k >= 2)
            def _():
                garrived(CO, k, ec, ALLR)
                garrived(CX, k, sib_x, ALLR)
        @pl.when(h == 1)
        def _():
            arrived(CY, p, sib_y, ALLR)
            arrived(CA, p, sib_d, TOP)
            arrived(CB, p, sib_d, BOT)
            @pl.when(k >= 2)
            def _():
                garrived(CY, k, sib_y, ALLR)
                garrived(CA, k, sib_d, TOP)
                garrived(CB, k, sib_d, BOT)
        lane = lax.broadcasted_iota(jnp.int32, (4 * quarter, gate_lanes), 1)

        def expert_body(j, _):
            x = rows[p, pl.ds(first, 4), :, :width].reshape(4 * quarter, width)
            g = grads[k, pl.ds(first, 4)].reshape(4 * quarter, width)
            extra = rows[p, pl.ds(first, 4), :, width:].reshape(4 * quarter, gate_lanes).astype(f32)
            expert = e * experts_here + j
            mine = (lane == expert) | (lane == expert + gate_lanes // 2)
            gate = jnp.sum(jnp.where(mine, extra, 0.0), axis=1, keepdims=True)
            ga = jnp.dot(x, wg[j], preferred_element_type=f32)
            ua = jnp.dot(x, wu[j], preferred_element_type=f32)
            gh = lax.dot_general(g, wd[j], (((1,), (1,)), ((), ())), preferred_element_type=f32)
            sg = jax.nn.sigmoid(ga)
            silu = ga * sg
            hidden = silu * ua
            score = jnp.sum(hidden * gh, axis=1, keepdims=True)
            gh = gh * gate
            hg = (hidden * gate).astype(bf)
            da = (gh * ua * (sg * (1.0 + ga * (1.0 - sg)))).astype(bf)
            du = (gh * silu).astype(bf)
            @pl.when((step > 0) & (j == 0))
            def _(): store_copy(step - 1).wait()
            base = j * 3 * hid
            shape3 = (2, 2, quarter, hid)
            act[:, :, :, pl.ds(pl.multiple_of(base, hid), hid)] = da.reshape(shape3)
            act[:, :, :, pl.ds(pl.multiple_of(base + hid, hid), hid)] = du.reshape(shape3)
            act[:, :, :, pl.ds(pl.multiple_of(base + 2 * hid, hid), hid)] = hg.reshape(shape3)
            scores = jnp.where(lane == expert, score, 0.0).astype(bf).reshape(2, 2, quarter, gate_lanes)
            act[:, :, :, pl.ds(pl.multiple_of(experts_here * 3 * hid + j * gate_lanes, gate_lanes), gate_lanes)] = scores
            @pl.when(step == 0)
            def _():
                dg_ref[j] = jnp.zeros(dg_ref.shape[1:], f32)
                du_ref[j] = jnp.zeros(du_ref.shape[1:], f32)
                dd_ref[j] = jnp.zeros(dd_ref.shape[1:], f32)
            slot = 2 * step + j
            for at, work, which in (
                (1, serve_far, 0), (2, serve_sides, 1), (4, serve_far, 1), (5, serve_sides, 2),
                (7, serve_far, 2), (7, serve_sides, 3), (9, serve_far, 3),
                (3, grad_row, 2), (5, grad_row, 3), (6, grad_sides, 2), (8, grad_far, 2), (9, grad_sides, 3), (11, grad_far, 3)):
                @pl.when(slot == at)
                def _(): work(which)
            @pl.when((slot == 1) & middle)
            def _(): serve_line(3)
            @pl.when((slot == 1) & ~middle)
            def _(): serve_line(2)
            @pl.when((slot == 3) & ~middle)
            def _(): serve_line(3)
            dd_ref[j] += lax.dot_general(hg, g, TN, preferred_element_type=f32)
            dg_ref[j] += lax.dot_general(x, da, TN, preferred_element_type=f32)
            du_ref[j] += lax.dot_general(x, du, TN, preferred_element_type=f32)
            return 0
        lax.fori_loop(0, experts_here, expert_body, 0)
        store_copy(step).start()
        return 0
    lax.fori_loop(0, 8, step_body, 0)
    store_copy(7).wait()

    @pl.when(middle)
    def _():
        for c in (line_a, line_b, line_c):
            c().wait_send()
    def drain_grads(k, _):
        for c in (g_x, g_y, g_c, gfwd_y, gfwd_x, gc_x, gc_y, gc_a, gc_b):
            c(k).wait_send()
        return 0
    lax.fori_loop(2, 4, drain_grads, 0)
    def drain(k, _):
        p = plane_at(z, k)
        @pl.when((z < 3) & (p <= z))
        def _(): up(p).wait_send()
        @pl.when((z > 0) & (p >= z))
        def _(): down(p).wait_send()
        for c in (to_x, to_y, to_c, fwd_y, fwd_x, c_x, c_y, c_a, c_b):
            c(p).wait_send()
        return 0
    lax.fori_loop(0, 4, drain, 0)

def gather_experts(own, grads_all, wg, wu, wd):
    n_here, width, hid = wg.shape
    quarter, wide = own.shape
    lanes = wide - width
    cols = n_here * 3 * hid + n_here * lanes
    any_ = pl.BlockSpec(memory_space=pl.ANY)
    vm = pl.BlockSpec(memory_space=pltpu.VMEM)
    return pl.pallas_call(
        gather_kernel,
        out_shape=(jax.ShapeDtypeStruct((4, 2, 4, quarter, cols), bf),
                   jax.ShapeDtypeStruct(wg.shape, f32), jax.ShapeDtypeStruct(wu.shape, f32), jax.ShapeDtypeStruct(wd.shape, f32)),
        in_specs=[vm, any_, any_, any_, any_],
        out_specs=(any_, vm, vm, vm),
        scratch_shapes=[
            pltpu.VMEM((4, 8, quarter, wide), bf),
            pltpu.VMEM((4, 8, quarter, width), bf),
            pltpu.VMEM(wg.shape, bf), pltpu.VMEM(wu.shape, bf), pltpu.VMEM(wd.shape, bf),
            pltpu.VMEM((2, 2, quarter, cols), bf),
            pltpu.SemaphoreType.DMA((10, 4)), pltpu.SemaphoreType.DMA((4,)), pltpu.SemaphoreType.DMA((10, 4)),
            pltpu.SemaphoreType.DMA((10, 2)), pltpu.SemaphoreType.DMA((3,)), pltpu.SemaphoreType.DMA((10, 2)),
            pltpu.SemaphoreType.DMA((3,)), pltpu.SemaphoreType.DMA, pltpu.SemaphoreType.DMA((3,)),
        ],
        compiler_params=pltpu.CompilerParams(collective_id=1, has_side_effects=True, vmem_limit_bytes=63 << 20),
        cost_estimate=pl.CostEstimate(flops=12 * 4096 * 2048 * hid * n_here, bytes_accessed=64 << 20, transcendentals=0),
    )(own, grads_all, wg, wu, wd)


HZ, HX, HY, HFX, HFY, HC, HCX, HCY, HCA, HCB, HU, HD = range(12)

def opening_kernel(part_ref, grad_ref, out_ref, grads, line, rzu, rzd, send, up_send, recv, local):
    e = lax.axis_index("exp")
    z = lax.axis_index("tp")
    ex, ey, ec, ed = (jnp.bitwise_xor(e, m) for m in (2, 4, 1, 6))
    at_x, at_y, at_c = (ex, z), (ey, z), (ec, z)
    at_up, at_down = (e, z + 1), (e, z - 1)
    middle_plane = (z == 1) | (z == 2)
    quarter = grad_ref.shape[0]
    half = quarter // 2
    TOP, BOT, ALLR = pl.ds(0, half), pl.ds(half, half), pl.ds(0, quarter)

    bar = pltpu.get_barrier_semaphore()
    for d in (at_x, at_y, at_c):
        pl.semaphore_signal(bar, inc=1, device_id=d, device_id_type=MESH)
    @pl.when(z < 3)
    def _(): pl.semaphore_signal(bar, inc=1, device_id=at_up, device_id_type=MESH)
    @pl.when(z > 0)
    def _(): pl.semaphore_signal(bar, inc=1, device_id=at_down, device_id_type=MESH)
    pl.semaphore_wait(bar, 3 + jnp.where(z < 3, 1, 0) + jnp.where(z > 0, 1, 0))

    def copy(kind, plane, group, part, to, src=None, sem=None):
        place = grads.at[plane, group, part]
        return pltpu.make_async_remote_copy(
            src_ref=place if src is None else src, dst_ref=place,
            send_sem=send.at[kind, plane] if sem is None else sem, recv_sem=recv.at[kind, plane],
            device_id=to, device_id_type=MESH)
    def arrived(kind, plane, place):
        pltpu.make_async_copy(place, place, recv.at[kind, plane]).wait()
    def line_copy(kind, p, landing, to):
        return pltpu.make_async_remote_copy(src_ref=line.at[p], dst_ref=landing.at[p], send_sem=send.at[kind, p],
                                            recv_sem=recv.at[kind, p], device_id=to, device_id_type=MESH)
    def line_up(p): return line_copy(HU, p, rzu, at_up)
    def line_down(p): return line_copy(HD, p, rzd, at_down)
    def up(): return copy(HZ, z, e, ALLR, at_up, grad_ref, up_send)
    def down(): return copy(HZ, z, e, ALLR, at_down, grad_ref)
    def to_x(p, src=None): return copy(HX, p, e, ALLR, at_x, src)
    def to_y(p, src=None): return copy(HY, p, e, ALLR, at_y, src)
    def to_c(p, src=None): return copy(HC, p, e, ALLR, at_c, src)
    def fwd_y(p): return copy(HFY, p, ex, TOP, at_y)
    def fwd_x(p): return copy(HFX, p, ey, BOT, at_x)
    def c_x(p): return copy(HCX, p, ex, ALLR, at_c)
    def c_y(p): return copy(HCY, p, ey, ALLR, at_c)
    def c_a(p): return copy(HCA, p, ed, TOP, at_c)
    def c_b(p): return copy(HCB, p, ed, BOT, at_c)

    def serve_sides(k):
        p = plane_at(z, k)
        arrived(HX, p, grads.at[p, ex])
        fwd_y(p).start()
        c_x(p).start()
        arrived(HY, p, grads.at[p, ey])
        fwd_x(p).start()
        c_y(p).start()

    def serve_far(k):
        p = plane_at(z, k)
        arrived(HFY, p, grads.at[p, ed, TOP])
        c_a(p).start()
        arrived(HFX, p, grads.at[p, ed, BOT])
        c_b(p).start()

    def line_step(k):
        p = plane_at(z, 3 - k)
        line[p] = part_ref[p]
        @pl.when((z > 0) & (p >= z))
        def _():
            arrived(HU, p, rzu.at[p])
            line[p] = (line[p].astype(f32) + rzu[p].astype(f32)).astype(bf)
        @pl.when((z < 3) & (p <= z))
        def _():
            arrived(HD, p, rzd.at[p])
            line[p] = (line[p].astype(f32) + rzd[p].astype(f32)).astype(bf)
        @pl.when(p > z)
        def _(): line_up(p).start()
        @pl.when(p < z)
        def _(): line_down(p).start()

    def ends(f): pl.when(~middle_plane)(f)
    def mids(f): pl.when(middle_plane)(f)

    ends(lambda: line_step(0))
    @pl.when(z < 3)
    def _(): up().start()
    @pl.when(z > 0)
    def _(): down().start()
    to_x(z, grad_ref).start()
    to_y(z, grad_ref).start()
    to_c(z, grad_ref).start()
    own = pltpu.make_async_copy(grad_ref, grads.at[z, e], local)
    own.start()
    mids(lambda: line_step(0))
    ends(lambda: line_step(1))
    serve_sides(0)
    near = plane_at(z, 1)
    arrived(HZ, near, grads.at[near, e])
    to_x(near).start()
    to_y(near).start()
    to_c(near).start()
    serve_far(0)
    mids(lambda: line_step(1))
    mids(lambda: line_step(2))
    ends(lambda: line_step(2))
    serve_sides(1)
    @pl.when(middle_plane)
    def _():
        other = plane_at(z, 2)
        arrived(HZ, other, grads.at[other, e])
    out_ref[...] = part_ref[z].astype(f32)
    @pl.when(z > 0)
    def _():
        arrived(HU, z, rzu.at[z])
        out_ref[...] += rzu[z].astype(f32)
    @pl.when(z < 3)
    def _():
        arrived(HD, z, rzd.at[z])
        out_ref[...] += rzd[z].astype(f32)
    serve_far(1)
    own.wait()
    @pl.when(z < 3)
    def _(): up().wait_send()
    @pl.when(z > 0)
    def _(): down().wait_send()
    def drain(k, _):
        p = plane_at(z, k)
        for c in (to_x, to_y, to_c, fwd_y, fwd_x, c_x, c_y, c_a, c_b):
            c(p).wait_send()
        arrived(HC, p, grads.at[p, ec])
        arrived(HCX, p, grads.at[p, jnp.bitwise_xor(ec, 2)])
        arrived(HCY, p, grads.at[p, jnp.bitwise_xor(ec, 4)])
        arrived(HCA, p, grads.at[p, jnp.bitwise_xor(ec, 6), TOP])
        arrived(HCB, p, grads.at[p, jnp.bitwise_xor(ec, 6), BOT])
        return 0
    lax.fori_loop(0, 2, drain, 0)
    def drain_line(p, _):
        @pl.when(p > z)
        def _(): line_up(p).wait_send()
        @pl.when(p < z)
        def _(): line_down(p).wait_send()
        return 0
    lax.fori_loop(0, 4, drain_line, 0)

def open_exchange(part, grad, collective_id):
    vm = pl.BlockSpec(memory_space=pltpu.VMEM)
    any_ = pl.BlockSpec(memory_space=pl.ANY)
    _, quarter, width = part.shape
    return pl.pallas_call(
        opening_kernel,
        out_shape=(jax.ShapeDtypeStruct((quarter, width), f32), jax.ShapeDtypeStruct((4, 8, quarter, width), bf)),
        in_specs=[vm, any_],
        out_specs=(vm, any_),
        scratch_shapes=[pltpu.VMEM(part.shape, bf)] * 3 + [
            pltpu.SemaphoreType.DMA((12, 4)), pltpu.SemaphoreType.DMA, pltpu.SemaphoreType.DMA((12, 4)), pltpu.SemaphoreType.DMA],
        compiler_params=pltpu.CompilerParams(collective_id=collective_id, has_side_effects=True, vmem_limit_bytes=40 << 20),
    )(part, grad)


def input_product(acts, weights, cols):
    wg, wu = weights
    hid = wg.shape[2]
    total = None
    for j in range(wg.shape[0]):
        for w, i in ((wg, 0), (wu, 1)):
            lhs = acts[:, :, (3 * j + i) * hid:(3 * j + i + 1) * hid].reshape(-1, hid)
            part = lax.dot_general(lhs, w[j, cols, :], NT, preferred_element_type=f32)
            total = part if total is None else total + part
    return total

def output_product(acts, weights, cols):
    (wd,) = weights
    hid = wd.shape[1]
    total = None
    for j in range(wd.shape[0]):
        lhs = acts[:, :, (3 * j + 2) * hid:(3 * j + 3) * hid].reshape(-1, hid)
        part = jnp.dot(lhs, wd[j, :, cols], preferred_element_type=f32)
        total = part if total is None else total + part
    return total

C1, DT, DB, XT, XB, YT, YB, ZU, ZD, OU, OD = range(11)

def scatter_kernel(product, n_weights, width, score_at, carry, *refs):
    act_hbm, *rest = refs
    w_hbm, rest = rest[:n_weights], rest[n_weights:]
    if carry:
        row_ref, out_ref, rows, acts, *rest = rest
    else:
        out_ref, acts, *rest = rest
    weights, rest = rest[:n_weights], rest[n_weights:]
    sendbuf, acc, r1, rdt, rdb, rx, ry, rzu, rzd, send, recv, load, wload = rest
    e = lax.axis_index("exp")
    z = lax.axis_index("tp")
    quarter = acc.shape[2]
    half = quarter // 2
    chip = e // 2
    core = lax.rem(e, 2)
    chip_x, chip_y, chip_d = (jnp.bitwise_xor(chip, m) for m in (1, 2, 3))
    at_x, at_y, at_c = (jnp.bitwise_xor(e, 2), z), (jnp.bitwise_xor(e, 4), z), (jnp.bitwise_xor(e, 1), z)
    at_up, at_down = (e, z + 1), (e, z - 1)
    TOP, BOT = pl.ds(0, half), pl.ds(half, half)

    wcopies = [pltpu.make_async_copy(s, d, wload.at[i]) for i, (s, d) in enumerate(zip(w_hbm, weights))]
    for c in wcopies: c.start()

    def act_copy(n):
        k, own = n // 2, lax.rem(n, 2)
        which = jnp.bitwise_xor(core, 1 - own)
        return pltpu.make_async_copy(act_hbm.at[:, which, plane_at(z, 3 - k)], acts.at[own], load.at[own])
    act_copy(0).start()

    bar = pltpu.get_barrier_semaphore()
    for d in (at_x, at_y, at_c):
        pl.semaphore_signal(bar, inc=1, device_id=d, device_id_type=MESH)
    @pl.when(z < 3)
    def _(): pl.semaphore_signal(bar, inc=1, device_id=at_up, device_id_type=MESH)
    @pl.when(z > 0)
    def _(): pl.semaphore_signal(bar, inc=1, device_id=at_down, device_id_type=MESH)
    pl.semaphore_wait(bar, 3 + jnp.where(z < 3, 1, 0) + jnp.where(z > 0, 1, 0))
    for c in wcopies: c.wait()

    def remote(kind, k, src, dst, to):
        return pltpu.make_async_remote_copy(src_ref=src, dst_ref=dst, send_sem=send.at[kind, k], recv_sem=recv.at[kind, k],
                                            device_id=to, device_id_type=MESH)
    def to_core(k): return remote(C1, k, sendbuf.at[lax.rem(k, 2)], r1.at[k], at_c)
    def far_x(k): return remote(DT, k, acc.at[k, chip_d, TOP], rdt.at[k], at_x)
    def far_y(k): return remote(DB, k, acc.at[k, chip_d, BOT], rdb.at[k], at_y)
    def x_top(k): return remote(XT, k, acc.at[k, chip_x, TOP], rx.at[k, TOP], at_x)
    def x_bot(k): return remote(XB, k, acc.at[k, chip_x, BOT], rx.at[k, BOT], at_x)
    def y_top(k): return remote(YT, k, acc.at[k, chip_y, TOP], ry.at[k, TOP], at_y)
    def y_bot(k): return remote(YB, k, acc.at[k, chip_y, BOT], ry.at[k, BOT], at_y)
    def line_up(k, p): return remote(ZU, p, acc.at[k, chip], rzu.at[p], at_up)
    def line_down(k, p): return remote(ZD, p, acc.at[k, chip], rzd.at[p], at_down)
    def arrived(kind, k, place):
        pltpu.make_async_copy(place, place, recv.at[kind, k]).wait()
    def row_up(p): return remote(OU, p, rows.at[p], rows.at[p], at_up)
    def row_down(p): return remote(OD, p, rows.at[p], rows.at[p], at_down)
    def row_step(k):
        p = plane_at(z, k)
        @pl.when(p < z)
        def _(): arrived(OU, p, rows.at[p])
        @pl.when(p > z)
        def _(): arrived(OD, p, rows.at[p])
        @pl.when((p <= z) & (z < 3))
        def _(): row_up(p).start()
        @pl.when((p >= z) & (z > 0))
        def _(): row_down(p).start()
    if carry:
        rows[z] = row_ref[...]
        row_step(0)

    cols_step = 512
    def multiply(slot, target):
        def tile(n, _):
            cols = pl.ds(pl.multiple_of(n * cols_step, cols_step), cols_step)
            total = product(acts.at[slot], weights, cols)
            target[:, :, cols] = total.astype(bf).reshape(4, quarter, cols_step)
            return 0
        lax.fori_loop(0, width // cols_step, tile, 0)
        if score_at is not None:
            lanes = target.shape[2] - width
            target[:, :, width:] = acts[slot, :, :, score_at:score_at + lanes] + acts[slot, :, :, score_at + lanes:score_at + 2 * lanes]

    def add(place, other):
        place[...] = (place[...].astype(f32) + other[...].astype(f32)).astype(bf)

    def begin(k):
        act_copy(2 * k).wait()
        act_copy(2 * k + 1).start()
        @pl.when(k >= 2)
        def _(): to_core(k - 2).wait_send()
        multiply(0, sendbuf.at[lax.rem(k, 2)])
        to_core(k).start()
        act_copy(2 * k + 1).wait()
        @pl.when(k < 3)
        def _(): act_copy(2 * k + 2).start()
        multiply(1, acc.at[k])
        arrived(C1, k, r1.at[k])
        add(acc.at[k, chip_d], r1.at[k, chip_d])
        far_x(k).start()
        far_y(k).start()
        add(acc.at[k, chip_x], r1.at[k, chip_x])
        x_top(k).start()
        add(acc.at[k, chip_y], r1.at[k, chip_y])
        y_bot(k).start()
        add(acc.at[k, chip], r1.at[k, chip])

    def middle(k):
        arrived(DB, k, rdb.at[k])
        add(acc.at[k, chip_x, BOT], rdb.at[k])
        x_bot(k).start()
        arrived(DT, k, rdt.at[k])
        add(acc.at[k, chip_y, TOP], rdt.at[k])
        y_top(k).start()

    def finish(k):
        p = plane_at(z, 3 - k)
        arrived(XT, k, rx.at[k, TOP])
        arrived(YB, k, ry.at[k, BOT])
        arrived(XB, k, rx.at[k, BOT])
        arrived(YT, k, ry.at[k, TOP])
        total = acc[k, chip].astype(f32) + rx[k].astype(f32) + ry[k].astype(f32)
        out_ref[...] = total
        @pl.when((z > 0) & (p >= z))
        def _():
            arrived(ZU, p, rzu.at[p])
            out_ref[...] += rzu[p].astype(f32)
        @pl.when((z < 3) & (p <= z))
        def _():
            arrived(ZD, p, rzd.at[p])
            out_ref[...] += rzd[p].astype(f32)
        @pl.when(p != z)
        def _():
            acc[k, chip] = out_ref[...].astype(bf)
        @pl.when(p > z)
        def _(): line_up(k, p).start()
        @pl.when(p < z)
        def _(): line_down(k, p).start()

    def body(k, _):
        @pl.when(k < 4)
        def _(): begin(k)
        @pl.when(k > 0)
        def _(): finish(k - 1)
        @pl.when(k < 4)
        def _(): middle(k)
        if carry:
            @pl.when(k < 3)
            def _(): row_step(k + 1)
        return 0
    lax.fori_loop(0, 5, body, 0)

    def drain(k, _):
        p = plane_at(z, 3 - k)
        @pl.when(k >= 2)
        def _(): to_core(k).wait_send()
        for c in (far_x, far_y, x_top, x_bot, y_top, y_bot):
            c(k).wait_send()
        @pl.when(p > z)
        def _(): line_up(k, p).wait_send()
        @pl.when(p < z)
        def _(): line_down(k, p).wait_send()
        if carry:
            @pl.when((p <= z) & (z < 3))
            def _(): row_up(p).wait_send()
            @pl.when((p >= z) & (z > 0))
            def _(): row_down(p).wait_send()
        return 0
    lax.fori_loop(0, 4, drain, 0)

def scatter_sums(act, weights, product, scores, collective_id, rows=None):
    hid = min(weights[0].shape[1:])
    width = max(weights[0].shape[1:])
    n_here = weights[0].shape[0]
    quarter, cols = act.shape[3:]
    score_at = 3 * hid * n_here
    lanes = (cols - score_at) // n_here
    wide = width + (lanes if scores else 0)
    any_ = pl.BlockSpec(memory_space=pl.ANY)
    n = len(weights)
    vm = pl.BlockSpec(memory_space=pltpu.VMEM)
    total = jax.ShapeDtypeStruct((quarter, wide), f32)
    carry = () if rows is None else (rows,)
    return pl.pallas_call(
        functools.partial(scatter_kernel, product, n, width, score_at if scores else None, len(carry)),
        out_shape=(total,) + tuple(jax.ShapeDtypeStruct((4,) + r.shape, bf) for r in carry),
        in_specs=[any_] * (1 + n) + [vm] * len(carry),
        out_specs=(vm,) * (1 + len(carry)),
        scratch_shapes=[pltpu.VMEM((2, 4, quarter, cols), bf)] + [pltpu.VMEM(w.shape, bf) for w in weights] + [
            pltpu.VMEM((2, 4, quarter, wide), bf),
            pltpu.VMEM((4, 4, quarter, wide), bf),
            pltpu.VMEM((4, 4, quarter, wide), bf),
            pltpu.VMEM((4, quarter // 2, wide), bf), pltpu.VMEM((4, quarter // 2, wide), bf),
            pltpu.VMEM((4, quarter, wide), bf), pltpu.VMEM((4, quarter, wide), bf),
            pltpu.VMEM((4, quarter, wide), bf), pltpu.VMEM((4, quarter, wide), bf),
            pltpu.SemaphoreType.DMA((11, 4)), pltpu.SemaphoreType.DMA((11, 4)),
            pltpu.SemaphoreType.DMA((2,)), pltpu.SemaphoreType.DMA((n,)),
        ],
        compiler_params=pltpu.CompilerParams(collective_id=collective_id, has_side_effects=True, vmem_limit_bytes=60 << 20),
    )(act, *weights, *carry)


(SC, SDT, SDB, SXT, SXB, SYT, SYB, GX, GY, GFX, GFY, GC, GCX, GCY, GCA, GCB, LU, LD, RU, RD) = range(20)

def totals_kernel(*refs):
    part_ref, w_ref, refs = refs[0], refs[1:5], refs[5:]
    router_ref, ffn_ref, heads_ref, hidden_ref, resid_ref, gain_ref, refs = *refs[:6], refs[6:]
    res, rows, small_out, refs = refs[:4], refs[4], refs[5], refs[6:]
    r1, acc, rdt, rdb, rx, ry, refs = *(refs[4 * i : 4 * i + 4] for i in range(6)), refs[24:]
    rzu, rzd, line, sums, got, send, recv, ssend, srecv = refs
    e = lax.axis_index("exp")
    z = lax.axis_index("tp")
    chip, core = e // 2, lax.rem(e, 2)
    cx, cy, cd = (jnp.bitwise_xor(chip, m) for m in (1, 2, 3))
    at_x, at_y, at_c = (jnp.bitwise_xor(e, 2), z), (jnp.bitwise_xor(e, 4), z), (jnp.bitwise_xor(e, 1), z)
    at_up, at_down = (e, z + 1), (e, z - 1)
    partners = (at_c, at_x, at_y, (e, jnp.bitwise_xor(z, 1)), (e, jnp.bitwise_xor(z, 2)))
    middle_plane = (z == 1) | (z == 2)
    halves = [ref.shape[1] // 2 for ref in acc]
    TOP, BOT = [pl.ds(0, h) for h in halves], [pl.ds(h, h) for h in halves]

    bar = pltpu.get_barrier_semaphore()
    for d in (at_x, at_y, at_c, (e, jnp.bitwise_xor(z, 2))):
        pl.semaphore_signal(bar, inc=1, device_id=d, device_id_type=MESH)
    @pl.when(z < 3)
    def _(): pl.semaphore_signal(bar, inc=1, device_id=at_up, device_id_type=MESH)
    @pl.when(z > 0)
    def _(): pl.semaphore_signal(bar, inc=1, device_id=at_down, device_id_type=MESH)
    pl.semaphore_wait(bar, 4 + jnp.where(z < 3, 1, 0) + jnp.where(z > 0, 1, 0))

    def remote(kind, k, src, dst, to):
        return pltpu.make_async_remote_copy(src_ref=src, dst_ref=dst, send_sem=send.at[kind, k], recv_sem=recv.at[kind, k],
                                            device_id=to, device_id_type=MESH)
    def arrived(kind, k, place):
        pltpu.make_async_copy(place, place, recv.at[kind, k]).wait()
    def to_core(k): return remote(SC, k, w_ref[k].at[1 - core], r1[k], at_c)
    def far_x(k): return remote(SDT, k, acc[k].at[cd, TOP[k]], rdt[k], at_x)
    def far_y(k): return remote(SDB, k, acc[k].at[cd, BOT[k]], rdb[k], at_y)
    def x_top(k): return remote(SXT, k, acc[k].at[cx, TOP[k]], rx[k].at[TOP[k]], at_x)
    def x_bot(k): return remote(SXB, k, acc[k].at[cx, BOT[k]], rx[k].at[BOT[k]], at_x)
    def y_top(k): return remote(SYT, k, acc[k].at[cy, TOP[k]], ry[k].at[TOP[k]], at_y)
    def y_bot(k): return remote(SYB, k, acc[k].at[cy, BOT[k]], ry[k].at[BOT[k]], at_y)
    def same(kind, k, place, to): return remote(kind, k, place, place, to)
    def give_x(k): return same(GX, k, res[k].at[core, chip], at_x)
    def give_y(k): return same(GY, k, res[k].at[core, chip], at_y)
    def give_c(k): return same(GC, k, res[k].at[core, chip], at_c)
    def pass_y(k): return same(GFY, k, res[k].at[core, cx, TOP[k]], at_y)
    def pass_x(k): return same(GFX, k, res[k].at[core, cy, BOT[k]], at_x)
    def c_x(k): return same(GCX, k, res[k].at[core, cx], at_c)
    def c_y(k): return same(GCY, k, res[k].at[core, cy], at_c)
    def c_a(k): return same(GCA, k, res[k].at[core, cd, TOP[k]], at_c)
    def c_b(k): return same(GCB, k, res[k].at[core, cd, BOT[k]], at_c)
    def line_up(p): return remote(LU, p, line.at[p], rzu.at[p], at_up)
    def line_down(p): return remote(LD, p, line.at[p], rzd.at[p], at_down)
    def row_up(p): return same(RU, p, rows.at[p], at_up)
    def row_down(p): return same(RD, p, rows.at[p], at_down)

    def plus(a, b): return (a.astype(f32) + b.astype(f32)).astype(bf)

    def begin(k):
        arrived(SC, k, r1[k])
        acc[k][cd] = plus(w_ref[k][core, cd], r1[k][cd])
        far_x(k).start()
        far_y(k).start()
        acc[k][cx] = plus(w_ref[k][core, cx], r1[k][cx])
        x_top(k).start()
        acc[k][cy] = plus(w_ref[k][core, cy], r1[k][cy])
        y_bot(k).start()
        acc[k][chip] = plus(w_ref[k][core, chip], r1[k][chip])

    def middle(k):
        arrived(SDB, k, rdb[k])
        acc[k][cx, BOT[k]] = plus(acc[k][cx, BOT[k]], rdb[k][...])
        x_bot(k).start()
        arrived(SDT, k, rdt[k])
        acc[k][cy, TOP[k]] = plus(acc[k][cy, TOP[k]], rdt[k][...])
        y_top(k).start()

    def finish(k):
        arrived(SXT, k, rx[k].at[TOP[k]])
        arrived(SYB, k, ry[k].at[BOT[k]])
        arrived(SXB, k, rx[k].at[BOT[k]])
        arrived(SYT, k, ry[k].at[TOP[k]])
        res[k][core, chip] = (acc[k][chip].astype(f32) + rx[k][...].astype(f32) + ry[k][...].astype(f32)).astype(bf)
        give_x(k).start()
        give_y(k).start()
        give_c(k).start()

    def spread(k):
        arrived(GX, k, res[k].at[core, cx])
        pass_y(k).start()
        c_x(k).start()
        arrived(GY, k, res[k].at[core, cy])
        pass_x(k).start()
        c_y(k).start()

    def last(k):
        arrived(GFY, k, res[k].at[core, cd, TOP[k]])
        c_a(k).start()
        arrived(GFX, k, res[k].at[core, cd, BOT[k]])
        c_b(k).start()

    def line_step(k):
        p = plane_at(z, 3 - k)
        line[p] = part_ref[p]
        @pl.when((z > 0) & (p >= z))
        def _():
            arrived(LU, p, rzu.at[p])
            line[p] = plus(line[p], rzu[p])
        @pl.when((z < 3) & (p <= z))
        def _():
            arrived(LD, p, rzd.at[p])
            line[p] = plus(line[p], rzd[p])
        @pl.when(p > z)
        def _(): line_up(p).start()
        @pl.when(p < z)
        def _(): line_down(p).start()

    def unit_rows(p):
        value = hidden_ref[p].astype(f32)
        scale = lax.rsqrt(jnp.mean(value * value, axis=-1, keepdims=True) + eps)
        return scale, value * scale

    def gain_row():
        sums[0, 0:8] = jnp.zeros((8, sums.shape[2]), f32)
        sums[0, 1:2] = ffn_ref[...]
        sums[0, 2:3, 0 : heads_ref.shape[1]] = heads_ref[...]
        sums[0, 8:] = router_ref[...]
        def add_plane(p, _):
            sums[0, 0:1] += jnp.sum(part_ref[p].astype(f32) * unit_rows(p)[1], axis=0, keepdims=True)
            return 0
        lax.fori_loop(0, 4, add_plane, 0)
        small_copy(0).start()

    def own_rows():
        total = part_ref[z].astype(f32)
        @pl.when(z > 0)
        def _(): arrived(LU, z, rzu.at[z])
        @pl.when(z < 3)
        def _(): arrived(LD, z, rzd.at[z])
        total = total + jnp.where(z > 0, rzu[z].astype(f32), 0.0) + jnp.where(z < 3, rzd[z].astype(f32), 0.0)
        scale, unit = unit_rows(z)
        scaled = total * gain_ref[...]
        grad = scale * (scaled - unit * jnp.mean(unit * scaled, axis=-1, keepdims=True))
        rows[z] = (resid_ref[...] + grad).astype(bf)
        @pl.when(z < 3)
        def _(): row_up(z).start()
        @pl.when(z > 0)
        def _(): row_down(z).start()

    def row_step(k):
        p = plane_at(z, k)
        @pl.when(p < z)
        def _(): arrived(RU, p, rows.at[p])
        @pl.when(p > z)
        def _(): arrived(RD, p, rows.at[p])
        @pl.when((p < z) & (z < 3))
        def _(): row_up(p).start()
        @pl.when((p > z) & (z > 0))
        def _(): row_down(p).start()

    def small_copy(i):
        return pltpu.make_async_remote_copy(src_ref=sums.at[i], dst_ref=got.at[i], send_sem=ssend.at[i], recv_sem=srecv.at[i],
                                            device_id=partners[i], device_id_type=MESH)
    def small_step(i):
        small_copy(i).wait_recv()
        if i < 4:
            sums[i + 1] = sums[i] + got[i]
            small_copy(i + 1).start()
        else:
            small_out[...] = sums[i] + got[i]

    def ends(f):
        pl.when(~middle_plane)(f)
    def mids(f):
        pl.when(middle_plane)(f)

    for k in range(4):
        to_core(k).start()
    ends(lambda: line_step(0))
    gain_row()
    begin(0)
    begin(1)
    begin(2)
    begin(3)
    mids(lambda: line_step(0))
    ends(lambda: line_step(1))
    small_step(0)
    middle(0)
    middle(1)
    mids(lambda: line_step(1))
    mids(lambda: line_step(2))
    ends(lambda: line_step(2))
    middle(2)
    middle(3)
    small_step(1)
    own_rows()
    finish(0)
    finish(1)
    finish(2)
    finish(3)
    ends(lambda: row_step(1))
    mids(lambda: row_step(1))
    mids(lambda: row_step(2))
    spread(0)
    spread(1)
    small_step(2)
    mids(lambda: row_step(3))
    ends(lambda: row_step(2))
    spread(2)
    spread(3)
    last(0)
    small_step(3)
    ends(lambda: row_step(3))
    last(1)
    last(2)
    small_step(4)
    last(3)

    sib = 1 - core
    for k in range(4):
        for c in (to_core, far_x, far_y, x_top, x_bot, y_top, y_bot, give_x, give_y, give_c, pass_x, pass_y, c_x, c_y, c_a, c_b):
            c(k).wait_send()
        arrived(GC, k, res[k].at[sib, chip])
        arrived(GCX, k, res[k].at[sib, cx])
        arrived(GCY, k, res[k].at[sib, cy])
        arrived(GCA, k, res[k].at[sib, cd, TOP[k]])
        arrived(GCB, k, res[k].at[sib, cd, BOT[k]])
    def drain(p, _):
        @pl.when(p > z)
        def _(): line_up(p).wait_send()
        @pl.when(p < z)
        def _(): line_down(p).wait_send()
        @pl.when((z < 3) & (p <= z))
        def _(): row_up(p).wait_send()
        @pl.when((z > 0) & (p >= z))
        def _(): row_down(p).wait_send()
        return 0
    lax.fori_loop(0, 4, drain, 0)
    for i in range(5): small_copy(i).wait_send()

def final_totals(part, weights, router, ffn, heads, hidden, resid, gain, collective_id):
    vm = pl.BlockSpec(memory_space=pltpu.VMEM)
    planes = part.shape
    small = (5, 8 + router.shape[0], router.shape[1])
    whole = [pltpu.VMEM(w.shape[1:], bf) for w in weights]
    quarter = [pltpu.VMEM(w.shape[2:], bf) for w in weights]
    half = [pltpu.VMEM((w.shape[2] // 2, w.shape[3]), bf) for w in weights]
    return pl.pallas_call(
        totals_kernel,
        out_shape=tuple(jax.ShapeDtypeStruct(w.shape, bf) for w in weights) + (
            jax.ShapeDtypeStruct(planes, bf), jax.ShapeDtypeStruct(small[1:], f32)),
        in_specs=[vm] * 11,
        out_specs=(vm,) * 6,
        scratch_shapes=whole + whole + half + half + quarter + quarter + [
            pltpu.VMEM(planes, bf), pltpu.VMEM(planes, bf), pltpu.VMEM(planes, bf),
            pltpu.VMEM(small, f32), pltpu.VMEM(small, f32),
            pltpu.SemaphoreType.DMA((20, 4)), pltpu.SemaphoreType.DMA((20, 4)),
            pltpu.SemaphoreType.DMA((5,)), pltpu.SemaphoreType.DMA((5,)),
        ],
        compiler_params=pltpu.CompilerParams(collective_id=collective_id, has_side_effects=True, vmem_limit_bytes=60 << 20),
    )(part, *weights, router, ffn, heads, hidden, resid, gain)


def slot_experts(routed_low, gates, picked, grad_out, expert_routes, gate_weight, up_weight, down_weight):
    highest = lax.Precision.HIGHEST
    quarter, width = grad_out.shape
    top_count = expert_routes.shape[1]
    experts = picked.shape[2]
    capacity = max(2, 2 * quarter * top_count // experts)
    picked_wide = picked.astype(jnp.float32)
    grad_rows = grad_out.astype(jnp.float32)
    flat_route = expert_routes.reshape(-1)
    flat_pick = picked.reshape(-1, experts).astype(jnp.int32)
    rank = jnp.sum((jnp.cumsum(flat_pick, axis=0) - 1) * flat_pick, axis=1)
    place = flat_route * capacity + rank
    row_token = jnp.arange(quarter * top_count, dtype=jnp.int32) // top_count
    send_rows = (
        jnp.zeros((experts * capacity, width), jnp.bfloat16).at[place].set(routed_low[row_token])
    )
    arrived = lax.all_to_all(
        send_rows.reshape(experts, capacity, width), "exp", split_axis=0, concat_axis=1, tiled=True
    )
    rows_used = lax.all_gather(arrived, "tp", axis=1, tiled=True)
    gate_act = jnp.einsum(
        "erd,edf->erf", rows_used, gate_weight, preferred_element_type=jnp.float32
    )
    up_act = jnp.einsum("erd,edf->erf", rows_used, up_weight, preferred_element_type=jnp.float32)
    hidden_low = (jax.nn.silu(gate_act) * up_act).astype(jnp.bfloat16)
    partial_out = jnp.einsum(
        "erf,efd->erd", hidden_low, down_weight, preferred_element_type=jnp.float32
    )
    expert_out = lax.psum_scatter(partial_out, "tp", scatter_dimension=1, tiled=True)
    returned = lax.all_to_all(
        expert_out.astype(jnp.bfloat16), "exp", split_axis=1, concat_axis=0, tiled=True
    )
    back_rows = (
        returned.reshape(experts * capacity, width)[place]
        .reshape(quarter, top_count, width)
        .astype(jnp.float32)
    )
    moe = jnp.einsum("tk,tkd->td", gates, back_rows, precision=highest)
    grad_gates = jnp.einsum("tkd,td->tk", back_rows, grad_rows, precision=highest)
    grad_chosen = gates * (grad_gates - jnp.sum(gates * grad_gates, axis=-1, keepdims=True))
    grad_logits = jnp.einsum("tke,tk->te", picked_wide, grad_chosen, precision=highest)
    weighted_grad = (
        (gates[:, :, None] * grad_rows[:, None, :])
        .astype(jnp.bfloat16)
        .reshape(quarter * top_count, width)
    )
    send_grads = jnp.zeros((experts * capacity, width), jnp.bfloat16).at[place].set(weighted_grad)
    grad_arrived = lax.all_to_all(
        send_grads.reshape(experts, capacity, width), "exp", split_axis=0, concat_axis=1, tiled=True
    )
    sigmoid_gate = jax.nn.sigmoid(gate_act)
    silu_gate = gate_act * sigmoid_gate
    slope = sigmoid_gate * (1.0 + gate_act * (1.0 - sigmoid_gate))
    grad_used = lax.all_gather(grad_arrived, "tp", axis=1, tiled=True)
    grad_hid = jnp.einsum(
        "erd,efd->erf", grad_used, down_weight, preferred_element_type=jnp.float32
    )
    grad_down = jnp.einsum(
        "erf,erd->efd", hidden_low, grad_used, preferred_element_type=jnp.float32
    )
    grad_gate = (grad_hid * up_act * slope).astype(jnp.bfloat16)
    grad_up = (grad_hid * silu_gate).astype(jnp.bfloat16)
    grad_gate_w = jnp.einsum(
        "erd,erf->edf", rows_used, grad_gate, preferred_element_type=jnp.float32
    )
    grad_up_w = jnp.einsum("erd,erf->edf", rows_used, grad_up, preferred_element_type=jnp.float32)
    input_part = jnp.einsum(
        "erf,edf->erd", grad_gate, gate_weight, preferred_element_type=jnp.float32
    ) + jnp.einsum("erf,edf->erd", grad_up, up_weight, preferred_element_type=jnp.float32)
    grad_input = lax.psum_scatter(input_part, "tp", scatter_dimension=1, tiled=True).astype(
        jnp.bfloat16
    )
    grad_back = lax.all_to_all(grad_input, "exp", split_axis=1, concat_axis=0, tiled=True)
    expert_grad = jnp.sum(
        grad_back.reshape(experts * capacity, width)[place]
        .reshape(quarter, top_count, width)
        .astype(jnp.float32),
        axis=1,
    )
    return moe, grad_logits, expert_grad, grad_gate_w, grad_up_w, grad_down


def gate_pair(dense_gates):
    pad = ((0, 0), (0, gate_lanes // 2 - dense_gates.shape[1]))
    high = dense_gates.astype(bf)
    low = (dense_gates - high.astype(f32)).astype(bf)
    return [jnp.pad(high, pad), jnp.pad(low, pad)]


def per_device(
    fits,
    hidden_in,
    attn_gain,
    query_weight,
    key_weight,
    value_weight,
    qnorm_gain,
    knorm_gain,
    out_weight,
    ffn_gain,
    router_weight,
    gate_weight,
    up_weight,
    down_weight,
    expert_routes,
    seq_lengths,
    grad_out,
):
    highest = lax.Precision.HIGHEST
    group_rows = hidden_in.shape[0]
    width = hidden_in.shape[1]
    head_size = qnorm_gain.shape[0]
    quarter = grad_out.shape[0]
    experts = router_weight.shape[1]
    tp_index = lax.axis_index("tp")
    widened = hidden_in.astype(jnp.float32)
    normed_one = rms_norm(widened, attn_gain)
    normed_low = normed_one.astype(jnp.bfloat16)
    segment, cosine, sine = rotary_tables(seq_lengths[0], group_rows, head_size)
    same_seq = segment[:, None] == segment[None, :]

    def prepare(projected, gain):
        return head_prep(projected, gain, cosine, sine)

    query_proj = jnp.dot(normed_low, query_weight, preferred_element_type=jnp.float32)
    key_proj = jnp.dot(normed_low, key_weight, preferred_element_type=jnp.float32)
    value_proj = jnp.dot(normed_low, value_weight, preferred_element_type=jnp.float32)
    queries, query_back = jax.vjp(prepare, query_proj, qnorm_gain)
    keys, key_back = jax.vjp(prepare, key_proj, knorm_gain)
    query_low = queries.astype(jnp.bfloat16)
    key_low = keys.astype(jnp.bfloat16)
    value_low = value_proj.astype(jnp.bfloat16).reshape(group_rows, -1, head_size)
    scores = masked_scores(query_low, key_low, same_seq, head_size)
    top_score = jnp.max(scores, axis=-1, keepdims=True)
    log_total = top_score + jnp.log(jnp.sum(jnp.exp(scores - top_score), axis=-1, keepdims=True))
    probs_low = jnp.exp(scores - log_total).astype(jnp.bfloat16)
    mixed = jnp.einsum("hts,shd->thd", probs_low, value_low, preferred_element_type=jnp.float32)
    mixed_low = mixed.astype(jnp.bfloat16).reshape(group_rows, -1)
    attn_part = jnp.dot(mixed_low, out_weight, preferred_element_type=jnp.float32)
    if fits:
        planes = (4, quarter, width)
        attn_rows, near_grads = open_exchange(attn_part.astype(bf).reshape(planes), grad_out, 5)
    else:
        attn_rows = lax.psum_scatter(attn_part, "tp", scatter_dimension=0, tiled=True)
    own_rows = lax.dynamic_slice_in_dim(widened, tp_index * quarter, quarter, 0)
    resid = own_rows + attn_rows
    normed_two, norm_two_back = jax.vjp(rms_norm, resid, ffn_gain)
    routed_low = normed_two.astype(jnp.bfloat16)
    logits = jnp.dot(routed_low, router_weight, preferred_element_type=jnp.float32)
    picked = expert_routes[:, :, None] == jnp.arange(experts, dtype=jnp.int32)[None, None, :]
    picked_wide = picked.astype(jnp.float32)
    chosen = jnp.einsum("tke,te->tk", picked_wide, logits, precision=highest)
    gates = jax.nn.softmax(chosen, axis=-1)
    grad_rows = grad_out.astype(jnp.float32)
    if fits:
        dense_gates = jnp.einsum("tke,tk->te", picked_wide, gates, precision=highest)
        act, grad_gate_w, grad_up_w, grad_down = gather_experts(
            jnp.concatenate([routed_low] + gate_pair(dense_gates), axis=1),
            near_grads,
            gate_weight,
            up_weight,
            down_weight,
        )
        (sums,) = scatter_sums(act, (gate_weight, up_weight), input_product, True, 2)
        expert_grad = sums[:, :width]
        grad_gates = sums[:, width : width + experts]
        grad_logits = dense_gates * (
            grad_gates - jnp.sum(dense_gates * grad_gates, axis=-1, keepdims=True)
        )
    else:
        moe, grad_logits, expert_grad, grad_gate_w, grad_up_w, grad_down = slot_experts(
            routed_low,
            gates,
            picked,
            grad_out,
            expert_routes,
            gate_weight,
            up_weight,
            down_weight,
        )
    grad_normed = (
        jnp.dot(grad_logits, router_weight.astype(jnp.float32).T, precision=highest) + expert_grad
    )
    grad_router = jnp.dot(routed_low.astype(jnp.float32).T, grad_logits, precision=highest)
    grad_resid, grad_ffn_gain = norm_two_back(grad_normed)
    grad_resid = grad_resid + grad_rows
    grad_low = grad_resid.astype(jnp.bfloat16)
    if fits:
        moe, grad_attn_low = scatter_sums(act, (down_weight,), output_product, False, 3, grad_low)
        grad_attn_low = grad_attn_low.reshape(group_rows, width)
    else:
        grad_attn_low = lax.all_gather(grad_low, "tp", axis=0, tiled=True)
    block_out = (resid + moe).astype(jnp.bfloat16)
    grad_out_weight = jnp.dot(mixed_low.T, grad_attn_low, preferred_element_type=jnp.float32)
    grad_mixed = jnp.dot(grad_attn_low, out_weight.T, preferred_element_type=jnp.float32)
    grad_mixed_low = grad_mixed.astype(jnp.bfloat16).reshape(group_rows, -1, head_size)
    probs = jnp.exp(masked_scores(query_low, key_low, same_seq, head_size) - log_total)
    grad_probs = jnp.einsum(
        "thd,shd->hts", grad_mixed_low, value_low, preferred_element_type=jnp.float32
    )
    grad_value = jnp.einsum(
        "hts,thd->shd", probs_low, grad_mixed_low, preferred_element_type=jnp.float32
    )
    row_delta = jnp.sum(probs * grad_probs, axis=-1, keepdims=True)
    grad_scores = (probs * (grad_probs - row_delta)).astype(jnp.bfloat16)
    grad_query = jnp.einsum(
        "hts,shd->thd", grad_scores, key_low, preferred_element_type=jnp.float32
    ) / math.sqrt(head_size)
    grad_key = jnp.einsum(
        "hts,thd->shd", grad_scores, query_low, preferred_element_type=jnp.float32
    ) / math.sqrt(head_size)
    grad_query_proj, grad_qgain = query_back(grad_query)
    grad_key_proj, grad_kgain = key_back(grad_key)
    grad_query_low = grad_query_proj.astype(jnp.bfloat16)
    grad_key_low = grad_key_proj.astype(jnp.bfloat16)
    grad_value_low = grad_value.reshape(group_rows, -1).astype(jnp.bfloat16)
    normed_part = (
        jnp.dot(grad_query_low, query_weight.T, preferred_element_type=jnp.float32)
        + jnp.dot(grad_key_low, key_weight.T, preferred_element_type=jnp.float32)
        + jnp.dot(grad_value_low, value_weight.T, preferred_element_type=jnp.float32)
    )
    grad_query_w = jnp.dot(normed_low.T, grad_query_low, preferred_element_type=jnp.float32)
    grad_key_w = jnp.dot(normed_low.T, grad_key_low, preferred_element_type=jnp.float32)
    grad_value_w = jnp.dot(normed_low.T, grad_value_low, preferred_element_type=jnp.float32)
    if fits:
        weights = [
            part.astype(bf).reshape(2, 4, part.shape[0] // 8, part.shape[1])
            for part in (grad_query_w, grad_key_w, grad_value_w, grad_out_weight)
        ]
        *sums, grad_input_rows, small = final_totals(
            normed_part.astype(bf).reshape(planes),
            weights,
            grad_router.T,
            grad_ffn_gain[None],
            jnp.concatenate([grad_qgain, grad_kgain])[None],
            hidden_in.reshape(planes),
            grad_resid,
            attn_gain[None],
            4,
        )
        grad_input_rows = grad_input_rows.reshape(group_rows, width)
        totals = tuple(
            part.reshape(-1, part.shape[3]).astype(f32) for part in sums
        ) + (
            small[0],
            small[2, :head_size],
            small[2, head_size : 2 * head_size],
            small[1],
            small[8:].T,
        )
    else:
        scale_one = lax.rsqrt(jnp.mean(widened * widened, axis=-1, keepdims=True) + eps)
        unit_one = widened * scale_one
        grad_attn_gain = jnp.sum(normed_part * unit_one, axis=0)
        grad_normed_one = lax.psum(normed_part.astype(bf), "tp").astype(f32)
        scaled = grad_normed_one * attn_gain
        grad_from_norm = scale_one * (
            scaled - unit_one * jnp.mean(unit_one * scaled, axis=-1, keepdims=True)
        )
        grad_input_rows = (grad_attn_low.astype(f32) + grad_from_norm).astype(jnp.bfloat16)
        low_totals = lax.psum(
            tuple(
                part.astype(jnp.bfloat16)
                for part in (grad_query_w, grad_key_w, grad_value_w, grad_out_weight)
            ),
            "exp",
        )
        small = lax.psum(
            (grad_attn_gain, grad_qgain, grad_kgain, grad_ffn_gain, grad_router), ("exp", "tp")
        )
        totals = tuple(part.astype(jnp.float32) for part in low_totals) + small
    return (
        block_out,
        grad_input_rows,
        totals[4],
        totals[0],
        totals[1],
        totals[2],
        totals[3],
        totals[5],
        totals[6],
        totals[7],
        totals[8],
        grad_gate_w,
        grad_up_w,
        grad_down,
    )


def solution(mesh):
    in_specs = (
        P("exp", None),
        P(),
        P(None, "tp"),
        P(None, "tp"),
        P(None, "tp"),
        P(),
        P(),
        P("tp", None),
        P(),
        P(),
        P("exp", None, "tp"),
        P("exp", None, "tp"),
        P("exp", "tp", None),
        P(("exp", "tp"), None),
        P("exp", None),
        P(("exp", "tp"), None),
    )
    out_specs = (
        P(("exp", "tp"), None),
        P("exp", None),
        P(),
        P(None, "tp"),
        P(None, "tp"),
        P(None, "tp"),
        P("tp", None),
        P(),
        P(),
        P(),
        P(),
        P("exp", None, "tp"),
        P("exp", None, "tp"),
        P("exp", "tp", None),
    )
    fits = dict(mesh.shape) == {"exp": 8, "tp": 4}
    return jax.shard_map(
        functools.partial(per_device, fits), mesh=mesh, in_specs=in_specs, out_specs=out_specs, check_vma=False
    )
```

```python
import functools
import math

import jax
import jax.numpy as jnp
from jax import lax
from jax.experimental import pallas as pl
from jax.experimental.pallas import tpu as pltpu
from jax.sharding import PartitionSpec as P

eps = 1e-06
rope_base = 10000.0
gate_lanes = 128
MESH = pl.DeviceIdType.MESH
bf = jnp.bfloat16
f32 = jnp.float32
NT = (((1,), (1,)), ((), ()))
TN = (((0,), (0,)), ((), ()))


def rms_norm(values, gain):
    return values * lax.rsqrt(jnp.mean(values * values, axis=-1, keepdims=True) + eps) * gain


def rotary_tables(lengths_row, count, head_size):
    token_index = jnp.arange(count, dtype=jnp.int32)
    seq_ends = jnp.cumsum(lengths_row)
    starts = seq_ends - lengths_row
    member = (
        (token_index[:, None] >= starts[None, :]) & (token_index[:, None] < seq_ends[None, :])
    ).astype(jnp.int32)
    segment = jnp.sum(member * jnp.arange(lengths_row.shape[0], dtype=jnp.int32)[None, :], axis=1)
    offset = jnp.sum(member * starts[None, :], axis=1)
    position = (token_index - offset).astype(jnp.float32)
    frequency = rope_base ** (-jnp.arange(0, head_size, 2, dtype=jnp.float32) / head_size)
    angles = position[:, None] * frequency[None, :]
    return (segment, jnp.cos(angles)[:, None, :], jnp.sin(angles)[:, None, :])


def rotate(values, cosine, sine):
    half = values.shape[-1] // 2
    first = values[..., :half]
    second = values[..., half:]
    return jnp.concatenate(
        [first * cosine - second * sine, second * cosine + first * sine], axis=-1
    )


def head_prep(projected, gain, cosine, sine):
    head_size = gain.shape[0]
    shaped = projected.reshape(projected.shape[0], projected.shape[1] // head_size, head_size)
    return rotate(rms_norm(shaped, gain), cosine, sine)


def masked_scores(query_low, key_low, same_seq, head_size):
    scores = jnp.einsum(
        "thd,shd->hts", query_low, key_low, preferred_element_type=jnp.float32
    ) / math.sqrt(head_size)
    return jnp.where(same_seq[None], scores, -1e30)


def plane_at(z, step):
    from_end = step
    from_middle = jnp.where(step == 0, 1, jnp.where(step == 1, 0, step))
    base = jnp.where((z == 0) | (z == 3), from_end, from_middle)
    return jnp.where(z < 2, base, 3 - base)

Z, X, Y, FX, FY, CO, CX, CY, CA, CB = range(10)

def gather_kernel(own_ref, grad_hbm, wg_hbm, wu_hbm, wd_hbm,
                  act_hbm, dg_ref, du_ref, dd_ref,
                  rows, grads, wg, wu, wd, act, send, up_send, recv, gsend, gline, grecv, load, store, wload):
    e = lax.axis_index("exp")
    z = lax.axis_index("tp")
    ex, ey, ec, ed = (jnp.bitwise_xor(e, m) for m in (2, 4, 1, 6))
    width = wg.shape[1]
    quarter = own_ref.shape[0]
    half = quarter // 2
    hid = wg.shape[2]
    experts_here = wg.shape[0]
    at_x, at_y, at_c = (ex, z), (ey, z), (ec, z)
    at_up, at_down = (e, z + 1), (e, z - 1)

    wcopies = [pltpu.make_async_copy(s, d, wload.at[i]) for i, (s, d) in enumerate(((wg_hbm, wg), (wu_hbm, wu), (wd_hbm, wd)))]
    for c in wcopies: c.start()

    loads = [pltpu.make_async_copy(grad_hbm.at[plane_at(z, k)], grads.at[k], load.at[k]) for k in range(2)]
    for c in loads: c.start()
    middle = (z == 1) | (z == 2)
    def second_load():
        return pltpu.make_async_copy(grad_hbm.at[plane_at(z, 2), e], grads.at[2, e], load.at[2])
    @pl.when(middle)
    def _(): second_load().start()

    bar = pltpu.get_barrier_semaphore()
    for d in (at_x, at_y, at_c):
        pl.semaphore_signal(bar, inc=1, device_id=d, device_id_type=MESH)
    @pl.when(z < 3)
    def _(): pl.semaphore_signal(bar, inc=1, device_id=at_up, device_id_type=MESH)
    @pl.when(z > 0)
    def _(): pl.semaphore_signal(bar, inc=1, device_id=at_down, device_id_type=MESH)
    pl.semaphore_wait(bar, 3 + jnp.where(z < 3, 1, 0) + jnp.where(z > 0, 1, 0))

    TOP, BOT, ALLR = pl.ds(0, half), pl.ds(half, half), pl.ds(0, quarter)

    def copy(kind, plane, group, part, to, src=None, sem=None):
        place = rows.at[plane, group, part]
        return pltpu.make_async_remote_copy(
            src_ref=place if src is None else src, dst_ref=place,
            send_sem=(send.at[kind, plane] if sem is None else sem), recv_sem=recv.at[kind, plane],
            device_id=to, device_id_type=MESH)

    def up(plane, src=None): return copy(Z, plane, e, ALLR, at_up, src, up_send.at[plane])
    def down(plane, src=None): return copy(Z, plane, e, ALLR, at_down, src)
    def to_x(plane, src=None): return copy(X, plane, e, ALLR, at_x, src)
    def to_y(plane, src=None): return copy(Y, plane, e, ALLR, at_y, src)
    def to_c(plane, src=None): return copy(CO, plane, e, ALLR, at_c, src)
    def fwd_y(plane): return copy(FY, plane, ex, TOP, at_y)
    def fwd_x(plane): return copy(FX, plane, ey, BOT, at_x)
    def c_x(plane): return copy(CX, plane, ex, ALLR, at_c)
    def c_y(plane): return copy(CY, plane, ey, ALLR, at_c)
    def c_a(plane): return copy(CA, plane, ed, TOP, at_c)
    def c_b(plane): return copy(CB, plane, ed, BOT, at_c)

    def arrived(kind, plane, group, part):
        place = rows.at[plane, group, part]
        pltpu.make_async_copy(place, place, recv.at[kind, plane]).wait()

    outward = (e, jnp.where(z == 1, 0, 3))
    inward = (e, 3 - z)
    def grad_line(which, src, step, to):
        return pltpu.make_async_remote_copy(src_ref=src, dst_ref=grads.at[step, e], send_sem=gline.at[which],
                                            recv_sem=grecv.at[Z, step - 2], device_id=to, device_id_type=MESH)
    def line_a(): return grad_line(0, grad_hbm.at[plane_at(z, 2), e], 2, outward)
    def line_b(): return grad_line(1, grad_hbm.at[plane_at(z, 1), e], 3, inward)
    def line_c(): return grad_line(2, grads.at[3, e], 3, outward)
    def gcopy(kind, k, group, part, to):
        place = grads.at[k, group, part]
        return pltpu.make_async_remote_copy(src_ref=place, dst_ref=place, send_sem=gsend.at[kind, k - 2],
                                            recv_sem=grecv.at[kind, k - 2], device_id=to, device_id_type=MESH)
    def g_x(k): return gcopy(X, k, e, ALLR, at_x)
    def g_y(k): return gcopy(Y, k, e, ALLR, at_y)
    def g_c(k): return gcopy(CO, k, e, ALLR, at_c)
    def gfwd_y(k): return gcopy(FY, k, ex, TOP, at_y)
    def gfwd_x(k): return gcopy(FX, k, ey, BOT, at_x)
    def gc_x(k): return gcopy(CX, k, ex, ALLR, at_c)
    def gc_y(k): return gcopy(CY, k, ey, ALLR, at_c)
    def gc_a(k): return gcopy(CA, k, ed, TOP, at_c)
    def gc_b(k): return gcopy(CB, k, ed, BOT, at_c)
    def garrived(kind, k, group, part):
        place = grads.at[k, group, part]
        pltpu.make_async_copy(place, place, grecv.at[kind, k - 2]).wait()

    def grad_row(k):
        if k == 2:
            @pl.when(middle)
            def _(): second_load().wait()
            @pl.when(~middle)
            def _(): garrived(Z, 2, e, ALLR)
        else:
            garrived(Z, 3, e, ALLR)
            @pl.when(middle)
            def _(): line_c().start()
        g_x(k).start()
        g_y(k).start()
        g_c(k).start()

    def grad_sides(k):
        garrived(X, k, ex, ALLR)
        gfwd_y(k).start()
        gc_x(k).start()
        garrived(Y, k, ey, ALLR)
        gfwd_x(k).start()
        gc_y(k).start()

    def grad_far(k):
        garrived(FY, k, ed, TOP)
        gc_a(k).start()
        garrived(FX, k, ed, BOT)
        gc_b(k).start()

    @pl.when(z < 3)
    def _(): up(z, own_ref).start()
    @pl.when(z > 0)
    def _(): down(z, own_ref).start()
    to_x(z, own_ref).start()
    to_y(z, own_ref).start()
    to_c(z, own_ref).start()
    rows[z, e] = own_ref[...]

    def serve_line(k):
        p = plane_at(z, k)
        arrived(Z, p, e, ALLR)
        @pl.when((p < z) & (z < 3))
        def _(): up(p).start()
        @pl.when((p > z) & (z > 0))
        def _(): down(p).start()
        to_x(p).start()
        to_y(p).start()
        to_c(p).start()

    def serve_sides(k):
        p = plane_at(z, k)
        arrived(X, p, ex, ALLR)
        fwd_y(p).start()
        c_x(p).start()
        arrived(Y, p, ey, ALLR)
        fwd_x(p).start()
        c_y(p).start()

    def serve_far(k):
        p = plane_at(z, k)
        arrived(FY, p, ed, TOP)
        c_a(p).start()
        arrived(FX, p, ed, BOT)
        c_b(p).start()

    def store_copy(step):
        k, h = step // 2, lax.rem(step, 2)
        first = jnp.bitwise_xor(jnp.bitwise_and(e, 4), h * 4)
        return pltpu.make_async_copy(act, act_hbm.at[pl.ds(first // 2, 2), :, plane_at(z, k)], store)

    @pl.when(middle)
    def _():
        line_a().start()
        line_b().start()
    serve_line(1)
    @pl.when(middle)
    def _(): serve_line(2)
    serve_sides(0)
    for c in wcopies + loads: c.wait()

    def step_body(step, _):
        k, h = step // 2, lax.rem(step, 2)
        p = plane_at(z, k)
        first = jnp.bitwise_xor(jnp.bitwise_and(e, 4), h * 4)
        sib_x = jnp.bitwise_xor(ec, 2)
        sib_y = jnp.bitwise_xor(ec, 4)
        sib_d = jnp.bitwise_xor(ec, 6)
        @pl.when(h == 0)
        def _():
            arrived(CO, p, ec, ALLR)
            arrived(CX, p, sib_x, ALLR)
            @pl.when(k >= 2)
            def _():
                garrived(CO, k, ec, ALLR)
                garrived(CX, k, sib_x, ALLR)
        @pl.when(h == 1)
        def _():
            arrived(CY, p, sib_y, ALLR)
            arrived(CA, p, sib_d, TOP)
            arrived(CB, p, sib_d, BOT)
            @pl.when(k >= 2)
            def _():
                garrived(CY, k, sib_y, ALLR)
                garrived(CA, k, sib_d, TOP)
                garrived(CB, k, sib_d, BOT)
        lane = lax.broadcasted_iota(jnp.int32, (4 * quarter, gate_lanes), 1)

        def expert_body(j, _):
            x = rows[p, pl.ds(first, 4), :, :width].reshape(4 * quarter, width)
            g = grads[k, pl.ds(first, 4)].reshape(4 * quarter, width)
            extra = rows[p, pl.ds(first, 4), :, width:].reshape(4 * quarter, gate_lanes).astype(f32)
            expert = e * experts_here + j
            mine = (lane == expert) | (lane == expert + gate_lanes // 2)
            gate = jnp.sum(jnp.where(mine, extra, 0.0), axis=1, keepdims=True)
            ga = jnp.dot(x, wg[j], preferred_element_type=f32)
            ua = jnp.dot(x, wu[j], preferred_element_type=f32)
            gh = lax.dot_general(g, wd[j], (((1,), (1,)), ((), ())), preferred_element_type=f32)
            sg = jax.nn.sigmoid(ga)
            silu = ga * sg
            hidden = silu * ua
            score = jnp.sum(hidden * gh, axis=1, keepdims=True)
            gh = gh * gate
            hg = (hidden * gate).astype(bf)
            da = (gh * ua * (sg * (1.0 + ga * (1.0 - sg)))).astype(bf)
            du = (gh * silu).astype(bf)
            @pl.when((step > 0) & (j == 0))
            def _(): store_copy(step - 1).wait()
            base = j * 2 * hid
            shape3 = (2, 2, quarter, hid)
            act[:, :, :, pl.ds(pl.multiple_of(base, hid), hid)] = da.reshape(shape3)
            act[:, :, :, pl.ds(pl.multiple_of(base + hid, hid), hid)] = du.reshape(shape3)
            act[:, :, :, pl.ds(pl.multiple_of((2 * experts_here + j) * hid, hid), hid)] = hg.reshape(shape3)
            scores = jnp.where(lane == expert, score, 0.0).astype(bf).reshape(2, 2, quarter, gate_lanes)
            act[:, :, :, pl.ds(pl.multiple_of(experts_here * 3 * hid + j * gate_lanes, gate_lanes), gate_lanes)] = scores
            @pl.when(step == 0)
            def _():
                dg_ref[j] = jnp.zeros(dg_ref.shape[1:], f32)
                du_ref[j] = jnp.zeros(du_ref.shape[1:], f32)
                dd_ref[j] = jnp.zeros(dd_ref.shape[1:], f32)
            slot = 2 * step + j
            for at, work, which in (
                (1, serve_far, 0),
                (2, serve_sides, 1),
                (4, grad_row, 2),
                (5, serve_far, 1),
                (5, serve_sides, 2),
                (6, grad_row, 3),
                (7, grad_sides, 2),
                (8, serve_far, 2),
                (8, serve_sides, 3),
                (9, grad_far, 2),
                (11, serve_far, 3),
                (11, grad_sides, 3),
                (13, grad_far, 3),
            ):
                @pl.when(slot == at)
                def _(): work(which)
            @pl.when((slot == 1) & middle)
            def _(): serve_line(3)
            @pl.when((slot == 1) & ~middle)
            def _(): serve_line(2)
            @pl.when((slot == 3) & ~middle)
            def _(): serve_line(3)
            dd_ref[j] += lax.dot_general(hg, g, TN, preferred_element_type=f32)
            dg_ref[j] += lax.dot_general(x, da, TN, preferred_element_type=f32)
            du_ref[j] += lax.dot_general(x, du, TN, preferred_element_type=f32)
            return 0
        lax.fori_loop(0, experts_here, expert_body, 0)
        store_copy(step).start()
        return 0
    lax.fori_loop(0, 8, step_body, 0)
    store_copy(7).wait()

    @pl.when(middle)
    def _():
        for c in (line_a, line_b, line_c):
            c().wait_send()
    def drain_grads(k, _):
        for c in (g_x, g_y, g_c, gfwd_y, gfwd_x, gc_x, gc_y, gc_a, gc_b):
            c(k).wait_send()
        return 0
    lax.fori_loop(2, 4, drain_grads, 0)
    def drain(k, _):
        p = plane_at(z, k)
        @pl.when((z < 3) & (p <= z))
        def _(): up(p).wait_send()
        @pl.when((z > 0) & (p >= z))
        def _(): down(p).wait_send()
        for c in (to_x, to_y, to_c, fwd_y, fwd_x, c_x, c_y, c_a, c_b):
            c(p).wait_send()
        return 0
    lax.fori_loop(0, 4, drain, 0)

def gather_experts(own, grads_all, wg, wu, wd):
    n_here, width, hid = wg.shape
    quarter, wide = own.shape
    lanes = wide - width
    cols = n_here * 3 * hid + n_here * lanes
    any_ = pl.BlockSpec(memory_space=pl.ANY)
    vm = pl.BlockSpec(memory_space=pltpu.VMEM)
    return pl.pallas_call(
        gather_kernel,
        out_shape=(jax.ShapeDtypeStruct((4, 2, 4, quarter, cols), bf),
                   jax.ShapeDtypeStruct(wg.shape, f32), jax.ShapeDtypeStruct(wu.shape, f32), jax.ShapeDtypeStruct(wd.shape, f32)),
        in_specs=[vm, any_, any_, any_, any_],
        out_specs=(any_, vm, vm, vm),
        scratch_shapes=[
            pltpu.VMEM((4, 8, quarter, wide), bf),
            pltpu.VMEM((4, 8, quarter, width), bf),
            pltpu.VMEM(wg.shape, bf), pltpu.VMEM(wu.shape, bf), pltpu.VMEM(wd.shape, bf),
            pltpu.VMEM((2, 2, quarter, cols), bf),
            pltpu.SemaphoreType.DMA((10, 4)), pltpu.SemaphoreType.DMA((4,)), pltpu.SemaphoreType.DMA((10, 4)),
            pltpu.SemaphoreType.DMA((10, 2)), pltpu.SemaphoreType.DMA((3,)), pltpu.SemaphoreType.DMA((10, 2)),
            pltpu.SemaphoreType.DMA((3,)), pltpu.SemaphoreType.DMA, pltpu.SemaphoreType.DMA((3,)),
        ],
        compiler_params=pltpu.CompilerParams(collective_id=1, has_side_effects=True, vmem_limit_bytes=63 << 20),
        cost_estimate=pl.CostEstimate(flops=12 * 4096 * 2048 * hid * n_here, bytes_accessed=64 << 20, transcendentals=0),
    )(own, grads_all, wg, wu, wd)


def head_scores(queries, keys, same, head_size):
    scores = lax.dot_general(queries, keys, NT, preferred_element_type=f32) / math.sqrt(head_size)
    scores = jnp.where(same, scores, -1e30)
    grown = jnp.exp(scores - jnp.max(scores, axis=-1, keepdims=True))
    return grown / jnp.sum(grown, axis=-1, keepdims=True)

def mixed_back(grad_rows, out_w, mixed, grad_mixed, grad_out_w):
    grads = grad_rows[...].reshape(-1, grad_rows.shape[2])
    grad_mixed[...] = lax.dot_general(grads, out_w[...], NT, preferred_element_type=f32).astype(bf)
    grad_out_w[...] = lax.dot_general(mixed[...], grads, TN, preferred_element_type=f32).astype(bf)

def head_back(h, queries, keys, values, projected, gains, cosine, sine, seg_col, seg_row, grad_mixed, grad_heads, grad_gains):
    head_size = cosine.shape[1]
    at = pl.ds(pl.multiple_of(h * head_size, head_size), head_size)
    same = seg_col[...] == seg_row[...]
    q, k, v, gm = queries[:, at], keys[:, at], values[:, at], grad_mixed[:, at]
    probs = head_scores(q, k, same, head_size)
    grad_probs = lax.dot_general(gm, v, NT, preferred_element_type=f32)
    grad_heads[2, :, at] = lax.dot_general(probs.astype(bf), gm, TN, preferred_element_type=f32).astype(bf)
    delta = jnp.sum(probs * grad_probs, axis=-1, keepdims=True)
    grad_scores = (probs * (grad_probs - delta)).astype(bf)
    back = (
        jnp.dot(grad_scores, k, preferred_element_type=f32),
        lax.dot_general(grad_scores, q, TN, preferred_element_type=f32),
    )
    for i in range(2):
        grad = back[i] / math.sqrt(head_size)
        grad = grad * cosine[...] - pltpu.roll(grad, head_size // 2, axis=1) * sine[...]
        value = projected[i][:, at]
        scale = lax.rsqrt(jnp.mean(value * value, axis=-1, keepdims=True) + eps)
        unit = value * scale
        grad_gains[i : i + 1] += jnp.sum(grad * unit, axis=0, keepdims=True)
        scaled = grad * gains[i : i + 1]
        grad_heads[i, :, at] = (scale * (scaled - unit * jnp.mean(unit * scaled, axis=-1, keepdims=True))).astype(bf)

def input_back(weights, grad_heads, part, cols):
    total = None
    for i, w in enumerate(weights):
        one = lax.dot_general(grad_heads[i], w[cols, :], NT, preferred_element_type=f32)
        total = one if total is None else total + one
    part[:, :, cols] = total.astype(bf).reshape(part.shape[0], part.shape[1], -1)


HZ, HX, HY, HFX, HFY, HC, HCX, HCY, HCA, HCB, HU, HD = range(12)

def opening_kernel(part_ref, grad_ref, out_ref, grads, line, rzu, rzd, send, up_send, recv, local):
    e = lax.axis_index("exp")
    z = lax.axis_index("tp")
    ex, ey, ec, ed = (jnp.bitwise_xor(e, m) for m in (2, 4, 1, 6))
    at_x, at_y, at_c = (ex, z), (ey, z), (ec, z)
    at_up, at_down = (e, z + 1), (e, z - 1)
    middle_plane = (z == 1) | (z == 2)
    quarter = grad_ref.shape[0]
    half = quarter // 2
    TOP, BOT, ALLR = pl.ds(0, half), pl.ds(half, half), pl.ds(0, quarter)

    bar = pltpu.get_barrier_semaphore()
    for d in (at_x, at_y, at_c):
        pl.semaphore_signal(bar, inc=1, device_id=d, device_id_type=MESH)
    @pl.when(z < 3)
    def _(): pl.semaphore_signal(bar, inc=1, device_id=at_up, device_id_type=MESH)
    @pl.when(z > 0)
    def _(): pl.semaphore_signal(bar, inc=1, device_id=at_down, device_id_type=MESH)
    pl.semaphore_wait(bar, 3 + jnp.where(z < 3, 1, 0) + jnp.where(z > 0, 1, 0))

    def copy(kind, plane, group, part, to, src=None, sem=None):
        place = grads.at[plane, group, part]
        return pltpu.make_async_remote_copy(
            src_ref=place if src is None else src, dst_ref=place,
            send_sem=send.at[kind, plane] if sem is None else sem, recv_sem=recv.at[kind, plane],
            device_id=to, device_id_type=MESH)
    def arrived(kind, plane, place):
        pltpu.make_async_copy(place, place, recv.at[kind, plane]).wait()
    def line_copy(kind, p, landing, to):
        return pltpu.make_async_remote_copy(src_ref=line.at[p], dst_ref=landing.at[p], send_sem=send.at[kind, p],
                                            recv_sem=recv.at[kind, p], device_id=to, device_id_type=MESH)
    def line_up(p): return line_copy(HU, p, rzu, at_up)
    def line_down(p): return line_copy(HD, p, rzd, at_down)
    def up(): return copy(HZ, z, e, ALLR, at_up, grad_ref, up_send)
    def down(): return copy(HZ, z, e, ALLR, at_down, grad_ref)
    def to_x(p, src=None): return copy(HX, p, e, ALLR, at_x, src)
    def to_y(p, src=None): return copy(HY, p, e, ALLR, at_y, src)
    def to_c(p, src=None): return copy(HC, p, e, ALLR, at_c, src)
    def fwd_y(p): return copy(HFY, p, ex, TOP, at_y)
    def fwd_x(p): return copy(HFX, p, ey, BOT, at_x)
    def c_x(p): return copy(HCX, p, ex, ALLR, at_c)
    def c_y(p): return copy(HCY, p, ey, ALLR, at_c)
    def c_a(p): return copy(HCA, p, ed, TOP, at_c)
    def c_b(p): return copy(HCB, p, ed, BOT, at_c)

    def serve_sides(k):
        p = plane_at(z, k)
        arrived(HX, p, grads.at[p, ex])
        fwd_y(p).start()
        c_x(p).start()
        arrived(HY, p, grads.at[p, ey])
        fwd_x(p).start()
        c_y(p).start()

    def serve_far(k):
        p = plane_at(z, k)
        arrived(HFY, p, grads.at[p, ed, TOP])
        c_a(p).start()
        arrived(HFX, p, grads.at[p, ed, BOT])
        c_b(p).start()

    def line_step(k):
        p = plane_at(z, 3 - k)
        line[p] = part_ref[p]
        @pl.when((z > 0) & (p >= z))
        def _():
            arrived(HU, p, rzu.at[p])
            line[p] = (line[p].astype(f32) + rzu[p].astype(f32)).astype(bf)
        @pl.when((z < 3) & (p <= z))
        def _():
            arrived(HD, p, rzd.at[p])
            line[p] = (line[p].astype(f32) + rzd[p].astype(f32)).astype(bf)
        @pl.when(p > z)
        def _(): line_up(p).start()
        @pl.when(p < z)
        def _(): line_down(p).start()

    def ends(f): pl.when(~middle_plane)(f)
    def mids(f): pl.when(middle_plane)(f)

    ends(lambda: line_step(0))
    @pl.when(z < 3)
    def _(): up().start()
    @pl.when(z > 0)
    def _(): down().start()
    to_x(z, grad_ref).start()
    to_y(z, grad_ref).start()
    to_c(z, grad_ref).start()
    own = pltpu.make_async_copy(grad_ref, grads.at[z, e], local)
    own.start()
    mids(lambda: line_step(0))
    ends(lambda: line_step(1))
    serve_sides(0)
    near = plane_at(z, 1)
    arrived(HZ, near, grads.at[near, e])
    to_x(near).start()
    to_y(near).start()
    to_c(near).start()
    serve_far(0)
    mids(lambda: line_step(1))
    mids(lambda: line_step(2))
    ends(lambda: line_step(2))
    serve_sides(1)
    @pl.when(middle_plane)
    def _():
        other = plane_at(z, 2)
        arrived(HZ, other, grads.at[other, e])
    out_ref[...] = part_ref[z].astype(f32)
    @pl.when(z > 0)
    def _():
        arrived(HU, z, rzu.at[z])
        out_ref[...] += rzu[z].astype(f32)
    @pl.when(z < 3)
    def _():
        arrived(HD, z, rzd.at[z])
        out_ref[...] += rzd[z].astype(f32)
    serve_far(1)
    own.wait()
    @pl.when(z < 3)
    def _(): up().wait_send()
    @pl.when(z > 0)
    def _(): down().wait_send()
    def drain(k, _):
        p = plane_at(z, k)
        for c in (to_x, to_y, to_c, fwd_y, fwd_x, c_x, c_y, c_a, c_b):
            c(p).wait_send()
        arrived(HC, p, grads.at[p, ec])
        arrived(HCX, p, grads.at[p, jnp.bitwise_xor(ec, 2)])
        arrived(HCY, p, grads.at[p, jnp.bitwise_xor(ec, 4)])
        arrived(HCA, p, grads.at[p, jnp.bitwise_xor(ec, 6), TOP])
        arrived(HCB, p, grads.at[p, jnp.bitwise_xor(ec, 6), BOT])
        return 0
    lax.fori_loop(0, 2, drain, 0)
    def drain_line(p, _):
        @pl.when(p > z)
        def _(): line_up(p).wait_send()
        @pl.when(p < z)
        def _(): line_down(p).wait_send()
        return 0
    lax.fori_loop(0, 4, drain_line, 0)

def open_exchange(part, grad, collective_id):
    vm = pl.BlockSpec(memory_space=pltpu.VMEM)
    any_ = pl.BlockSpec(memory_space=pl.ANY)
    _, quarter, width = part.shape
    return pl.pallas_call(
        opening_kernel,
        out_shape=(jax.ShapeDtypeStruct((quarter, width), f32), jax.ShapeDtypeStruct((4, 8, quarter, width), bf)),
        in_specs=[vm, any_],
        out_specs=(vm, any_),
        scratch_shapes=[pltpu.VMEM(part.shape, bf)] * 3 + [
            pltpu.SemaphoreType.DMA((12, 4)), pltpu.SemaphoreType.DMA, pltpu.SemaphoreType.DMA((12, 4)), pltpu.SemaphoreType.DMA],
        compiler_params=pltpu.CompilerParams(collective_id=collective_id, has_side_effects=True, vmem_limit_bytes=40 << 20),
    )(part, grad)


def input_product(acts, weights, cols):
    wg, wu = weights
    hid = wg.shape[2]
    total = None
    for j in range(wg.shape[0]):
        for w, i in ((wg, 0), (wu, 1)):
            lhs = acts[:, :, (2 * j + i) * hid:(2 * j + i + 1) * hid].reshape(-1, hid)
            part = lax.dot_general(lhs, w[j, cols, :], NT, preferred_element_type=f32)
            total = part if total is None else total + part
    return total

def output_product(acts, weights, cols):
    (wd,) = weights
    hid = wd.shape[1]
    total = None
    for j in range(wd.shape[0]):
        lhs = acts[:, :, j * hid:(j + 1) * hid].reshape(-1, hid)
        part = jnp.dot(lhs, wd[j, :, cols], preferred_element_type=f32)
        total = part if total is None else total + part
    return total

C1, DT, DB, XT, XB, YT, YB, ZU, ZD, OU, OD = range(11)

def scatter_kernel(product, n_weights, width, cols, score_at, carry, *refs):
    act_hbm, *rest = refs
    w_hbm, rest = rest[:n_weights], rest[n_weights:]
    if carry:
        row_ref, out_w, mixed, queries, keys, values, query_proj, key_proj, gains, cosine, sine, seg_col, seg_row, *rest = rest
        projected = (query_proj, key_proj)
        out_ref, grad_heads, grad_out_w, grad_gains, acts, *rest = rest
        *rest, rows, grad_mixed = rest
    else:
        out_ref, acts, *rest = rest
    weights, rest = rest[:n_weights], rest[n_weights:]
    sendbuf, acc, r1, rdt, rdb, rx, ry, rzu, rzd, send, recv, load, wload = rest
    e = lax.axis_index("exp")
    z = lax.axis_index("tp")
    quarter = acc.shape[2]
    half = quarter // 2
    chip = e // 2
    core = lax.rem(e, 2)
    chip_x, chip_y, chip_d = (jnp.bitwise_xor(chip, m) for m in (1, 2, 3))
    at_x, at_y, at_c = (jnp.bitwise_xor(e, 2), z), (jnp.bitwise_xor(e, 4), z), (jnp.bitwise_xor(e, 1), z)
    at_up, at_down = (e, z + 1), (e, z - 1)
    TOP, BOT = pl.ds(0, half), pl.ds(half, half)

    wcopies = [pltpu.make_async_copy(s, d, wload.at[i]) for i, (s, d) in enumerate(zip(w_hbm, weights))]
    for c in wcopies: c.start()

    def act_copy(n):
        k, own = n // 2, n % 2
        which = jnp.bitwise_xor(core, 1 - own)
        return pltpu.make_async_copy(act_hbm.at[:, which, plane_at(z, 3 - k), :, cols], acts.at[own], load.at[own])
    act_copy(0).start()

    bar = pltpu.get_barrier_semaphore()
    for d in (at_x, at_y, at_c):
        pl.semaphore_signal(bar, inc=1, device_id=d, device_id_type=MESH)
    @pl.when(z < 3)
    def _(): pl.semaphore_signal(bar, inc=1, device_id=at_up, device_id_type=MESH)
    @pl.when(z > 0)
    def _(): pl.semaphore_signal(bar, inc=1, device_id=at_down, device_id_type=MESH)
    pl.semaphore_wait(bar, 3 + jnp.where(z < 3, 1, 0) + jnp.where(z > 0, 1, 0))
    for c in wcopies: c.wait()

    def remote(kind, k, src, dst, to):
        return pltpu.make_async_remote_copy(src_ref=src, dst_ref=dst, send_sem=send.at[kind, k], recv_sem=recv.at[kind, k],
                                            device_id=to, device_id_type=MESH)
    def to_core(k): return remote(C1, k, sendbuf.at[k % 2], r1.at[k], at_c)
    def far_x(k): return remote(DT, k, acc.at[k, chip_d, TOP], rdt.at[k], at_x)
    def far_y(k): return remote(DB, k, acc.at[k, chip_d, BOT], rdb.at[k], at_y)
    def x_top(k): return remote(XT, k, acc.at[k, chip_x, TOP], rx.at[k, TOP], at_x)
    def x_bot(k): return remote(XB, k, acc.at[k, chip_x, BOT], rx.at[k, BOT], at_x)
    def y_top(k): return remote(YT, k, acc.at[k, chip_y, TOP], ry.at[k, TOP], at_y)
    def y_bot(k): return remote(YB, k, acc.at[k, chip_y, BOT], ry.at[k, BOT], at_y)
    def line_up(k, p): return remote(ZU, p, acc.at[k, chip], rzu.at[p], at_up)
    def line_down(k, p): return remote(ZD, p, acc.at[k, chip], rzd.at[p], at_down)
    def arrived(kind, k, place):
        pltpu.make_async_copy(place, place, recv.at[kind, k]).wait()
    def row_up(p): return remote(OU, p, rows.at[p], rows.at[p], at_up)
    def row_down(p): return remote(OD, p, rows.at[p], rows.at[p], at_down)
    def row_step(k):
        p = plane_at(z, k)
        @pl.when(p < z)
        def _(): arrived(OU, p, rows.at[p])
        @pl.when(p > z)
        def _(): arrived(OD, p, rows.at[p])
        @pl.when((p <= z) & (z < 3))
        def _(): row_up(p).start()
        @pl.when((p >= z) & (z > 0))
        def _(): row_down(p).start()
    if carry:
        rows[z] = row_ref[...]
        row_step(0)

    cols_step = 512
    def multiply(slot, target):
        def tile(n, _):
            cols = pl.ds(pl.multiple_of(n * cols_step, cols_step), cols_step)
            total = product(acts.at[slot], weights, cols)
            target[:, :, cols] = total.astype(bf).reshape(4, quarter, cols_step)
            return 0
        lax.fori_loop(0, width // cols_step, tile, 0)
        if score_at is not None:
            lanes = target.shape[2] - width
            target[:, :, width:] = acts[slot, :, :, score_at:score_at + lanes] + acts[slot, :, :, score_at + lanes:score_at + 2 * lanes]

    def add(place, other):
        place[...] = (place[...].astype(f32) + other[...].astype(f32)).astype(bf)

    def begin(k):
        act_copy(2 * k).wait()
        act_copy(2 * k + 1).start()
        if k >= 2:
            to_core(k - 2).wait_send()
        multiply(0, sendbuf.at[k % 2])
        to_core(k).start()
        act_copy(2 * k + 1).wait()
        if k < 3:
            act_copy(2 * k + 2).start()
        multiply(1, acc.at[k])
        arrived(C1, k, r1.at[k])
        add(acc.at[k, chip_d], r1.at[k, chip_d])
        far_x(k).start()
        far_y(k).start()
        add(acc.at[k, chip_x], r1.at[k, chip_x])
        x_top(k).start()
        add(acc.at[k, chip_y], r1.at[k, chip_y])
        y_bot(k).start()
        add(acc.at[k, chip], r1.at[k, chip])

    def middle(k):
        arrived(DB, k, rdb.at[k])
        add(acc.at[k, chip_x, BOT], rdb.at[k])
        x_bot(k).start()
        arrived(DT, k, rdt.at[k])
        add(acc.at[k, chip_y, TOP], rdt.at[k])
        y_top(k).start()

    def finish(k):
        p = plane_at(z, 3 - k)
        arrived(XT, k, rx.at[k, TOP])
        arrived(YB, k, ry.at[k, BOT])
        arrived(XB, k, rx.at[k, BOT])
        arrived(YT, k, ry.at[k, TOP])
        total = acc[k, chip].astype(f32) + rx[k].astype(f32) + ry[k].astype(f32)
        out_ref[...] = total
        @pl.when((z > 0) & (p >= z))
        def _():
            arrived(ZU, p, rzu.at[p])
            out_ref[...] += rzu[p].astype(f32)
        @pl.when((z < 3) & (p <= z))
        def _():
            arrived(ZD, p, rzd.at[p])
            out_ref[...] += rzd[p].astype(f32)
        @pl.when(p != z)
        def _():
            acc[k, chip] = out_ref[...].astype(bf)
        @pl.when(p > z)
        def _(): line_up(k, p).start()
        @pl.when(p < z)
        def _(): line_down(k, p).start()

    def one_head(h):
        head_back(h, queries, keys, values, projected, gains, cosine, sine, seg_col, seg_row, grad_mixed, grad_heads, grad_gains)

    if carry:
        grad_gains[...] = jnp.zeros(grad_gains.shape, f32)
        begin(0)
        row_step(1)
        begin(1)
        middle(0)
        row_step(2)
        begin(2)
        middle(1)
        row_step(3)
        begin(3)
        mixed_back(rows, out_w, mixed, grad_mixed, grad_out_w)
        middle(2)
        one_head(0)
        finish(0)
        one_head(1)
        middle(3)
        finish(1)
        one_head(2)
        finish(2)
        one_head(3)
        finish(3)
    else:
        begin(0)
        middle(0)
        begin(1)
        finish(0)
        middle(1)
        begin(2)
        finish(1)
        middle(2)
        begin(3)
        finish(2)
        middle(3)
        finish(3)

    for k in (2, 3):
        to_core(k).wait_send()
    def drain(k, _):
        p = plane_at(z, 3 - k)
        for c in (far_x, far_y, x_top, x_bot, y_top, y_bot):
            c(k).wait_send()
        @pl.when(p > z)
        def _(): line_up(k, p).wait_send()
        @pl.when(p < z)
        def _(): line_down(k, p).wait_send()
        if carry:
            @pl.when((p <= z) & (z < 3))
            def _(): row_up(p).wait_send()
            @pl.when((p >= z) & (z > 0))
            def _(): row_down(p).wait_send()
        return 0
    lax.fori_loop(0, 4, drain, 0)

def scatter_sums(act, weights, scores, collective_id, attention=()):
    hid = min(weights[0].shape[1:])
    width = max(weights[0].shape[1:])
    n_here = weights[0].shape[0]
    quarter, cols = act.shape[3:]
    score_at = 3 * hid * n_here
    lanes = (cols - score_at) // n_here
    wide = width + (lanes if scores else 0)
    taken = pl.ds(0, cols) if scores else pl.ds(2 * hid * n_here, hid * n_here)
    product = input_product if scores else output_product
    any_ = pl.BlockSpec(memory_space=pl.ANY)
    vm = pl.BlockSpec(memory_space=pltpu.VMEM)
    n = len(weights)
    out_shape = (jax.ShapeDtypeStruct((quarter, wide), f32),)
    extra = []
    if attention:
        heads, head_size = attention[2].shape, attention[8].shape[1]
        out_shape += (
            jax.ShapeDtypeStruct((3,) + heads, bf),
            jax.ShapeDtypeStruct(attention[1].shape, bf),
            jax.ShapeDtypeStruct((2, head_size), f32),
        )
        extra = [pltpu.VMEM((4, quarter, width), bf), pltpu.VMEM(heads, bf)]
    return pl.pallas_call(
        functools.partial(scatter_kernel, product, n, width, taken, score_at if scores else None, bool(attention)),
        out_shape=out_shape,
        in_specs=[any_] * (1 + n) + [vm] * len(attention),
        out_specs=(vm,) * len(out_shape),
        scratch_shapes=[pltpu.VMEM((2, 4, quarter, taken.size), bf)] + [pltpu.VMEM(w.shape, bf) for w in weights] + [
            pltpu.VMEM((2, 4, quarter, wide), bf),
            pltpu.VMEM((4, 4, quarter, wide), bf),
            pltpu.VMEM((4, 4, quarter, wide), bf),
            pltpu.VMEM((4, quarter // 2, wide), bf), pltpu.VMEM((4, quarter // 2, wide), bf),
            pltpu.VMEM((4, quarter, wide), bf), pltpu.VMEM((4, quarter, wide), bf),
            pltpu.VMEM((4, quarter, wide), bf), pltpu.VMEM((4, quarter, wide), bf),
            pltpu.SemaphoreType.DMA((11, 4)), pltpu.SemaphoreType.DMA((11, 4)),
            pltpu.SemaphoreType.DMA((2,)), pltpu.SemaphoreType.DMA((n,)),
        ] + extra,
        compiler_params=pltpu.CompilerParams(collective_id=collective_id, has_side_effects=True, vmem_limit_bytes=62 << 20),
    )(act, *weights, *attention)


(SC, SDT, SDB, SXT, SXB, SYT, SYB, GX, GY, GFX, GFY, GC, GCX, GCY, GCA, GCB, LU, LD, RU, RD) = range(20)

def totals_kernel(*refs):
    grad_heads, normed_ref, proj_w, grad_out_w, refs = refs[0], refs[1], refs[2:5], refs[5], refs[6:]
    router_ref, ffn_ref, heads_ref, hidden_ref, resid_ref, gain_ref, refs = *refs[:6], refs[6:]
    res, rows, small_out, refs = refs[:4], refs[4], refs[5], refs[6:]
    w_ref, refs = (grad_out_w, *refs[:3]), refs[3:]
    r1, acc, rdt, rdb, rx, ry, refs = *(refs[4 * i : 4 * i + 4] for i in range(6)), refs[24:]
    part_ref, rzu, rzd, line, sums, got, send, recv, ssend, srecv = refs
    e = lax.axis_index("exp")
    z = lax.axis_index("tp")
    chip, core = e // 2, lax.rem(e, 2)
    cx, cy, cd = (jnp.bitwise_xor(chip, m) for m in (1, 2, 3))
    at_x, at_y, at_c = (jnp.bitwise_xor(e, 2), z), (jnp.bitwise_xor(e, 4), z), (jnp.bitwise_xor(e, 1), z)
    at_up, at_down = (e, z + 1), (e, z - 1)
    partners = (at_c, at_x, at_y, (e, jnp.bitwise_xor(z, 1)), (e, jnp.bitwise_xor(z, 2)))
    middle_plane = (z == 1) | (z == 2)
    halves = [ref.shape[1] // 2 for ref in acc]
    TOP, BOT = [pl.ds(0, h) for h in halves], [pl.ds(h, h) for h in halves]

    bar = pltpu.get_barrier_semaphore()
    for d in (at_x, at_y, at_c, (e, jnp.bitwise_xor(z, 2))):
        pl.semaphore_signal(bar, inc=1, device_id=d, device_id_type=MESH)
    @pl.when(z < 3)
    def _(): pl.semaphore_signal(bar, inc=1, device_id=at_up, device_id_type=MESH)
    @pl.when(z > 0)
    def _(): pl.semaphore_signal(bar, inc=1, device_id=at_down, device_id_type=MESH)
    pl.semaphore_wait(bar, 4 + jnp.where(z < 3, 1, 0) + jnp.where(z > 0, 1, 0))

    def remote(kind, k, src, dst, to):
        return pltpu.make_async_remote_copy(src_ref=src, dst_ref=dst, send_sem=send.at[kind, k], recv_sem=recv.at[kind, k],
                                            device_id=to, device_id_type=MESH)
    def arrived(kind, k, place):
        pltpu.make_async_copy(place, place, recv.at[kind, k]).wait()
    def to_core(k): return remote(SC, k, w_ref[k].at[1 - core], r1[k], at_c)
    def far_x(k): return remote(SDT, k, acc[k].at[cd, TOP[k]], rdt[k], at_x)
    def far_y(k): return remote(SDB, k, acc[k].at[cd, BOT[k]], rdb[k], at_y)
    def x_top(k): return remote(SXT, k, acc[k].at[cx, TOP[k]], rx[k].at[TOP[k]], at_x)
    def x_bot(k): return remote(SXB, k, acc[k].at[cx, BOT[k]], rx[k].at[BOT[k]], at_x)
    def y_top(k): return remote(SYT, k, acc[k].at[cy, TOP[k]], ry[k].at[TOP[k]], at_y)
    def y_bot(k): return remote(SYB, k, acc[k].at[cy, BOT[k]], ry[k].at[BOT[k]], at_y)
    def same(kind, k, place, to): return remote(kind, k, place, place, to)
    def give_x(k): return same(GX, k, res[k].at[core, chip], at_x)
    def give_y(k): return same(GY, k, res[k].at[core, chip], at_y)
    def give_c(k): return same(GC, k, res[k].at[core, chip], at_c)
    def pass_y(k): return same(GFY, k, res[k].at[core, cx, TOP[k]], at_y)
    def pass_x(k): return same(GFX, k, res[k].at[core, cy, BOT[k]], at_x)
    def c_x(k): return same(GCX, k, res[k].at[core, cx], at_c)
    def c_y(k): return same(GCY, k, res[k].at[core, cy], at_c)
    def c_a(k): return same(GCA, k, res[k].at[core, cd, TOP[k]], at_c)
    def c_b(k): return same(GCB, k, res[k].at[core, cd, BOT[k]], at_c)
    def line_up(p): return remote(LU, p, line.at[p], rzu.at[p], at_up)
    def line_down(p): return remote(LD, p, line.at[p], rzd.at[p], at_down)
    def row_up(p): return same(RU, p, rows.at[p], at_up)
    def row_down(p): return same(RD, p, rows.at[p], at_down)

    def plus(a, b): return (a.astype(f32) + b.astype(f32)).astype(bf)

    def input_part():
        def tile(n, _):
            input_back(proj_w, grad_heads, part_ref, pl.ds(pl.multiple_of(n * 512, 512), 512))
            return 0
        lax.fori_loop(0, part_ref.shape[2] // 512, tile, 0)

    def weight_part(k):
        part = lax.dot_general(normed_ref[...], grad_heads[k - 1], TN, preferred_element_type=f32)
        w_ref[k][...] = part.astype(bf).reshape(w_ref[k].shape)
        to_core(k).start()

    def begin(k):
        arrived(SC, k, r1[k])
        acc[k][cd] = plus(w_ref[k][core, cd], r1[k][cd])
        far_x(k).start()
        far_y(k).start()
        acc[k][cx] = plus(w_ref[k][core, cx], r1[k][cx])
        x_top(k).start()
        acc[k][cy] = plus(w_ref[k][core, cy], r1[k][cy])
        y_bot(k).start()
        acc[k][chip] = plus(w_ref[k][core, chip], r1[k][chip])

    def middle(k):
        arrived(SDB, k, rdb[k])
        acc[k][cx, BOT[k]] = plus(acc[k][cx, BOT[k]], rdb[k][...])
        x_bot(k).start()
        arrived(SDT, k, rdt[k])
        acc[k][cy, TOP[k]] = plus(acc[k][cy, TOP[k]], rdt[k][...])
        y_top(k).start()

    def finish(k):
        arrived(SXT, k, rx[k].at[TOP[k]])
        arrived(SYB, k, ry[k].at[BOT[k]])
        arrived(SXB, k, rx[k].at[BOT[k]])
        arrived(SYT, k, ry[k].at[TOP[k]])
        res[k][core, chip] = (acc[k][chip].astype(f32) + rx[k][...].astype(f32) + ry[k][...].astype(f32)).astype(bf)
        give_x(k).start()
        give_y(k).start()
        give_c(k).start()

    def spread(k):
        arrived(GX, k, res[k].at[core, cx])
        pass_y(k).start()
        c_x(k).start()
        arrived(GY, k, res[k].at[core, cy])
        pass_x(k).start()
        c_y(k).start()

    def last(k):
        arrived(GFY, k, res[k].at[core, cd, TOP[k]])
        c_a(k).start()
        arrived(GFX, k, res[k].at[core, cd, BOT[k]])
        c_b(k).start()

    def line_step(k):
        p = plane_at(z, 3 - k)
        line[p] = part_ref[p]
        @pl.when((z > 0) & (p >= z))
        def _():
            arrived(LU, p, rzu.at[p])
            line[p] = plus(line[p], rzu[p])
        @pl.when((z < 3) & (p <= z))
        def _():
            arrived(LD, p, rzd.at[p])
            line[p] = plus(line[p], rzd[p])
        @pl.when(p > z)
        def _(): line_up(p).start()
        @pl.when(p < z)
        def _(): line_down(p).start()

    def unit_rows(p):
        value = hidden_ref[p].astype(f32)
        scale = lax.rsqrt(jnp.mean(value * value, axis=-1, keepdims=True) + eps)
        return scale, value * scale

    def gain_row():
        sums[0, 0:8] = jnp.zeros((8, sums.shape[2]), f32)
        sums[0, 1:2] = ffn_ref[...]
        head_size = heads_ref.shape[1]
        sums[0, 2:3, 0:head_size] = heads_ref[0:1]
        sums[0, 2:3, head_size : 2 * head_size] = heads_ref[1:2]
        sums[0, 8:] = router_ref[...]
        def add_plane(p, _):
            sums[0, 0:1] += jnp.sum(part_ref[p].astype(f32) * unit_rows(p)[1], axis=0, keepdims=True)
            return 0
        lax.fori_loop(0, 4, add_plane, 0)
        small_copy(0).start()

    def own_rows():
        total = part_ref[z].astype(f32)
        @pl.when(z > 0)
        def _(): arrived(LU, z, rzu.at[z])
        @pl.when(z < 3)
        def _(): arrived(LD, z, rzd.at[z])
        total = total + jnp.where(z > 0, rzu[z].astype(f32), 0.0) + jnp.where(z < 3, rzd[z].astype(f32), 0.0)
        scale, unit = unit_rows(z)
        scaled = total * gain_ref[...]
        grad = scale * (scaled - unit * jnp.mean(unit * scaled, axis=-1, keepdims=True))
        rows[z] = (resid_ref[...] + grad).astype(bf)
        @pl.when(z < 3)
        def _(): row_up(z).start()
        @pl.when(z > 0)
        def _(): row_down(z).start()

    def row_step(k):
        p = plane_at(z, k)
        @pl.when(p < z)
        def _(): arrived(RU, p, rows.at[p])
        @pl.when(p > z)
        def _(): arrived(RD, p, rows.at[p])
        @pl.when((p < z) & (z < 3))
        def _(): row_up(p).start()
        @pl.when((p > z) & (z > 0))
        def _(): row_down(p).start()

    def small_copy(i):
        return pltpu.make_async_remote_copy(src_ref=sums.at[i], dst_ref=got.at[i], send_sem=ssend.at[i], recv_sem=srecv.at[i],
                                            device_id=partners[i], device_id_type=MESH)
    def small_step(i):
        small_copy(i).wait_recv()
        if i < 4:
            sums[i + 1] = sums[i] + got[i]
            small_copy(i + 1).start()
        else:
            small_out[...] = sums[i] + got[i]

    def ends(f):
        pl.when(~middle_plane)(f)
    def mids(f):
        pl.when(middle_plane)(f)

    to_core(0).start()
    input_part()
    ends(lambda: line_step(0))
    weight_part(1)
    begin(0)
    weight_part(2)
    begin(1)
    weight_part(3)
    begin(2)
    gain_row()
    begin(3)
    mids(lambda: line_step(0))
    ends(lambda: line_step(1))
    small_step(0)
    middle(0)
    middle(1)
    mids(lambda: line_step(1))
    mids(lambda: line_step(2))
    ends(lambda: line_step(2))
    middle(2)
    middle(3)
    small_step(1)
    own_rows()
    finish(0)
    finish(1)
    finish(2)
    finish(3)
    ends(lambda: row_step(1))
    mids(lambda: row_step(1))
    mids(lambda: row_step(2))
    spread(0)
    spread(1)
    small_step(2)
    mids(lambda: row_step(3))
    ends(lambda: row_step(2))
    spread(2)
    spread(3)
    last(0)
    small_step(3)
    ends(lambda: row_step(3))
    last(1)
    last(2)
    small_step(4)
    last(3)

    sib = 1 - core
    for k in range(4):
        for c in (to_core, far_x, far_y, x_top, x_bot, y_top, y_bot, give_x, give_y, give_c, pass_x, pass_y, c_x, c_y, c_a, c_b):
            c(k).wait_send()
        arrived(GC, k, res[k].at[sib, chip])
        arrived(GCX, k, res[k].at[sib, cx])
        arrived(GCY, k, res[k].at[sib, cy])
        arrived(GCA, k, res[k].at[sib, cd, TOP[k]])
        arrived(GCB, k, res[k].at[sib, cd, BOT[k]])
    def drain(p, _):
        @pl.when(p > z)
        def _(): line_up(p).wait_send()
        @pl.when(p < z)
        def _(): line_down(p).wait_send()
        @pl.when((z < 3) & (p <= z))
        def _(): row_up(p).wait_send()
        @pl.when((z > 0) & (p >= z))
        def _(): row_down(p).wait_send()
        return 0
    lax.fori_loop(0, 4, drain, 0)
    for i in range(5): small_copy(i).wait_send()

def final_totals(grad_heads, normed, proj_w, grad_out_w, router, ffn, heads, hidden, resid, gain, collective_id):
    vm = pl.BlockSpec(memory_space=pltpu.VMEM)
    planes = hidden.shape
    one = (2, 4, proj_w[0].shape[0] // 8, proj_w[0].shape[1])
    shapes = (grad_out_w.shape, one, one, one)
    small = (5, 8 + router.shape[0], router.shape[1])
    own = [pltpu.VMEM(one, bf)] * 3
    whole = [pltpu.VMEM(s[1:], bf) for s in shapes]
    quarter = [pltpu.VMEM(s[2:], bf) for s in shapes]
    half = [pltpu.VMEM((s[2] // 2, s[3]), bf) for s in shapes]
    return pl.pallas_call(
        totals_kernel,
        out_shape=tuple(jax.ShapeDtypeStruct(s, bf) for s in shapes) + (
            jax.ShapeDtypeStruct(planes, bf), jax.ShapeDtypeStruct(small[1:], f32)),
        in_specs=[vm] * 12,
        out_specs=(vm,) * 6,
        scratch_shapes=own + whole + whole + half + half + quarter + quarter + [
            pltpu.VMEM(planes, bf), pltpu.VMEM(planes, bf), pltpu.VMEM(planes, bf), pltpu.VMEM(planes, bf),
            pltpu.VMEM(small, f32), pltpu.VMEM(small, f32),
            pltpu.SemaphoreType.DMA((20, 4)), pltpu.SemaphoreType.DMA((20, 4)),
            pltpu.SemaphoreType.DMA((5,)), pltpu.SemaphoreType.DMA((5,)),
        ],
        compiler_params=pltpu.CompilerParams(collective_id=collective_id, has_side_effects=True, vmem_limit_bytes=62 << 20),
    )(grad_heads, normed, *proj_w, grad_out_w, router, ffn, heads, hidden, resid, gain)


def slot_experts(routed_low, gates, picked, grad_out, expert_routes, gate_weight, up_weight, down_weight):
    highest = lax.Precision.HIGHEST
    quarter, width = grad_out.shape
    top_count = expert_routes.shape[1]
    experts = picked.shape[2]
    capacity = max(2, 2 * quarter * top_count // experts)
    picked_wide = picked.astype(jnp.float32)
    grad_rows = grad_out.astype(jnp.float32)
    flat_route = expert_routes.reshape(-1)
    flat_pick = picked.reshape(-1, experts).astype(jnp.int32)
    rank = jnp.sum((jnp.cumsum(flat_pick, axis=0) - 1) * flat_pick, axis=1)
    place = flat_route * capacity + rank
    row_token = jnp.arange(quarter * top_count, dtype=jnp.int32) // top_count
    send_rows = (
        jnp.zeros((experts * capacity, width), jnp.bfloat16).at[place].set(routed_low[row_token])
    )
    arrived = lax.all_to_all(
        send_rows.reshape(experts, capacity, width), "exp", split_axis=0, concat_axis=1, tiled=True
    )
    rows_used = lax.all_gather(arrived, "tp", axis=1, tiled=True)
    gate_act = jnp.einsum(
        "erd,edf->erf", rows_used, gate_weight, preferred_element_type=jnp.float32
    )
    up_act = jnp.einsum("erd,edf->erf", rows_used, up_weight, preferred_element_type=jnp.float32)
    hidden_low = (jax.nn.silu(gate_act) * up_act).astype(jnp.bfloat16)
    partial_out = jnp.einsum(
        "erf,efd->erd", hidden_low, down_weight, preferred_element_type=jnp.float32
    )
    expert_out = lax.psum_scatter(partial_out, "tp", scatter_dimension=1, tiled=True)
    returned = lax.all_to_all(
        expert_out.astype(jnp.bfloat16), "exp", split_axis=1, concat_axis=0, tiled=True
    )
    back_rows = (
        returned.reshape(experts * capacity, width)[place]
        .reshape(quarter, top_count, width)
        .astype(jnp.float32)
    )
    moe = jnp.einsum("tk,tkd->td", gates, back_rows, precision=highest)
    grad_gates = jnp.einsum("tkd,td->tk", back_rows, grad_rows, precision=highest)
    grad_chosen = gates * (grad_gates - jnp.sum(gates * grad_gates, axis=-1, keepdims=True))
    grad_logits = jnp.einsum("tke,tk->te", picked_wide, grad_chosen, precision=highest)
    weighted_grad = (
        (gates[:, :, None] * grad_rows[:, None, :])
        .astype(jnp.bfloat16)
        .reshape(quarter * top_count, width)
    )
    send_grads = jnp.zeros((experts * capacity, width), jnp.bfloat16).at[place].set(weighted_grad)
    grad_arrived = lax.all_to_all(
        send_grads.reshape(experts, capacity, width), "exp", split_axis=0, concat_axis=1, tiled=True
    )
    sigmoid_gate = jax.nn.sigmoid(gate_act)
    silu_gate = gate_act * sigmoid_gate
    slope = sigmoid_gate * (1.0 + gate_act * (1.0 - sigmoid_gate))
    grad_used = lax.all_gather(grad_arrived, "tp", axis=1, tiled=True)
    grad_hid = jnp.einsum(
        "erd,efd->erf", grad_used, down_weight, preferred_element_type=jnp.float32
    )
    grad_down = jnp.einsum(
        "erf,erd->efd", hidden_low, grad_used, preferred_element_type=jnp.float32
    )
    grad_gate = (grad_hid * up_act * slope).astype(jnp.bfloat16)
    grad_up = (grad_hid * silu_gate).astype(jnp.bfloat16)
    grad_gate_w = jnp.einsum(
        "erd,erf->edf", rows_used, grad_gate, preferred_element_type=jnp.float32
    )
    grad_up_w = jnp.einsum("erd,erf->edf", rows_used, grad_up, preferred_element_type=jnp.float32)
    input_part = jnp.einsum(
        "erf,edf->erd", grad_gate, gate_weight, preferred_element_type=jnp.float32
    ) + jnp.einsum("erf,edf->erd", grad_up, up_weight, preferred_element_type=jnp.float32)
    grad_input = lax.psum_scatter(input_part, "tp", scatter_dimension=1, tiled=True).astype(
        jnp.bfloat16
    )
    grad_back = lax.all_to_all(grad_input, "exp", split_axis=1, concat_axis=0, tiled=True)
    expert_grad = jnp.sum(
        grad_back.reshape(experts * capacity, width)[place]
        .reshape(quarter, top_count, width)
        .astype(jnp.float32),
        axis=1,
    )
    return moe, grad_logits, expert_grad, grad_gate_w, grad_up_w, grad_down


def gate_pair(dense_gates):
    pad = ((0, 0), (0, gate_lanes // 2 - dense_gates.shape[1]))
    high = dense_gates.astype(bf)
    low = (dense_gates - high.astype(f32)).astype(bf)
    return [jnp.pad(high, pad), jnp.pad(low, pad)]


def per_device(
    fits,
    hidden_in,
    attn_gain,
    query_weight,
    key_weight,
    value_weight,
    qnorm_gain,
    knorm_gain,
    out_weight,
    ffn_gain,
    router_weight,
    gate_weight,
    up_weight,
    down_weight,
    expert_routes,
    seq_lengths,
    grad_out,
):
    highest = lax.Precision.HIGHEST
    group_rows = hidden_in.shape[0]
    width = hidden_in.shape[1]
    head_size = qnorm_gain.shape[0]
    quarter = grad_out.shape[0]
    experts = router_weight.shape[1]
    tp_index = lax.axis_index("tp")
    widened = hidden_in.astype(jnp.float32)
    normed_one = rms_norm(widened, attn_gain)
    normed_low = normed_one.astype(jnp.bfloat16)
    segment, cosine, sine = rotary_tables(seq_lengths[0], group_rows, head_size)
    same_seq = segment[:, None] == segment[None, :]

    def prepare(projected, gain):
        return head_prep(projected, gain, cosine, sine)

    query_proj = jnp.dot(normed_low, query_weight, preferred_element_type=jnp.float32)
    key_proj = jnp.dot(normed_low, key_weight, preferred_element_type=jnp.float32)
    value_proj = jnp.dot(normed_low, value_weight, preferred_element_type=jnp.float32)
    queries, query_back = jax.vjp(prepare, query_proj, qnorm_gain)
    keys, key_back = jax.vjp(prepare, key_proj, knorm_gain)
    query_low = queries.astype(jnp.bfloat16)
    key_low = keys.astype(jnp.bfloat16)
    value_low = value_proj.astype(jnp.bfloat16).reshape(group_rows, -1, head_size)
    scores = masked_scores(query_low, key_low, same_seq, head_size)
    top_score = jnp.max(scores, axis=-1, keepdims=True)
    log_total = top_score + jnp.log(jnp.sum(jnp.exp(scores - top_score), axis=-1, keepdims=True))
    probs_low = jnp.exp(scores - log_total).astype(jnp.bfloat16)
    mixed = jnp.einsum("hts,shd->thd", probs_low, value_low, preferred_element_type=jnp.float32)
    mixed_low = mixed.astype(jnp.bfloat16).reshape(group_rows, -1)
    attn_part = jnp.dot(mixed_low, out_weight, preferred_element_type=jnp.float32)
    if fits:
        planes = (4, quarter, width)
        attn_rows, near_grads = open_exchange(attn_part.astype(bf).reshape(planes), grad_out, 5)
    else:
        attn_rows = lax.psum_scatter(attn_part, "tp", scatter_dimension=0, tiled=True)
    own_rows = lax.dynamic_slice_in_dim(widened, tp_index * quarter, quarter, 0)
    resid = own_rows + attn_rows
    normed_two, norm_two_back = jax.vjp(rms_norm, resid, ffn_gain)
    routed_low = normed_two.astype(jnp.bfloat16)
    logits = jnp.dot(routed_low, router_weight, preferred_element_type=jnp.float32)
    picked = expert_routes[:, :, None] == jnp.arange(experts, dtype=jnp.int32)[None, None, :]
    picked_wide = picked.astype(jnp.float32)
    chosen = jnp.einsum("tke,te->tk", picked_wide, logits, precision=highest)
    gates = jax.nn.softmax(chosen, axis=-1)
    grad_rows = grad_out.astype(jnp.float32)
    if fits:
        dense_gates = jnp.einsum("tke,tk->te", picked_wide, gates, precision=highest)
        act, grad_gate_w, grad_up_w, grad_down = gather_experts(
            jnp.concatenate([routed_low] + gate_pair(dense_gates), axis=1),
            near_grads,
            gate_weight,
            up_weight,
            down_weight,
        )
        (sums,) = scatter_sums(act, (gate_weight, up_weight), True, 2)
        expert_grad = sums[:, :width]
        grad_gates = sums[:, width : width + experts]
        grad_logits = dense_gates * (
            grad_gates - jnp.sum(dense_gates * grad_gates, axis=-1, keepdims=True)
        )
    else:
        moe, grad_logits, expert_grad, grad_gate_w, grad_up_w, grad_down = slot_experts(
            routed_low,
            gates,
            picked,
            grad_out,
            expert_routes,
            gate_weight,
            up_weight,
            down_weight,
        )
    grad_normed = (
        jnp.dot(grad_logits, router_weight.astype(jnp.float32).T, precision=highest) + expert_grad
    )
    grad_router = jnp.dot(routed_low.astype(jnp.float32).T, grad_logits, precision=highest)
    grad_resid, grad_ffn_gain = norm_two_back(grad_normed)
    grad_resid = grad_resid + grad_rows
    grad_low = grad_resid.astype(jnp.bfloat16)
    if fits:
        wide_cosine = jnp.concatenate([cosine[:, 0], cosine[:, 0]], axis=1)
        wide_sine = jnp.concatenate([-sine[:, 0], sine[:, 0]], axis=1)
        moe, grad_heads, grad_out_w, grad_gains = scatter_sums(
            act,
            (down_weight,),
            False,
            3,
            (
                grad_low,
                out_weight,
                mixed_low,
                query_low.reshape(group_rows, -1),
                key_low.reshape(group_rows, -1),
                value_low.reshape(group_rows, -1),
                query_proj,
                key_proj,
                jnp.stack([qnorm_gain, knorm_gain]),
                wide_cosine,
                wide_sine,
                segment[:, None],
                segment[None],
            ),
        )
        grad_out_sum, *sums, grad_input_rows, small = final_totals(
            grad_heads,
            normed_low,
            (query_weight, key_weight, value_weight),
            grad_out_w.reshape(2, 4, -1, width),
            grad_router.T,
            grad_ffn_gain[None],
            grad_gains,
            hidden_in.reshape(planes),
            grad_resid,
            attn_gain[None],
            4,
        )
        grad_input_rows = grad_input_rows.reshape(group_rows, width)
        totals = tuple(
            part.reshape(-1, part.shape[3]).astype(f32) for part in (*sums, grad_out_sum)
        ) + (
            small[0],
            small[2, :head_size],
            small[2, head_size : 2 * head_size],
            small[1],
            small[8:].T,
        )
    else:
        grad_attn_low = lax.all_gather(grad_low, "tp", axis=0, tiled=True)
        grad_out_weight = jnp.dot(mixed_low.T, grad_attn_low, preferred_element_type=jnp.float32)
        grad_mixed = jnp.dot(grad_attn_low, out_weight.T, preferred_element_type=jnp.float32)
        grad_mixed_low = grad_mixed.astype(jnp.bfloat16).reshape(group_rows, -1, head_size)
        probs = jnp.exp(masked_scores(query_low, key_low, same_seq, head_size) - log_total)
        grad_probs = jnp.einsum(
            "thd,shd->hts", grad_mixed_low, value_low, preferred_element_type=jnp.float32
        )
        grad_value = jnp.einsum(
            "hts,thd->shd", probs_low, grad_mixed_low, preferred_element_type=jnp.float32
        )
        row_delta = jnp.sum(probs * grad_probs, axis=-1, keepdims=True)
        grad_scores = (probs * (grad_probs - row_delta)).astype(jnp.bfloat16)
        grad_query = jnp.einsum(
            "hts,shd->thd", grad_scores, key_low, preferred_element_type=jnp.float32
        ) / math.sqrt(head_size)
        grad_key = jnp.einsum(
            "hts,thd->shd", grad_scores, query_low, preferred_element_type=jnp.float32
        ) / math.sqrt(head_size)
        grad_query_proj, grad_qgain = query_back(grad_query)
        grad_key_proj, grad_kgain = key_back(grad_key)
        grad_query_low = grad_query_proj.astype(jnp.bfloat16)
        grad_key_low = grad_key_proj.astype(jnp.bfloat16)
        grad_value_low = grad_value.reshape(group_rows, -1).astype(jnp.bfloat16)
        normed_part = (
            jnp.dot(grad_query_low, query_weight.T, preferred_element_type=jnp.float32)
            + jnp.dot(grad_key_low, key_weight.T, preferred_element_type=jnp.float32)
            + jnp.dot(grad_value_low, value_weight.T, preferred_element_type=jnp.float32)
        )
        grad_query_w = jnp.dot(normed_low.T, grad_query_low, preferred_element_type=jnp.float32)
        grad_key_w = jnp.dot(normed_low.T, grad_key_low, preferred_element_type=jnp.float32)
        grad_value_w = jnp.dot(normed_low.T, grad_value_low, preferred_element_type=jnp.float32)
        scale_one = lax.rsqrt(jnp.mean(widened * widened, axis=-1, keepdims=True) + eps)
        unit_one = widened * scale_one
        grad_attn_gain = jnp.sum(normed_part * unit_one, axis=0)
        grad_normed_one = lax.psum(normed_part.astype(bf), "tp").astype(f32)
        scaled = grad_normed_one * attn_gain
        grad_from_norm = scale_one * (
            scaled - unit_one * jnp.mean(unit_one * scaled, axis=-1, keepdims=True)
        )
        grad_input_rows = (grad_attn_low.astype(f32) + grad_from_norm).astype(jnp.bfloat16)
        low_totals = lax.psum(
            tuple(
                part.astype(jnp.bfloat16)
                for part in (grad_query_w, grad_key_w, grad_value_w, grad_out_weight)
            ),
            "exp",
        )
        small = lax.psum(
            (grad_attn_gain, grad_qgain, grad_kgain, grad_ffn_gain, grad_router), ("exp", "tp")
        )
        totals = tuple(part.astype(jnp.float32) for part in low_totals) + small
    block_out = (resid + moe).astype(jnp.bfloat16)
    return (
        block_out,
        grad_input_rows,
        totals[4],
        totals[0],
        totals[1],
        totals[2],
        totals[3],
        totals[5],
        totals[6],
        totals[7],
        totals[8],
        grad_gate_w,
        grad_up_w,
        grad_down,
    )


def solution(mesh):
    in_specs = (
        P("exp", None),
        P(),
        P(None, "tp"),
        P(None, "tp"),
        P(None, "tp"),
        P(),
        P(),
        P("tp", None),
        P(),
        P(),
        P("exp", None, "tp"),
        P("exp", None, "tp"),
        P("exp", "tp", None),
        P(("exp", "tp"), None),
        P("exp", None),
        P(("exp", "tp"), None),
    )
    out_specs = (
        P(("exp", "tp"), None),
        P("exp", None),
        P(),
        P(None, "tp"),
        P(None, "tp"),
        P(None, "tp"),
        P("tp", None),
        P(),
        P(),
        P(),
        P(),
        P("exp", None, "tp"),
        P("exp", None, "tp"),
        P("exp", "tp", None),
    )
    fits = dict(mesh.shape) == {"exp": 8, "tp": 4}
    return jax.shard_map(
        functools.partial(per_device, fits), mesh=mesh, in_specs=in_specs, out_specs=out_specs, check_vma=False
    )
```

```python
import functools
import math

import jax
import jax.numpy as jnp
from jax import lax
from jax.experimental import pallas as pl
from jax.experimental.pallas import tpu as pltpu
from jax.sharding import PartitionSpec as P

eps = 1e-06
rope_base = 10000.0
gate_lanes = 128
MESH = pl.DeviceIdType.MESH
bf = jnp.bfloat16
f32 = jnp.float32
NT = (((1,), (1,)), ((), ()))
TN = (((0,), (0,)), ((), ()))


def rms_norm(values, gain):
    return values * lax.rsqrt(jnp.mean(values * values, axis=-1, keepdims=True) + eps) * gain


def rotary_tables(lengths_row, count, head_size):
    token_index = jnp.arange(count, dtype=jnp.int32)
    seq_ends = jnp.cumsum(lengths_row)
    starts = seq_ends - lengths_row
    member = (
        (token_index[:, None] >= starts[None, :]) & (token_index[:, None] < seq_ends[None, :])
    ).astype(jnp.int32)
    segment = jnp.sum(member * jnp.arange(lengths_row.shape[0], dtype=jnp.int32)[None, :], axis=1)
    offset = jnp.sum(member * starts[None, :], axis=1)
    position = (token_index - offset).astype(jnp.float32)
    frequency = rope_base ** (-jnp.arange(0, head_size, 2, dtype=jnp.float32) / head_size)
    angles = position[:, None] * frequency[None, :]
    return (segment, jnp.cos(angles)[:, None, :], jnp.sin(angles)[:, None, :])


def rotate(values, cosine, sine):
    half = values.shape[-1] // 2
    first = values[..., :half]
    second = values[..., half:]
    return jnp.concatenate(
        [first * cosine - second * sine, second * cosine + first * sine], axis=-1
    )


def head_prep(projected, gain, cosine, sine):
    head_size = gain.shape[0]
    shaped = projected.reshape(projected.shape[0], projected.shape[1] // head_size, head_size)
    return rotate(rms_norm(shaped, gain), cosine, sine)


def masked_scores(query_low, key_low, same_seq, head_size):
    scores = jnp.einsum(
        "thd,shd->hts", query_low, key_low, preferred_element_type=jnp.float32
    ) / math.sqrt(head_size)
    return jnp.where(same_seq[None], scores, -1e30)


def plane_at(z, step):
    from_end = step
    from_middle = jnp.where(step == 0, 1, jnp.where(step == 1, 0, step))
    base = jnp.where((z == 0) | (z == 3), from_end, from_middle)
    return jnp.where(z < 2, base, 3 - base)

Z, X, Y, FX, FY, CO, CX, CY, CA, CB = range(10)

def gather_kernel(own_ref, grad_hbm, wg_hbm, wu_hbm, wd_hbm,
                  act_hbm, dg_ref, du_ref, dd_ref,
                  rows, grads, wg, wu, wd, act, send, up_send, recv, load, store, wload):
    e = lax.axis_index("exp")
    z = lax.axis_index("tp")
    ex, ey, ec, ed = (jnp.bitwise_xor(e, m) for m in (2, 4, 1, 6))
    width = wg.shape[1]
    quarter = own_ref.shape[0]
    half = quarter // 2
    hid = wg.shape[2]
    experts_here = wg.shape[0]
    at_x, at_y, at_c = (ex, z), (ey, z), (ec, z)
    at_up, at_down = (e, z + 1), (e, z - 1)

    wcopies = [pltpu.make_async_copy(s, d, wload.at[i]) for i, (s, d) in enumerate(((wg_hbm, wg), (wu_hbm, wu), (wd_hbm, wd)))]
    for c in wcopies: c.start()

    loads = [pltpu.make_async_copy(grad_hbm.at[plane_at(z, k)], grads.at[k], load.at[k]) for k in range(4)]
    for c in loads: c.start()
    middle = (z == 1) | (z == 2)

    bar = pltpu.get_barrier_semaphore()
    for d in (at_x, at_y, at_c):
        pl.semaphore_signal(bar, inc=1, device_id=d, device_id_type=MESH)
    @pl.when(z < 3)
    def _(): pl.semaphore_signal(bar, inc=1, device_id=at_up, device_id_type=MESH)
    @pl.when(z > 0)
    def _(): pl.semaphore_signal(bar, inc=1, device_id=at_down, device_id_type=MESH)
    pl.semaphore_wait(bar, 3 + jnp.where(z < 3, 1, 0) + jnp.where(z > 0, 1, 0))

    TOP, BOT, ALLR = pl.ds(0, half), pl.ds(half, half), pl.ds(0, quarter)

    def copy(kind, plane, group, part, to, src=None, sem=None):
        place = rows.at[plane, group, part]
        return pltpu.make_async_remote_copy(
            src_ref=place if src is None else src, dst_ref=place,
            send_sem=(send.at[kind, plane] if sem is None else sem), recv_sem=recv.at[kind, plane],
            device_id=to, device_id_type=MESH)

    def up(plane, src=None): return copy(Z, plane, e, ALLR, at_up, src, up_send.at[plane])
    def down(plane, src=None): return copy(Z, plane, e, ALLR, at_down, src)
    def to_x(plane, src=None): return copy(X, plane, e, ALLR, at_x, src)
    def to_y(plane, src=None): return copy(Y, plane, e, ALLR, at_y, src)
    def to_c(plane, src=None): return copy(CO, plane, e, ALLR, at_c, src)
    def fwd_y(plane): return copy(FY, plane, ex, TOP, at_y)
    def fwd_x(plane): return copy(FX, plane, ey, BOT, at_x)
    def c_x(plane): return copy(CX, plane, ex, ALLR, at_c)
    def c_y(plane): return copy(CY, plane, ey, ALLR, at_c)
    def c_a(plane): return copy(CA, plane, ed, TOP, at_c)
    def c_b(plane): return copy(CB, plane, ed, BOT, at_c)

    def arrived(kind, plane, group, part):
        place = rows.at[plane, group, part]
        pltpu.make_async_copy(place, place, recv.at[kind, plane]).wait()

    @pl.when(z < 3)
    def _(): up(z, own_ref).start()
    @pl.when(z > 0)
    def _(): down(z, own_ref).start()
    to_x(z, own_ref).start()
    to_y(z, own_ref).start()
    to_c(z, own_ref).start()
    rows[z, e] = own_ref[...]

    def serve_line(k):
        p = plane_at(z, k)
        arrived(Z, p, e, ALLR)
        @pl.when((p < z) & (z < 3))
        def _(): up(p).start()
        @pl.when((p > z) & (z > 0))
        def _(): down(p).start()

    def serve_rows(k):
        p = plane_at(z, k)
        to_x(p).start()
        to_y(p).start()
        to_c(p).start()

    def serve_sides(k):
        p = plane_at(z, k)
        arrived(X, p, ex, ALLR)
        fwd_y(p).start()
        c_x(p).start()
        arrived(Y, p, ey, ALLR)
        fwd_x(p).start()
        c_y(p).start()

    def serve_far(k):
        p = plane_at(z, k)
        arrived(FY, p, ed, TOP)
        c_a(p).start()
        arrived(FX, p, ed, BOT)
        c_b(p).start()

    def store_copy(step):
        k, h = step // 2, lax.rem(step, 2)
        first = jnp.bitwise_xor(jnp.bitwise_and(e, 4), h * 4)
        return pltpu.make_async_copy(act, act_hbm.at[pl.ds(first // 2, 2), :, plane_at(z, k)], store)

    serve_line(1)
    serve_rows(1)
    @pl.when(middle)
    def _(): serve_line(2)
    serve_sides(0)
    for c in wcopies + loads: c.wait()

    def step_body(step, _):
        k, h = step // 2, lax.rem(step, 2)
        p = plane_at(z, k)
        first = jnp.bitwise_xor(jnp.bitwise_and(e, 4), h * 4)
        sib_x = jnp.bitwise_xor(ec, 2)
        sib_y = jnp.bitwise_xor(ec, 4)
        sib_d = jnp.bitwise_xor(ec, 6)
        @pl.when(h == 0)
        def _():
            arrived(CO, p, ec, ALLR)
            arrived(CX, p, sib_x, ALLR)
        @pl.when(h == 1)
        def _():
            arrived(CY, p, sib_y, ALLR)
            arrived(CA, p, sib_d, TOP)
            arrived(CB, p, sib_d, BOT)
        lane = lax.broadcasted_iota(jnp.int32, (4 * quarter, gate_lanes), 1)

        def expert_body(j, _):
            x = rows[p, pl.ds(first, 4), :, :width].reshape(4 * quarter, width)
            g = grads[k, pl.ds(first, 4)].reshape(4 * quarter, width)
            extra = rows[p, pl.ds(first, 4), :, width:].reshape(4 * quarter, gate_lanes).astype(f32)
            expert = e * experts_here + j
            mine = (lane == expert) | (lane == expert + gate_lanes // 2)
            gate = jnp.sum(jnp.where(mine, extra, 0.0), axis=1, keepdims=True)
            ga = jnp.dot(x, wg[j], preferred_element_type=f32)
            ua = jnp.dot(x, wu[j], preferred_element_type=f32)
            gh = lax.dot_general(g, wd[j], (((1,), (1,)), ((), ())), preferred_element_type=f32)
            sg = jax.nn.sigmoid(ga)
            silu = ga * sg
            hidden = silu * ua
            score = jnp.sum(hidden * gh, axis=1, keepdims=True)
            gh = gh * gate
            hg = (hidden * gate).astype(bf)
            da = (gh * ua * (sg * (1.0 + ga * (1.0 - sg)))).astype(bf)
            du = (gh * silu).astype(bf)
            @pl.when((step > 0) & (j == 0))
            def _(): store_copy(step - 1).wait()
            base = j * 2 * hid
            shape3 = (2, 2, quarter, hid)
            act[:, :, :, pl.ds(pl.multiple_of(base, hid), hid)] = da.reshape(shape3)
            act[:, :, :, pl.ds(pl.multiple_of(base + hid, hid), hid)] = du.reshape(shape3)
            act[:, :, :, pl.ds(pl.multiple_of((2 * experts_here + j) * hid, hid), hid)] = hg.reshape(shape3)
            scores = jnp.where(lane == expert, score, 0.0).astype(bf).reshape(2, 2, quarter, gate_lanes)
            act[:, :, :, pl.ds(pl.multiple_of(experts_here * 3 * hid + j * gate_lanes, gate_lanes), gate_lanes)] = scores
            @pl.when(step == 0)
            def _():
                dg_ref[j] = jnp.zeros(dg_ref.shape[1:], f32)
                du_ref[j] = jnp.zeros(du_ref.shape[1:], f32)
                dd_ref[j] = jnp.zeros(dd_ref.shape[1:], f32)
            slot = 2 * step + j
            for at, work, which in (
                (1, serve_far, 0),
                (3, serve_sides, 1),
                (5, serve_rows, 3),
                (5, serve_far, 1),
                (7, serve_sides, 2),
                (9, serve_far, 2),
                (9, serve_sides, 3),
                (12, serve_far, 3),
            ):
                @pl.when(slot == at)
                def _(): work(which)
            @pl.when((slot == 1) & middle)
            def _(): serve_line(3)
            @pl.when((slot == 1) & ~middle)
            def _(): serve_line(2)
            @pl.when(slot == 1)
            def _(): serve_rows(2)
            @pl.when((slot == 3) & ~middle)
            def _(): serve_line(3)
            dd_ref[j] += lax.dot_general(hg, g, TN, preferred_element_type=f32)
            dg_ref[j] += lax.dot_general(x, da, TN, preferred_element_type=f32)
            du_ref[j] += lax.dot_general(x, du, TN, preferred_element_type=f32)
            return 0
        lax.fori_loop(0, experts_here, expert_body, 0)
        store_copy(step).start()
        return 0
    lax.fori_loop(0, 8, step_body, 0)
    store_copy(7).wait()

    def drain(k, _):
        p = plane_at(z, k)
        @pl.when((z < 3) & (p <= z))
        def _(): up(p).wait_send()
        @pl.when((z > 0) & (p >= z))
        def _(): down(p).wait_send()
        for c in (to_x, to_y, to_c, fwd_y, fwd_x, c_x, c_y, c_a, c_b):
            c(p).wait_send()
        return 0
    lax.fori_loop(0, 4, drain, 0)

def gather_experts(own, grads_all, wg, wu, wd):
    n_here, width, hid = wg.shape
    quarter, wide = own.shape
    lanes = wide - width
    cols = n_here * 3 * hid + n_here * lanes
    any_ = pl.BlockSpec(memory_space=pl.ANY)
    vm = pl.BlockSpec(memory_space=pltpu.VMEM)
    return pl.pallas_call(
        gather_kernel,
        out_shape=(jax.ShapeDtypeStruct((4, 2, 4, quarter, cols), bf),
                   jax.ShapeDtypeStruct(wg.shape, f32), jax.ShapeDtypeStruct(wu.shape, f32), jax.ShapeDtypeStruct(wd.shape, f32)),
        in_specs=[vm, any_, any_, any_, any_],
        out_specs=(any_, vm, vm, vm),
        scratch_shapes=[
            pltpu.VMEM((4, 8, quarter, wide), bf),
            pltpu.VMEM((4, 8, quarter, width), bf),
            pltpu.VMEM(wg.shape, bf), pltpu.VMEM(wu.shape, bf), pltpu.VMEM(wd.shape, bf),
            pltpu.VMEM((2, 2, quarter, cols), bf),
            pltpu.SemaphoreType.DMA((10, 4)), pltpu.SemaphoreType.DMA((4,)), pltpu.SemaphoreType.DMA((10, 4)),
            pltpu.SemaphoreType.DMA((4,)), pltpu.SemaphoreType.DMA, pltpu.SemaphoreType.DMA((3,)),
        ],
        compiler_params=pltpu.CompilerParams(collective_id=1, has_side_effects=True, vmem_limit_bytes=63 << 20),
        cost_estimate=pl.CostEstimate(flops=12 * 4096 * 2048 * hid * n_here, bytes_accessed=64 << 20, transcendentals=0),
    )(own, grads_all, wg, wu, wd)


def head_scores(queries, keys, same, head_size):
    scores = lax.dot_general(queries, keys, NT, preferred_element_type=f32) / math.sqrt(head_size)
    scores = jnp.where(same, scores, -1e30)
    grown = jnp.exp(scores - jnp.max(scores, axis=-1, keepdims=True))
    return grown / jnp.sum(grown, axis=-1, keepdims=True)

def mixed_back(grad_rows, out_w, mixed, grad_mixed, grad_out_w):
    grads = grad_rows[...].reshape(-1, grad_rows.shape[2])
    grad_mixed[...] = lax.dot_general(grads, out_w[...], NT, preferred_element_type=f32).astype(bf)
    grad_out_w[...] = lax.dot_general(mixed[...], grads, TN, preferred_element_type=f32).astype(bf)

def head_back(h, queries, keys, values, projected, gains, cosine, sine, seg_col, seg_row, grad_mixed, grad_heads, grad_gains):
    head_size = cosine.shape[1]
    at = pl.ds(pl.multiple_of(h * head_size, head_size), head_size)
    same = seg_col[...] == seg_row[...]
    q, k, v, gm = queries[:, at], keys[:, at], values[:, at], grad_mixed[:, at]
    probs = head_scores(q, k, same, head_size)
    grad_probs = lax.dot_general(gm, v, NT, preferred_element_type=f32)
    grad_heads[2, :, at] = lax.dot_general(probs.astype(bf), gm, TN, preferred_element_type=f32).astype(bf)
    delta = jnp.sum(probs * grad_probs, axis=-1, keepdims=True)
    grad_scores = (probs * (grad_probs - delta)).astype(bf)
    back = (
        jnp.dot(grad_scores, k, preferred_element_type=f32),
        lax.dot_general(grad_scores, q, TN, preferred_element_type=f32),
    )
    for i in range(2):
        grad = back[i] / math.sqrt(head_size)
        grad = grad * cosine[...] - pltpu.roll(grad, head_size // 2, axis=1) * sine[...]
        value = projected[i][:, at]
        scale = lax.rsqrt(jnp.mean(value * value, axis=-1, keepdims=True) + eps)
        unit = value * scale
        grad_gains[i : i + 1] += jnp.sum(grad * unit, axis=0, keepdims=True)
        scaled = grad * gains[i : i + 1]
        grad_heads[i, :, at] = (scale * (scaled - unit * jnp.mean(unit * scaled, axis=-1, keepdims=True))).astype(bf)

def input_back(weights, grad_heads, part, cols):
    total = None
    for i, w in enumerate(weights):
        one = lax.dot_general(grad_heads[i], w[cols, :], NT, preferred_element_type=f32)
        total = one if total is None else total + one
    part[:, :, cols] = total.astype(bf).reshape(part.shape[0], part.shape[1], -1)

def norm_rows(hidden, gain, normed):
    rows = hidden.shape[1]
    def plane(p, _):
        value = hidden[p].astype(f32)
        scale = lax.rsqrt(jnp.mean(value * value, axis=-1, keepdims=True) + eps)
        normed[pl.ds(pl.multiple_of(p * rows, rows), rows), :] = (value * scale * gain[...]).astype(bf)
        return 0
    lax.fori_loop(0, hidden.shape[0], plane, 0)

def project(normed, weight, out):
    out[...] = jnp.dot(normed[...], weight[...], preferred_element_type=f32).astype(out.dtype)

def head_forward(h, projected, gains, cosine, sine, seg_col, seg_row, lows, values, mixed):
    head_size = cosine.shape[1]
    at = pl.ds(pl.multiple_of(h * head_size, head_size), head_size)
    for i in range(2):
        value = projected[i][:, at]
        scale = lax.rsqrt(jnp.mean(value * value, axis=-1, keepdims=True) + eps)
        scaled = value * scale * gains[i : i + 1]
        lows[i][:, at] = (scaled * cosine[...] + pltpu.roll(scaled, head_size // 2, axis=1) * sine[...]).astype(bf)
    probs = head_scores(lows[0][:, at], lows[1][:, at], seg_col[...] == seg_row[...], head_size)
    mixed[:, at] = jnp.dot(probs.astype(bf), values[:, at], preferred_element_type=f32).astype(bf)

def output_part(mixed, weight, part):
    def tile(n, _):
        cols = pl.ds(pl.multiple_of(n * 512, 512), 512)
        total = jnp.dot(mixed[...], weight[:, cols], preferred_element_type=f32)
        part[:, :, cols] = total.astype(bf).reshape(part.shape[0], part.shape[1], -1)
        return 0
    lax.fori_loop(0, part.shape[2] // 512, tile, 0)


HZ, HX, HY, HFX, HFY, HC, HCX, HCY, HCA, HCB, HU, HD = range(12)

def opening_kernel(hidden, gain, wq_hbm, wk_hbm, wv_hbm, out_hbm, gains, cosine, sine, seg_col, seg_row, grad_ref,
                   out_ref, normed, query_proj, key_proj, queries, keys, values, mixed, grads,
                   wq, wk, wv, out_w, part_ref, line, rzu, rzd, send, up_send, recv, local, wload):
    e = lax.axis_index("exp")
    z = lax.axis_index("tp")
    ex, ey, ec, ed = (jnp.bitwise_xor(e, m) for m in (2, 4, 1, 6))
    at_x, at_y, at_c = (ex, z), (ey, z), (ec, z)
    at_up, at_down = (e, z + 1), (e, z - 1)
    middle_plane = (z == 1) | (z == 2)
    quarter = grad_ref.shape[0]
    half = quarter // 2
    TOP, BOT, ALLR = pl.ds(0, half), pl.ds(half, half), pl.ds(0, quarter)

    wcopies = [pltpu.make_async_copy(s, d, wload.at[i]) for i, (s, d) in enumerate(zip((wq_hbm, wk_hbm, wv_hbm, out_hbm), (wq, wk, wv, out_w)))]
    for c in wcopies: c.start()

    bar = pltpu.get_barrier_semaphore()
    for d in (at_x, at_y, at_c):
        pl.semaphore_signal(bar, inc=1, device_id=d, device_id_type=MESH)
    @pl.when(z < 3)
    def _(): pl.semaphore_signal(bar, inc=1, device_id=at_up, device_id_type=MESH)
    @pl.when(z > 0)
    def _(): pl.semaphore_signal(bar, inc=1, device_id=at_down, device_id_type=MESH)
    pl.semaphore_wait(bar, 3 + jnp.where(z < 3, 1, 0) + jnp.where(z > 0, 1, 0))

    def copy(kind, plane, group, part, to, src=None, sem=None):
        place = grads.at[plane, group, part]
        return pltpu.make_async_remote_copy(
            src_ref=place if src is None else src, dst_ref=place,
            send_sem=send.at[kind, plane] if sem is None else sem, recv_sem=recv.at[kind, plane],
            device_id=to, device_id_type=MESH)
    def arrived(kind, plane, place):
        pltpu.make_async_copy(place, place, recv.at[kind, plane]).wait()
    def line_copy(kind, p, landing, to):
        return pltpu.make_async_remote_copy(src_ref=line.at[p], dst_ref=landing.at[p], send_sem=send.at[kind, p],
                                            recv_sem=recv.at[kind, p], device_id=to, device_id_type=MESH)
    def line_up(p): return line_copy(HU, p, rzu, at_up)
    def line_down(p): return line_copy(HD, p, rzd, at_down)
    def up(p, src=None): return copy(HZ, p, e, ALLR, at_up, src, up_send.at[p])
    def down(p, src=None): return copy(HZ, p, e, ALLR, at_down, src)
    def to_x(p, src=None): return copy(HX, p, e, ALLR, at_x, src)
    def to_y(p, src=None): return copy(HY, p, e, ALLR, at_y, src)
    def to_c(p, src=None): return copy(HC, p, e, ALLR, at_c, src)
    def fwd_y(p): return copy(HFY, p, ex, TOP, at_y)
    def fwd_x(p): return copy(HFX, p, ey, BOT, at_x)
    def c_x(p): return copy(HCX, p, ex, ALLR, at_c)
    def c_y(p): return copy(HCY, p, ey, ALLR, at_c)
    def c_a(p): return copy(HCA, p, ed, TOP, at_c)
    def c_b(p): return copy(HCB, p, ed, BOT, at_c)

    def serve_line(k):
        p = plane_at(z, k)
        arrived(HZ, p, grads.at[p, e])
        @pl.when((p < z) & (z < 3))
        def _(): up(p).start()
        @pl.when((p > z) & (z > 0))
        def _(): down(p).start()

    def serve_rows(k):
        p = plane_at(z, k)
        to_x(p).start()
        to_y(p).start()
        to_c(p).start()

    def serve_sides(k):
        p = plane_at(z, k)
        arrived(HX, p, grads.at[p, ex])
        fwd_y(p).start()
        c_x(p).start()
        arrived(HY, p, grads.at[p, ey])
        fwd_x(p).start()
        c_y(p).start()

    def serve_far(k):
        p = plane_at(z, k)
        arrived(HFY, p, grads.at[p, ed, TOP])
        c_a(p).start()
        arrived(HFX, p, grads.at[p, ed, BOT])
        c_b(p).start()

    def line_step(k):
        p = plane_at(z, 3 - k)
        line[p] = part_ref[p]
        @pl.when((z > 0) & (p >= z))
        def _():
            arrived(HU, p, rzu.at[p])
            line[p] = (line[p].astype(f32) + rzu[p].astype(f32)).astype(bf)
        @pl.when((z < 3) & (p <= z))
        def _():
            arrived(HD, p, rzd.at[p])
            line[p] = (line[p].astype(f32) + rzd[p].astype(f32)).astype(bf)
        @pl.when(p > z)
        def _(): line_up(p).start()
        @pl.when(p < z)
        def _(): line_down(p).start()

    def ends(f): pl.when(~middle_plane)(f)
    def mids(f): pl.when(middle_plane)(f)

    def one_head(h):
        head_forward(h, (query_proj, key_proj), gains, cosine, sine, seg_col, seg_row, (queries, keys), values, mixed)

    def own_sum():
        out_ref[...] = part_ref[z].astype(f32)
        @pl.when(z > 0)
        def _():
            arrived(HU, z, rzu.at[z])
            out_ref[...] += rzu[z].astype(f32)
        @pl.when(z < 3)
        def _():
            arrived(HD, z, rzd.at[z])
            out_ref[...] += rzd[z].astype(f32)

    @pl.when(z < 3)
    def _(): up(z, grad_ref).start()
    @pl.when(z > 0)
    def _(): down(z, grad_ref).start()
    to_x(z, grad_ref).start()
    to_y(z, grad_ref).start()
    to_c(z, grad_ref).start()
    own = pltpu.make_async_copy(grad_ref, grads.at[z, e], local)
    own.start()

    norm_rows(hidden, gain, normed)
    for c in wcopies: c.wait()
    project(normed, wq, query_proj)
    project(normed, wk, key_proj)
    project(normed, wv, values)
    serve_line(1)
    serve_rows(1)
    mids(lambda: serve_line(2))
    serve_sides(0)
    one_head(0)
    one_head(1)
    serve_far(0)
    mids(lambda: serve_line(3))
    ends(lambda: serve_line(2))
    serve_rows(2)
    one_head(2)
    one_head(3)
    output_part(mixed, out_w, part_ref)
    ends(lambda: line_step(0))
    serve_sides(1)
    mids(lambda: line_step(0))
    ends(lambda: line_step(1))
    ends(lambda: serve_line(3))
    serve_rows(3)
    serve_far(1)
    mids(lambda: line_step(1))
    mids(lambda: line_step(2))
    ends(lambda: line_step(2))
    serve_sides(2)
    serve_far(2)
    own_sum()
    serve_sides(3)
    serve_far(3)
    own.wait()
    def drain(k, _):
        p = plane_at(z, k)
        @pl.when((z < 3) & (p <= z))
        def _(): up(p).wait_send()
        @pl.when((z > 0) & (p >= z))
        def _(): down(p).wait_send()
        for c in (to_x, to_y, to_c, fwd_y, fwd_x, c_x, c_y, c_a, c_b):
            c(p).wait_send()
        arrived(HC, p, grads.at[p, ec])
        arrived(HCX, p, grads.at[p, jnp.bitwise_xor(ec, 2)])
        arrived(HCY, p, grads.at[p, jnp.bitwise_xor(ec, 4)])
        arrived(HCA, p, grads.at[p, jnp.bitwise_xor(ec, 6), TOP])
        arrived(HCB, p, grads.at[p, jnp.bitwise_xor(ec, 6), BOT])
        return 0
    lax.fori_loop(0, 4, drain, 0)
    def drain_line(p, _):
        @pl.when(p > z)
        def _(): line_up(p).wait_send()
        @pl.when(p < z)
        def _(): line_down(p).wait_send()
        return 0
    lax.fori_loop(0, 4, drain_line, 0)

def open_exchange(hidden, gain, weights, gains, cosine, sine, seg_col, seg_row, grad, collective_id):
    vm = pl.BlockSpec(memory_space=pltpu.VMEM)
    any_ = pl.BlockSpec(memory_space=pl.ANY)
    planes = hidden.shape
    _, quarter, width = planes
    tokens = cosine.shape[0]
    heads = (tokens, weights[0].shape[1])
    return pl.pallas_call(
        opening_kernel,
        out_shape=(
            jax.ShapeDtypeStruct((quarter, width), f32),
            jax.ShapeDtypeStruct((tokens, width), bf),
            jax.ShapeDtypeStruct(heads, f32), jax.ShapeDtypeStruct(heads, f32),
            jax.ShapeDtypeStruct(heads, bf), jax.ShapeDtypeStruct(heads, bf), jax.ShapeDtypeStruct(heads, bf), jax.ShapeDtypeStruct(heads, bf),
            jax.ShapeDtypeStruct((4, 8, quarter, width), bf),
        ),
        in_specs=[vm, vm] + [any_] * 4 + [vm] * 5 + [any_],
        out_specs=(vm,) * 8 + (any_,),
        scratch_shapes=[pltpu.VMEM(w.shape, bf) for w in weights] + [pltpu.VMEM(planes, bf)] * 4 + [
            pltpu.SemaphoreType.DMA((12, 4)), pltpu.SemaphoreType.DMA((4,)), pltpu.SemaphoreType.DMA((12, 4)), pltpu.SemaphoreType.DMA,
            pltpu.SemaphoreType.DMA((4,))],
        compiler_params=pltpu.CompilerParams(collective_id=collective_id, has_side_effects=True, vmem_limit_bytes=56 << 20),
    )(hidden, gain, *weights, gains, cosine, sine, seg_col, seg_row, grad)


def input_product(acts, weights, cols):
    wg, wu = weights
    hid = wg.shape[2]
    total = None
    for j in range(wg.shape[0]):
        for w, i in ((wg, 0), (wu, 1)):
            lhs = acts[:, :, (2 * j + i) * hid:(2 * j + i + 1) * hid].reshape(-1, hid)
            part = lax.dot_general(lhs, w[j, cols, :], NT, preferred_element_type=f32)
            total = part if total is None else total + part
    return total

def output_product(acts, weights, cols):
    (wd,) = weights
    hid = wd.shape[1]
    total = None
    for j in range(wd.shape[0]):
        lhs = acts[:, :, j * hid:(j + 1) * hid].reshape(-1, hid)
        part = jnp.dot(lhs, wd[j, :, cols], preferred_element_type=f32)
        total = part if total is None else total + part
    return total

C1, DT, DB, XT, XB, YT, YB, ZU, ZD, OU, OD = range(11)

def scatter_kernel(product, n_weights, width, cols, score_at, carry, *refs):
    act_hbm, *rest = refs
    w_hbm, rest = rest[:n_weights], rest[n_weights:]
    if carry:
        row_ref, out_w, mixed, queries, keys, values, query_proj, key_proj, gains, cosine, sine, seg_col, seg_row, *rest = rest
        projected = (query_proj, key_proj)
        out_ref, grad_heads, grad_out_w, grad_gains, acts, *rest = rest
        *rest, rows, grad_mixed = rest
    else:
        out_ref, acts, *rest = rest
    weights, rest = rest[:n_weights], rest[n_weights:]
    sendbuf, acc, r1, rdt, rdb, rx, ry, rzu, rzd, send, recv, load, wload = rest
    e = lax.axis_index("exp")
    z = lax.axis_index("tp")
    quarter = acc.shape[2]
    half = quarter // 2
    chip = e // 2
    core = lax.rem(e, 2)
    chip_x, chip_y, chip_d = (jnp.bitwise_xor(chip, m) for m in (1, 2, 3))
    at_x, at_y, at_c = (jnp.bitwise_xor(e, 2), z), (jnp.bitwise_xor(e, 4), z), (jnp.bitwise_xor(e, 1), z)
    at_up, at_down = (e, z + 1), (e, z - 1)
    TOP, BOT = pl.ds(0, half), pl.ds(half, half)

    wcopies = [pltpu.make_async_copy(s, d, wload.at[i]) for i, (s, d) in enumerate(zip(w_hbm, weights))]
    for c in wcopies: c.start()

    def act_copy(n):
        k, own = n // 2, n % 2
        which = jnp.bitwise_xor(core, 1 - own)
        return pltpu.make_async_copy(act_hbm.at[:, which, plane_at(z, 3 - k), :, cols], acts.at[own], load.at[own])
    act_copy(0).start()

    bar = pltpu.get_barrier_semaphore()
    for d in (at_x, at_y, at_c):
        pl.semaphore_signal(bar, inc=1, device_id=d, device_id_type=MESH)
    @pl.when(z < 3)
    def _(): pl.semaphore_signal(bar, inc=1, device_id=at_up, device_id_type=MESH)
    @pl.when(z > 0)
    def _(): pl.semaphore_signal(bar, inc=1, device_id=at_down, device_id_type=MESH)
    pl.semaphore_wait(bar, 3 + jnp.where(z < 3, 1, 0) + jnp.where(z > 0, 1, 0))
    for c in wcopies: c.wait()

    def remote(kind, k, src, dst, to):
        return pltpu.make_async_remote_copy(src_ref=src, dst_ref=dst, send_sem=send.at[kind, k], recv_sem=recv.at[kind, k],
                                            device_id=to, device_id_type=MESH)
    def to_core(k): return remote(C1, k, sendbuf.at[k % 2], r1.at[k], at_c)
    def far_x(k): return remote(DT, k, acc.at[k, chip_d, TOP], rdt.at[k], at_x)
    def far_y(k): return remote(DB, k, acc.at[k, chip_d, BOT], rdb.at[k], at_y)
    def x_top(k): return remote(XT, k, acc.at[k, chip_x, TOP], rx.at[k, TOP], at_x)
    def x_bot(k): return remote(XB, k, acc.at[k, chip_x, BOT], rx.at[k, BOT], at_x)
    def y_top(k): return remote(YT, k, acc.at[k, chip_y, TOP], ry.at[k, TOP], at_y)
    def y_bot(k): return remote(YB, k, acc.at[k, chip_y, BOT], ry.at[k, BOT], at_y)
    def line_up(k, p): return remote(ZU, p, acc.at[k, chip], rzu.at[p], at_up)
    def line_down(k, p): return remote(ZD, p, acc.at[k, chip], rzd.at[p], at_down)
    def arrived(kind, k, place):
        pltpu.make_async_copy(place, place, recv.at[kind, k]).wait()
    def row_up(p): return remote(OU, p, rows.at[p], rows.at[p], at_up)
    def row_down(p): return remote(OD, p, rows.at[p], rows.at[p], at_down)
    def row_step(k):
        p = plane_at(z, k)
        @pl.when(p < z)
        def _(): arrived(OU, p, rows.at[p])
        @pl.when(p > z)
        def _(): arrived(OD, p, rows.at[p])
        @pl.when((p <= z) & (z < 3))
        def _(): row_up(p).start()
        @pl.when((p >= z) & (z > 0))
        def _(): row_down(p).start()
    if carry:
        rows[z] = row_ref[...]
        row_step(0)

    cols_step = 512
    def multiply(slot, target):
        def tile(n, _):
            cols = pl.ds(pl.multiple_of(n * cols_step, cols_step), cols_step)
            total = product(acts.at[slot], weights, cols)
            target[:, :, cols] = total.astype(bf).reshape(4, quarter, cols_step)
            return 0
        lax.fori_loop(0, width // cols_step, tile, 0)
        if score_at is not None:
            lanes = target.shape[2] - width
            target[:, :, width:] = acts[slot, :, :, score_at:score_at + lanes] + acts[slot, :, :, score_at + lanes:score_at + 2 * lanes]

    def add(place, other):
        place[...] = (place[...].astype(f32) + other[...].astype(f32)).astype(bf)

    def begin(k):
        act_copy(2 * k).wait()
        act_copy(2 * k + 1).start()
        if k >= 2:
            to_core(k - 2).wait_send()
        multiply(0, sendbuf.at[k % 2])
        to_core(k).start()
        act_copy(2 * k + 1).wait()
        if k < 3:
            act_copy(2 * k + 2).start()
        multiply(1, acc.at[k])
        arrived(C1, k, r1.at[k])
        add(acc.at[k, chip_d], r1.at[k, chip_d])
        far_x(k).start()
        far_y(k).start()
        add(acc.at[k, chip_x], r1.at[k, chip_x])
        x_top(k).start()
        add(acc.at[k, chip_y], r1.at[k, chip_y])
        y_bot(k).start()
        add(acc.at[k, chip], r1.at[k, chip])

    def middle(k):
        arrived(DB, k, rdb.at[k])
        add(acc.at[k, chip_x, BOT], rdb.at[k])
        x_bot(k).start()
        arrived(DT, k, rdt.at[k])
        add(acc.at[k, chip_y, TOP], rdt.at[k])
        y_top(k).start()

    def finish(k):
        p = plane_at(z, 3 - k)
        arrived(XT, k, rx.at[k, TOP])
        arrived(YB, k, ry.at[k, BOT])
        arrived(XB, k, rx.at[k, BOT])
        arrived(YT, k, ry.at[k, TOP])
        total = acc[k, chip].astype(f32) + rx[k].astype(f32) + ry[k].astype(f32)
        out_ref[...] = total
        @pl.when((z > 0) & (p >= z))
        def _():
            arrived(ZU, p, rzu.at[p])
            out_ref[...] += rzu[p].astype(f32)
        @pl.when((z < 3) & (p <= z))
        def _():
            arrived(ZD, p, rzd.at[p])
            out_ref[...] += rzd[p].astype(f32)
        @pl.when(p != z)
        def _():
            acc[k, chip] = out_ref[...].astype(bf)
        @pl.when(p > z)
        def _(): line_up(k, p).start()
        @pl.when(p < z)
        def _(): line_down(k, p).start()

    def one_head(h):
        head_back(h, queries, keys, values, projected, gains, cosine, sine, seg_col, seg_row, grad_mixed, grad_heads, grad_gains)

    def ends(f):
        pl.when((z == 0) | (z == 3))(f)
    def mids(f):
        pl.when((z == 1) | (z == 2))(f)

    if carry:
        grad_gains[...] = jnp.zeros(grad_gains.shape, f32)
        begin(0)
        row_step(1)
        begin(1)
        middle(0)
        row_step(2)
        begin(2)
        middle(1)
        row_step(3)
        ends(lambda: finish(0))
        begin(3)
        mixed_back(rows, out_w, mixed, grad_mixed, grad_out_w)
        middle(2)
        one_head(0)
        mids(lambda: finish(0))
        ends(lambda: finish(1))
        one_head(1)
        middle(3)
        mids(lambda: finish(1))
        one_head(2)
        finish(2)
        one_head(3)
        finish(3)
    else:
        begin(0)
        begin(1)
        middle(0)
        begin(2)
        middle(1)
        ends(lambda: finish(0))
        begin(3)
        middle(2)
        mids(lambda: finish(0))
        ends(lambda: finish(1))
        middle(3)
        mids(lambda: finish(1))
        finish(2)
        finish(3)

    for k in (2, 3):
        to_core(k).wait_send()
    def drain(k, _):
        p = plane_at(z, 3 - k)
        for c in (far_x, far_y, x_top, x_bot, y_top, y_bot):
            c(k).wait_send()
        @pl.when(p > z)
        def _(): line_up(k, p).wait_send()
        @pl.when(p < z)
        def _(): line_down(k, p).wait_send()
        if carry:
            @pl.when((p <= z) & (z < 3))
            def _(): row_up(p).wait_send()
            @pl.when((p >= z) & (z > 0))
            def _(): row_down(p).wait_send()
        return 0
    lax.fori_loop(0, 4, drain, 0)

def scatter_sums(act, weights, scores, collective_id, attention=()):
    hid = min(weights[0].shape[1:])
    width = max(weights[0].shape[1:])
    n_here = weights[0].shape[0]
    quarter, cols = act.shape[3:]
    score_at = 3 * hid * n_here
    lanes = (cols - score_at) // n_here
    wide = width + (lanes if scores else 0)
    taken = pl.ds(0, cols) if scores else pl.ds(2 * hid * n_here, hid * n_here)
    product = input_product if scores else output_product
    any_ = pl.BlockSpec(memory_space=pl.ANY)
    vm = pl.BlockSpec(memory_space=pltpu.VMEM)
    n = len(weights)
    out_shape = (jax.ShapeDtypeStruct((quarter, wide), f32),)
    extra = []
    if attention:
        heads, head_size = attention[2].shape, attention[8].shape[1]
        out_shape += (
            jax.ShapeDtypeStruct((3,) + heads, bf),
            jax.ShapeDtypeStruct(attention[1].shape, bf),
            jax.ShapeDtypeStruct((2, head_size), f32),
        )
        extra = [pltpu.VMEM((4, quarter, width), bf), pltpu.VMEM(heads, bf)]
    return pl.pallas_call(
        functools.partial(scatter_kernel, product, n, width, taken, score_at if scores else None, bool(attention)),
        out_shape=out_shape,
        in_specs=[any_] * (1 + n) + [vm] * len(attention),
        out_specs=(vm,) * len(out_shape),
        scratch_shapes=[pltpu.VMEM((2, 4, quarter, taken.size), bf)] + [pltpu.VMEM(w.shape, bf) for w in weights] + [
            pltpu.VMEM((2, 4, quarter, wide), bf),
            pltpu.VMEM((4, 4, quarter, wide), bf),
            pltpu.VMEM((4, 4, quarter, wide), bf),
            pltpu.VMEM((4, quarter // 2, wide), bf), pltpu.VMEM((4, quarter // 2, wide), bf),
            pltpu.VMEM((4, quarter, wide), bf), pltpu.VMEM((4, quarter, wide), bf),
            pltpu.VMEM((4, quarter, wide), bf), pltpu.VMEM((4, quarter, wide), bf),
            pltpu.SemaphoreType.DMA((11, 4)), pltpu.SemaphoreType.DMA((11, 4)),
            pltpu.SemaphoreType.DMA((2,)), pltpu.SemaphoreType.DMA((n,)),
        ] + extra,
        compiler_params=pltpu.CompilerParams(collective_id=collective_id, has_side_effects=True, vmem_limit_bytes=62 << 20),
    )(act, *weights, *attention)


(SC, SDT, SDB, SXT, SXB, SYT, SYB, GX, GY, GFX, GFY, GC, GCX, GCY, GCA, GCB, LU, LD, RU, RD) = range(20)

def totals_kernel(*refs):
    grad_heads, normed_ref, proj_w, grad_out_w, refs = refs[0], refs[1], refs[2:5], refs[5], refs[6:]
    router_ref, ffn_ref, heads_ref, hidden_ref, resid_ref, gain_ref, refs = *refs[:6], refs[6:]
    res, rows, small_out, refs = refs[:4], refs[4], refs[5], refs[6:]
    w_ref, refs = (grad_out_w, *refs[:3]), refs[3:]
    r1, acc, rdt, rdb, rx, ry, refs = *(refs[4 * i : 4 * i + 4] for i in range(6)), refs[24:]
    part_ref, rzu, rzd, line, sums, got, send, recv, ssend, srecv = refs
    e = lax.axis_index("exp")
    z = lax.axis_index("tp")
    chip, core = e // 2, lax.rem(e, 2)
    cx, cy, cd = (jnp.bitwise_xor(chip, m) for m in (1, 2, 3))
    at_x, at_y, at_c = (jnp.bitwise_xor(e, 2), z), (jnp.bitwise_xor(e, 4), z), (jnp.bitwise_xor(e, 1), z)
    at_up, at_down = (e, z + 1), (e, z - 1)
    partners = (at_c, at_x, at_y, (e, jnp.bitwise_xor(z, 1)), (e, jnp.bitwise_xor(z, 2)))
    middle_plane = (z == 1) | (z == 2)
    halves = [ref.shape[1] // 2 for ref in acc]
    TOP, BOT = [pl.ds(0, h) for h in halves], [pl.ds(h, h) for h in halves]

    bar = pltpu.get_barrier_semaphore()
    for d in (at_x, at_y, at_c, (e, jnp.bitwise_xor(z, 2))):
        pl.semaphore_signal(bar, inc=1, device_id=d, device_id_type=MESH)
    @pl.when(z < 3)
    def _(): pl.semaphore_signal(bar, inc=1, device_id=at_up, device_id_type=MESH)
    @pl.when(z > 0)
    def _(): pl.semaphore_signal(bar, inc=1, device_id=at_down, device_id_type=MESH)
    pl.semaphore_wait(bar, 4 + jnp.where(z < 3, 1, 0) + jnp.where(z > 0, 1, 0))

    def remote(kind, k, src, dst, to):
        return pltpu.make_async_remote_copy(src_ref=src, dst_ref=dst, send_sem=send.at[kind, k], recv_sem=recv.at[kind, k],
                                            device_id=to, device_id_type=MESH)
    def arrived(kind, k, place):
        pltpu.make_async_copy(place, place, recv.at[kind, k]).wait()
    def to_core(k): return remote(SC, k, w_ref[k].at[1 - core], r1[k], at_c)
    def far_x(k): return remote(SDT, k, acc[k].at[cd, TOP[k]], rdt[k], at_x)
    def far_y(k): return remote(SDB, k, acc[k].at[cd, BOT[k]], rdb[k], at_y)
    def x_top(k): return remote(SXT, k, acc[k].at[cx, TOP[k]], rx[k].at[TOP[k]], at_x)
    def x_bot(k): return remote(SXB, k, acc[k].at[cx, BOT[k]], rx[k].at[BOT[k]], at_x)
    def y_top(k): return remote(SYT, k, acc[k].at[cy, TOP[k]], ry[k].at[TOP[k]], at_y)
    def y_bot(k): return remote(SYB, k, acc[k].at[cy, BOT[k]], ry[k].at[BOT[k]], at_y)
    def same(kind, k, place, to): return remote(kind, k, place, place, to)
    def give_x(k): return same(GX, k, res[k].at[core, chip], at_x)
    def give_y(k): return same(GY, k, res[k].at[core, chip], at_y)
    def give_c(k): return same(GC, k, res[k].at[core, chip], at_c)
    def pass_y(k): return same(GFY, k, res[k].at[core, cx, TOP[k]], at_y)
    def pass_x(k): return same(GFX, k, res[k].at[core, cy, BOT[k]], at_x)
    def c_x(k): return same(GCX, k, res[k].at[core, cx], at_c)
    def c_y(k): return same(GCY, k, res[k].at[core, cy], at_c)
    def c_a(k): return same(GCA, k, res[k].at[core, cd, TOP[k]], at_c)
    def c_b(k): return same(GCB, k, res[k].at[core, cd, BOT[k]], at_c)
    def line_up(p): return remote(LU, p, line.at[p], rzu.at[p], at_up)
    def line_down(p): return remote(LD, p, line.at[p], rzd.at[p], at_down)
    def row_up(p): return same(RU, p, rows.at[p], at_up)
    def row_down(p): return same(RD, p, rows.at[p], at_down)

    def plus(a, b): return (a.astype(f32) + b.astype(f32)).astype(bf)

    def input_part():
        def tile(n, _):
            input_back(proj_w, grad_heads, part_ref, pl.ds(pl.multiple_of(n * 512, 512), 512))
            return 0
        lax.fori_loop(0, part_ref.shape[2] // 512, tile, 0)

    def weight_part(k):
        part = lax.dot_general(normed_ref[...], grad_heads[k - 1], TN, preferred_element_type=f32)
        w_ref[k][...] = part.astype(bf).reshape(w_ref[k].shape)
        to_core(k).start()

    def begin(k):
        arrived(SC, k, r1[k])
        acc[k][cd] = plus(w_ref[k][core, cd], r1[k][cd])
        far_x(k).start()
        far_y(k).start()
        acc[k][cx] = plus(w_ref[k][core, cx], r1[k][cx])
        x_top(k).start()
        acc[k][cy] = plus(w_ref[k][core, cy], r1[k][cy])
        y_bot(k).start()
        acc[k][chip] = plus(w_ref[k][core, chip], r1[k][chip])

    def middle(k):
        arrived(SDB, k, rdb[k])
        acc[k][cx, BOT[k]] = plus(acc[k][cx, BOT[k]], rdb[k][...])
        x_bot(k).start()
        arrived(SDT, k, rdt[k])
        acc[k][cy, TOP[k]] = plus(acc[k][cy, TOP[k]], rdt[k][...])
        y_top(k).start()

    def finish(k):
        arrived(SXT, k, rx[k].at[TOP[k]])
        arrived(SYB, k, ry[k].at[BOT[k]])
        arrived(SXB, k, rx[k].at[BOT[k]])
        arrived(SYT, k, ry[k].at[TOP[k]])
        res[k][core, chip] = (acc[k][chip].astype(f32) + rx[k][...].astype(f32) + ry[k][...].astype(f32)).astype(bf)
        give_x(k).start()
        give_y(k).start()
        give_c(k).start()

    def spread(k):
        arrived(GX, k, res[k].at[core, cx])
        pass_y(k).start()
        c_x(k).start()
        arrived(GY, k, res[k].at[core, cy])
        pass_x(k).start()
        c_y(k).start()

    def last(k):
        arrived(GFY, k, res[k].at[core, cd, TOP[k]])
        c_a(k).start()
        arrived(GFX, k, res[k].at[core, cd, BOT[k]])
        c_b(k).start()

    def line_step(k):
        p = plane_at(z, 3 - k)
        line[p] = part_ref[p]
        @pl.when((z > 0) & (p >= z))
        def _():
            arrived(LU, p, rzu.at[p])
            line[p] = plus(line[p], rzu[p])
        @pl.when((z < 3) & (p <= z))
        def _():
            arrived(LD, p, rzd.at[p])
            line[p] = plus(line[p], rzd[p])
        @pl.when(p > z)
        def _(): line_up(p).start()
        @pl.when(p < z)
        def _(): line_down(p).start()

    def unit_rows(p):
        value = hidden_ref[p].astype(f32)
        scale = lax.rsqrt(jnp.mean(value * value, axis=-1, keepdims=True) + eps)
        return scale, value * scale

    def gain_row():
        sums[0, 0:8] = jnp.zeros((8, sums.shape[2]), f32)
        sums[0, 1:2] = ffn_ref[...]
        head_size = heads_ref.shape[1]
        sums[0, 2:3, 0:head_size] = heads_ref[0:1]
        sums[0, 2:3, head_size : 2 * head_size] = heads_ref[1:2]
        sums[0, 8:] = router_ref[...]
        def add_plane(p, _):
            sums[0, 0:1] += jnp.sum(part_ref[p].astype(f32) * unit_rows(p)[1], axis=0, keepdims=True)
            return 0
        lax.fori_loop(0, 4, add_plane, 0)
        small_copy(0).start()

    def own_rows():
        total = part_ref[z].astype(f32)
        @pl.when(z > 0)
        def _(): arrived(LU, z, rzu.at[z])
        @pl.when(z < 3)
        def _(): arrived(LD, z, rzd.at[z])
        total = total + jnp.where(z > 0, rzu[z].astype(f32), 0.0) + jnp.where(z < 3, rzd[z].astype(f32), 0.0)
        scale, unit = unit_rows(z)
        scaled = total * gain_ref[...]
        grad = scale * (scaled - unit * jnp.mean(unit * scaled, axis=-1, keepdims=True))
        rows[z] = (resid_ref[...] + grad).astype(bf)
        @pl.when(z < 3)
        def _(): row_up(z).start()
        @pl.when(z > 0)
        def _(): row_down(z).start()

    def row_step(k):
        p = plane_at(z, k)
        @pl.when(p < z)
        def _(): arrived(RU, p, rows.at[p])
        @pl.when(p > z)
        def _(): arrived(RD, p, rows.at[p])
        @pl.when((p < z) & (z < 3))
        def _(): row_up(p).start()
        @pl.when((p > z) & (z > 0))
        def _(): row_down(p).start()

    def small_copy(i):
        return pltpu.make_async_remote_copy(src_ref=sums.at[i], dst_ref=got.at[i], send_sem=ssend.at[i], recv_sem=srecv.at[i],
                                            device_id=partners[i], device_id_type=MESH)
    def small_step(i):
        small_copy(i).wait_recv()
        if i < 4:
            sums[i + 1] = sums[i] + got[i]
            small_copy(i + 1).start()
        else:
            small_out[...] = sums[i] + got[i]

    def ends(f):
        pl.when(~middle_plane)(f)
    def mids(f):
        pl.when(middle_plane)(f)

    to_core(0).start()
    input_part()
    ends(lambda: line_step(0))
    weight_part(1)
    begin(0)
    weight_part(2)
    begin(1)
    weight_part(3)
    begin(2)
    gain_row()
    begin(3)
    mids(lambda: line_step(0))
    ends(lambda: line_step(1))
    small_step(0)
    middle(0)
    middle(1)
    mids(lambda: line_step(1))
    mids(lambda: line_step(2))
    ends(lambda: line_step(2))
    middle(2)
    middle(3)
    small_step(1)
    own_rows()
    finish(0)
    finish(1)
    finish(2)
    finish(3)
    ends(lambda: row_step(1))
    mids(lambda: row_step(1))
    mids(lambda: row_step(2))
    spread(0)
    spread(1)
    small_step(2)
    mids(lambda: row_step(3))
    ends(lambda: row_step(2))
    spread(2)
    spread(3)
    last(0)
    small_step(3)
    ends(lambda: row_step(3))
    last(1)
    last(2)
    small_step(4)
    last(3)

    sib = 1 - core
    for k in range(4):
        for c in (to_core, far_x, far_y, x_top, x_bot, y_top, y_bot, give_x, give_y, give_c, pass_x, pass_y, c_x, c_y, c_a, c_b):
            c(k).wait_send()
        arrived(GC, k, res[k].at[sib, chip])
        arrived(GCX, k, res[k].at[sib, cx])
        arrived(GCY, k, res[k].at[sib, cy])
        arrived(GCA, k, res[k].at[sib, cd, TOP[k]])
        arrived(GCB, k, res[k].at[sib, cd, BOT[k]])
    def drain(p, _):
        @pl.when(p > z)
        def _(): line_up(p).wait_send()
        @pl.when(p < z)
        def _(): line_down(p).wait_send()
        @pl.when((z < 3) & (p <= z))
        def _(): row_up(p).wait_send()
        @pl.when((z > 0) & (p >= z))
        def _(): row_down(p).wait_send()
        return 0
    lax.fori_loop(0, 4, drain, 0)
    for i in range(5): small_copy(i).wait_send()

def final_totals(grad_heads, normed, proj_w, grad_out_w, router, ffn, heads, hidden, resid, gain, collective_id):
    vm = pl.BlockSpec(memory_space=pltpu.VMEM)
    planes = hidden.shape
    one = (2, 4, proj_w[0].shape[0] // 8, proj_w[0].shape[1])
    shapes = (grad_out_w.shape, one, one, one)
    small = (5, 8 + router.shape[0], router.shape[1])
    own = [pltpu.VMEM(one, bf)] * 3
    whole = [pltpu.VMEM(s[1:], bf) for s in shapes]
    quarter = [pltpu.VMEM(s[2:], bf) for s in shapes]
    half = [pltpu.VMEM((s[2] // 2, s[3]), bf) for s in shapes]
    return pl.pallas_call(
        totals_kernel,
        out_shape=tuple(jax.ShapeDtypeStruct(s, bf) for s in shapes) + (
            jax.ShapeDtypeStruct(planes, bf), jax.ShapeDtypeStruct(small[1:], f32)),
        in_specs=[vm] * 12,
        out_specs=(vm,) * 6,
        scratch_shapes=own + whole + whole + half + half + quarter + quarter + [
            pltpu.VMEM(planes, bf), pltpu.VMEM(planes, bf), pltpu.VMEM(planes, bf), pltpu.VMEM(planes, bf),
            pltpu.VMEM(small, f32), pltpu.VMEM(small, f32),
            pltpu.SemaphoreType.DMA((20, 4)), pltpu.SemaphoreType.DMA((20, 4)),
            pltpu.SemaphoreType.DMA((5,)), pltpu.SemaphoreType.DMA((5,)),
        ],
        compiler_params=pltpu.CompilerParams(collective_id=collective_id, has_side_effects=True, vmem_limit_bytes=62 << 20),
    )(grad_heads, normed, *proj_w, grad_out_w, router, ffn, heads, hidden, resid, gain)


def slot_experts(routed_low, gates, picked, grad_out, expert_routes, gate_weight, up_weight, down_weight):
    highest = lax.Precision.HIGHEST
    quarter, width = grad_out.shape
    top_count = expert_routes.shape[1]
    experts = picked.shape[2]
    capacity = max(2, 2 * quarter * top_count // experts)
    picked_wide = picked.astype(jnp.float32)
    grad_rows = grad_out.astype(jnp.float32)
    flat_route = expert_routes.reshape(-1)
    flat_pick = picked.reshape(-1, experts).astype(jnp.int32)
    rank = jnp.sum((jnp.cumsum(flat_pick, axis=0) - 1) * flat_pick, axis=1)
    place = flat_route * capacity + rank
    row_token = jnp.arange(quarter * top_count, dtype=jnp.int32) // top_count
    send_rows = (
        jnp.zeros((experts * capacity, width), jnp.bfloat16).at[place].set(routed_low[row_token])
    )
    arrived = lax.all_to_all(
        send_rows.reshape(experts, capacity, width), "exp", split_axis=0, concat_axis=1, tiled=True
    )
    rows_used = lax.all_gather(arrived, "tp", axis=1, tiled=True)
    gate_act = jnp.einsum(
        "erd,edf->erf", rows_used, gate_weight, preferred_element_type=jnp.float32
    )
    up_act = jnp.einsum("erd,edf->erf", rows_used, up_weight, preferred_element_type=jnp.float32)
    hidden_low = (jax.nn.silu(gate_act) * up_act).astype(jnp.bfloat16)
    partial_out = jnp.einsum(
        "erf,efd->erd", hidden_low, down_weight, preferred_element_type=jnp.float32
    )
    expert_out = lax.psum_scatter(partial_out, "tp", scatter_dimension=1, tiled=True)
    returned = lax.all_to_all(
        expert_out.astype(jnp.bfloat16), "exp", split_axis=1, concat_axis=0, tiled=True
    )
    back_rows = (
        returned.reshape(experts * capacity, width)[place]
        .reshape(quarter, top_count, width)
        .astype(jnp.float32)
    )
    moe = jnp.einsum("tk,tkd->td", gates, back_rows, precision=highest)
    grad_gates = jnp.einsum("tkd,td->tk", back_rows, grad_rows, precision=highest)
    grad_chosen = gates * (grad_gates - jnp.sum(gates * grad_gates, axis=-1, keepdims=True))
    grad_logits = jnp.einsum("tke,tk->te", picked_wide, grad_chosen, precision=highest)
    weighted_grad = (
        (gates[:, :, None] * grad_rows[:, None, :])
        .astype(jnp.bfloat16)
        .reshape(quarter * top_count, width)
    )
    send_grads = jnp.zeros((experts * capacity, width), jnp.bfloat16).at[place].set(weighted_grad)
    grad_arrived = lax.all_to_all(
        send_grads.reshape(experts, capacity, width), "exp", split_axis=0, concat_axis=1, tiled=True
    )
    sigmoid_gate = jax.nn.sigmoid(gate_act)
    silu_gate = gate_act * sigmoid_gate
    slope = sigmoid_gate * (1.0 + gate_act * (1.0 - sigmoid_gate))
    grad_used = lax.all_gather(grad_arrived, "tp", axis=1, tiled=True)
    grad_hid = jnp.einsum(
        "erd,efd->erf", grad_used, down_weight, preferred_element_type=jnp.float32
    )
    grad_down = jnp.einsum(
        "erf,erd->efd", hidden_low, grad_used, preferred_element_type=jnp.float32
    )
    grad_gate = (grad_hid * up_act * slope).astype(jnp.bfloat16)
    grad_up = (grad_hid * silu_gate).astype(jnp.bfloat16)
    grad_gate_w = jnp.einsum(
        "erd,erf->edf", rows_used, grad_gate, preferred_element_type=jnp.float32
    )
    grad_up_w = jnp.einsum("erd,erf->edf", rows_used, grad_up, preferred_element_type=jnp.float32)
    input_part = jnp.einsum(
        "erf,edf->erd", grad_gate, gate_weight, preferred_element_type=jnp.float32
    ) + jnp.einsum("erf,edf->erd", grad_up, up_weight, preferred_element_type=jnp.float32)
    grad_input = lax.psum_scatter(input_part, "tp", scatter_dimension=1, tiled=True).astype(
        jnp.bfloat16
    )
    grad_back = lax.all_to_all(grad_input, "exp", split_axis=1, concat_axis=0, tiled=True)
    expert_grad = jnp.sum(
        grad_back.reshape(experts * capacity, width)[place]
        .reshape(quarter, top_count, width)
        .astype(jnp.float32),
        axis=1,
    )
    return moe, grad_logits, expert_grad, grad_gate_w, grad_up_w, grad_down


def gate_pair(dense_gates):
    pad = ((0, 0), (0, gate_lanes // 2 - dense_gates.shape[1]))
    high = dense_gates.astype(bf)
    low = (dense_gates - high.astype(f32)).astype(bf)
    return [jnp.pad(high, pad), jnp.pad(low, pad)]


def per_device(
    fits,
    hidden_in,
    attn_gain,
    query_weight,
    key_weight,
    value_weight,
    qnorm_gain,
    knorm_gain,
    out_weight,
    ffn_gain,
    router_weight,
    gate_weight,
    up_weight,
    down_weight,
    expert_routes,
    seq_lengths,
    grad_out,
):
    highest = lax.Precision.HIGHEST
    group_rows = hidden_in.shape[0]
    width = hidden_in.shape[1]
    head_size = qnorm_gain.shape[0]
    quarter = grad_out.shape[0]
    experts = router_weight.shape[1]
    tp_index = lax.axis_index("tp")
    widened = hidden_in.astype(jnp.float32)
    segment, cosine, sine = rotary_tables(seq_lengths[0], group_rows, head_size)
    if fits:
        planes = (4, quarter, width)
        gains = jnp.stack([qnorm_gain, knorm_gain])
        tables = (
            jnp.concatenate([cosine[:, 0], cosine[:, 0]], axis=1),
            jnp.concatenate([-sine[:, 0], sine[:, 0]], axis=1),
            segment[:, None],
            segment[None],
        )
        attn_rows, normed_low, query_proj, key_proj, *heads, mixed_low, grads_all = open_exchange(
            hidden_in.reshape(planes),
            attn_gain[None],
            (query_weight, key_weight, value_weight, out_weight),
            gains,
            *tables,
            grad_out,
            5,
        )
    else:
        normed_one = rms_norm(widened, attn_gain)
        normed_low = normed_one.astype(jnp.bfloat16)
        same_seq = segment[:, None] == segment[None, :]

        def prepare(projected, gain):
            return head_prep(projected, gain, cosine, sine)

        query_proj = jnp.dot(normed_low, query_weight, preferred_element_type=jnp.float32)
        key_proj = jnp.dot(normed_low, key_weight, preferred_element_type=jnp.float32)
        value_proj = jnp.dot(normed_low, value_weight, preferred_element_type=jnp.float32)
        queries, query_back = jax.vjp(prepare, query_proj, qnorm_gain)
        keys, key_back = jax.vjp(prepare, key_proj, knorm_gain)
        query_low = queries.astype(jnp.bfloat16)
        key_low = keys.astype(jnp.bfloat16)
        value_low = value_proj.astype(jnp.bfloat16).reshape(group_rows, -1, head_size)
        scores = masked_scores(query_low, key_low, same_seq, head_size)
        top_score = jnp.max(scores, axis=-1, keepdims=True)
        log_total = top_score + jnp.log(jnp.sum(jnp.exp(scores - top_score), axis=-1, keepdims=True))
        probs_low = jnp.exp(scores - log_total).astype(jnp.bfloat16)
        mixed = jnp.einsum("hts,shd->thd", probs_low, value_low, preferred_element_type=jnp.float32)
        mixed_low = mixed.astype(jnp.bfloat16).reshape(group_rows, -1)
        attn_part = jnp.dot(mixed_low, out_weight, preferred_element_type=jnp.float32)
        attn_rows = lax.psum_scatter(attn_part, "tp", scatter_dimension=0, tiled=True)
    own_rows = lax.dynamic_slice_in_dim(widened, tp_index * quarter, quarter, 0)
    resid = own_rows + attn_rows
    normed_two, norm_two_back = jax.vjp(rms_norm, resid, ffn_gain)
    routed_low = normed_two.astype(jnp.bfloat16)
    logits = jnp.dot(routed_low, router_weight, preferred_element_type=jnp.float32)
    picked = expert_routes[:, :, None] == jnp.arange(experts, dtype=jnp.int32)[None, None, :]
    picked_wide = picked.astype(jnp.float32)
    chosen = jnp.einsum("tke,te->tk", picked_wide, logits, precision=highest)
    gates = jax.nn.softmax(chosen, axis=-1)
    grad_rows = grad_out.astype(jnp.float32)
    if fits:
        dense_gates = jnp.einsum("tke,tk->te", picked_wide, gates, precision=highest)
        act, grad_gate_w, grad_up_w, grad_down = gather_experts(
            jnp.concatenate([routed_low] + gate_pair(dense_gates), axis=1),
            grads_all,
            gate_weight,
            up_weight,
            down_weight,
        )
        (sums,) = scatter_sums(act, (gate_weight, up_weight), True, 2)
        expert_grad = sums[:, :width]
        grad_gates = sums[:, width : width + experts]
        grad_logits = dense_gates * (
            grad_gates - jnp.sum(dense_gates * grad_gates, axis=-1, keepdims=True)
        )
    else:
        moe, grad_logits, expert_grad, grad_gate_w, grad_up_w, grad_down = slot_experts(
            routed_low,
            gates,
            picked,
            grad_out,
            expert_routes,
            gate_weight,
            up_weight,
            down_weight,
        )
    grad_normed = (
        jnp.dot(grad_logits, router_weight.astype(jnp.float32).T, precision=highest) + expert_grad
    )
    grad_router = jnp.dot(routed_low.astype(jnp.float32).T, grad_logits, precision=highest)
    grad_resid, grad_ffn_gain = norm_two_back(grad_normed)
    grad_resid = grad_resid + grad_rows
    grad_low = grad_resid.astype(jnp.bfloat16)
    if fits:
        moe, grad_heads, grad_out_w, grad_gains = scatter_sums(
            act,
            (down_weight,),
            False,
            3,
            (
                grad_low,
                out_weight,
                mixed_low,
                *heads,
                query_proj,
                key_proj,
                gains,
                *tables,
            ),
        )
        grad_out_sum, *sums, grad_input_rows, small = final_totals(
            grad_heads,
            normed_low,
            (query_weight, key_weight, value_weight),
            grad_out_w.reshape(2, 4, -1, width),
            grad_router.T,
            grad_ffn_gain[None],
            grad_gains,
            hidden_in.reshape(planes),
            grad_resid,
            attn_gain[None],
            4,
        )
        grad_input_rows = grad_input_rows.reshape(group_rows, width)
        totals = tuple(
            part.reshape(-1, part.shape[3]).astype(f32) for part in (*sums, grad_out_sum)
        ) + (
            small[0],
            small[2, :head_size],
            small[2, head_size : 2 * head_size],
            small[1],
            small[8:].T,
        )
    else:
        grad_attn_low = lax.all_gather(grad_low, "tp", axis=0, tiled=True)
        grad_out_weight = jnp.dot(mixed_low.T, grad_attn_low, preferred_element_type=jnp.float32)
        grad_mixed = jnp.dot(grad_attn_low, out_weight.T, preferred_element_type=jnp.float32)
        grad_mixed_low = grad_mixed.astype(jnp.bfloat16).reshape(group_rows, -1, head_size)
        probs = jnp.exp(masked_scores(query_low, key_low, same_seq, head_size) - log_total)
        grad_probs = jnp.einsum(
            "thd,shd->hts", grad_mixed_low, value_low, preferred_element_type=jnp.float32
        )
        grad_value = jnp.einsum(
            "hts,thd->shd", probs_low, grad_mixed_low, preferred_element_type=jnp.float32
        )
        row_delta = jnp.sum(probs * grad_probs, axis=-1, keepdims=True)
        grad_scores = (probs * (grad_probs - row_delta)).astype(jnp.bfloat16)
        grad_query = jnp.einsum(
            "hts,shd->thd", grad_scores, key_low, preferred_element_type=jnp.float32
        ) / math.sqrt(head_size)
        grad_key = jnp.einsum(
            "hts,thd->shd", grad_scores, query_low, preferred_element_type=jnp.float32
        ) / math.sqrt(head_size)
        grad_query_proj, grad_qgain = query_back(grad_query)
        grad_key_proj, grad_kgain = key_back(grad_key)
        grad_query_low = grad_query_proj.astype(jnp.bfloat16)
        grad_key_low = grad_key_proj.astype(jnp.bfloat16)
        grad_value_low = grad_value.reshape(group_rows, -1).astype(jnp.bfloat16)
        normed_part = (
            jnp.dot(grad_query_low, query_weight.T, preferred_element_type=jnp.float32)
            + jnp.dot(grad_key_low, key_weight.T, preferred_element_type=jnp.float32)
            + jnp.dot(grad_value_low, value_weight.T, preferred_element_type=jnp.float32)
        )
        grad_query_w = jnp.dot(normed_low.T, grad_query_low, preferred_element_type=jnp.float32)
        grad_key_w = jnp.dot(normed_low.T, grad_key_low, preferred_element_type=jnp.float32)
        grad_value_w = jnp.dot(normed_low.T, grad_value_low, preferred_element_type=jnp.float32)
        scale_one = lax.rsqrt(jnp.mean(widened * widened, axis=-1, keepdims=True) + eps)
        unit_one = widened * scale_one
        grad_attn_gain = jnp.sum(normed_part * unit_one, axis=0)
        grad_normed_one = lax.psum(normed_part.astype(bf), "tp").astype(f32)
        scaled = grad_normed_one * attn_gain
        grad_from_norm = scale_one * (
            scaled - unit_one * jnp.mean(unit_one * scaled, axis=-1, keepdims=True)
        )
        grad_input_rows = (grad_attn_low.astype(f32) + grad_from_norm).astype(jnp.bfloat16)
        low_totals = lax.psum(
            tuple(
                part.astype(jnp.bfloat16)
                for part in (grad_query_w, grad_key_w, grad_value_w, grad_out_weight)
            ),
            "exp",
        )
        small = lax.psum(
            (grad_attn_gain, grad_qgain, grad_kgain, grad_ffn_gain, grad_router), ("exp", "tp")
        )
        totals = tuple(part.astype(jnp.float32) for part in low_totals) + small
    block_out = (resid + moe).astype(jnp.bfloat16)
    return (
        block_out,
        grad_input_rows,
        totals[4],
        totals[0],
        totals[1],
        totals[2],
        totals[3],
        totals[5],
        totals[6],
        totals[7],
        totals[8],
        grad_gate_w,
        grad_up_w,
        grad_down,
    )


def solution(mesh):
    in_specs = (
        P("exp", None),
        P(),
        P(None, "tp"),
        P(None, "tp"),
        P(None, "tp"),
        P(),
        P(),
        P("tp", None),
        P(),
        P(),
        P("exp", None, "tp"),
        P("exp", None, "tp"),
        P("exp", "tp", None),
        P(("exp", "tp"), None),
        P("exp", None),
        P(("exp", "tp"), None),
    )
    out_specs = (
        P(("exp", "tp"), None),
        P("exp", None),
        P(),
        P(None, "tp"),
        P(None, "tp"),
        P(None, "tp"),
        P("tp", None),
        P(),
        P(),
        P(),
        P(),
        P("exp", None, "tp"),
        P("exp", None, "tp"),
        P("exp", "tp", None),
    )
    fits = dict(mesh.shape) == {"exp": 8, "tp": 4}
    return jax.shard_map(
        functools.partial(per_device, fits), mesh=mesh, in_specs=in_specs, out_specs=out_specs, check_vma=False
    )
```

```python
import functools
import math

import jax
import jax.numpy as jnp
from jax import lax
from jax.experimental import pallas as pl
from jax.experimental.pallas import tpu as pltpu
from jax.sharding import PartitionSpec as P

eps = 1e-06
rope_base = 10000.0
gate_lanes = 128
MESH = pl.DeviceIdType.MESH
bf = jnp.bfloat16
f32 = jnp.float32
NT = (((1,), (1,)), ((), ()))
TN = (((0,), (0,)), ((), ()))


def rms_norm(values, gain):
    return values * lax.rsqrt(jnp.mean(values * values, axis=-1, keepdims=True) + eps) * gain


def rotary_tables(lengths_row, count, head_size):
    token_index = jnp.arange(count, dtype=jnp.int32)
    seq_ends = jnp.cumsum(lengths_row)
    starts = seq_ends - lengths_row
    member = (
        (token_index[:, None] >= starts[None, :]) & (token_index[:, None] < seq_ends[None, :])
    ).astype(jnp.int32)
    segment = jnp.sum(member * jnp.arange(lengths_row.shape[0], dtype=jnp.int32)[None, :], axis=1)
    offset = jnp.sum(member * starts[None, :], axis=1)
    position = (token_index - offset).astype(jnp.float32)
    frequency = rope_base ** (-jnp.arange(0, head_size, 2, dtype=jnp.float32) / head_size)
    angles = position[:, None] * frequency[None, :]
    return (segment, jnp.cos(angles)[:, None, :], jnp.sin(angles)[:, None, :])


def rotate(values, cosine, sine):
    half = values.shape[-1] // 2
    first = values[..., :half]
    second = values[..., half:]
    return jnp.concatenate(
        [first * cosine - second * sine, second * cosine + first * sine], axis=-1
    )


def head_prep(projected, gain, cosine, sine):
    head_size = gain.shape[0]
    shaped = projected.reshape(projected.shape[0], projected.shape[1] // head_size, head_size)
    return rotate(rms_norm(shaped, gain), cosine, sine)


def masked_scores(query_low, key_low, same_seq, head_size):
    scores = jnp.einsum(
        "thd,shd->hts", query_low, key_low, preferred_element_type=jnp.float32
    ) / math.sqrt(head_size)
    return jnp.where(same_seq[None], scores, -1e30)


def plane_at(z, step):
    from_end = step
    from_middle = jnp.where(step == 0, 1, jnp.where(step == 1, 0, step))
    base = jnp.where((z == 0) | (z == 3), from_end, from_middle)
    return jnp.where(z < 2, base, 3 - base)

Z, X, Y, FX, FY, CO, CX, CY, CA, CB = range(10)

def gather_kernel(own_ref, grad_hbm, wg_hbm, wu_hbm, wd_hbm,
                  act_hbm, dg_ref, du_ref, dd_ref,
                  rows, grads, wg, wu, wd, act, send, up_send, recv, load, store, wload):
    e = lax.axis_index("exp")
    z = lax.axis_index("tp")
    ex, ey, ec, ed = (jnp.bitwise_xor(e, m) for m in (2, 4, 1, 6))
    width = wg.shape[1]
    quarter = own_ref.shape[0]
    half = quarter // 2
    hid = wg.shape[2]
    experts_here = wg.shape[0]
    at_x, at_y, at_c = (ex, z), (ey, z), (ec, z)
    at_up, at_down = (e, z + 1), (e, z - 1)

    wcopies = [pltpu.make_async_copy(s, d, wload.at[i]) for i, (s, d) in enumerate(((wg_hbm, wg), (wu_hbm, wu), (wd_hbm, wd)))]
    for c in wcopies: c.start()

    loads = [pltpu.make_async_copy(grad_hbm.at[plane_at(z, k)], grads.at[k], load.at[k]) for k in range(4)]
    for c in loads: c.start()
    middle = (z == 1) | (z == 2)

    bar = pltpu.get_barrier_semaphore()
    for d in (at_x, at_y, at_c):
        pl.semaphore_signal(bar, inc=1, device_id=d, device_id_type=MESH)
    @pl.when(z < 3)
    def _(): pl.semaphore_signal(bar, inc=1, device_id=at_up, device_id_type=MESH)
    @pl.when(z > 0)
    def _(): pl.semaphore_signal(bar, inc=1, device_id=at_down, device_id_type=MESH)
    pl.semaphore_wait(bar, 3 + jnp.where(z < 3, 1, 0) + jnp.where(z > 0, 1, 0))

    TOP, BOT, ALLR = pl.ds(0, half), pl.ds(half, half), pl.ds(0, quarter)

    def copy(kind, plane, group, part, to, src=None, sem=None):
        place = rows.at[plane, group, part]
        return pltpu.make_async_remote_copy(
            src_ref=place if src is None else src, dst_ref=place,
            send_sem=(send.at[kind, plane] if sem is None else sem), recv_sem=recv.at[kind, plane],
            device_id=to, device_id_type=MESH)

    def up(plane, src=None): return copy(Z, plane, e, ALLR, at_up, src, up_send.at[plane])
    def down(plane, src=None): return copy(Z, plane, e, ALLR, at_down, src)
    def to_x(plane, src=None): return copy(X, plane, e, ALLR, at_x, src)
    def to_y(plane, src=None): return copy(Y, plane, e, ALLR, at_y, src)
    def to_c(plane, src=None): return copy(CO, plane, e, ALLR, at_c, src)
    def fwd_y(plane): return copy(FY, plane, ex, TOP, at_y)
    def fwd_x(plane): return copy(FX, plane, ey, BOT, at_x)
    def c_x(plane): return copy(CX, plane, ex, ALLR, at_c)
    def c_y(plane): return copy(CY, plane, ey, ALLR, at_c)
    def c_a(plane): return copy(CA, plane, ed, TOP, at_c)
    def c_b(plane): return copy(CB, plane, ed, BOT, at_c)

    def arrived(kind, plane, group, part):
        place = rows.at[plane, group, part]
        pltpu.make_async_copy(place, place, recv.at[kind, plane]).wait()

    @pl.when(z < 3)
    def _(): up(z, own_ref).start()
    @pl.when(z > 0)
    def _(): down(z, own_ref).start()
    to_x(z, own_ref).start()
    to_y(z, own_ref).start()
    to_c(z, own_ref).start()
    rows[z, e] = own_ref[...]

    def serve_line(k):
        p = plane_at(z, k)
        arrived(Z, p, e, ALLR)
        @pl.when((p < z) & (z < 3))
        def _(): up(p).start()
        @pl.when((p > z) & (z > 0))
        def _(): down(p).start()

    def serve_rows(k):
        p = plane_at(z, k)
        to_x(p).start()
        to_y(p).start()
        to_c(p).start()

    def serve_sides(k):
        p = plane_at(z, k)
        arrived(X, p, ex, ALLR)
        fwd_y(p).start()
        c_x(p).start()
        arrived(Y, p, ey, ALLR)
        fwd_x(p).start()
        c_y(p).start()

    def serve_far(k):
        p = plane_at(z, k)
        arrived(FY, p, ed, TOP)
        c_a(p).start()
        arrived(FX, p, ed, BOT)
        c_b(p).start()

    def store_copy(step):
        k, h = step // 2, lax.rem(step, 2)
        first = jnp.bitwise_xor(jnp.bitwise_and(e, 4), h * 4)
        return pltpu.make_async_copy(act, act_hbm.at[pl.ds(first // 2, 2), :, plane_at(z, k)], store)

    serve_line(1)
    serve_rows(1)
    @pl.when(middle)
    def _(): serve_line(2)
    serve_sides(0)
    for c in wcopies + loads: c.wait()

    def step_body(step, _):
        k, h = step // 2, lax.rem(step, 2)
        p = plane_at(z, k)
        first = jnp.bitwise_xor(jnp.bitwise_and(e, 4), h * 4)
        sib_x = jnp.bitwise_xor(ec, 2)
        sib_y = jnp.bitwise_xor(ec, 4)
        sib_d = jnp.bitwise_xor(ec, 6)
        @pl.when(h == 0)
        def _():
            arrived(CO, p, ec, ALLR)
            arrived(CX, p, sib_x, ALLR)
        @pl.when(h == 1)
        def _():
            arrived(CY, p, sib_y, ALLR)
            arrived(CA, p, sib_d, TOP)
            arrived(CB, p, sib_d, BOT)
        lane = lax.broadcasted_iota(jnp.int32, (4 * quarter, gate_lanes), 1)

        def expert_body(j, _):
            x = rows[p, pl.ds(first, 4), :, :width].reshape(4 * quarter, width)
            g = grads[k, pl.ds(first, 4)].reshape(4 * quarter, width)
            extra = rows[p, pl.ds(first, 4), :, width:].reshape(4 * quarter, gate_lanes).astype(f32)
            expert = e * experts_here + j
            mine = (lane == expert) | (lane == expert + gate_lanes // 2)
            gate = jnp.sum(jnp.where(mine, extra, 0.0), axis=1, keepdims=True)
            ga = jnp.dot(x, wg[j], preferred_element_type=f32)
            ua = jnp.dot(x, wu[j], preferred_element_type=f32)
            gh = lax.dot_general(g, wd[j], (((1,), (1,)), ((), ())), preferred_element_type=f32)
            sg = jax.nn.sigmoid(ga)
            silu = ga * sg
            hidden = silu * ua
            score = jnp.sum(hidden * gh, axis=1, keepdims=True)
            gh = gh * gate
            hg = (hidden * gate).astype(bf)
            da = (gh * ua * (sg * (1.0 + ga * (1.0 - sg)))).astype(bf)
            du = (gh * silu).astype(bf)
            @pl.when((step > 0) & (j == 0))
            def _(): store_copy(step - 1).wait()
            base = j * 2 * hid
            shape3 = (2, 2, quarter, hid)
            act[:, :, :, pl.ds(pl.multiple_of(base, hid), hid)] = da.reshape(shape3)
            act[:, :, :, pl.ds(pl.multiple_of(base + hid, hid), hid)] = du.reshape(shape3)
            act[:, :, :, pl.ds(pl.multiple_of((2 * experts_here + j) * hid, hid), hid)] = hg.reshape(shape3)
            scores = jnp.where(lane == expert, score, 0.0).astype(bf).reshape(2, 2, quarter, gate_lanes)
            act[:, :, :, pl.ds(pl.multiple_of(experts_here * 3 * hid + j * gate_lanes, gate_lanes), gate_lanes)] = scores
            @pl.when(step == 0)
            def _():
                dg_ref[j] = jnp.zeros(dg_ref.shape[1:], f32)
                du_ref[j] = jnp.zeros(du_ref.shape[1:], f32)
                dd_ref[j] = jnp.zeros(dd_ref.shape[1:], f32)
            slot = 2 * step + j
            for at, work, which in (
                (1, serve_far, 0),
                (3, serve_sides, 1),
                (5, serve_rows, 3),
                (5, serve_far, 1),
                (7, serve_sides, 2),
                (9, serve_far, 2),
                (9, serve_sides, 3),
                (12, serve_far, 3),
            ):
                @pl.when(slot == at)
                def _(): work(which)
            @pl.when((slot == 1) & middle)
            def _(): serve_line(3)
            @pl.when((slot == 1) & ~middle)
            def _(): serve_line(2)
            @pl.when(slot == 1)
            def _(): serve_rows(2)
            @pl.when((slot == 3) & ~middle)
            def _(): serve_line(3)
            dd_ref[j] += lax.dot_general(hg, g, TN, preferred_element_type=f32)
            dg_ref[j] += lax.dot_general(x, da, TN, preferred_element_type=f32)
            du_ref[j] += lax.dot_general(x, du, TN, preferred_element_type=f32)
            return 0
        lax.fori_loop(0, experts_here, expert_body, 0)
        store_copy(step).start()
        return 0
    lax.fori_loop(0, 8, step_body, 0)
    store_copy(7).wait()

    def drain(k, _):
        p = plane_at(z, k)
        @pl.when((z < 3) & (p <= z))
        def _(): up(p).wait_send()
        @pl.when((z > 0) & (p >= z))
        def _(): down(p).wait_send()
        for c in (to_x, to_y, to_c, fwd_y, fwd_x, c_x, c_y, c_a, c_b):
            c(p).wait_send()
        return 0
    lax.fori_loop(0, 4, drain, 0)

def gather_experts(own, grads_all, wg, wu, wd):
    n_here, width, hid = wg.shape
    quarter, wide = own.shape
    lanes = wide - width
    cols = n_here * 3 * hid + n_here * lanes
    any_ = pl.BlockSpec(memory_space=pl.ANY)
    vm = pl.BlockSpec(memory_space=pltpu.VMEM)
    return pl.pallas_call(
        gather_kernel,
        out_shape=(jax.ShapeDtypeStruct((4, 2, 4, quarter, cols), bf),
                   jax.ShapeDtypeStruct(wg.shape, f32), jax.ShapeDtypeStruct(wu.shape, f32), jax.ShapeDtypeStruct(wd.shape, f32)),
        in_specs=[vm, any_, any_, any_, any_],
        out_specs=(any_, vm, vm, vm),
        scratch_shapes=[
            pltpu.VMEM((4, 8, quarter, wide), bf),
            pltpu.VMEM((4, 8, quarter, width), bf),
            pltpu.VMEM(wg.shape, bf), pltpu.VMEM(wu.shape, bf), pltpu.VMEM(wd.shape, bf),
            pltpu.VMEM((2, 2, quarter, cols), bf),
            pltpu.SemaphoreType.DMA((10, 4)), pltpu.SemaphoreType.DMA((4,)), pltpu.SemaphoreType.DMA((10, 4)),
            pltpu.SemaphoreType.DMA((4,)), pltpu.SemaphoreType.DMA, pltpu.SemaphoreType.DMA((3,)),
        ],
        compiler_params=pltpu.CompilerParams(collective_id=1, has_side_effects=True, vmem_limit_bytes=63 << 20),
        cost_estimate=pl.CostEstimate(flops=12 * 4096 * 2048 * hid * n_here, bytes_accessed=64 << 20, transcendentals=0),
    )(own, grads_all, wg, wu, wd)


def head_scores(queries, keys, same, head_size):
    scores = lax.dot_general(queries, keys, NT, preferred_element_type=f32) / math.sqrt(head_size)
    scores = jnp.where(same, scores, -1e30)
    grown = jnp.exp(scores - jnp.max(scores, axis=-1, keepdims=True))
    return grown / jnp.sum(grown, axis=-1, keepdims=True)

def mixed_back(grad_rows, out_w, mixed, grad_mixed, grad_out_w):
    grads = grad_rows[...].reshape(-1, grad_rows.shape[2])
    grad_mixed[...] = lax.dot_general(grads, out_w[...], NT, preferred_element_type=f32).astype(bf)
    grad_out_w[...] = lax.dot_general(mixed[...], grads, TN, preferred_element_type=f32).astype(bf)

def head_back(h, queries, keys, values, projected, gains, cosine, sine, seg_col, seg_row, grad_mixed, grad_heads, grad_gains):
    head_size = cosine.shape[1]
    at = pl.ds(pl.multiple_of(h * head_size, head_size), head_size)
    same = seg_col[...] == seg_row[...]
    q, k, v, gm = queries[:, at], keys[:, at], values[:, at], grad_mixed[:, at]
    probs = head_scores(q, k, same, head_size)
    grad_probs = lax.dot_general(gm, v, NT, preferred_element_type=f32)
    grad_heads[2, :, at] = lax.dot_general(probs.astype(bf), gm, TN, preferred_element_type=f32).astype(bf)
    delta = jnp.sum(probs * grad_probs, axis=-1, keepdims=True)
    grad_scores = (probs * (grad_probs - delta)).astype(bf)
    back = (
        jnp.dot(grad_scores, k, preferred_element_type=f32),
        lax.dot_general(grad_scores, q, TN, preferred_element_type=f32),
    )
    for i in range(2):
        grad = back[i] / math.sqrt(head_size)
        grad = grad * cosine[...] - pltpu.roll(grad, head_size // 2, axis=1) * sine[...]
        value = projected[i][:, at]
        scale = lax.rsqrt(jnp.mean(value * value, axis=-1, keepdims=True) + eps)
        unit = value * scale
        grad_gains[i : i + 1] += jnp.sum(grad * unit, axis=0, keepdims=True)
        scaled = grad * gains[i : i + 1]
        grad_heads[i, :, at] = (scale * (scaled - unit * jnp.mean(unit * scaled, axis=-1, keepdims=True))).astype(bf)

def input_back(weights, grad_heads, part, cols):
    total = None
    for i, w in enumerate(weights):
        one = lax.dot_general(grad_heads[i], w[cols, :], NT, preferred_element_type=f32)
        total = one if total is None else total + one
    part[:, :, cols] = total.astype(bf).reshape(part.shape[0], part.shape[1], -1)

def norm_rows(hidden, gain, normed):
    rows = hidden.shape[1]
    def plane(p, _):
        value = hidden[p].astype(f32)
        scale = lax.rsqrt(jnp.mean(value * value, axis=-1, keepdims=True) + eps)
        normed[pl.ds(pl.multiple_of(p * rows, rows), rows), :] = (value * scale * gain[...]).astype(bf)
        return 0
    lax.fori_loop(0, hidden.shape[0], plane, 0)

def project(normed, weight, out):
    out[...] = jnp.dot(normed[...], weight[...], preferred_element_type=f32).astype(out.dtype)

def head_forward(h, projected, gains, cosine, sine, seg_col, seg_row, lows, values, mixed):
    head_size = cosine.shape[1]
    at = pl.ds(pl.multiple_of(h * head_size, head_size), head_size)
    for i in range(2):
        value = projected[i][:, at]
        scale = lax.rsqrt(jnp.mean(value * value, axis=-1, keepdims=True) + eps)
        scaled = value * scale * gains[i : i + 1]
        lows[i][:, at] = (scaled * cosine[...] + pltpu.roll(scaled, head_size // 2, axis=1) * sine[...]).astype(bf)
    probs = head_scores(lows[0][:, at], lows[1][:, at], seg_col[...] == seg_row[...], head_size)
    mixed[:, at] = jnp.dot(probs.astype(bf), values[:, at], preferred_element_type=f32).astype(bf)

def output_part(mixed, weight, part):
    def tile(n, _):
        cols = pl.ds(pl.multiple_of(n * 512, 512), 512)
        total = jnp.dot(mixed[...], weight[:, cols], preferred_element_type=f32)
        part[:, :, cols] = total.astype(bf).reshape(part.shape[0], part.shape[1], -1)
        return 0
    lax.fori_loop(0, part.shape[2] // 512, tile, 0)


HZ, HX, HY, HFX, HFY, HC, HCX, HCY, HCA, HCB, HU, HD = range(12)

def opening_kernel(hidden, gain, wq_hbm, wk_hbm, wv_hbm, out_hbm, gains, cosine, sine, seg_col, seg_row, grad_ref,
                   out_ref, normed, query_proj, key_proj, queries, keys, values, mixed, grads,
                   wq, wk, wv, out_w, part_ref, line, rzu, rzd, send, up_send, recv, local, wload):
    e = lax.axis_index("exp")
    z = lax.axis_index("tp")
    ex, ey, ec, ed = (jnp.bitwise_xor(e, m) for m in (2, 4, 1, 6))
    at_x, at_y, at_c = (ex, z), (ey, z), (ec, z)
    at_up, at_down = (e, z + 1), (e, z - 1)
    middle_plane = (z == 1) | (z == 2)
    quarter = grad_ref.shape[0]
    half = quarter // 2
    TOP, BOT, ALLR = pl.ds(0, half), pl.ds(half, half), pl.ds(0, quarter)

    wcopies = [pltpu.make_async_copy(s, d, wload.at[i]) for i, (s, d) in enumerate(zip((wq_hbm, wk_hbm, wv_hbm, out_hbm), (wq, wk, wv, out_w)))]
    for c in wcopies: c.start()

    bar = pltpu.get_barrier_semaphore()
    for d in (at_x, at_y, at_c):
        pl.semaphore_signal(bar, inc=1, device_id=d, device_id_type=MESH)
    @pl.when(z < 3)
    def _(): pl.semaphore_signal(bar, inc=1, device_id=at_up, device_id_type=MESH)
    @pl.when(z > 0)
    def _(): pl.semaphore_signal(bar, inc=1, device_id=at_down, device_id_type=MESH)
    pl.semaphore_wait(bar, 3 + jnp.where(z < 3, 1, 0) + jnp.where(z > 0, 1, 0))

    def copy(kind, plane, group, part, to, src=None, sem=None):
        place = grads.at[plane, group, part]
        return pltpu.make_async_remote_copy(
            src_ref=place if src is None else src, dst_ref=place,
            send_sem=send.at[kind, plane] if sem is None else sem, recv_sem=recv.at[kind, plane],
            device_id=to, device_id_type=MESH)
    def arrived(kind, plane, place):
        pltpu.make_async_copy(place, place, recv.at[kind, plane]).wait()
    def line_copy(kind, p, landing, to):
        return pltpu.make_async_remote_copy(src_ref=line.at[p], dst_ref=landing.at[p], send_sem=send.at[kind, p],
                                            recv_sem=recv.at[kind, p], device_id=to, device_id_type=MESH)
    def line_up(p): return line_copy(HU, p, rzu, at_up)
    def line_down(p): return line_copy(HD, p, rzd, at_down)
    def up(p, src=None): return copy(HZ, p, e, ALLR, at_up, src, up_send.at[p])
    def down(p, src=None): return copy(HZ, p, e, ALLR, at_down, src)
    def to_x(p, src=None): return copy(HX, p, e, ALLR, at_x, src)
    def to_y(p, src=None): return copy(HY, p, e, ALLR, at_y, src)
    def to_c(p, src=None): return copy(HC, p, e, ALLR, at_c, src)
    def fwd_y(p): return copy(HFY, p, ex, TOP, at_y)
    def fwd_x(p): return copy(HFX, p, ey, BOT, at_x)
    def c_x(p): return copy(HCX, p, ex, ALLR, at_c)
    def c_y(p): return copy(HCY, p, ey, ALLR, at_c)
    def c_a(p): return copy(HCA, p, ed, TOP, at_c)
    def c_b(p): return copy(HCB, p, ed, BOT, at_c)

    def serve_line(k):
        p = plane_at(z, k)
        arrived(HZ, p, grads.at[p, e])
        @pl.when((p < z) & (z < 3))
        def _(): up(p).start()
        @pl.when((p > z) & (z > 0))
        def _(): down(p).start()

    def serve_rows(k):
        p = plane_at(z, k)
        to_x(p).start()
        to_y(p).start()
        to_c(p).start()

    def serve_sides(k):
        p = plane_at(z, k)
        arrived(HX, p, grads.at[p, ex])
        fwd_y(p).start()
        c_x(p).start()
        arrived(HY, p, grads.at[p, ey])
        fwd_x(p).start()
        c_y(p).start()

    def serve_far(k):
        p = plane_at(z, k)
        arrived(HFY, p, grads.at[p, ed, TOP])
        c_a(p).start()
        arrived(HFX, p, grads.at[p, ed, BOT])
        c_b(p).start()

    def line_step(k):
        p = plane_at(z, 3 - k)
        line[p] = part_ref[p]
        @pl.when((z > 0) & (p >= z))
        def _():
            arrived(HU, p, rzu.at[p])
            line[p] = (line[p].astype(f32) + rzu[p].astype(f32)).astype(bf)
        @pl.when((z < 3) & (p <= z))
        def _():
            arrived(HD, p, rzd.at[p])
            line[p] = (line[p].astype(f32) + rzd[p].astype(f32)).astype(bf)
        @pl.when(p > z)
        def _(): line_up(p).start()
        @pl.when(p < z)
        def _(): line_down(p).start()

    def ends(f): pl.when(~middle_plane)(f)
    def mids(f): pl.when(middle_plane)(f)

    def one_head(h):
        head_forward(h, (query_proj, key_proj), gains, cosine, sine, seg_col, seg_row, (queries, keys), values, mixed)

    def own_sum():
        out_ref[...] = part_ref[z].astype(f32)
        @pl.when(z > 0)
        def _():
            arrived(HU, z, rzu.at[z])
            out_ref[...] += rzu[z].astype(f32)
        @pl.when(z < 3)
        def _():
            arrived(HD, z, rzd.at[z])
            out_ref[...] += rzd[z].astype(f32)

    @pl.when(z < 3)
    def _(): up(z, grad_ref).start()
    @pl.when(z > 0)
    def _(): down(z, grad_ref).start()
    to_x(z, grad_ref).start()
    to_y(z, grad_ref).start()
    to_c(z, grad_ref).start()
    own = pltpu.make_async_copy(grad_ref, grads.at[z, e], local)
    own.start()

    norm_rows(hidden, gain, normed)
    for c in wcopies: c.wait()
    project(normed, wq, query_proj)
    project(normed, wk, key_proj)
    project(normed, wv, values)
    serve_line(1)
    serve_rows(1)
    serve_sides(0)
    mids(lambda: serve_line(2))
    one_head(0)
    serve_far(0)
    one_head(1)
    mids(lambda: serve_line(3))
    ends(lambda: serve_line(2))
    serve_rows(2)
    one_head(2)
    serve_sides(1)
    one_head(3)
    output_part(mixed, out_w, part_ref)
    ends(lambda: line_step(0))
    ends(lambda: serve_line(3))
    serve_rows(3)
    serve_far(1)
    mids(lambda: line_step(0))
    ends(lambda: line_step(1))
    serve_sides(2)
    mids(lambda: line_step(1))
    mids(lambda: line_step(2))
    ends(lambda: line_step(2))
    serve_far(2)
    serve_sides(3)
    own_sum()
    serve_far(3)
    own.wait()
    def drain(k, _):
        p = plane_at(z, k)
        @pl.when((z < 3) & (p <= z))
        def _(): up(p).wait_send()
        @pl.when((z > 0) & (p >= z))
        def _(): down(p).wait_send()
        for c in (to_x, to_y, to_c, fwd_y, fwd_x, c_x, c_y, c_a, c_b):
            c(p).wait_send()
        arrived(HC, p, grads.at[p, ec])
        arrived(HCX, p, grads.at[p, jnp.bitwise_xor(ec, 2)])
        arrived(HCY, p, grads.at[p, jnp.bitwise_xor(ec, 4)])
        arrived(HCA, p, grads.at[p, jnp.bitwise_xor(ec, 6), TOP])
        arrived(HCB, p, grads.at[p, jnp.bitwise_xor(ec, 6), BOT])
        return 0
    lax.fori_loop(0, 4, drain, 0)
    def drain_line(p, _):
        @pl.when(p > z)
        def _(): line_up(p).wait_send()
        @pl.when(p < z)
        def _(): line_down(p).wait_send()
        return 0
    lax.fori_loop(0, 4, drain_line, 0)

def open_exchange(hidden, gain, weights, gains, cosine, sine, seg_col, seg_row, grad, collective_id):
    vm = pl.BlockSpec(memory_space=pltpu.VMEM)
    any_ = pl.BlockSpec(memory_space=pl.ANY)
    planes = hidden.shape
    _, quarter, width = planes
    tokens = cosine.shape[0]
    heads = (tokens, weights[0].shape[1])
    return pl.pallas_call(
        opening_kernel,
        out_shape=(
            jax.ShapeDtypeStruct((quarter, width), f32),
            jax.ShapeDtypeStruct((tokens, width), bf),
            jax.ShapeDtypeStruct(heads, f32), jax.ShapeDtypeStruct(heads, f32),
            jax.ShapeDtypeStruct(heads, bf), jax.ShapeDtypeStruct(heads, bf), jax.ShapeDtypeStruct(heads, bf), jax.ShapeDtypeStruct(heads, bf),
            jax.ShapeDtypeStruct((4, 8, quarter, width), bf),
        ),
        in_specs=[vm, vm] + [any_] * 4 + [vm] * 5 + [any_],
        out_specs=(vm,) * 8 + (any_,),
        scratch_shapes=[pltpu.VMEM(w.shape, bf) for w in weights] + [pltpu.VMEM(planes, bf)] * 4 + [
            pltpu.SemaphoreType.DMA((12, 4)), pltpu.SemaphoreType.DMA((4,)), pltpu.SemaphoreType.DMA((12, 4)), pltpu.SemaphoreType.DMA,
            pltpu.SemaphoreType.DMA((4,))],
        compiler_params=pltpu.CompilerParams(collective_id=collective_id, has_side_effects=True, vmem_limit_bytes=56 << 20),
    )(hidden, gain, *weights, gains, cosine, sine, seg_col, seg_row, grad)


def input_product(acts, weights, cols):
    wg, wu = weights
    hid = wg.shape[2]
    total = None
    for j in range(wg.shape[0]):
        for w, i in ((wg, 0), (wu, 1)):
            lhs = acts[:, :, (2 * j + i) * hid:(2 * j + i + 1) * hid].reshape(-1, hid)
            part = lax.dot_general(lhs, w[j, cols, :], NT, preferred_element_type=f32)
            total = part if total is None else total + part
    return total

def output_product(acts, weights, cols):
    (wd,) = weights
    hid = wd.shape[1]
    total = None
    for j in range(wd.shape[0]):
        lhs = acts[:, :, j * hid:(j + 1) * hid].reshape(-1, hid)
        part = jnp.dot(lhs, wd[j, :, cols], preferred_element_type=f32)
        total = part if total is None else total + part
    return total

C1, DT, DB, XT, XB, YT, YB, ZU, ZD, OU, OD = range(11)

def scatter_kernel(product, n_weights, width, cols, score_at, carry, *refs):
    act_hbm, *rest = refs
    w_hbm, rest = rest[:n_weights], rest[n_weights:]
    if carry:
        row_ref, out_w, mixed, queries, keys, values, query_proj, key_proj, gains, cosine, sine, seg_col, seg_row, *rest = rest
        projected = (query_proj, key_proj)
        out_ref, grad_heads, grad_out_w, grad_gains, acts, *rest = rest
        *rest, rows, grad_mixed = rest
    else:
        out_ref, acts, *rest = rest
    weights, rest = rest[:n_weights], rest[n_weights:]
    sendbuf, acc, r1, rdt, rdb, rx, ry, rzu, rzd, send, recv, load, wload = rest
    e = lax.axis_index("exp")
    z = lax.axis_index("tp")
    quarter = acc.shape[2]
    half = quarter // 2
    chip = e // 2
    core = lax.rem(e, 2)
    chip_x, chip_y, chip_d = (jnp.bitwise_xor(chip, m) for m in (1, 2, 3))
    at_x, at_y, at_c = (jnp.bitwise_xor(e, 2), z), (jnp.bitwise_xor(e, 4), z), (jnp.bitwise_xor(e, 1), z)
    at_up, at_down = (e, z + 1), (e, z - 1)
    TOP, BOT = pl.ds(0, half), pl.ds(half, half)

    wcopies = [pltpu.make_async_copy(s, d, wload.at[i]) for i, (s, d) in enumerate(zip(w_hbm, weights))]
    for c in wcopies: c.start()

    def act_copy(n):
        k, own = n // 2, n % 2
        which = jnp.bitwise_xor(core, 1 - own)
        return pltpu.make_async_copy(act_hbm.at[:, which, plane_at(z, 3 - k), :, cols], acts.at[own], load.at[own])
    act_copy(0).start()

    bar = pltpu.get_barrier_semaphore()
    for d in (at_x, at_y, at_c):
        pl.semaphore_signal(bar, inc=1, device_id=d, device_id_type=MESH)
    @pl.when(z < 3)
    def _(): pl.semaphore_signal(bar, inc=1, device_id=at_up, device_id_type=MESH)
    @pl.when(z > 0)
    def _(): pl.semaphore_signal(bar, inc=1, device_id=at_down, device_id_type=MESH)
    pl.semaphore_wait(bar, 3 + jnp.where(z < 3, 1, 0) + jnp.where(z > 0, 1, 0))
    for c in wcopies: c.wait()

    def remote(kind, k, src, dst, to):
        return pltpu.make_async_remote_copy(src_ref=src, dst_ref=dst, send_sem=send.at[kind, k], recv_sem=recv.at[kind, k],
                                            device_id=to, device_id_type=MESH)
    def to_core(k): return remote(C1, k, sendbuf.at[k % 2], r1.at[k], at_c)
    def far_x(k): return remote(DT, k, acc.at[k, chip_d, TOP], rdt.at[k], at_x)
    def far_y(k): return remote(DB, k, acc.at[k, chip_d, BOT], rdb.at[k], at_y)
    def x_top(k): return remote(XT, k, acc.at[k, chip_x, TOP], rx.at[k, TOP], at_x)
    def x_bot(k): return remote(XB, k, acc.at[k, chip_x, BOT], rx.at[k, BOT], at_x)
    def y_top(k): return remote(YT, k, acc.at[k, chip_y, TOP], ry.at[k, TOP], at_y)
    def y_bot(k): return remote(YB, k, acc.at[k, chip_y, BOT], ry.at[k, BOT], at_y)
    def line_up(k, p): return remote(ZU, p, acc.at[k, chip], rzu.at[p], at_up)
    def line_down(k, p): return remote(ZD, p, acc.at[k, chip], rzd.at[p], at_down)
    def arrived(kind, k, place):
        pltpu.make_async_copy(place, place, recv.at[kind, k]).wait()
    def row_up(p): return remote(OU, p, rows.at[p], rows.at[p], at_up)
    def row_down(p): return remote(OD, p, rows.at[p], rows.at[p], at_down)
    def row_step(k):
        p = plane_at(z, k)
        @pl.when(p < z)
        def _(): arrived(OU, p, rows.at[p])
        @pl.when(p > z)
        def _(): arrived(OD, p, rows.at[p])
        @pl.when((p <= z) & (z < 3))
        def _(): row_up(p).start()
        @pl.when((p >= z) & (z > 0))
        def _(): row_down(p).start()
    if carry:
        rows[z] = row_ref[...]
        row_step(0)

    cols_step = 512
    def multiply(slot, target):
        def tile(n, _):
            cols = pl.ds(pl.multiple_of(n * cols_step, cols_step), cols_step)
            total = product(acts.at[slot], weights, cols)
            target[:, :, cols] = total.astype(bf).reshape(4, quarter, cols_step)
            return 0
        lax.fori_loop(0, width // cols_step, tile, 0)
        if score_at is not None:
            lanes = target.shape[2] - width
            target[:, :, width:] = acts[slot, :, :, score_at:score_at + lanes] + acts[slot, :, :, score_at + lanes:score_at + 2 * lanes]

    def add(place, other):
        place[...] = (place[...].astype(f32) + other[...].astype(f32)).astype(bf)

    def begin(k):
        act_copy(2 * k).wait()
        act_copy(2 * k + 1).start()
        if k >= 2:
            to_core(k - 2).wait_send()
        multiply(0, sendbuf.at[k % 2])
        to_core(k).start()
        act_copy(2 * k + 1).wait()
        if k < 3:
            act_copy(2 * k + 2).start()
        multiply(1, acc.at[k])
        arrived(C1, k, r1.at[k])
        add(acc.at[k, chip_d], r1.at[k, chip_d])
        far_x(k).start()
        far_y(k).start()
        add(acc.at[k, chip_x], r1.at[k, chip_x])
        x_top(k).start()
        add(acc.at[k, chip_y], r1.at[k, chip_y])
        y_bot(k).start()
        add(acc.at[k, chip], r1.at[k, chip])

    def middle(k):
        arrived(DB, k, rdb.at[k])
        add(acc.at[k, chip_x, BOT], rdb.at[k])
        x_bot(k).start()
        arrived(DT, k, rdt.at[k])
        add(acc.at[k, chip_y, TOP], rdt.at[k])
        y_top(k).start()

    def finish(k):
        p = plane_at(z, 3 - k)
        arrived(XT, k, rx.at[k, TOP])
        arrived(YB, k, ry.at[k, BOT])
        arrived(XB, k, rx.at[k, BOT])
        arrived(YT, k, ry.at[k, TOP])
        total = acc[k, chip].astype(f32) + rx[k].astype(f32) + ry[k].astype(f32)
        out_ref[...] = total
        @pl.when((z > 0) & (p >= z))
        def _():
            arrived(ZU, p, rzu.at[p])
            out_ref[...] += rzu[p].astype(f32)
        @pl.when((z < 3) & (p <= z))
        def _():
            arrived(ZD, p, rzd.at[p])
            out_ref[...] += rzd[p].astype(f32)
        @pl.when(p != z)
        def _():
            acc[k, chip] = out_ref[...].astype(bf)
        @pl.when(p > z)
        def _(): line_up(k, p).start()
        @pl.when(p < z)
        def _(): line_down(k, p).start()

    def one_head(h):
        head_back(h, queries, keys, values, projected, gains, cosine, sine, seg_col, seg_row, grad_mixed, grad_heads, grad_gains)

    def ends(f):
        pl.when((z == 0) | (z == 3))(f)
    def mids(f):
        pl.when((z == 1) | (z == 2))(f)

    if carry:
        grad_gains[...] = jnp.zeros(grad_gains.shape, f32)
        begin(0)
        row_step(1)
        begin(1)
        middle(0)
        row_step(2)
        begin(2)
        middle(1)
        row_step(3)
        ends(lambda: finish(0))
        begin(3)
        mixed_back(rows, out_w, mixed, grad_mixed, grad_out_w)
        middle(2)
        one_head(0)
        mids(lambda: finish(0))
        ends(lambda: finish(1))
        one_head(1)
        middle(3)
        mids(lambda: finish(1))
        one_head(2)
        finish(2)
        one_head(3)
        finish(3)
    else:
        begin(0)
        begin(1)
        middle(0)
        begin(2)
        middle(1)
        ends(lambda: finish(0))
        begin(3)
        middle(2)
        mids(lambda: finish(0))
        ends(lambda: finish(1))
        middle(3)
        mids(lambda: finish(1))
        finish(2)
        finish(3)

    for k in (2, 3):
        to_core(k).wait_send()
    def drain(k, _):
        p = plane_at(z, 3 - k)
        for c in (far_x, far_y, x_top, x_bot, y_top, y_bot):
            c(k).wait_send()
        @pl.when(p > z)
        def _(): line_up(k, p).wait_send()
        @pl.when(p < z)
        def _(): line_down(k, p).wait_send()
        if carry:
            @pl.when((p <= z) & (z < 3))
            def _(): row_up(p).wait_send()
            @pl.when((p >= z) & (z > 0))
            def _(): row_down(p).wait_send()
        return 0
    lax.fori_loop(0, 4, drain, 0)

def scatter_sums(act, weights, scores, collective_id, attention=()):
    hid = min(weights[0].shape[1:])
    width = max(weights[0].shape[1:])
    n_here = weights[0].shape[0]
    quarter, cols = act.shape[3:]
    score_at = 3 * hid * n_here
    lanes = (cols - score_at) // n_here
    wide = width + (lanes if scores else 0)
    taken = pl.ds(0, cols) if scores else pl.ds(2 * hid * n_here, hid * n_here)
    product = input_product if scores else output_product
    any_ = pl.BlockSpec(memory_space=pl.ANY)
    vm = pl.BlockSpec(memory_space=pltpu.VMEM)
    n = len(weights)
    out_shape = (jax.ShapeDtypeStruct((quarter, wide), f32),)
    extra = []
    if attention:
        heads, head_size = attention[2].shape, attention[8].shape[1]
        out_shape += (
            jax.ShapeDtypeStruct((3,) + heads, bf),
            jax.ShapeDtypeStruct(attention[1].shape, bf),
            jax.ShapeDtypeStruct((2, head_size), f32),
        )
        extra = [pltpu.VMEM((4, quarter, width), bf), pltpu.VMEM(heads, bf)]
    return pl.pallas_call(
        functools.partial(scatter_kernel, product, n, width, taken, score_at if scores else None, bool(attention)),
        out_shape=out_shape,
        in_specs=[any_] * (1 + n) + [vm] * len(attention),
        out_specs=(vm,) * len(out_shape),
        scratch_shapes=[pltpu.VMEM((2, 4, quarter, taken.size), bf)] + [pltpu.VMEM(w.shape, bf) for w in weights] + [
            pltpu.VMEM((2, 4, quarter, wide), bf),
            pltpu.VMEM((4, 4, quarter, wide), bf),
            pltpu.VMEM((4, 4, quarter, wide), bf),
            pltpu.VMEM((4, quarter // 2, wide), bf), pltpu.VMEM((4, quarter // 2, wide), bf),
            pltpu.VMEM((4, quarter, wide), bf), pltpu.VMEM((4, quarter, wide), bf),
            pltpu.VMEM((4, quarter, wide), bf), pltpu.VMEM((4, quarter, wide), bf),
            pltpu.SemaphoreType.DMA((11, 4)), pltpu.SemaphoreType.DMA((11, 4)),
            pltpu.SemaphoreType.DMA((2,)), pltpu.SemaphoreType.DMA((n,)),
        ] + extra,
        compiler_params=pltpu.CompilerParams(collective_id=collective_id, has_side_effects=True, vmem_limit_bytes=62 << 20),
    )(act, *weights, *attention)


(SC, SDT, SDB, SXT, SXB, SYT, SYB, GX, GY, GFX, GFY, GC, GCX, GCY, GCA, GCB, LU, LD, RU, RD) = range(20)

def totals_kernel(*refs):
    grad_heads, normed_ref, proj_w, grad_out_w, refs = refs[0], refs[1], refs[2:5], refs[5], refs[6:]
    router_ref, ffn_ref, heads_ref, hidden_ref, resid_ref, gain_ref, refs = *refs[:6], refs[6:]
    res, rows, small_out, refs = refs[:4], refs[4], refs[5], refs[6:]
    w_ref, refs = (grad_out_w, *refs[:3]), refs[3:]
    r1, acc, rdt, rdb, rx, ry, refs = *(refs[4 * i : 4 * i + 4] for i in range(6)), refs[24:]
    part_ref, rzu, rzd, line, sums, got, send, recv, ssend, srecv = refs
    e = lax.axis_index("exp")
    z = lax.axis_index("tp")
    chip, core = e // 2, lax.rem(e, 2)
    cx, cy, cd = (jnp.bitwise_xor(chip, m) for m in (1, 2, 3))
    at_x, at_y, at_c = (jnp.bitwise_xor(e, 2), z), (jnp.bitwise_xor(e, 4), z), (jnp.bitwise_xor(e, 1), z)
    at_up, at_down = (e, z + 1), (e, z - 1)
    partners = (at_c, at_x, at_y, (e, jnp.bitwise_xor(z, 1)), (e, jnp.bitwise_xor(z, 2)))
    middle_plane = (z == 1) | (z == 2)
    halves = [ref.shape[1] // 2 for ref in acc]
    TOP, BOT = [pl.ds(0, h) for h in halves], [pl.ds(h, h) for h in halves]

    bar = pltpu.get_barrier_semaphore()
    for d in (at_x, at_y, at_c, (e, jnp.bitwise_xor(z, 2))):
        pl.semaphore_signal(bar, inc=1, device_id=d, device_id_type=MESH)
    @pl.when(z < 3)
    def _(): pl.semaphore_signal(bar, inc=1, device_id=at_up, device_id_type=MESH)
    @pl.when(z > 0)
    def _(): pl.semaphore_signal(bar, inc=1, device_id=at_down, device_id_type=MESH)
    pl.semaphore_wait(bar, 4 + jnp.where(z < 3, 1, 0) + jnp.where(z > 0, 1, 0))

    def remote(kind, k, src, dst, to):
        return pltpu.make_async_remote_copy(src_ref=src, dst_ref=dst, send_sem=send.at[kind, k], recv_sem=recv.at[kind, k],
                                            device_id=to, device_id_type=MESH)
    def arrived(kind, k, place):
        pltpu.make_async_copy(place, place, recv.at[kind, k]).wait()
    def to_core(k): return remote(SC, k, w_ref[k].at[1 - core], r1[k], at_c)
    def far_x(k): return remote(SDT, k, acc[k].at[cd, TOP[k]], rdt[k], at_x)
    def far_y(k): return remote(SDB, k, acc[k].at[cd, BOT[k]], rdb[k], at_y)
    def x_top(k): return remote(SXT, k, acc[k].at[cx, TOP[k]], rx[k].at[TOP[k]], at_x)
    def x_bot(k): return remote(SXB, k, acc[k].at[cx, BOT[k]], rx[k].at[BOT[k]], at_x)
    def y_top(k): return remote(SYT, k, acc[k].at[cy, TOP[k]], ry[k].at[TOP[k]], at_y)
    def y_bot(k): return remote(SYB, k, acc[k].at[cy, BOT[k]], ry[k].at[BOT[k]], at_y)
    def same(kind, k, place, to): return remote(kind, k, place, place, to)
    def give_x(k): return same(GX, k, res[k].at[core, chip], at_x)
    def give_y(k): return same(GY, k, res[k].at[core, chip], at_y)
    def give_c(k): return same(GC, k, res[k].at[core, chip], at_c)
    def pass_y(k): return same(GFY, k, res[k].at[core, cx, TOP[k]], at_y)
    def pass_x(k): return same(GFX, k, res[k].at[core, cy, BOT[k]], at_x)
    def c_x(k): return same(GCX, k, res[k].at[core, cx], at_c)
    def c_y(k): return same(GCY, k, res[k].at[core, cy], at_c)
    def c_a(k): return same(GCA, k, res[k].at[core, cd, TOP[k]], at_c)
    def c_b(k): return same(GCB, k, res[k].at[core, cd, BOT[k]], at_c)
    def line_up(p): return remote(LU, p, line.at[p], rzu.at[p], at_up)
    def line_down(p): return remote(LD, p, line.at[p], rzd.at[p], at_down)
    def row_up(p): return same(RU, p, rows.at[p], at_up)
    def row_down(p): return same(RD, p, rows.at[p], at_down)

    def plus(a, b): return (a.astype(f32) + b.astype(f32)).astype(bf)

    def input_part():
        def tile(n, _):
            input_back(proj_w, grad_heads, part_ref, pl.ds(pl.multiple_of(n * 512, 512), 512))
            return 0
        lax.fori_loop(0, part_ref.shape[2] // 512, tile, 0)

    def weight_part(k):
        part = lax.dot_general(normed_ref[...], grad_heads[k - 1], TN, preferred_element_type=f32)
        w_ref[k][...] = part.astype(bf).reshape(w_ref[k].shape)
        to_core(k).start()

    def begin(k):
        arrived(SC, k, r1[k])
        acc[k][cd] = plus(w_ref[k][core, cd], r1[k][cd])
        far_x(k).start()
        far_y(k).start()
        acc[k][cx] = plus(w_ref[k][core, cx], r1[k][cx])
        x_top(k).start()
        acc[k][cy] = plus(w_ref[k][core, cy], r1[k][cy])
        y_bot(k).start()
        acc[k][chip] = plus(w_ref[k][core, chip], r1[k][chip])

    def middle(k):
        arrived(SDB, k, rdb[k])
        acc[k][cx, BOT[k]] = plus(acc[k][cx, BOT[k]], rdb[k][...])
        x_bot(k).start()
        arrived(SDT, k, rdt[k])
        acc[k][cy, TOP[k]] = plus(acc[k][cy, TOP[k]], rdt[k][...])
        y_top(k).start()

    def finish(k):
        arrived(SXT, k, rx[k].at[TOP[k]])
        arrived(SYB, k, ry[k].at[BOT[k]])
        arrived(SXB, k, rx[k].at[BOT[k]])
        arrived(SYT, k, ry[k].at[TOP[k]])
        res[k][core, chip] = (acc[k][chip].astype(f32) + rx[k][...].astype(f32) + ry[k][...].astype(f32)).astype(bf)
        give_x(k).start()
        give_y(k).start()
        give_c(k).start()

    def spread(k):
        arrived(GX, k, res[k].at[core, cx])
        pass_y(k).start()
        c_x(k).start()
        arrived(GY, k, res[k].at[core, cy])
        pass_x(k).start()
        c_y(k).start()

    def last(k):
        arrived(GFY, k, res[k].at[core, cd, TOP[k]])
        c_a(k).start()
        arrived(GFX, k, res[k].at[core, cd, BOT[k]])
        c_b(k).start()

    def line_step(k):
        p = plane_at(z, 3 - k)
        line[p] = part_ref[p]
        @pl.when((z > 0) & (p >= z))
        def _():
            arrived(LU, p, rzu.at[p])
            line[p] = plus(line[p], rzu[p])
        @pl.when((z < 3) & (p <= z))
        def _():
            arrived(LD, p, rzd.at[p])
            line[p] = plus(line[p], rzd[p])
        @pl.when(p > z)
        def _(): line_up(p).start()
        @pl.when(p < z)
        def _(): line_down(p).start()

    def unit_rows(p):
        value = hidden_ref[p].astype(f32)
        scale = lax.rsqrt(jnp.mean(value * value, axis=-1, keepdims=True) + eps)
        return scale, value * scale

    def gain_row():
        sums[0, 0:8] = jnp.zeros((8, sums.shape[2]), f32)
        sums[0, 1:2] = ffn_ref[...]
        head_size = heads_ref.shape[1]
        sums[0, 2:3, 0:head_size] = heads_ref[0:1]
        sums[0, 2:3, head_size : 2 * head_size] = heads_ref[1:2]
        sums[0, 8:] = router_ref[...]
        def add_plane(p, _):
            sums[0, 0:1] += jnp.sum(part_ref[p].astype(f32) * unit_rows(p)[1], axis=0, keepdims=True)
            return 0
        lax.fori_loop(0, 4, add_plane, 0)
        small_copy(0).start()

    def own_rows():
        total = part_ref[z].astype(f32)
        @pl.when(z > 0)
        def _(): arrived(LU, z, rzu.at[z])
        @pl.when(z < 3)
        def _(): arrived(LD, z, rzd.at[z])
        total = total + jnp.where(z > 0, rzu[z].astype(f32), 0.0) + jnp.where(z < 3, rzd[z].astype(f32), 0.0)
        scale, unit = unit_rows(z)
        scaled = total * gain_ref[...]
        grad = scale * (scaled - unit * jnp.mean(unit * scaled, axis=-1, keepdims=True))
        rows[z] = (resid_ref[...] + grad).astype(bf)
        @pl.when(z < 3)
        def _(): row_up(z).start()
        @pl.when(z > 0)
        def _(): row_down(z).start()

    def row_step(k):
        p = plane_at(z, k)
        @pl.when(p < z)
        def _(): arrived(RU, p, rows.at[p])
        @pl.when(p > z)
        def _(): arrived(RD, p, rows.at[p])
        @pl.when((p < z) & (z < 3))
        def _(): row_up(p).start()
        @pl.when((p > z) & (z > 0))
        def _(): row_down(p).start()

    def small_copy(i):
        return pltpu.make_async_remote_copy(src_ref=sums.at[i], dst_ref=got.at[i], send_sem=ssend.at[i], recv_sem=srecv.at[i],
                                            device_id=partners[i], device_id_type=MESH)
    def small_step(i):
        small_copy(i).wait_recv()
        if i < 4:
            sums[i + 1] = sums[i] + got[i]
            small_copy(i + 1).start()
        else:
            small_out[...] = sums[i] + got[i]

    def ends(f):
        pl.when(~middle_plane)(f)
    def mids(f):
        pl.when(middle_plane)(f)

    to_core(0).start()
    input_part()
    ends(lambda: line_step(0))
    weight_part(1)
    begin(0)
    weight_part(2)
    begin(1)
    weight_part(3)
    begin(2)
    gain_row()
    begin(3)
    mids(lambda: line_step(0))
    ends(lambda: line_step(1))
    small_step(0)
    middle(0)
    middle(1)
    mids(lambda: line_step(1))
    mids(lambda: line_step(2))
    ends(lambda: line_step(2))
    middle(2)
    middle(3)
    small_step(1)
    own_rows()
    finish(0)
    finish(1)
    finish(2)
    finish(3)
    ends(lambda: row_step(1))
    mids(lambda: row_step(1))
    mids(lambda: row_step(2))
    spread(0)
    spread(1)
    small_step(2)
    mids(lambda: row_step(3))
    ends(lambda: row_step(2))
    spread(2)
    spread(3)
    last(0)
    small_step(3)
    ends(lambda: row_step(3))
    last(1)
    last(2)
    small_step(4)
    last(3)

    sib = 1 - core
    for k in range(4):
        for c in (to_core, far_x, far_y, x_top, x_bot, y_top, y_bot, give_x, give_y, give_c, pass_x, pass_y, c_x, c_y, c_a, c_b):
            c(k).wait_send()
        arrived(GC, k, res[k].at[sib, chip])
        arrived(GCX, k, res[k].at[sib, cx])
        arrived(GCY, k, res[k].at[sib, cy])
        arrived(GCA, k, res[k].at[sib, cd, TOP[k]])
        arrived(GCB, k, res[k].at[sib, cd, BOT[k]])
    def drain(p, _):
        @pl.when(p > z)
        def _(): line_up(p).wait_send()
        @pl.when(p < z)
        def _(): line_down(p).wait_send()
        @pl.when((z < 3) & (p <= z))
        def _(): row_up(p).wait_send()
        @pl.when((z > 0) & (p >= z))
        def _(): row_down(p).wait_send()
        return 0
    lax.fori_loop(0, 4, drain, 0)
    for i in range(5): small_copy(i).wait_send()

def final_totals(grad_heads, normed, proj_w, grad_out_w, router, ffn, heads, hidden, resid, gain, collective_id):
    vm = pl.BlockSpec(memory_space=pltpu.VMEM)
    planes = hidden.shape
    one = (2, 4, proj_w[0].shape[0] // 8, proj_w[0].shape[1])
    shapes = (grad_out_w.shape, one, one, one)
    small = (5, 8 + router.shape[0], router.shape[1])
    own = [pltpu.VMEM(one, bf)] * 3
    whole = [pltpu.VMEM(s[1:], bf) for s in shapes]
    quarter = [pltpu.VMEM(s[2:], bf) for s in shapes]
    half = [pltpu.VMEM((s[2] // 2, s[3]), bf) for s in shapes]
    return pl.pallas_call(
        totals_kernel,
        out_shape=tuple(jax.ShapeDtypeStruct(s, bf) for s in shapes) + (
            jax.ShapeDtypeStruct(planes, bf), jax.ShapeDtypeStruct(small[1:], f32)),
        in_specs=[vm] * 12,
        out_specs=(vm,) * 6,
        scratch_shapes=own + whole + whole + half + half + quarter + quarter + [
            pltpu.VMEM(planes, bf), pltpu.VMEM(planes, bf), pltpu.VMEM(planes, bf), pltpu.VMEM(planes, bf),
            pltpu.VMEM(small, f32), pltpu.VMEM(small, f32),
            pltpu.SemaphoreType.DMA((20, 4)), pltpu.SemaphoreType.DMA((20, 4)),
            pltpu.SemaphoreType.DMA((5,)), pltpu.SemaphoreType.DMA((5,)),
        ],
        compiler_params=pltpu.CompilerParams(collective_id=collective_id, has_side_effects=True, vmem_limit_bytes=62 << 20),
    )(grad_heads, normed, *proj_w, grad_out_w, router, ffn, heads, hidden, resid, gain)


def slot_experts(routed_low, gates, picked, grad_out, expert_routes, gate_weight, up_weight, down_weight):
    highest = lax.Precision.HIGHEST
    quarter, width = grad_out.shape
    top_count = expert_routes.shape[1]
    experts = picked.shape[2]
    capacity = max(2, 2 * quarter * top_count // experts)
    picked_wide = picked.astype(jnp.float32)
    grad_rows = grad_out.astype(jnp.float32)
    flat_route = expert_routes.reshape(-1)
    flat_pick = picked.reshape(-1, experts).astype(jnp.int32)
    rank = jnp.sum((jnp.cumsum(flat_pick, axis=0) - 1) * flat_pick, axis=1)
    place = flat_route * capacity + rank
    row_token = jnp.arange(quarter * top_count, dtype=jnp.int32) // top_count
    send_rows = (
        jnp.zeros((experts * capacity, width), jnp.bfloat16).at[place].set(routed_low[row_token])
    )
    arrived = lax.all_to_all(
        send_rows.reshape(experts, capacity, width), "exp", split_axis=0, concat_axis=1, tiled=True
    )
    rows_used = lax.all_gather(arrived, "tp", axis=1, tiled=True)
    gate_act = jnp.einsum(
        "erd,edf->erf", rows_used, gate_weight, preferred_element_type=jnp.float32
    )
    up_act = jnp.einsum("erd,edf->erf", rows_used, up_weight, preferred_element_type=jnp.float32)
    hidden_low = (jax.nn.silu(gate_act) * up_act).astype(jnp.bfloat16)
    partial_out = jnp.einsum(
        "erf,efd->erd", hidden_low, down_weight, preferred_element_type=jnp.float32
    )
    expert_out = lax.psum_scatter(partial_out, "tp", scatter_dimension=1, tiled=True)
    returned = lax.all_to_all(
        expert_out.astype(jnp.bfloat16), "exp", split_axis=1, concat_axis=0, tiled=True
    )
    back_rows = (
        returned.reshape(experts * capacity, width)[place]
        .reshape(quarter, top_count, width)
        .astype(jnp.float32)
    )
    moe = jnp.einsum("tk,tkd->td", gates, back_rows, precision=highest)
    grad_gates = jnp.einsum("tkd,td->tk", back_rows, grad_rows, precision=highest)
    grad_chosen = gates * (grad_gates - jnp.sum(gates * grad_gates, axis=-1, keepdims=True))
    grad_logits = jnp.einsum("tke,tk->te", picked_wide, grad_chosen, precision=highest)
    weighted_grad = (
        (gates[:, :, None] * grad_rows[:, None, :])
        .astype(jnp.bfloat16)
        .reshape(quarter * top_count, width)
    )
    send_grads = jnp.zeros((experts * capacity, width), jnp.bfloat16).at[place].set(weighted_grad)
    grad_arrived = lax.all_to_all(
        send_grads.reshape(experts, capacity, width), "exp", split_axis=0, concat_axis=1, tiled=True
    )
    sigmoid_gate = jax.nn.sigmoid(gate_act)
    silu_gate = gate_act * sigmoid_gate
    slope = sigmoid_gate * (1.0 + gate_act * (1.0 - sigmoid_gate))
    grad_used = lax.all_gather(grad_arrived, "tp", axis=1, tiled=True)
    grad_hid = jnp.einsum(
        "erd,efd->erf", grad_used, down_weight, preferred_element_type=jnp.float32
    )
    grad_down = jnp.einsum(
        "erf,erd->efd", hidden_low, grad_used, preferred_element_type=jnp.float32
    )
    grad_gate = (grad_hid * up_act * slope).astype(jnp.bfloat16)
    grad_up = (grad_hid * silu_gate).astype(jnp.bfloat16)
    grad_gate_w = jnp.einsum(
        "erd,erf->edf", rows_used, grad_gate, preferred_element_type=jnp.float32
    )
    grad_up_w = jnp.einsum("erd,erf->edf", rows_used, grad_up, preferred_element_type=jnp.float32)
    input_part = jnp.einsum(
        "erf,edf->erd", grad_gate, gate_weight, preferred_element_type=jnp.float32
    ) + jnp.einsum("erf,edf->erd", grad_up, up_weight, preferred_element_type=jnp.float32)
    grad_input = lax.psum_scatter(input_part, "tp", scatter_dimension=1, tiled=True).astype(
        jnp.bfloat16
    )
    grad_back = lax.all_to_all(grad_input, "exp", split_axis=1, concat_axis=0, tiled=True)
    expert_grad = jnp.sum(
        grad_back.reshape(experts * capacity, width)[place]
        .reshape(quarter, top_count, width)
        .astype(jnp.float32),
        axis=1,
    )
    return moe, grad_logits, expert_grad, grad_gate_w, grad_up_w, grad_down


def gate_pair(dense_gates):
    pad = ((0, 0), (0, gate_lanes // 2 - dense_gates.shape[1]))
    high = dense_gates.astype(bf)
    low = (dense_gates - high.astype(f32)).astype(bf)
    return [jnp.pad(high, pad), jnp.pad(low, pad)]


def per_device(
    fits,
    hidden_in,
    attn_gain,
    query_weight,
    key_weight,
    value_weight,
    qnorm_gain,
    knorm_gain,
    out_weight,
    ffn_gain,
    router_weight,
    gate_weight,
    up_weight,
    down_weight,
    expert_routes,
    seq_lengths,
    grad_out,
):
    highest = lax.Precision.HIGHEST
    group_rows = hidden_in.shape[0]
    width = hidden_in.shape[1]
    head_size = qnorm_gain.shape[0]
    quarter = grad_out.shape[0]
    experts = router_weight.shape[1]
    tp_index = lax.axis_index("tp")
    widened = hidden_in.astype(jnp.float32)
    segment, cosine, sine = rotary_tables(seq_lengths[0], group_rows, head_size)
    if fits:
        planes = (4, quarter, width)
        gains = jnp.stack([qnorm_gain, knorm_gain])
        tables = (
            jnp.concatenate([cosine[:, 0], cosine[:, 0]], axis=1),
            jnp.concatenate([-sine[:, 0], sine[:, 0]], axis=1),
            segment[:, None],
            segment[None],
        )
        attn_rows, normed_low, query_proj, key_proj, *heads, mixed_low, grads_all = open_exchange(
            hidden_in.reshape(planes),
            attn_gain[None],
            (query_weight, key_weight, value_weight, out_weight),
            gains,
            *tables,
            grad_out,
            5,
        )
    else:
        normed_one = rms_norm(widened, attn_gain)
        normed_low = normed_one.astype(jnp.bfloat16)
        same_seq = segment[:, None] == segment[None, :]

        def prepare(projected, gain):
            return head_prep(projected, gain, cosine, sine)

        query_proj = jnp.dot(normed_low, query_weight, preferred_element_type=jnp.float32)
        key_proj = jnp.dot(normed_low, key_weight, preferred_element_type=jnp.float32)
        value_proj = jnp.dot(normed_low, value_weight, preferred_element_type=jnp.float32)
        queries, query_back = jax.vjp(prepare, query_proj, qnorm_gain)
        keys, key_back = jax.vjp(prepare, key_proj, knorm_gain)
        query_low = queries.astype(jnp.bfloat16)
        key_low = keys.astype(jnp.bfloat16)
        value_low = value_proj.astype(jnp.bfloat16).reshape(group_rows, -1, head_size)
        scores = masked_scores(query_low, key_low, same_seq, head_size)
        top_score = jnp.max(scores, axis=-1, keepdims=True)
        log_total = top_score + jnp.log(jnp.sum(jnp.exp(scores - top_score), axis=-1, keepdims=True))
        probs_low = jnp.exp(scores - log_total).astype(jnp.bfloat16)
        mixed = jnp.einsum("hts,shd->thd", probs_low, value_low, preferred_element_type=jnp.float32)
        mixed_low = mixed.astype(jnp.bfloat16).reshape(group_rows, -1)
        attn_part = jnp.dot(mixed_low, out_weight, preferred_element_type=jnp.float32)
        attn_rows = lax.psum_scatter(attn_part, "tp", scatter_dimension=0, tiled=True)
    own_rows = lax.dynamic_slice_in_dim(widened, tp_index * quarter, quarter, 0)
    resid = own_rows + attn_rows
    normed_two, norm_two_back = jax.vjp(rms_norm, resid, ffn_gain)
    routed_low = normed_two.astype(jnp.bfloat16)
    logits = jnp.dot(routed_low, router_weight, preferred_element_type=jnp.float32)
    picked = expert_routes[:, :, None] == jnp.arange(experts, dtype=jnp.int32)[None, None, :]
    picked_wide = picked.astype(jnp.float32)
    chosen = jnp.einsum("tke,te->tk", picked_wide, logits, precision=highest)
    gates = jax.nn.softmax(chosen, axis=-1)
    grad_rows = grad_out.astype(jnp.float32)
    if fits:
        dense_gates = jnp.einsum("tke,tk->te", picked_wide, gates, precision=highest)
        act, grad_gate_w, grad_up_w, grad_down = gather_experts(
            jnp.concatenate([routed_low] + gate_pair(dense_gates), axis=1),
            grads_all,
            gate_weight,
            up_weight,
            down_weight,
        )
        (sums,) = scatter_sums(act, (gate_weight, up_weight), True, 2)
        expert_grad = sums[:, :width]
        grad_gates = sums[:, width : width + experts]
        grad_logits = dense_gates * (
            grad_gates - jnp.sum(dense_gates * grad_gates, axis=-1, keepdims=True)
        )
    else:
        moe, grad_logits, expert_grad, grad_gate_w, grad_up_w, grad_down = slot_experts(
            routed_low,
            gates,
            picked,
            grad_out,
            expert_routes,
            gate_weight,
            up_weight,
            down_weight,
        )
    grad_normed = (
        jnp.dot(grad_logits, router_weight.astype(jnp.float32).T, precision=highest) + expert_grad
    )
    grad_router = jnp.dot(routed_low.astype(jnp.float32).T, grad_logits, precision=highest)
    grad_resid, grad_ffn_gain = norm_two_back(grad_normed)
    grad_resid = grad_resid + grad_rows
    grad_low = grad_resid.astype(jnp.bfloat16)
    if fits:
        moe, grad_heads, grad_out_w, grad_gains = scatter_sums(
            act,
            (down_weight,),
            False,
            3,
            (
                grad_low,
                out_weight,
                mixed_low,
                *heads,
                query_proj,
                key_proj,
                gains,
                *tables,
            ),
        )
        grad_out_sum, *sums, grad_input_rows, small = final_totals(
            grad_heads,
            normed_low,
            (query_weight, key_weight, value_weight),
            grad_out_w.reshape(2, 4, -1, width),
            grad_router.T,
            grad_ffn_gain[None],
            grad_gains,
            hidden_in.reshape(planes),
            grad_resid,
            attn_gain[None],
            4,
        )
        grad_input_rows = grad_input_rows.reshape(group_rows, width)
        totals = tuple(
            part.reshape(-1, part.shape[3]).astype(f32) for part in (*sums, grad_out_sum)
        ) + (
            small[0],
            small[2, :head_size],
            small[2, head_size : 2 * head_size],
            small[1],
            small[8:].T,
        )
    else:
        grad_attn_low = lax.all_gather(grad_low, "tp", axis=0, tiled=True)
        grad_out_weight = jnp.dot(mixed_low.T, grad_attn_low, preferred_element_type=jnp.float32)
        grad_mixed = jnp.dot(grad_attn_low, out_weight.T, preferred_element_type=jnp.float32)
        grad_mixed_low = grad_mixed.astype(jnp.bfloat16).reshape(group_rows, -1, head_size)
        probs = jnp.exp(masked_scores(query_low, key_low, same_seq, head_size) - log_total)
        grad_probs = jnp.einsum(
            "thd,shd->hts", grad_mixed_low, value_low, preferred_element_type=jnp.float32
        )
        grad_value = jnp.einsum(
            "hts,thd->shd", probs_low, grad_mixed_low, preferred_element_type=jnp.float32
        )
        row_delta = jnp.sum(probs * grad_probs, axis=-1, keepdims=True)
        grad_scores = (probs * (grad_probs - row_delta)).astype(jnp.bfloat16)
        grad_query = jnp.einsum(
            "hts,shd->thd", grad_scores, key_low, preferred_element_type=jnp.float32
        ) / math.sqrt(head_size)
        grad_key = jnp.einsum(
            "hts,thd->shd", grad_scores, query_low, preferred_element_type=jnp.float32
        ) / math.sqrt(head_size)
        grad_query_proj, grad_qgain = query_back(grad_query)
        grad_key_proj, grad_kgain = key_back(grad_key)
        grad_query_low = grad_query_proj.astype(jnp.bfloat16)
        grad_key_low = grad_key_proj.astype(jnp.bfloat16)
        grad_value_low = grad_value.reshape(group_rows, -1).astype(jnp.bfloat16)
        normed_part = (
            jnp.dot(grad_query_low, query_weight.T, preferred_element_type=jnp.float32)
            + jnp.dot(grad_key_low, key_weight.T, preferred_element_type=jnp.float32)
            + jnp.dot(grad_value_low, value_weight.T, preferred_element_type=jnp.float32)
        )
        grad_query_w = jnp.dot(normed_low.T, grad_query_low, preferred_element_type=jnp.float32)
        grad_key_w = jnp.dot(normed_low.T, grad_key_low, preferred_element_type=jnp.float32)
        grad_value_w = jnp.dot(normed_low.T, grad_value_low, preferred_element_type=jnp.float32)
        scale_one = lax.rsqrt(jnp.mean(widened * widened, axis=-1, keepdims=True) + eps)
        unit_one = widened * scale_one
        grad_attn_gain = jnp.sum(normed_part * unit_one, axis=0)
        grad_normed_one = lax.psum(normed_part.astype(bf), "tp").astype(f32)
        scaled = grad_normed_one * attn_gain
        grad_from_norm = scale_one * (
            scaled - unit_one * jnp.mean(unit_one * scaled, axis=-1, keepdims=True)
        )
        grad_input_rows = (grad_attn_low.astype(f32) + grad_from_norm).astype(jnp.bfloat16)
        low_totals = lax.psum(
            tuple(
                part.astype(jnp.bfloat16)
                for part in (grad_query_w, grad_key_w, grad_value_w, grad_out_weight)
            ),
            "exp",
        )
        small = lax.psum(
            (grad_attn_gain, grad_qgain, grad_kgain, grad_ffn_gain, grad_router), ("exp", "tp")
        )
        totals = tuple(part.astype(jnp.float32) for part in low_totals) + small
    block_out = (resid + moe).astype(jnp.bfloat16)
    return (
        block_out,
        grad_input_rows,
        totals[4],
        totals[0],
        totals[1],
        totals[2],
        totals[3],
        totals[5],
        totals[6],
        totals[7],
        totals[8],
        grad_gate_w,
        grad_up_w,
        grad_down,
    )


def solution(mesh):
    in_specs = (
        P("exp", None),
        P(),
        P(None, "tp"),
        P(None, "tp"),
        P(None, "tp"),
        P(),
        P(),
        P("tp", None),
        P(),
        P(),
        P("exp", None, "tp"),
        P("exp", None, "tp"),
        P("exp", "tp", None),
        P(("exp", "tp"), None),
        P("exp", None),
        P(("exp", "tp"), None),
    )
    out_specs = (
        P(("exp", "tp"), None),
        P("exp", None),
        P(),
        P(None, "tp"),
        P(None, "tp"),
        P(None, "tp"),
        P("tp", None),
        P(),
        P(),
        P(),
        P(),
        P("exp", None, "tp"),
        P("exp", None, "tp"),
        P("exp", "tp", None),
    )
    fits = dict(mesh.shape) == {"exp": 8, "tp": 4}
    return jax.shard_map(
        functools.partial(per_device, fits), mesh=mesh, in_specs=in_specs, out_specs=out_specs, check_vma=False
    )
```

```python
import functools
import math

import jax
import jax.numpy as jnp
from jax import lax
from jax.experimental import pallas as pl
from jax.experimental.pallas import tpu as pltpu
from jax.sharding import PartitionSpec as P

eps = 1e-06
rope_base = 10000.0
gate_lanes = 128
MESH = pl.DeviceIdType.MESH
bf = jnp.bfloat16
f32 = jnp.float32
NT = (((1,), (1,)), ((), ()))
TN = (((0,), (0,)), ((), ()))


def rms_norm(values, gain):
    return values * lax.rsqrt(jnp.mean(values * values, axis=-1, keepdims=True) + eps) * gain


def rotary_tables(lengths_row, count, head_size):
    token_index = jnp.arange(count, dtype=jnp.int32)
    seq_ends = jnp.cumsum(lengths_row)
    starts = seq_ends - lengths_row
    member = (
        (token_index[:, None] >= starts[None, :]) & (token_index[:, None] < seq_ends[None, :])
    ).astype(jnp.int32)
    segment = jnp.sum(member * jnp.arange(lengths_row.shape[0], dtype=jnp.int32)[None, :], axis=1)
    offset = jnp.sum(member * starts[None, :], axis=1)
    position = (token_index - offset).astype(jnp.float32)
    frequency = rope_base ** (-jnp.arange(0, head_size, 2, dtype=jnp.float32) / head_size)
    angles = position[:, None] * frequency[None, :]
    return (segment, jnp.cos(angles)[:, None, :], jnp.sin(angles)[:, None, :])


def rotate(values, cosine, sine):
    half = values.shape[-1] // 2
    first = values[..., :half]
    second = values[..., half:]
    return jnp.concatenate(
        [first * cosine - second * sine, second * cosine + first * sine], axis=-1
    )


def head_prep(projected, gain, cosine, sine):
    head_size = gain.shape[0]
    shaped = projected.reshape(projected.shape[0], projected.shape[1] // head_size, head_size)
    return rotate(rms_norm(shaped, gain), cosine, sine)


def masked_scores(query_low, key_low, same_seq, head_size):
    scores = jnp.einsum(
        "thd,shd->hts", query_low, key_low, preferred_element_type=jnp.float32
    ) / math.sqrt(head_size)
    return jnp.where(same_seq[None], scores, -1e30)


def plane_at(z, step):
    from_end = step
    from_middle = jnp.where(step == 0, 1, jnp.where(step == 1, 0, step))
    base = jnp.where((z == 0) | (z == 3), from_end, from_middle)
    return jnp.where(z < 2, base, 3 - base)

Z, X, Y, FX, FY, CO, CX, CY, CA, CB = range(10)

def gather_kernel(own_ref, grad_hbm, wg_hbm, wu_hbm, wd_hbm,
                  act_hbm, dg_ref, du_ref, dd_ref,
                  rows, grads, wg, wu, wd, act, send, up_send, recv, load, store, wload):
    e = lax.axis_index("exp")
    z = lax.axis_index("tp")
    ex, ey, ec, ed = (jnp.bitwise_xor(e, m) for m in (2, 4, 1, 6))
    width = wg.shape[1]
    quarter = own_ref.shape[0]
    half = quarter // 2
    hid = wg.shape[2]
    experts_here = wg.shape[0]
    at_x, at_y, at_c = (ex, z), (ey, z), (ec, z)
    at_up, at_down = (e, z + 1), (e, z - 1)

    wcopies = [pltpu.make_async_copy(s, d, wload.at[i]) for i, (s, d) in enumerate(((wg_hbm, wg), (wu_hbm, wu), (wd_hbm, wd)))]
    for c in wcopies: c.start()

    def grad_load(k):
        return pltpu.make_async_copy(grad_hbm.at[plane_at(z, k)], grads.at[k], load.at[k])
    grad_load(0).start()
    middle = (z == 1) | (z == 2)

    bar = pltpu.get_barrier_semaphore()
    for d in (at_x, at_y, at_c):
        pl.semaphore_signal(bar, inc=1, device_id=d, device_id_type=MESH)
    @pl.when(z < 3)
    def _(): pl.semaphore_signal(bar, inc=1, device_id=at_up, device_id_type=MESH)
    @pl.when(z > 0)
    def _(): pl.semaphore_signal(bar, inc=1, device_id=at_down, device_id_type=MESH)
    pl.semaphore_wait(bar, 3 + jnp.where(z < 3, 1, 0) + jnp.where(z > 0, 1, 0))

    TOP, BOT, ALLR = pl.ds(0, half), pl.ds(half, half), pl.ds(0, quarter)

    def copy(kind, plane, group, part, to, src=None, sem=None):
        place = rows.at[plane, group, part]
        return pltpu.make_async_remote_copy(
            src_ref=place if src is None else src, dst_ref=place,
            send_sem=(send.at[kind, plane] if sem is None else sem), recv_sem=recv.at[kind, plane],
            device_id=to, device_id_type=MESH)

    def up(plane, src=None): return copy(Z, plane, e, ALLR, at_up, src, up_send.at[plane])
    def down(plane, src=None): return copy(Z, plane, e, ALLR, at_down, src)
    def to_x(plane, src=None): return copy(X, plane, e, ALLR, at_x, src)
    def to_y(plane, src=None): return copy(Y, plane, e, ALLR, at_y, src)
    def to_c(plane, src=None): return copy(CO, plane, e, ALLR, at_c, src)
    def fwd_y(plane): return copy(FY, plane, ex, TOP, at_y)
    def fwd_x(plane): return copy(FX, plane, ey, BOT, at_x)
    def c_x(plane): return copy(CX, plane, ex, ALLR, at_c)
    def c_y(plane): return copy(CY, plane, ey, ALLR, at_c)
    def c_a(plane): return copy(CA, plane, ed, TOP, at_c)
    def c_b(plane): return copy(CB, plane, ed, BOT, at_c)

    def arrived(kind, plane, group, part):
        place = rows.at[plane, group, part]
        pltpu.make_async_copy(place, place, recv.at[kind, plane]).wait()

    @pl.when(z < 3)
    def _(): up(z, own_ref).start()
    @pl.when(z > 0)
    def _(): down(z, own_ref).start()
    to_x(z, own_ref).start()
    to_y(z, own_ref).start()
    to_c(z, own_ref).start()
    rows[z, e] = own_ref[...]

    def serve_line(k):
        p = plane_at(z, k)
        arrived(Z, p, e, ALLR)
        @pl.when((p < z) & (z < 3))
        def _(): up(p).start()
        @pl.when((p > z) & (z > 0))
        def _(): down(p).start()

    def serve_rows(k):
        p = plane_at(z, k)
        to_x(p).start()
        to_y(p).start()
        to_c(p).start()

    def serve_sides(k):
        p = plane_at(z, k)
        arrived(X, p, ex, ALLR)
        fwd_y(p).start()
        c_x(p).start()
        arrived(Y, p, ey, ALLR)
        fwd_x(p).start()
        c_y(p).start()

    def serve_far(k):
        p = plane_at(z, k)
        arrived(FY, p, ed, TOP)
        c_a(p).start()
        arrived(FX, p, ed, BOT)
        c_b(p).start()

    def store_copy(step):
        k, h = step // 2, lax.rem(step, 2)
        first = jnp.bitwise_xor(jnp.bitwise_and(e, 4), h * 4)
        return pltpu.make_async_copy(act, act_hbm.at[pl.ds(first // 2, 2), :, plane_at(z, k)], store)

    serve_line(1)
    serve_rows(1)
    @pl.when(middle)
    def _(): serve_line(2)
    serve_sides(0)
    for c in wcopies: c.wait()

    def step_body(step, _):
        k, h = step // 2, lax.rem(step, 2)
        p = plane_at(z, k)
        first = jnp.bitwise_xor(jnp.bitwise_and(e, 4), h * 4)
        sib_x = jnp.bitwise_xor(ec, 2)
        sib_y = jnp.bitwise_xor(ec, 4)
        sib_d = jnp.bitwise_xor(ec, 6)
        @pl.when(h == 0)
        def _():
            grad_load(k).wait()
            @pl.when(step < 6)
            def _(): grad_load(k + 1).start()
            arrived(CO, p, ec, ALLR)
            arrived(CX, p, sib_x, ALLR)
        @pl.when(h == 1)
        def _():
            arrived(CY, p, sib_y, ALLR)
            arrived(CA, p, sib_d, TOP)
            arrived(CB, p, sib_d, BOT)
        lane = lax.broadcasted_iota(jnp.int32, (4 * quarter, gate_lanes), 1)

        def expert_body(j, _):
            x = rows[p, pl.ds(first, 4), :, :width].reshape(4 * quarter, width)
            g = grads[k, pl.ds(first, 4)].reshape(4 * quarter, width)
            extra = rows[p, pl.ds(first, 4), :, width:].reshape(4 * quarter, gate_lanes).astype(f32)
            expert = e * experts_here + j
            mine = (lane == expert) | (lane == expert + gate_lanes // 2)
            gate = jnp.sum(jnp.where(mine, extra, 0.0), axis=1, keepdims=True)
            ga = jnp.dot(x, wg[j], preferred_element_type=f32)
            ua = jnp.dot(x, wu[j], preferred_element_type=f32)
            gh = lax.dot_general(g, wd[j], (((1,), (1,)), ((), ())), preferred_element_type=f32)
            sg = jax.nn.sigmoid(ga)
            silu = ga * sg
            hidden = silu * ua
            score = jnp.sum(hidden * gh, axis=1, keepdims=True)
            gh = gh * gate
            hg = (hidden * gate).astype(bf)
            da = (gh * ua * (sg * (1.0 + ga * (1.0 - sg)))).astype(bf)
            du = (gh * silu).astype(bf)
            @pl.when((step > 0) & (j == 0))
            def _(): store_copy(step - 1).wait()
            base = j * 2 * hid
            shape3 = (2, 2, quarter, hid)
            act[:, :, :, pl.ds(pl.multiple_of(base, hid), hid)] = da.reshape(shape3)
            act[:, :, :, pl.ds(pl.multiple_of(base + hid, hid), hid)] = du.reshape(shape3)
            act[:, :, :, pl.ds(pl.multiple_of((2 * experts_here + j) * hid, hid), hid)] = hg.reshape(shape3)
            scores = jnp.where(lane == expert, score, 0.0).astype(bf).reshape(2, 2, quarter, gate_lanes)
            act[:, :, :, pl.ds(pl.multiple_of(experts_here * 3 * hid + j * gate_lanes, gate_lanes), gate_lanes)] = scores
            @pl.when(step == 0)
            def _():
                dg_ref[j] = jnp.zeros(dg_ref.shape[1:], f32)
                du_ref[j] = jnp.zeros(du_ref.shape[1:], f32)
                dd_ref[j] = jnp.zeros(dd_ref.shape[1:], f32)
            slot = 2 * step + j
            for at, work, which in (
                (1, serve_far, 0),
                (3, serve_sides, 1),
                (5, serve_rows, 3),
                (5, serve_far, 1),
                (7, serve_sides, 2),
                (9, serve_far, 2),
                (9, serve_sides, 3),
                (12, serve_far, 3),
            ):
                @pl.when(slot == at)
                def _(): work(which)
            @pl.when((slot == 1) & middle)
            def _(): serve_line(3)
            @pl.when((slot == 1) & ~middle)
            def _(): serve_line(2)
            @pl.when(slot == 1)
            def _(): serve_rows(2)
            @pl.when((slot == 3) & ~middle)
            def _(): serve_line(3)
            dd_ref[j] += lax.dot_general(hg, g, TN, preferred_element_type=f32)
            dg_ref[j] += lax.dot_general(x, da, TN, preferred_element_type=f32)
            du_ref[j] += lax.dot_general(x, du, TN, preferred_element_type=f32)
            return 0
        lax.fori_loop(0, experts_here, expert_body, 0)
        store_copy(step).start()
        return 0
    lax.fori_loop(0, 8, step_body, 0)
    store_copy(7).wait()

    def drain(k, _):
        p = plane_at(z, k)
        @pl.when((z < 3) & (p <= z))
        def _(): up(p).wait_send()
        @pl.when((z > 0) & (p >= z))
        def _(): down(p).wait_send()
        for c in (to_x, to_y, to_c, fwd_y, fwd_x, c_x, c_y, c_a, c_b):
            c(p).wait_send()
        return 0
    lax.fori_loop(0, 4, drain, 0)

def gather_experts(own, grads_all, wg, wu, wd):
    n_here, width, hid = wg.shape
    quarter, wide = own.shape
    lanes = wide - width
    cols = n_here * 3 * hid + n_here * lanes
    any_ = pl.BlockSpec(memory_space=pl.ANY)
    vm = pl.BlockSpec(memory_space=pltpu.VMEM)
    return pl.pallas_call(
        gather_kernel,
        out_shape=(jax.ShapeDtypeStruct((4, 2, 4, quarter, cols), bf),
                   jax.ShapeDtypeStruct(wg.shape, f32), jax.ShapeDtypeStruct(wu.shape, f32), jax.ShapeDtypeStruct(wd.shape, f32)),
        in_specs=[vm, any_, any_, any_, any_],
        out_specs=(any_, vm, vm, vm),
        scratch_shapes=[
            pltpu.VMEM((4, 8, quarter, wide), bf),
            pltpu.VMEM((4, 8, quarter, width), bf),
            pltpu.VMEM(wg.shape, bf), pltpu.VMEM(wu.shape, bf), pltpu.VMEM(wd.shape, bf),
            pltpu.VMEM((2, 2, quarter, cols), bf),
            pltpu.SemaphoreType.DMA((10, 4)), pltpu.SemaphoreType.DMA((4,)), pltpu.SemaphoreType.DMA((10, 4)),
            pltpu.SemaphoreType.DMA((4,)), pltpu.SemaphoreType.DMA, pltpu.SemaphoreType.DMA((3,)),
        ],
        compiler_params=pltpu.CompilerParams(collective_id=1, has_side_effects=True, vmem_limit_bytes=63 << 20),
        cost_estimate=pl.CostEstimate(flops=12 * 4096 * 2048 * hid * n_here, bytes_accessed=64 << 20, transcendentals=0),
    )(own, grads_all, wg, wu, wd)


def head_scores(queries, keys, same, head_size):
    scores = lax.dot_general(queries, keys, NT, preferred_element_type=f32) / math.sqrt(head_size)
    scores = jnp.where(same, scores, -1e30)
    grown = jnp.exp(scores - jnp.max(scores, axis=-1, keepdims=True))
    return grown / jnp.sum(grown, axis=-1, keepdims=True)

def mixed_back(grad_rows, out_w, mixed, grad_mixed, grad_out_w):
    grads = grad_rows[...].reshape(-1, grad_rows.shape[2])
    grad_mixed[...] = lax.dot_general(grads, out_w[...], NT, preferred_element_type=f32).astype(bf)
    grad_out_w[...] = lax.dot_general(mixed[...], grads, TN, preferred_element_type=f32).astype(bf)

def head_back(h, queries, keys, values, projected, gains, cosine, sine, seg_col, seg_row, grad_mixed, grad_heads, grad_gains):
    head_size = cosine.shape[1]
    at = pl.ds(pl.multiple_of(h * head_size, head_size), head_size)
    same = seg_col[...] == seg_row[...]
    q, k, v, gm = queries[:, at], keys[:, at], values[:, at], grad_mixed[:, at]
    probs = head_scores(q, k, same, head_size)
    grad_probs = lax.dot_general(gm, v, NT, preferred_element_type=f32)
    grad_heads[2, :, at] = lax.dot_general(probs.astype(bf), gm, TN, preferred_element_type=f32).astype(bf)
    delta = jnp.sum(probs * grad_probs, axis=-1, keepdims=True)
    grad_scores = (probs * (grad_probs - delta)).astype(bf)
    back = (
        jnp.dot(grad_scores, k, preferred_element_type=f32),
        lax.dot_general(grad_scores, q, TN, preferred_element_type=f32),
    )
    for i in range(2):
        grad = back[i] / math.sqrt(head_size)
        grad = grad * cosine[...] - pltpu.roll(grad, head_size // 2, axis=1) * sine[...]
        value = projected[i][:, at]
        scale = lax.rsqrt(jnp.mean(value * value, axis=-1, keepdims=True) + eps)
        unit = value * scale
        grad_gains[i : i + 1] += jnp.sum(grad * unit, axis=0, keepdims=True)
        scaled = grad * gains[i : i + 1]
        grad_heads[i, :, at] = (scale * (scaled - unit * jnp.mean(unit * scaled, axis=-1, keepdims=True))).astype(bf)

def input_back(weights, grad_heads, part, cols):
    total = None
    for i, w in enumerate(weights):
        one = lax.dot_general(grad_heads[i], w[cols, :], NT, preferred_element_type=f32)
        total = one if total is None else total + one
    part[:, :, cols] = total.astype(bf).reshape(part.shape[0], part.shape[1], -1)

def norm_rows(hidden, gain, normed):
    rows = hidden.shape[1]
    def plane(p, _):
        value = hidden[p].astype(f32)
        scale = lax.rsqrt(jnp.mean(value * value, axis=-1, keepdims=True) + eps)
        normed[pl.ds(pl.multiple_of(p * rows, rows), rows), :] = (value * scale * gain[...]).astype(bf)
        return 0
    lax.fori_loop(0, hidden.shape[0], plane, 0)

def project(normed, weight, out):
    out[...] = jnp.dot(normed[...], weight[...], preferred_element_type=f32).astype(out.dtype)

def head_forward(h, projected, gains, cosine, sine, seg_col, seg_row, lows, values, mixed):
    head_size = cosine.shape[1]
    at = pl.ds(pl.multiple_of(h * head_size, head_size), head_size)
    for i in range(2):
        value = projected[i][:, at]
        scale = lax.rsqrt(jnp.mean(value * value, axis=-1, keepdims=True) + eps)
        scaled = value * scale * gains[i : i + 1]
        lows[i][:, at] = (scaled * cosine[...] + pltpu.roll(scaled, head_size // 2, axis=1) * sine[...]).astype(bf)
    probs = head_scores(lows[0][:, at], lows[1][:, at], seg_col[...] == seg_row[...], head_size)
    mixed[:, at] = jnp.dot(probs.astype(bf), values[:, at], preferred_element_type=f32).astype(bf)

def output_part(mixed, weight, part):
    def tile(n, _):
        cols = pl.ds(pl.multiple_of(n * 512, 512), 512)
        total = jnp.dot(mixed[...], weight[:, cols], preferred_element_type=f32)
        part[:, :, cols] = total.astype(bf).reshape(part.shape[0], part.shape[1], -1)
        return 0
    lax.fori_loop(0, part.shape[2] // 512, tile, 0)


HZ, HX, HY, HFX, HFY, HC, HCX, HCY, HCA, HCB, HU, HD = range(12)

def opening_kernel(hidden, gain, wq_hbm, wk_hbm, wv_hbm, out_hbm, gains, cosine, sine, seg_col, seg_row, grad_ref,
                   out_ref, normed, query_proj, key_proj, queries, keys, values, mixed, grads,
                   wq, wk, wv, out_w, part_ref, line, rzu, rzd, send, up_send, recv, local, wload):
    e = lax.axis_index("exp")
    z = lax.axis_index("tp")
    ex, ey, ec, ed = (jnp.bitwise_xor(e, m) for m in (2, 4, 1, 6))
    at_x, at_y, at_c = (ex, z), (ey, z), (ec, z)
    at_up, at_down = (e, z + 1), (e, z - 1)
    middle_plane = (z == 1) | (z == 2)
    quarter = grad_ref.shape[0]
    half = quarter // 2
    TOP, BOT, ALLR = pl.ds(0, half), pl.ds(half, half), pl.ds(0, quarter)

    wcopies = [pltpu.make_async_copy(s, d, wload.at[i]) for i, (s, d) in enumerate(zip((wq_hbm, wk_hbm, wv_hbm, out_hbm), (wq, wk, wv, out_w)))]
    for c in wcopies: c.start()

    bar = pltpu.get_barrier_semaphore()
    for d in (at_x, at_y, at_c):
        pl.semaphore_signal(bar, inc=1, device_id=d, device_id_type=MESH)
    @pl.when(z < 3)
    def _(): pl.semaphore_signal(bar, inc=1, device_id=at_up, device_id_type=MESH)
    @pl.when(z > 0)
    def _(): pl.semaphore_signal(bar, inc=1, device_id=at_down, device_id_type=MESH)
    pl.semaphore_wait(bar, 3 + jnp.where(z < 3, 1, 0) + jnp.where(z > 0, 1, 0))

    def copy(kind, plane, group, part, to, src=None, sem=None):
        place = grads.at[plane, group, part]
        return pltpu.make_async_remote_copy(
            src_ref=place if src is None else src, dst_ref=place,
            send_sem=send.at[kind, plane] if sem is None else sem, recv_sem=recv.at[kind, plane],
            device_id=to, device_id_type=MESH)
    def arrived(kind, plane, place):
        pltpu.make_async_copy(place, place, recv.at[kind, plane]).wait()
    def line_copy(kind, p, landing, to):
        return pltpu.make_async_remote_copy(src_ref=line.at[p], dst_ref=landing.at[p], send_sem=send.at[kind, p],
                                            recv_sem=recv.at[kind, p], device_id=to, device_id_type=MESH)
    def line_up(p): return line_copy(HU, p, rzu, at_up)
    def line_down(p): return line_copy(HD, p, rzd, at_down)
    def up(p, src=None): return copy(HZ, p, e, ALLR, at_up, src, up_send.at[p])
    def down(p, src=None): return copy(HZ, p, e, ALLR, at_down, src)
    def to_x(p, src=None): return copy(HX, p, e, ALLR, at_x, src)
    def to_y(p, src=None): return copy(HY, p, e, ALLR, at_y, src)
    def to_c(p, src=None): return copy(HC, p, e, ALLR, at_c, src)
    def fwd_y(p): return copy(HFY, p, ex, TOP, at_y)
    def fwd_x(p): return copy(HFX, p, ey, BOT, at_x)
    def c_x(p): return copy(HCX, p, ex, ALLR, at_c)
    def c_y(p): return copy(HCY, p, ey, ALLR, at_c)
    def c_a(p): return copy(HCA, p, ed, TOP, at_c)
    def c_b(p): return copy(HCB, p, ed, BOT, at_c)

    def serve_line(k):
        p = plane_at(z, k)
        arrived(HZ, p, grads.at[p, e])
        @pl.when((p < z) & (z < 3))
        def _(): up(p).start()
        @pl.when((p > z) & (z > 0))
        def _(): down(p).start()

    def serve_rows(k):
        p = plane_at(z, k)
        to_x(p).start()
        to_y(p).start()
        to_c(p).start()

    def serve_sides(k):
        p = plane_at(z, k)
        arrived(HX, p, grads.at[p, ex])
        fwd_y(p).start()
        c_x(p).start()
        arrived(HY, p, grads.at[p, ey])
        fwd_x(p).start()
        c_y(p).start()

    def serve_far(k):
        p = plane_at(z, k)
        arrived(HFY, p, grads.at[p, ed, TOP])
        c_a(p).start()
        arrived(HFX, p, grads.at[p, ed, BOT])
        c_b(p).start()

    def line_step(k):
        p = plane_at(z, 3 - k)
        line[p] = part_ref[p]
        @pl.when((z > 0) & (p >= z))
        def _():
            arrived(HU, p, rzu.at[p])
            line[p] = (line[p].astype(f32) + rzu[p].astype(f32)).astype(bf)
        @pl.when((z < 3) & (p <= z))
        def _():
            arrived(HD, p, rzd.at[p])
            line[p] = (line[p].astype(f32) + rzd[p].astype(f32)).astype(bf)
        @pl.when(p > z)
        def _(): line_up(p).start()
        @pl.when(p < z)
        def _(): line_down(p).start()

    def ends(f): pl.when(~middle_plane)(f)
    def mids(f): pl.when(middle_plane)(f)

    def one_head(h):
        head_forward(h, (query_proj, key_proj), gains, cosine, sine, seg_col, seg_row, (queries, keys), values, mixed)

    def own_sum():
        out_ref[...] = part_ref[z].astype(f32)
        @pl.when(z > 0)
        def _():
            arrived(HU, z, rzu.at[z])
            out_ref[...] += rzu[z].astype(f32)
        @pl.when(z < 3)
        def _():
            arrived(HD, z, rzd.at[z])
            out_ref[...] += rzd[z].astype(f32)

    @pl.when(z < 3)
    def _(): up(z, grad_ref).start()
    @pl.when(z > 0)
    def _(): down(z, grad_ref).start()
    to_x(z, grad_ref).start()
    to_y(z, grad_ref).start()
    to_c(z, grad_ref).start()
    own = pltpu.make_async_copy(grad_ref, grads.at[z, e], local)
    own.start()

    norm_rows(hidden, gain, normed)
    for c, weight, out in zip(wcopies, (wq, wk, wv), (query_proj, key_proj, values)):
        c.wait()
        project(normed, weight, out)
    serve_line(1)
    serve_rows(1)
    serve_sides(0)
    mids(lambda: serve_line(2))
    one_head(0)
    serve_far(0)
    one_head(1)
    mids(lambda: serve_line(3))
    ends(lambda: serve_line(2))
    serve_rows(2)
    one_head(2)
    serve_sides(1)
    one_head(3)
    wcopies[3].wait()
    output_part(mixed, out_w, part_ref)
    ends(lambda: line_step(0))
    ends(lambda: serve_line(3))
    serve_rows(3)
    serve_far(1)
    mids(lambda: line_step(0))
    ends(lambda: line_step(1))
    serve_sides(2)
    mids(lambda: line_step(1))
    mids(lambda: line_step(2))
    ends(lambda: line_step(2))
    serve_far(2)
    serve_sides(3)
    own_sum()
    serve_far(3)
    own.wait()
    def drain(k, _):
        p = plane_at(z, k)
        @pl.when((z < 3) & (p <= z))
        def _(): up(p).wait_send()
        @pl.when((z > 0) & (p >= z))
        def _(): down(p).wait_send()
        for c in (to_x, to_y, to_c, fwd_y, fwd_x, c_x, c_y, c_a, c_b):
            c(p).wait_send()
        arrived(HC, p, grads.at[p, ec])
        arrived(HCX, p, grads.at[p, jnp.bitwise_xor(ec, 2)])
        arrived(HCY, p, grads.at[p, jnp.bitwise_xor(ec, 4)])
        arrived(HCA, p, grads.at[p, jnp.bitwise_xor(ec, 6), TOP])
        arrived(HCB, p, grads.at[p, jnp.bitwise_xor(ec, 6), BOT])
        return 0
    lax.fori_loop(0, 4, drain, 0)
    def drain_line(p, _):
        @pl.when(p > z)
        def _(): line_up(p).wait_send()
        @pl.when(p < z)
        def _(): line_down(p).wait_send()
        return 0
    lax.fori_loop(0, 4, drain_line, 0)

def open_exchange(hidden, gain, weights, gains, cosine, sine, seg_col, seg_row, grad, collective_id):
    vm = pl.BlockSpec(memory_space=pltpu.VMEM)
    any_ = pl.BlockSpec(memory_space=pl.ANY)
    planes = hidden.shape
    _, quarter, width = planes
    tokens = cosine.shape[0]
    heads = (tokens, weights[0].shape[1])
    return pl.pallas_call(
        opening_kernel,
        out_shape=(
            jax.ShapeDtypeStruct((quarter, width), f32),
            jax.ShapeDtypeStruct((tokens, width), bf),
            jax.ShapeDtypeStruct(heads, f32), jax.ShapeDtypeStruct(heads, f32),
            jax.ShapeDtypeStruct(heads, bf), jax.ShapeDtypeStruct(heads, bf), jax.ShapeDtypeStruct(heads, bf), jax.ShapeDtypeStruct(heads, bf),
            jax.ShapeDtypeStruct((4, 8, quarter, width), bf),
        ),
        in_specs=[vm, vm] + [any_] * 4 + [vm] * 5 + [any_],
        out_specs=(vm,) * 8 + (any_,),
        scratch_shapes=[pltpu.VMEM(w.shape, bf) for w in weights] + [pltpu.VMEM(planes, bf)] * 4 + [
            pltpu.SemaphoreType.DMA((12, 4)), pltpu.SemaphoreType.DMA((4,)), pltpu.SemaphoreType.DMA((12, 4)), pltpu.SemaphoreType.DMA,
            pltpu.SemaphoreType.DMA((4,))],
        compiler_params=pltpu.CompilerParams(collective_id=collective_id, has_side_effects=True, vmem_limit_bytes=56 << 20),
    )(hidden, gain, *weights, gains, cosine, sine, seg_col, seg_row, grad)


def input_product(acts, weights, cols):
    wg, wu = weights
    hid = wg.shape[2]
    total = None
    for j in range(wg.shape[0]):
        for w, i in ((wg, 0), (wu, 1)):
            lhs = acts[:, :, (2 * j + i) * hid:(2 * j + i + 1) * hid].reshape(-1, hid)
            part = lax.dot_general(lhs, w[j, cols, :], NT, preferred_element_type=f32)
            total = part if total is None else total + part
    return total

def output_product(acts, weights, cols):
    (wd,) = weights
    hid = wd.shape[1]
    total = None
    for j in range(wd.shape[0]):
        lhs = acts[:, :, j * hid:(j + 1) * hid].reshape(-1, hid)
        part = jnp.dot(lhs, wd[j, :, cols], preferred_element_type=f32)
        total = part if total is None else total + part
    return total

C1, DT, DB, XT, XB, YT, YB, ZU, ZD, OU, OD = range(11)

def scatter_kernel(product, n_weights, width, cols, score_at, carry, *refs):
    act_hbm, *rest = refs
    w_hbm, rest = rest[:n_weights], rest[n_weights:]
    if carry:
        row_ref, out_w, mixed, queries, keys, values, query_proj, key_proj, gains, cosine, sine, seg_col, seg_row, *rest = rest
        projected = (query_proj, key_proj)
        out_ref, grad_heads, grad_out_w, grad_gains, acts, *rest = rest
        *rest, rows, grad_mixed = rest
    else:
        out_ref, acts, *rest = rest
    weights, rest = rest[:n_weights], rest[n_weights:]
    sendbuf, acc, r1, rdt, rdb, rx, ry, rzu, rzd, send, recv, load, wload = rest
    e = lax.axis_index("exp")
    z = lax.axis_index("tp")
    quarter = acc.shape[2]
    half = quarter // 2
    chip = e // 2
    core = lax.rem(e, 2)
    chip_x, chip_y, chip_d = (jnp.bitwise_xor(chip, m) for m in (1, 2, 3))
    at_x, at_y, at_c = (jnp.bitwise_xor(e, 2), z), (jnp.bitwise_xor(e, 4), z), (jnp.bitwise_xor(e, 1), z)
    at_up, at_down = (e, z + 1), (e, z - 1)
    TOP, BOT = pl.ds(0, half), pl.ds(half, half)

    wcopies = [pltpu.make_async_copy(s, d, wload.at[i]) for i, (s, d) in enumerate(zip(w_hbm, weights))]
    for c in wcopies: c.start()

    def act_copy(n):
        k, own = n // 2, n % 2
        which = jnp.bitwise_xor(core, 1 - own)
        return pltpu.make_async_copy(act_hbm.at[:, which, plane_at(z, 3 - k), :, cols], acts.at[own], load.at[own])
    act_copy(0).start()

    bar = pltpu.get_barrier_semaphore()
    for d in (at_x, at_y, at_c):
        pl.semaphore_signal(bar, inc=1, device_id=d, device_id_type=MESH)
    @pl.when(z < 3)
    def _(): pl.semaphore_signal(bar, inc=1, device_id=at_up, device_id_type=MESH)
    @pl.when(z > 0)
    def _(): pl.semaphore_signal(bar, inc=1, device_id=at_down, device_id_type=MESH)
    pl.semaphore_wait(bar, 3 + jnp.where(z < 3, 1, 0) + jnp.where(z > 0, 1, 0))
    for c in wcopies: c.wait()

    def remote(kind, k, src, dst, to):
        return pltpu.make_async_remote_copy(src_ref=src, dst_ref=dst, send_sem=send.at[kind, k], recv_sem=recv.at[kind, k],
                                            device_id=to, device_id_type=MESH)
    def to_core(k): return remote(C1, k, sendbuf.at[k % 2], r1.at[k], at_c)
    def far_x(k): return remote(DT, k, acc.at[k, chip_d, TOP], rdt.at[k], at_x)
    def far_y(k): return remote(DB, k, acc.at[k, chip_d, BOT], rdb.at[k], at_y)
    def x_top(k): return remote(XT, k, acc.at[k, chip_x, TOP], rx.at[k, TOP], at_x)
    def x_bot(k): return remote(XB, k, acc.at[k, chip_x, BOT], rx.at[k, BOT], at_x)
    def y_top(k): return remote(YT, k, acc.at[k, chip_y, TOP], ry.at[k, TOP], at_y)
    def y_bot(k): return remote(YB, k, acc.at[k, chip_y, BOT], ry.at[k, BOT], at_y)
    def line_up(k, p): return remote(ZU, p, acc.at[k, chip], rzu.at[p], at_up)
    def line_down(k, p): return remote(ZD, p, acc.at[k, chip], rzd.at[p], at_down)
    def arrived(kind, k, place):
        pltpu.make_async_copy(place, place, recv.at[kind, k]).wait()
    def row_up(p): return remote(OU, p, rows.at[p], rows.at[p], at_up)
    def row_down(p): return remote(OD, p, rows.at[p], rows.at[p], at_down)
    def row_step(k):
        p = plane_at(z, k)
        @pl.when(p < z)
        def _(): arrived(OU, p, rows.at[p])
        @pl.when(p > z)
        def _(): arrived(OD, p, rows.at[p])
        @pl.when((p <= z) & (z < 3))
        def _(): row_up(p).start()
        @pl.when((p >= z) & (z > 0))
        def _(): row_down(p).start()
    if carry:
        rows[z] = row_ref[...]
        row_step(0)

    cols_step = 512
    def multiply(slot, target):
        def tile(n, _):
            cols = pl.ds(pl.multiple_of(n * cols_step, cols_step), cols_step)
            total = product(acts.at[slot], weights, cols)
            target[:, :, cols] = total.astype(bf).reshape(4, quarter, cols_step)
            return 0
        lax.fori_loop(0, width // cols_step, tile, 0)
        if score_at is not None:
            lanes = target.shape[2] - width
            target[:, :, width:] = acts[slot, :, :, score_at:score_at + lanes] + acts[slot, :, :, score_at + lanes:score_at + 2 * lanes]

    def add(place, other):
        place[...] = (place[...].astype(f32) + other[...].astype(f32)).astype(bf)

    def begin(k):
        act_copy(2 * k).wait()
        act_copy(2 * k + 1).start()
        if k >= 2:
            to_core(k - 2).wait_send()
        multiply(0, sendbuf.at[k % 2])
        to_core(k).start()
        act_copy(2 * k + 1).wait()
        if k < 3:
            act_copy(2 * k + 2).start()
        multiply(1, acc.at[k])
        arrived(C1, k, r1.at[k])
        add(acc.at[k, chip_d], r1.at[k, chip_d])
        far_x(k).start()
        far_y(k).start()
        add(acc.at[k, chip_x], r1.at[k, chip_x])
        x_top(k).start()
        add(acc.at[k, chip_y], r1.at[k, chip_y])
        y_bot(k).start()
        add(acc.at[k, chip], r1.at[k, chip])

    def middle(k):
        arrived(DB, k, rdb.at[k])
        add(acc.at[k, chip_x, BOT], rdb.at[k])
        x_bot(k).start()
        arrived(DT, k, rdt.at[k])
        add(acc.at[k, chip_y, TOP], rdt.at[k])
        y_top(k).start()

    def finish(k):
        p = plane_at(z, 3 - k)
        arrived(XT, k, rx.at[k, TOP])
        arrived(YB, k, ry.at[k, BOT])
        arrived(XB, k, rx.at[k, BOT])
        arrived(YT, k, ry.at[k, TOP])
        total = acc[k, chip].astype(f32) + rx[k].astype(f32) + ry[k].astype(f32)
        out_ref[...] = total
        @pl.when((z > 0) & (p >= z))
        def _():
            arrived(ZU, p, rzu.at[p])
            out_ref[...] += rzu[p].astype(f32)
        @pl.when((z < 3) & (p <= z))
        def _():
            arrived(ZD, p, rzd.at[p])
            out_ref[...] += rzd[p].astype(f32)
        @pl.when(p != z)
        def _():
            acc[k, chip] = out_ref[...].astype(bf)
        @pl.when(p > z)
        def _(): line_up(k, p).start()
        @pl.when(p < z)
        def _(): line_down(k, p).start()

    def one_head(h):
        head_back(h, queries, keys, values, projected, gains, cosine, sine, seg_col, seg_row, grad_mixed, grad_heads, grad_gains)

    def ends(f):
        pl.when((z == 0) | (z == 3))(f)
    def mids(f):
        pl.when((z == 1) | (z == 2))(f)

    if carry:
        grad_gains[...] = jnp.zeros(grad_gains.shape, f32)
        begin(0)
        row_step(1)
        begin(1)
        middle(0)
        row_step(2)
        begin(2)
        middle(1)
        row_step(3)
        ends(lambda: finish(0))
        begin(3)
        mixed_back(rows, out_w, mixed, grad_mixed, grad_out_w)
        middle(2)
        one_head(0)
        mids(lambda: finish(0))
        ends(lambda: finish(1))
        one_head(1)
        middle(3)
        mids(lambda: finish(1))
        one_head(2)
        finish(2)
        one_head(3)
        finish(3)
    else:
        begin(0)
        begin(1)
        middle(0)
        begin(2)
        middle(1)
        ends(lambda: finish(0))
        begin(3)
        middle(2)
        mids(lambda: finish(0))
        ends(lambda: finish(1))
        middle(3)
        mids(lambda: finish(1))
        finish(2)
        finish(3)

    for k in (2, 3):
        to_core(k).wait_send()
    def drain(k, _):
        p = plane_at(z, 3 - k)
        for c in (far_x, far_y, x_top, x_bot, y_top, y_bot):
            c(k).wait_send()
        @pl.when(p > z)
        def _(): line_up(k, p).wait_send()
        @pl.when(p < z)
        def _(): line_down(k, p).wait_send()
        if carry:
            @pl.when((p <= z) & (z < 3))
            def _(): row_up(p).wait_send()
            @pl.when((p >= z) & (z > 0))
            def _(): row_down(p).wait_send()
        return 0
    lax.fori_loop(0, 4, drain, 0)

def scatter_sums(act, weights, scores, collective_id, attention=()):
    hid = min(weights[0].shape[1:])
    width = max(weights[0].shape[1:])
    n_here = weights[0].shape[0]
    quarter, cols = act.shape[3:]
    score_at = 3 * hid * n_here
    lanes = (cols - score_at) // n_here
    wide = width + (lanes if scores else 0)
    taken = pl.ds(0, cols) if scores else pl.ds(2 * hid * n_here, hid * n_here)
    product = input_product if scores else output_product
    any_ = pl.BlockSpec(memory_space=pl.ANY)
    vm = pl.BlockSpec(memory_space=pltpu.VMEM)
    n = len(weights)
    out_shape = (jax.ShapeDtypeStruct((quarter, wide), f32),)
    extra = []
    if attention:
        heads, head_size = attention[2].shape, attention[8].shape[1]
        out_shape += (
            jax.ShapeDtypeStruct((3,) + heads, bf),
            jax.ShapeDtypeStruct(attention[1].shape, bf),
            jax.ShapeDtypeStruct((2, head_size), f32),
        )
        extra = [pltpu.VMEM((4, quarter, width), bf), pltpu.VMEM(heads, bf)]
    return pl.pallas_call(
        functools.partial(scatter_kernel, product, n, width, taken, score_at if scores else None, bool(attention)),
        out_shape=out_shape,
        in_specs=[any_] * (1 + n) + [vm] * len(attention),
        out_specs=(vm,) * len(out_shape),
        scratch_shapes=[pltpu.VMEM((2, 4, quarter, taken.size), bf)] + [pltpu.VMEM(w.shape, bf) for w in weights] + [
            pltpu.VMEM((2, 4, quarter, wide), bf),
            pltpu.VMEM((4, 4, quarter, wide), bf),
            pltpu.VMEM((4, 4, quarter, wide), bf),
            pltpu.VMEM((4, quarter // 2, wide), bf), pltpu.VMEM((4, quarter // 2, wide), bf),
            pltpu.VMEM((4, quarter, wide), bf), pltpu.VMEM((4, quarter, wide), bf),
            pltpu.VMEM((4, quarter, wide), bf), pltpu.VMEM((4, quarter, wide), bf),
            pltpu.SemaphoreType.DMA((11, 4)), pltpu.SemaphoreType.DMA((11, 4)),
            pltpu.SemaphoreType.DMA((2,)), pltpu.SemaphoreType.DMA((n,)),
        ] + extra,
        compiler_params=pltpu.CompilerParams(collective_id=collective_id, has_side_effects=True, vmem_limit_bytes=62 << 20),
    )(act, *weights, *attention)


(SC, SDT, SDB, SXT, SXB, SYT, SYB, GX, GY, GFX, GFY, GC, GCX, GCY, GCA, GCB, LU, LD, RU, RD) = range(20)

def totals_kernel(*refs):
    grad_heads, normed_ref, proj_w, grad_out_w, refs = refs[0], refs[1], refs[2:5], refs[5], refs[6:]
    router_ref, ffn_ref, heads_ref, hidden_ref, resid_ref, gain_ref, refs = *refs[:6], refs[6:]
    res, rows, small_out, refs = refs[:4], refs[4], refs[5], refs[6:]
    w_ref, refs = (grad_out_w, *refs[:3]), refs[3:]
    r1, acc, rdt, rdb, rx, ry, refs = *(refs[4 * i : 4 * i + 4] for i in range(6)), refs[24:]
    part_ref, rzu, rzd, line, sums, got, send, recv, ssend, srecv = refs
    e = lax.axis_index("exp")
    z = lax.axis_index("tp")
    chip, core = e // 2, lax.rem(e, 2)
    cx, cy, cd = (jnp.bitwise_xor(chip, m) for m in (1, 2, 3))
    at_x, at_y, at_c = (jnp.bitwise_xor(e, 2), z), (jnp.bitwise_xor(e, 4), z), (jnp.bitwise_xor(e, 1), z)
    at_up, at_down = (e, z + 1), (e, z - 1)
    partners = (at_c, at_x, at_y, (e, jnp.bitwise_xor(z, 1)), (e, jnp.bitwise_xor(z, 2)))
    middle_plane = (z == 1) | (z == 2)
    halves = [ref.shape[1] // 2 for ref in acc]
    TOP, BOT = [pl.ds(0, h) for h in halves], [pl.ds(h, h) for h in halves]

    bar = pltpu.get_barrier_semaphore()
    for d in (at_x, at_y, at_c, (e, jnp.bitwise_xor(z, 2))):
        pl.semaphore_signal(bar, inc=1, device_id=d, device_id_type=MESH)
    @pl.when(z < 3)
    def _(): pl.semaphore_signal(bar, inc=1, device_id=at_up, device_id_type=MESH)
    @pl.when(z > 0)
    def _(): pl.semaphore_signal(bar, inc=1, device_id=at_down, device_id_type=MESH)
    pl.semaphore_wait(bar, 4 + jnp.where(z < 3, 1, 0) + jnp.where(z > 0, 1, 0))

    def remote(kind, k, src, dst, to):
        return pltpu.make_async_remote_copy(src_ref=src, dst_ref=dst, send_sem=send.at[kind, k], recv_sem=recv.at[kind, k],
                                            device_id=to, device_id_type=MESH)
    def arrived(kind, k, place):
        pltpu.make_async_copy(place, place, recv.at[kind, k]).wait()
    def to_core(k): return remote(SC, k, w_ref[k].at[1 - core], r1[k], at_c)
    def far_x(k): return remote(SDT, k, acc[k].at[cd, TOP[k]], rdt[k], at_x)
    def far_y(k): return remote(SDB, k, acc[k].at[cd, BOT[k]], rdb[k], at_y)
    def x_top(k): return remote(SXT, k, acc[k].at[cx, TOP[k]], rx[k].at[TOP[k]], at_x)
    def x_bot(k): return remote(SXB, k, acc[k].at[cx, BOT[k]], rx[k].at[BOT[k]], at_x)
    def y_top(k): return remote(SYT, k, acc[k].at[cy, TOP[k]], ry[k].at[TOP[k]], at_y)
    def y_bot(k): return remote(SYB, k, acc[k].at[cy, BOT[k]], ry[k].at[BOT[k]], at_y)
    def same(kind, k, place, to): return remote(kind, k, place, place, to)
    def give_x(k): return same(GX, k, res[k].at[core, chip], at_x)
    def give_y(k): return same(GY, k, res[k].at[core, chip], at_y)
    def give_c(k): return same(GC, k, res[k].at[core, chip], at_c)
    def pass_y(k): return same(GFY, k, res[k].at[core, cx, TOP[k]], at_y)
    def pass_x(k): return same(GFX, k, res[k].at[core, cy, BOT[k]], at_x)
    def c_x(k): return same(GCX, k, res[k].at[core, cx], at_c)
    def c_y(k): return same(GCY, k, res[k].at[core, cy], at_c)
    def c_a(k): return same(GCA, k, res[k].at[core, cd, TOP[k]], at_c)
    def c_b(k): return same(GCB, k, res[k].at[core, cd, BOT[k]], at_c)
    def line_up(p): return remote(LU, p, line.at[p], rzu.at[p], at_up)
    def line_down(p): return remote(LD, p, line.at[p], rzd.at[p], at_down)
    def row_up(p): return same(RU, p, rows.at[p], at_up)
    def row_down(p): return same(RD, p, rows.at[p], at_down)

    def plus(a, b): return (a.astype(f32) + b.astype(f32)).astype(bf)

    def input_part():
        def tile(n, _):
            input_back(proj_w, grad_heads, part_ref, pl.ds(pl.multiple_of(n * 512, 512), 512))
            return 0
        lax.fori_loop(0, part_ref.shape[2] // 512, tile, 0)

    def weight_part(k):
        part = lax.dot_general(normed_ref[...], grad_heads[k - 1], TN, preferred_element_type=f32)
        w_ref[k][...] = part.astype(bf).reshape(w_ref[k].shape)
        to_core(k).start()

    def begin(k):
        arrived(SC, k, r1[k])
        acc[k][cd] = plus(w_ref[k][core, cd], r1[k][cd])
        far_x(k).start()
        far_y(k).start()
        acc[k][cx] = plus(w_ref[k][core, cx], r1[k][cx])
        x_top(k).start()
        acc[k][cy] = plus(w_ref[k][core, cy], r1[k][cy])
        y_bot(k).start()
        acc[k][chip] = plus(w_ref[k][core, chip], r1[k][chip])

    def middle(k):
        arrived(SDB, k, rdb[k])
        acc[k][cx, BOT[k]] = plus(acc[k][cx, BOT[k]], rdb[k][...])
        x_bot(k).start()
        arrived(SDT, k, rdt[k])
        acc[k][cy, TOP[k]] = plus(acc[k][cy, TOP[k]], rdt[k][...])
        y_top(k).start()

    def finish(k):
        arrived(SXT, k, rx[k].at[TOP[k]])
        arrived(SYB, k, ry[k].at[BOT[k]])
        arrived(SXB, k, rx[k].at[BOT[k]])
        arrived(SYT, k, ry[k].at[TOP[k]])
        res[k][core, chip] = (acc[k][chip].astype(f32) + rx[k][...].astype(f32) + ry[k][...].astype(f32)).astype(bf)
        give_x(k).start()
        give_y(k).start()
        give_c(k).start()

    def spread(k):
        arrived(GX, k, res[k].at[core, cx])
        pass_y(k).start()
        c_x(k).start()
        arrived(GY, k, res[k].at[core, cy])
        pass_x(k).start()
        c_y(k).start()

    def last(k):
        arrived(GFY, k, res[k].at[core, cd, TOP[k]])
        c_a(k).start()
        arrived(GFX, k, res[k].at[core, cd, BOT[k]])
        c_b(k).start()

    def line_step(k):
        p = plane_at(z, 3 - k)
        line[p] = part_ref[p]
        @pl.when((z > 0) & (p >= z))
        def _():
            arrived(LU, p, rzu.at[p])
            line[p] = plus(line[p], rzu[p])
        @pl.when((z < 3) & (p <= z))
        def _():
            arrived(LD, p, rzd.at[p])
            line[p] = plus(line[p], rzd[p])
        @pl.when(p > z)
        def _(): line_up(p).start()
        @pl.when(p < z)
        def _(): line_down(p).start()

    def unit_rows(p):
        value = hidden_ref[p].astype(f32)
        scale = lax.rsqrt(jnp.mean(value * value, axis=-1, keepdims=True) + eps)
        return scale, value * scale

    def gain_row():
        sums[0, 0:8] = jnp.zeros((8, sums.shape[2]), f32)
        sums[0, 1:2] = ffn_ref[...]
        head_size = heads_ref.shape[1]
        sums[0, 2:3, 0:head_size] = heads_ref[0:1]
        sums[0, 2:3, head_size : 2 * head_size] = heads_ref[1:2]
        sums[0, 8:] = router_ref[...]
        def add_plane(p, _):
            sums[0, 0:1] += jnp.sum(part_ref[p].astype(f32) * unit_rows(p)[1], axis=0, keepdims=True)
            return 0
        lax.fori_loop(0, 4, add_plane, 0)
        small_copy(0).start()

    def own_rows():
        total = part_ref[z].astype(f32)
        @pl.when(z > 0)
        def _(): arrived(LU, z, rzu.at[z])
        @pl.when(z < 3)
        def _(): arrived(LD, z, rzd.at[z])
        total = total + jnp.where(z > 0, rzu[z].astype(f32), 0.0) + jnp.where(z < 3, rzd[z].astype(f32), 0.0)
        scale, unit = unit_rows(z)
        scaled = total * gain_ref[...]
        grad = scale * (scaled - unit * jnp.mean(unit * scaled, axis=-1, keepdims=True))
        rows[z] = (resid_ref[...] + grad).astype(bf)
        @pl.when(z < 3)
        def _(): row_up(z).start()
        @pl.when(z > 0)
        def _(): row_down(z).start()

    def row_step(k):
        p = plane_at(z, k)
        @pl.when(p < z)
        def _(): arrived(RU, p, rows.at[p])
        @pl.when(p > z)
        def _(): arrived(RD, p, rows.at[p])
        @pl.when((p < z) & (z < 3))
        def _(): row_up(p).start()
        @pl.when((p > z) & (z > 0))
        def _(): row_down(p).start()

    def small_copy(i):
        return pltpu.make_async_remote_copy(src_ref=sums.at[i], dst_ref=got.at[i], send_sem=ssend.at[i], recv_sem=srecv.at[i],
                                            device_id=partners[i], device_id_type=MESH)
    def small_step(i):
        small_copy(i).wait_recv()
        if i < 4:
            sums[i + 1] = sums[i] + got[i]
            small_copy(i + 1).start()
        else:
            small_out[...] = sums[i] + got[i]

    def ends(f):
        pl.when(~middle_plane)(f)
    def mids(f):
        pl.when(middle_plane)(f)

    to_core(0).start()
    input_part()
    ends(lambda: line_step(0))
    weight_part(1)
    begin(0)
    weight_part(2)
    begin(1)
    weight_part(3)
    begin(2)
    gain_row()
    begin(3)
    mids(lambda: line_step(0))
    ends(lambda: line_step(1))
    small_step(0)
    middle(0)
    middle(1)
    mids(lambda: line_step(1))
    mids(lambda: line_step(2))
    ends(lambda: line_step(2))
    middle(2)
    middle(3)
    small_step(1)
    own_rows()
    finish(0)
    finish(1)
    finish(2)
    finish(3)
    ends(lambda: row_step(1))
    mids(lambda: row_step(1))
    mids(lambda: row_step(2))
    spread(0)
    spread(1)
    small_step(2)
    mids(lambda: row_step(3))
    ends(lambda: row_step(2))
    spread(2)
    spread(3)
    last(0)
    small_step(3)
    ends(lambda: row_step(3))
    last(1)
    last(2)
    small_step(4)
    last(3)

    sib = 1 - core
    for k in range(4):
        for c in (to_core, far_x, far_y, x_top, x_bot, y_top, y_bot, give_x, give_y, give_c, pass_x, pass_y, c_x, c_y, c_a, c_b):
            c(k).wait_send()
        arrived(GC, k, res[k].at[sib, chip])
        arrived(GCX, k, res[k].at[sib, cx])
        arrived(GCY, k, res[k].at[sib, cy])
        arrived(GCA, k, res[k].at[sib, cd, TOP[k]])
        arrived(GCB, k, res[k].at[sib, cd, BOT[k]])
    def drain(p, _):
        @pl.when(p > z)
        def _(): line_up(p).wait_send()
        @pl.when(p < z)
        def _(): line_down(p).wait_send()
        @pl.when((z < 3) & (p <= z))
        def _(): row_up(p).wait_send()
        @pl.when((z > 0) & (p >= z))
        def _(): row_down(p).wait_send()
        return 0
    lax.fori_loop(0, 4, drain, 0)
    for i in range(5): small_copy(i).wait_send()

def final_totals(grad_heads, normed, proj_w, grad_out_w, router, ffn, heads, hidden, resid, gain, collective_id):
    vm = pl.BlockSpec(memory_space=pltpu.VMEM)
    planes = hidden.shape
    one = (2, 4, proj_w[0].shape[0] // 8, proj_w[0].shape[1])
    shapes = (grad_out_w.shape, one, one, one)
    small = (5, 8 + router.shape[0], router.shape[1])
    own = [pltpu.VMEM(one, bf)] * 3
    whole = [pltpu.VMEM(s[1:], bf) for s in shapes]
    quarter = [pltpu.VMEM(s[2:], bf) for s in shapes]
    half = [pltpu.VMEM((s[2] // 2, s[3]), bf) for s in shapes]
    return pl.pallas_call(
        totals_kernel,
        out_shape=tuple(jax.ShapeDtypeStruct(s, bf) for s in shapes) + (
            jax.ShapeDtypeStruct(planes, bf), jax.ShapeDtypeStruct(small[1:], f32)),
        in_specs=[vm] * 12,
        out_specs=(vm,) * 6,
        scratch_shapes=own + whole + whole + half + half + quarter + quarter + [
            pltpu.VMEM(planes, bf), pltpu.VMEM(planes, bf), pltpu.VMEM(planes, bf), pltpu.VMEM(planes, bf),
            pltpu.VMEM(small, f32), pltpu.VMEM(small, f32),
            pltpu.SemaphoreType.DMA((20, 4)), pltpu.SemaphoreType.DMA((20, 4)),
            pltpu.SemaphoreType.DMA((5,)), pltpu.SemaphoreType.DMA((5,)),
        ],
        compiler_params=pltpu.CompilerParams(collective_id=collective_id, has_side_effects=True, vmem_limit_bytes=62 << 20),
    )(grad_heads, normed, *proj_w, grad_out_w, router, ffn, heads, hidden, resid, gain)


def slot_experts(routed_low, gates, picked, grad_out, expert_routes, gate_weight, up_weight, down_weight):
    highest = lax.Precision.HIGHEST
    quarter, width = grad_out.shape
    top_count = expert_routes.shape[1]
    experts = picked.shape[2]
    capacity = max(2, 2 * quarter * top_count // experts)
    picked_wide = picked.astype(jnp.float32)
    grad_rows = grad_out.astype(jnp.float32)
    flat_route = expert_routes.reshape(-1)
    flat_pick = picked.reshape(-1, experts).astype(jnp.int32)
    rank = jnp.sum((jnp.cumsum(flat_pick, axis=0) - 1) * flat_pick, axis=1)
    place = flat_route * capacity + rank
    row_token = jnp.arange(quarter * top_count, dtype=jnp.int32) // top_count
    send_rows = (
        jnp.zeros((experts * capacity, width), jnp.bfloat16).at[place].set(routed_low[row_token])
    )
    arrived = lax.all_to_all(
        send_rows.reshape(experts, capacity, width), "exp", split_axis=0, concat_axis=1, tiled=True
    )
    rows_used = lax.all_gather(arrived, "tp", axis=1, tiled=True)
    gate_act = jnp.einsum(
        "erd,edf->erf", rows_used, gate_weight, preferred_element_type=jnp.float32
    )
    up_act = jnp.einsum("erd,edf->erf", rows_used, up_weight, preferred_element_type=jnp.float32)
    hidden_low = (jax.nn.silu(gate_act) * up_act).astype(jnp.bfloat16)
    partial_out = jnp.einsum(
        "erf,efd->erd", hidden_low, down_weight, preferred_element_type=jnp.float32
    )
    expert_out = lax.psum_scatter(partial_out, "tp", scatter_dimension=1, tiled=True)
    returned = lax.all_to_all(
        expert_out.astype(jnp.bfloat16), "exp", split_axis=1, concat_axis=0, tiled=True
    )
    back_rows = (
        returned.reshape(experts * capacity, width)[place]
        .reshape(quarter, top_count, width)
        .astype(jnp.float32)
    )
    moe = jnp.einsum("tk,tkd->td", gates, back_rows, precision=highest)
    grad_gates = jnp.einsum("tkd,td->tk", back_rows, grad_rows, precision=highest)
    grad_chosen = gates * (grad_gates - jnp.sum(gates * grad_gates, axis=-1, keepdims=True))
    grad_logits = jnp.einsum("tke,tk->te", picked_wide, grad_chosen, precision=highest)
    weighted_grad = (
        (gates[:, :, None] * grad_rows[:, None, :])
        .astype(jnp.bfloat16)
        .reshape(quarter * top_count, width)
    )
    send_grads = jnp.zeros((experts * capacity, width), jnp.bfloat16).at[place].set(weighted_grad)
    grad_arrived = lax.all_to_all(
        send_grads.reshape(experts, capacity, width), "exp", split_axis=0, concat_axis=1, tiled=True
    )
    sigmoid_gate = jax.nn.sigmoid(gate_act)
    silu_gate = gate_act * sigmoid_gate
    slope = sigmoid_gate * (1.0 + gate_act * (1.0 - sigmoid_gate))
    grad_used = lax.all_gather(grad_arrived, "tp", axis=1, tiled=True)
    grad_hid = jnp.einsum(
        "erd,efd->erf", grad_used, down_weight, preferred_element_type=jnp.float32
    )
    grad_down = jnp.einsum(
        "erf,erd->efd", hidden_low, grad_used, preferred_element_type=jnp.float32
    )
    grad_gate = (grad_hid * up_act * slope).astype(jnp.bfloat16)
    grad_up = (grad_hid * silu_gate).astype(jnp.bfloat16)
    grad_gate_w = jnp.einsum(
        "erd,erf->edf", rows_used, grad_gate, preferred_element_type=jnp.float32
    )
    grad_up_w = jnp.einsum("erd,erf->edf", rows_used, grad_up, preferred_element_type=jnp.float32)
    input_part = jnp.einsum(
        "erf,edf->erd", grad_gate, gate_weight, preferred_element_type=jnp.float32
    ) + jnp.einsum("erf,edf->erd", grad_up, up_weight, preferred_element_type=jnp.float32)
    grad_input = lax.psum_scatter(input_part, "tp", scatter_dimension=1, tiled=True).astype(
        jnp.bfloat16
    )
    grad_back = lax.all_to_all(grad_input, "exp", split_axis=1, concat_axis=0, tiled=True)
    expert_grad = jnp.sum(
        grad_back.reshape(experts * capacity, width)[place]
        .reshape(quarter, top_count, width)
        .astype(jnp.float32),
        axis=1,
    )
    return moe, grad_logits, expert_grad, grad_gate_w, grad_up_w, grad_down


def gate_pair(dense_gates):
    pad = ((0, 0), (0, gate_lanes // 2 - dense_gates.shape[1]))
    high = dense_gates.astype(bf)
    low = (dense_gates - high.astype(f32)).astype(bf)
    return [jnp.pad(high, pad), jnp.pad(low, pad)]


def per_device(
    fits,
    hidden_in,
    attn_gain,
    query_weight,
    key_weight,
    value_weight,
    qnorm_gain,
    knorm_gain,
    out_weight,
    ffn_gain,
    router_weight,
    gate_weight,
    up_weight,
    down_weight,
    expert_routes,
    seq_lengths,
    grad_out,
):
    highest = lax.Precision.HIGHEST
    group_rows = hidden_in.shape[0]
    width = hidden_in.shape[1]
    head_size = qnorm_gain.shape[0]
    quarter = grad_out.shape[0]
    experts = router_weight.shape[1]
    tp_index = lax.axis_index("tp")
    widened = hidden_in.astype(jnp.float32)
    segment, cosine, sine = rotary_tables(seq_lengths[0], group_rows, head_size)
    if fits:
        planes = (4, quarter, width)
        gains = jnp.stack([qnorm_gain, knorm_gain])
        tables = (
            jnp.concatenate([cosine[:, 0], cosine[:, 0]], axis=1),
            jnp.concatenate([-sine[:, 0], sine[:, 0]], axis=1),
            segment[:, None],
            segment[None],
        )
        attn_rows, normed_low, query_proj, key_proj, *heads, mixed_low, grads_all = open_exchange(
            hidden_in.reshape(planes),
            attn_gain[None],
            (query_weight, key_weight, value_weight, out_weight),
            gains,
            *tables,
            grad_out,
            5,
        )
    else:
        normed_one = rms_norm(widened, attn_gain)
        normed_low = normed_one.astype(jnp.bfloat16)
        same_seq = segment[:, None] == segment[None, :]

        def prepare(projected, gain):
            return head_prep(projected, gain, cosine, sine)

        query_proj = jnp.dot(normed_low, query_weight, preferred_element_type=jnp.float32)
        key_proj = jnp.dot(normed_low, key_weight, preferred_element_type=jnp.float32)
        value_proj = jnp.dot(normed_low, value_weight, preferred_element_type=jnp.float32)
        queries, query_back = jax.vjp(prepare, query_proj, qnorm_gain)
        keys, key_back = jax.vjp(prepare, key_proj, knorm_gain)
        query_low = queries.astype(jnp.bfloat16)
        key_low = keys.astype(jnp.bfloat16)
        value_low = value_proj.astype(jnp.bfloat16).reshape(group_rows, -1, head_size)
        scores = masked_scores(query_low, key_low, same_seq, head_size)
        top_score = jnp.max(scores, axis=-1, keepdims=True)
        log_total = top_score + jnp.log(jnp.sum(jnp.exp(scores - top_score), axis=-1, keepdims=True))
        probs_low = jnp.exp(scores - log_total).astype(jnp.bfloat16)
        mixed = jnp.einsum("hts,shd->thd", probs_low, value_low, preferred_element_type=jnp.float32)
        mixed_low = mixed.astype(jnp.bfloat16).reshape(group_rows, -1)
        attn_part = jnp.dot(mixed_low, out_weight, preferred_element_type=jnp.float32)
        attn_rows = lax.psum_scatter(attn_part, "tp", scatter_dimension=0, tiled=True)
    own_rows = lax.dynamic_slice_in_dim(widened, tp_index * quarter, quarter, 0)
    resid = own_rows + attn_rows
    normed_two, norm_two_back = jax.vjp(rms_norm, resid, ffn_gain)
    routed_low = normed_two.astype(jnp.bfloat16)
    logits = jnp.dot(routed_low, router_weight, preferred_element_type=jnp.float32)
    picked = expert_routes[:, :, None] == jnp.arange(experts, dtype=jnp.int32)[None, None, :]
    picked_wide = picked.astype(jnp.float32)
    chosen = jnp.einsum("tke,te->tk", picked_wide, logits, precision=highest)
    gates = jax.nn.softmax(chosen, axis=-1)
    grad_rows = grad_out.astype(jnp.float32)
    if fits:
        dense_gates = jnp.einsum("tke,tk->te", picked_wide, gates, precision=highest)
        act, grad_gate_w, grad_up_w, grad_down = gather_experts(
            jnp.concatenate([routed_low] + gate_pair(dense_gates), axis=1),
            grads_all,
            gate_weight,
            up_weight,
            down_weight,
        )
        (sums,) = scatter_sums(act, (gate_weight, up_weight), True, 2)
        expert_grad = sums[:, :width]
        grad_gates = sums[:, width : width + experts]
        grad_logits = dense_gates * (
            grad_gates - jnp.sum(dense_gates * grad_gates, axis=-1, keepdims=True)
        )
    else:
        moe, grad_logits, expert_grad, grad_gate_w, grad_up_w, grad_down = slot_experts(
            routed_low,
            gates,
            picked,
            grad_out,
            expert_routes,
            gate_weight,
            up_weight,
            down_weight,
        )
    grad_normed = (
        jnp.dot(grad_logits, router_weight.astype(jnp.float32).T, precision=highest) + expert_grad
    )
    grad_router = jnp.dot(routed_low.astype(jnp.float32).T, grad_logits, precision=highest)
    grad_resid, grad_ffn_gain = norm_two_back(grad_normed)
    grad_resid = grad_resid + grad_rows
    grad_low = grad_resid.astype(jnp.bfloat16)
    if fits:
        moe, grad_heads, grad_out_w, grad_gains = scatter_sums(
            act,
            (down_weight,),
            False,
            3,
            (
                grad_low,
                out_weight,
                mixed_low,
                *heads,
                query_proj,
                key_proj,
                gains,
                *tables,
            ),
        )
        grad_out_sum, *sums, grad_input_rows, small = final_totals(
            grad_heads,
            normed_low,
            (query_weight, key_weight, value_weight),
            grad_out_w.reshape(2, 4, -1, width),
            grad_router.T,
            grad_ffn_gain[None],
            grad_gains,
            hidden_in.reshape(planes),
            grad_resid,
            attn_gain[None],
            4,
        )
        grad_input_rows = grad_input_rows.reshape(group_rows, width)
        totals = tuple(
            part.reshape(-1, part.shape[3]).astype(f32) for part in (*sums, grad_out_sum)
        ) + (
            small[0],
            small[2, :head_size],
            small[2, head_size : 2 * head_size],
            small[1],
            small[8:].T,
        )
    else:
        grad_attn_low = lax.all_gather(grad_low, "tp", axis=0, tiled=True)
        grad_out_weight = jnp.dot(mixed_low.T, grad_attn_low, preferred_element_type=jnp.float32)
        grad_mixed = jnp.dot(grad_attn_low, out_weight.T, preferred_element_type=jnp.float32)
        grad_mixed_low = grad_mixed.astype(jnp.bfloat16).reshape(group_rows, -1, head_size)
        probs = jnp.exp(masked_scores(query_low, key_low, same_seq, head_size) - log_total)
        grad_probs = jnp.einsum(
            "thd,shd->hts", grad_mixed_low, value_low, preferred_element_type=jnp.float32
        )
        grad_value = jnp.einsum(
            "hts,thd->shd", probs_low, grad_mixed_low, preferred_element_type=jnp.float32
        )
        row_delta = jnp.sum(probs * grad_probs, axis=-1, keepdims=True)
        grad_scores = (probs * (grad_probs - row_delta)).astype(jnp.bfloat16)
        grad_query = jnp.einsum(
            "hts,shd->thd", grad_scores, key_low, preferred_element_type=jnp.float32
        ) / math.sqrt(head_size)
        grad_key = jnp.einsum(
            "hts,thd->shd", grad_scores, query_low, preferred_element_type=jnp.float32
        ) / math.sqrt(head_size)
        grad_query_proj, grad_qgain = query_back(grad_query)
        grad_key_proj, grad_kgain = key_back(grad_key)
        grad_query_low = grad_query_proj.astype(jnp.bfloat16)
        grad_key_low = grad_key_proj.astype(jnp.bfloat16)
        grad_value_low = grad_value.reshape(group_rows, -1).astype(jnp.bfloat16)
        normed_part = (
            jnp.dot(grad_query_low, query_weight.T, preferred_element_type=jnp.float32)
            + jnp.dot(grad_key_low, key_weight.T, preferred_element_type=jnp.float32)
            + jnp.dot(grad_value_low, value_weight.T, preferred_element_type=jnp.float32)
        )
        grad_query_w = jnp.dot(normed_low.T, grad_query_low, preferred_element_type=jnp.float32)
        grad_key_w = jnp.dot(normed_low.T, grad_key_low, preferred_element_type=jnp.float32)
        grad_value_w = jnp.dot(normed_low.T, grad_value_low, preferred_element_type=jnp.float32)
        scale_one = lax.rsqrt(jnp.mean(widened * widened, axis=-1, keepdims=True) + eps)
        unit_one = widened * scale_one
        grad_attn_gain = jnp.sum(normed_part * unit_one, axis=0)
        grad_normed_one = lax.psum(normed_part.astype(bf), "tp").astype(f32)
        scaled = grad_normed_one * attn_gain
        grad_from_norm = scale_one * (
            scaled - unit_one * jnp.mean(unit_one * scaled, axis=-1, keepdims=True)
        )
        grad_input_rows = (grad_attn_low.astype(f32) + grad_from_norm).astype(jnp.bfloat16)
        low_totals = lax.psum(
            tuple(
                part.astype(jnp.bfloat16)
                for part in (grad_query_w, grad_key_w, grad_value_w, grad_out_weight)
            ),
            "exp",
        )
        small = lax.psum(
            (grad_attn_gain, grad_qgain, grad_kgain, grad_ffn_gain, grad_router), ("exp", "tp")
        )
        totals = tuple(part.astype(jnp.float32) for part in low_totals) + small
    block_out = (resid + moe).astype(jnp.bfloat16)
    return (
        block_out,
        grad_input_rows,
        totals[4],
        totals[0],
        totals[1],
        totals[2],
        totals[3],
        totals[5],
        totals[6],
        totals[7],
        totals[8],
        grad_gate_w,
        grad_up_w,
        grad_down,
    )


def solution(mesh):
    in_specs = (
        P("exp", None),
        P(),
        P(None, "tp"),
        P(None, "tp"),
        P(None, "tp"),
        P(),
        P(),
        P("tp", None),
        P(),
        P(),
        P("exp", None, "tp"),
        P("exp", None, "tp"),
        P("exp", "tp", None),
        P(("exp", "tp"), None),
        P("exp", None),
        P(("exp", "tp"), None),
    )
    out_specs = (
        P(("exp", "tp"), None),
        P("exp", None),
        P(),
        P(None, "tp"),
        P(None, "tp"),
        P(None, "tp"),
        P("tp", None),
        P(),
        P(),
        P(),
        P(),
        P("exp", None, "tp"),
        P("exp", None, "tp"),
        P("exp", "tp", None),
    )
    fits = dict(mesh.shape) == {"exp": 8, "tp": 4}
    return jax.shard_map(
        functools.partial(per_device, fits), mesh=mesh, in_specs=in_specs, out_specs=out_specs, check_vma=False
    )
```
